32 devices in a mesh: dp: 16 (over z, y, core), mp: 2 (over x).
Axes of the slice: x: 2, y: 2, z: 4, core: 2. Of those that a mesh axis runs over, the one named last changes fastest.
Arguments:
- byte_states: bfloat16 [64, 2048, 512], P('dp', None, 'mp'), may hold values from -6 to 6
- frontier: float32 [64, 2048], P('dp'), may hold values from 0.05 to 0.95
- lengths: int32 [64], P('dp'), may hold values from 204 to 2048
- gain_attn: float32 [512], replicated, may hold values from 0.5 to 1.5
- w_query: bfloat16 [512, 512], P(None, 'mp'), may hold values from -0.125 to 0.125
- w_key: bfloat16 [512, 512], P(None, 'mp'), may hold values from -0.125 to 0.125
- w_value: bfloat16 [512, 512], P(None, 'mp'), may hold values from -0.25 to 0.25
- w_attn_out: bfloat16 [512, 512], P('mp'), may hold values from -1 to 1
- rel_bias: float32 [32, 8], P(None, 'mp'), may hold values from -4 to 4
- gain_mlp: float32 [512], replicated, may hold values from 0.5 to 1.5
- w_hidden: bfloat16 [512, 2048], P(None, 'mp'), may hold values from -0.25 to 0.25
- w_mlp_out: bfloat16 [2048, 512], P('mp'), may hold values from -0.125 to 0.125
- cotangent: bfloat16 [64, 512, 512], P('dp', None, 'mp'), may hold values from -6 to 6
Outputs:
- blocks: bfloat16 [64, 512, 512], P('dp', None, 'mp')
- grad_bytes: bfloat16 [64, 2048, 512], P('dp', None, 'mp')
- grad_frontier: float32 [64, 2048], P('dp')
- grad_gain_attn: float32 [512], replicated
- grad_w_query: float32 [512, 512], P(None, 'mp')
- grad_w_key: float32 [512, 512], P(None, 'mp')
- grad_w_value: float32 [512, 512], P(None, 'mp')
- grad_w_attn_out: float32 [512, 512], P('mp')
- grad_rel_bias: float32 [32, 8], P(None, 'mp')
- grad_gain_mlp: float32 [512], replicated
- grad_w_hidden: float32 [512, 2048], P(None, 'mp')
- grad_w_mlp_out: float32 [2048, 512], P('mp')
The draws below stay inside these ranges and needn't reach their ends.
All inputs are finite; a program needn't handle non-finite values.
Results may differ from the reference program's by a relative error of at most 0.022.
The reference program's roundings to bfloat16 on the way count: a program that leaves them out, or rounds other values in their place, can miss the bound.
Values may be sent and summed in bfloat16 or wider, within the bound.
No kernel may reach another device: no remote copies, remote signals or barrier semaphores. Data moves between devices by JAX's collectives and lax.ppermute only.
A program may use at most 192 MiB of HBM per device.

```python
import math
import jax
import jax.numpy as jnp
import numpy as np
from jax import lax

D = 512
HEADS = 8
HEAD = 64
FF = 2048
BUCKETS = 32
REACH = 128
BLOCKS = 512
BYTES = 2048
ITEMS = 64


def plant(drawn, own_key, low, largest):
    longest = drawn.shape.index(max(drawn.shape))
    spots = []
    for shift in (0, 1):
        where = [jax.random.randint(jax.random.fold_in(own_key, axis), (), 0, length) for axis, length in enumerate(drawn.shape)]
        where[longest] = (where[longest] + shift) % drawn.shape[longest]
        spots.append(tuple(where))
    return drawn.at[spots[0]].set(low).at[spots[1]].set(largest)


def levels(key, shape, shards, low, largest):
    level, own = 1.0, jax.random.fold_in(key, 6)
    for dim, shards_of in shards:
        heights = jnp.exp(jax.random.uniform(jax.random.fold_in(own, dim), (shards_of,), jnp.float32, low / len(shards), largest / len(shards)))
        level = level * jnp.repeat(heights, shape[dim] // shards_of).reshape([-1 if axis == dim else 1 for axis in range(len(shape))])
    return level


def normal_values(rng, extent, deviation, reach, pieces=(), kind=jnp.bfloat16):
    values = jax.random.normal(rng, extent, jnp.float32) * deviation
    if len(pieces) > 0:
        values = levels(rng, extent, pieces, -0.22, 0.18) * values
    return jnp.clip(values, min=-reach, max=reach).astype(kind)


def setup_inputs(seed: int = 0) -> dict:
    key_of = jax.random.split(jax.random.key(seed), 14)
    return {
        "byte_states": normal_values(key_of[0], (ITEMS, BYTES, D), 1.0, 6.0, ((0, 16), (2, 2))),
        "frontier": jnp.clip(jnp.exp(math.log(0.95) - 2.944439 * jax.random.uniform(key_of[1], (ITEMS, BYTES), jnp.float32) ** levels(key_of[1], (ITEMS, BYTES), ((0, 16),), -0.2, 0.2)), 0.05, 0.95),
        "lengths": plant(jax.random.randint(key_of[2], (ITEMS,), BYTES // 10, BYTES + 1), jax.random.fold_in(key_of[2], 1), BYTES // 10, BYTES).astype(jnp.int32),
        "gain_attn": jnp.clip(1.0 + 0.1 * jax.random.normal(key_of[3], (D,), jnp.float32), 0.5, 1.5),
        "w_query": normal_values(key_of[4], (D, HEADS * HEAD), (4 * D) ** -0.5, 0.125, ((1, 2),)),
        "w_key": normal_values(key_of[5], (D, HEADS * HEAD), (4 * D) ** -0.5, 0.125, ((1, 2),)),
        "w_value": normal_values(key_of[6], (D, HEADS * HEAD), D ** -0.5, 0.25, ((1, 2),)),
        "w_attn_out": normal_values(key_of[7], (HEADS * HEAD, D), (HEADS * HEAD // 16) ** -0.5, 1.0, ((0, 2),)),
        "rel_bias": normal_values(key_of[8], (BUCKETS, HEADS), 1.0, 4.0, ((1, 2),), jnp.float32),
        "gain_mlp": jnp.clip(1.0 + 0.1 * jax.random.normal(key_of[9], (D,), jnp.float32), 0.5, 1.5),
        "w_hidden": normal_values(key_of[10], (D, FF), D ** -0.5, 0.25, ((1, 2),)),
        "w_mlp_out": normal_values(key_of[11], (FF, D), FF ** -0.5, 0.125, ((0, 2),)),
        "cotangent": normal_values(key_of[12], (ITEMS, BLOCKS, D), 1.0, 6.0, ((0, 16), (2, 2))),
    }


EPSILON = 1e-06
SHARPNESS = 2.0
MASKED_SCORE = -1000000000.0
PRECISE = lax.Precision.HIGHEST

@jax.custom_vjp
def low(v):
    return lax.optimization_barrier(v.astype(jnp.bfloat16)).astype(jnp.float32)

@jax.custom_vjp
def low_back(v):
    return v

def low_keep(v):
    return (low(v), None)

def low_pass(kept, grad):
    return (grad,)

def back_keep(v):
    return (v, None)

def back_low(kept, grad):
    return (low(grad),)
low.defvjp(low_keep, low_pass)
low_back.defvjp(back_keep, back_low)

def bucket_onehot(blocks, buckets, max_reach):
    half_count = buckets // 2
    exact_count = half_count // 2
    chosen = []
    for offset in range(1 - blocks, blocks):
        distance = abs(offset)
        if distance < exact_count:
            place = distance
        else:
            place = min(half_count - 1, exact_count + math.floor(math.log(distance / exact_count) / math.log(max_reach / exact_count) * (half_count - exact_count)))
        chosen.append(place + (half_count if offset > 0 else 0))
    return np.eye(buckets, dtype=np.float32)[np.array(chosen, dtype=np.int32)]

def relative_index(blocks):
    return np.arange(blocks)[None, :] - np.arange(blocks)[:, None] + blocks - 1

def rms_normed(values, gain):
    return values * lax.rsqrt(lax.optimization_barrier(jnp.mean(values * values, axis=-1, keepdims=True)) + EPSILON) * gain

def smooth_gelu(values):
    return 0.5 * values * (1.0 + jnp.tanh(0.7978845608028654 * (values + 0.044715 * values * values * values)))

def pool_kernel(frontier_row, length, blocks):
    byte_count = frontier_row.shape[0]
    valid_bytes = (jnp.arange(byte_count) < length).astype(jnp.float32)
    block_count = (length + 3) // 4
    live_blocks = (jnp.arange(blocks) < block_count).astype(jnp.float32)
    running = jnp.cumsum(frontier_row * valid_bytes)
    positions = block_count.astype(jnp.float32) * running / running[-1]
    offset = positions[None, :] - jnp.arange(blocks).astype(jnp.float32)[:, None] - 0.5
    return live_blocks[:, None] * valid_bytes[None, :] * jnp.exp(-SHARPNESS * offset * offset)

def layer_item(params, item):
    gain_attn, w_query, w_key, w_value, w_attn_out, rel_bias, gain_mlp, w_hidden, w_mlp_out = params
    byte_rows, frontier_row, length = item
    blocks = BLOCKS
    kernel = low(pool_kernel(frontier_row, length, blocks))
    pooled = low(low_back(jnp.dot(kernel, byte_rows.astype(jnp.float32), precision=PRECISE)))
    live_blocks = (jnp.arange(blocks) < (length + 3) // 4).astype(jnp.float32)
    normed_first = low(rms_normed(pooled, gain_attn))
    query = low(low_back(jnp.dot(normed_first, w_query, precision=PRECISE))).reshape(blocks, HEADS, HEAD)
    key_rows = low(low_back(jnp.dot(normed_first, w_key, precision=PRECISE))).reshape(blocks, HEADS, HEAD)
    value_rows = low(low_back(jnp.dot(normed_first, w_value, precision=PRECISE))).reshape(blocks, HEADS, HEAD)
    table = jnp.asarray(bucket_onehot(blocks, BUCKETS, REACH), jnp.float32)
    spread = jnp.dot(table, rel_bias, precision=PRECISE)
    bias = spread.T[:, relative_index(blocks)]
    scores = low_back(jnp.einsum('qhd,khd->hqk', query, key_rows, precision=PRECISE) + bias)
    scores = jnp.where(live_blocks[None, None, :] > 0.5, scores, MASKED_SCORE)
    top_score = lax.optimization_barrier(jnp.max(scores, axis=-1, keepdims=True))
    expo = jnp.exp(scores - top_score)
    weights = low(expo / lax.optimization_barrier(jnp.sum(expo, axis=-1, keepdims=True)))
    attended = low(low_back(jnp.einsum('hqk,khd->qhd', weights, value_rows, precision=PRECISE).reshape(blocks, HEADS * HEAD)))
    mixed = low_back(jnp.dot(attended, w_attn_out, precision=PRECISE))
    middle = pooled + mixed
    normed_second = low(rms_normed(middle, gain_mlp))
    hidden_pre = low_back(jnp.dot(normed_second, w_hidden, precision=PRECISE))
    hidden_act = low(smooth_gelu(hidden_pre))
    result = low_back(jnp.dot(hidden_act, w_mlp_out, precision=PRECISE))
    return live_blocks[:, None] * (middle + result)

def reference(byte_states, frontier, lengths, gain_attn, w_query, w_key, w_value, w_attn_out, rel_bias, gain_mlp, w_hidden, w_mlp_out, cotangent):
    params = tuple((weight.astype(jnp.float32) for weight in (gain_attn, w_query, w_key, w_value, w_attn_out, rel_bias, gain_mlp, w_hidden, w_mlp_out)))

    def forward(byte_input, frontier_input, params_input):

        def one_item(carry, item):
            return (carry, jax.checkpoint(layer_item)(params_input, item))
        _, stacked = lax.scan(one_item, jnp.zeros((), jnp.float32), (byte_input, frontier_input, lengths))
        return stacked
    outputs, pull = jax.vjp(forward, byte_states, frontier, params)
    grad_input, grad_front, grad_params = pull(cotangent.astype(jnp.float32))
    return (outputs.astype(jnp.bfloat16), grad_input.astype(jnp.bfloat16), grad_front, grad_params[0], grad_params[1], grad_params[2], grad_params[3], grad_params[4], grad_params[5], grad_params[6], grad_params[7], grad_params[8])
```

```python
import functools
import math

import jax
import jax.numpy as jnp
import numpy as np
from jax import lax
from jax.experimental import pallas as pl
from jax.experimental.pallas import tpu as pltpu
from jax.sharding import PartitionSpec as P

BUCKETS = 32
REACH = 128
BLOCKS = 512
WRAP = 2 * BLOCKS
SHARDS = 8

EPSILON = 1e-06
SHARPNESS = 2.0
MASKED_SCORE = -1000000000.0
OUTSIDE = -10000.0
REACH_OUT = 8.0
PRECISE = lax.Precision.HIGHEST
ROOT = 0.7978845608028654
CUBIC = 0.044715
VMEM_LIMIT = 60 * 1024 * 1024

F32 = jnp.float32
BF16 = jnp.bfloat16
ANY = pl.BlockSpec(memory_space=pl.ANY)
NN = (((1,), (0,)), ((), ()))
NT = (((1,), (1,)), ((), ()))
TN = (((0,), (0,)), ((), ()))


def mm(a, b, dims=NN):
    return lax.dot_general(a, b, dims, preferred_element_type=F32)


def bucket_of(offset):
    half_count = BUCKETS // 2
    exact_count = half_count // 2
    distance = abs(offset)
    if distance < exact_count:
        place = distance
    else:
        place = min(
            half_count - 1,
            exact_count
            + math.floor(
                math.log(distance / exact_count)
                / math.log(REACH / exact_count)
                * (half_count - exact_count)
            ),
        )
    return place + (half_count if offset > 0 else 0)


def offset_tables():
    forward = np.zeros((WRAP, BUCKETS), np.float32)
    backward = np.zeros((WRAP, BUCKETS), np.float32)
    collect = np.zeros((WRAP, 128), np.float32)
    for offset in range(1 - BLOCKS, BLOCKS):
        bucket = bucket_of(offset)
        forward[offset % WRAP, bucket] = 1.0
        backward[(-offset) % WRAP, bucket] = 1.0
        collect[(384 - offset) % WRAP, bucket] = 1.0
    return forward, backward, collect


def params(semantics=None):
    return pltpu.CompilerParams(
        vmem_limit_bytes=VMEM_LIMIT,
        dimension_semantics=semantics,
    )


def pool_rows(item, length, count, pos_ref, bytes_ref, out_ref, acc):
    acc[...] = jnp.zeros_like(acc)
    chunks = bytes_ref.shape[1] // 256
    rows, lows, highs = [], [], []
    for chunk in range(chunks):
        row = pos_ref[pl.ds(item, 1), chunk * 256 : (chunk + 1) * 256]
        rows.append(row)
        lows.append(jnp.min(jnp.where(row < 0.0, 1e6, row)))
        highs.append(jnp.max(row))
    for chunk in range(chunks):
        for tile in range(BLOCKS // 128):
            near = jnp.logical_and(
                highs[chunk] > tile * 128 - REACH_OUT,
                lows[chunk] < tile * 128 + 128 + REACH_OUT,
            )

            @pl.when(jnp.logical_and(near, tile * 128 < count))
            def _():
                centre = (
                    lax.broadcasted_iota(jnp.int32, (128, 256), 0).astype(F32) + tile * 128 + 0.5
                )
                offset = rows[chunk] - centre
                kernel = jnp.exp(-SHARPNESS * offset * offset).astype(BF16)
                acc[tile * 128 : (tile + 1) * 128, :] += mm(
                    kernel, bytes_ref[0, chunk * 256 : (chunk + 1) * 256, :]
                )

    live = lax.broadcasted_iota(jnp.int32, acc.shape, 0) < count
    out_ref[0] = jnp.where(live, acc[...], 0.0).astype(BF16)


def masked_positions(info, frontier_ref, pos_ref):
    items, byte_count = frontier_ref.shape
    lane = lax.broadcasted_iota(jnp.int32, (items, byte_count), 1)
    row = lax.broadcasted_iota(jnp.int32, (items, byte_count), 0)
    length = jnp.zeros((items, byte_count), jnp.int32)
    for item in range(items):
        length = jnp.where(row == item, info[4 + item], length)
    valid = lane < length
    running = jnp.where(valid, frontier_ref[...], 0.0)
    step = 1
    while step < byte_count:
        running = running + jnp.where(lane >= step, pltpu.roll(running, step, 1), 0.0)
        step *= 2
    count = lax.shift_right_logical(length + 3, 2).astype(F32)
    total = running[:, byte_count - 1 :]
    pos_ref[...] = jnp.where(valid, count * running / total, OUTSIDE)


def pool_first_kernel(info, frontier_ref, bytes_ref, out_ref, pos_ref, acc):
    step = pl.program_id(0)

    @pl.when(step == 0)
    def _():
        masked_positions(info, frontier_ref, pos_ref)

    item = (1 - info[0]) * 2 + step
    length = info[4 + item]
    pool_rows(item, length, lax.shift_right_logical(length + 3, 2), pos_ref, bytes_ref, out_ref, acc)


def pool_second_kernel(info, pos_ref, bytes_ref, out_ref, acc):
    item = info[0] * 2 + pl.program_id(0)
    length = info[4 + item]
    pool_rows(item, length, lax.shift_right_logical(length + 3, 2), pos_ref, bytes_ref, out_ref, acc)


def pool_forward(info, frontier, byte_states):
    items, byte_count, share = byte_states.shape
    half = items // 2
    out_block = pl.BlockSpec((1, BLOCKS, share), lambda i, info: (i, 0, 0))
    rows_block = pl.BlockSpec((items, byte_count), lambda i, info: (0, 0))
    out_shape = jax.ShapeDtypeStruct((half, BLOCKS, share), BF16)
    send, positions = pl.pallas_call(
        pool_first_kernel,
        grid_spec=pltpu.PrefetchScalarGridSpec(
            num_scalar_prefetch=1,
            grid=(half,),
            in_specs=[
                rows_block,
                pl.BlockSpec((1, byte_count, share), lambda i, info: ((1 - info[0]) * 2 + i, 0, 0)),
            ],
            out_specs=[out_block, rows_block],
            scratch_shapes=[pltpu.VMEM((BLOCKS, share), F32)],
        ),
        out_shape=[out_shape, jax.ShapeDtypeStruct((items, byte_count), F32)],
        compiler_params=params(("arbitrary",)),
        name="pool_send",
    )(info, frontier, byte_states)
    keep = pl.pallas_call(
        pool_second_kernel,
        grid_spec=pltpu.PrefetchScalarGridSpec(
            num_scalar_prefetch=1,
            grid=(half,),
            in_specs=[
                rows_block,
                pl.BlockSpec((1, byte_count, share), lambda i, info: (info[0] * 2 + i, 0, 0)),
            ],
            out_specs=out_block,
            scratch_shapes=[pltpu.VMEM((BLOCKS, share), F32)],
        ),
        out_shape=out_shape,
        compiler_params=params(("arbitrary",)),
        name="pool_keep",
    )(info, positions, byte_states)
    return send, keep, positions


def pool_back_body(item, length, pos_ref, bytes_ref, grads_ref, out_ref, part_ref):
    count = lax.shift_right_logical(length + 3, 2)
    chunks = bytes_ref.shape[1] // 256
    rows, lows, highs = [], [], []
    for chunk in range(chunks):
        row = pos_ref[pl.ds(item, 1), chunk * 256 : (chunk + 1) * 256]
        rows.append(row)
        lows.append(jnp.min(jnp.where(row < 0.0, 1e6, row)))
        highs.append(jnp.max(row))
    ones = jnp.ones((8, 128), BF16)

    def scoped(acc, terms):
        for chunk in range(chunks):
            span = slice(chunk * 256, (chunk + 1) * 256)

            @pl.when(chunk * 256 >= length)
            def _():
                out_ref[0, span, :] = jnp.zeros((256, out_ref.shape[2]), BF16)
                part_ref[0, :, span] = jnp.zeros((1, 256), F32)

            @pl.when(chunk * 256 < length)
            def _():
                acc[...] = jnp.zeros_like(acc)
                terms[...] = jnp.zeros_like(terms)
                column = jnp.transpose(jnp.broadcast_to(rows[chunk], (128, 256)))
                for tile in range(BLOCKS // 128):
                    near = jnp.logical_and(
                        highs[chunk] > tile * 128 - REACH_OUT,
                        lows[chunk] < tile * 128 + 128 + REACH_OUT,
                    )

                    @pl.when(jnp.logical_and(near, tile * 128 < count))
                    def _():
                        centre = (
                            lax.broadcasted_iota(jnp.int32, (256, 128), 1).astype(F32)
                            + tile * 128
                            + 0.5
                        )
                        offset = column - centre
                        kernel = jnp.exp(-SHARPNESS * offset * offset)
                        grads = grads_ref[tile * 128 : (tile + 1) * 128, :]
                        acc[...] += mm(kernel.astype(BF16), grads)
                        slope = mm(bytes_ref[0, span, :], grads, NT)
                        terms[...] += slope * kernel * offset

                out_ref[0, span, :] = acc[...].astype(BF16)
                term = terms[...]
                high = term.astype(BF16)
                low = (term - high.astype(F32)).astype(BF16)
                summed = mm(ones, high, NT) + mm(ones, low, NT)
                part_ref[0, :, span] = -4.0 * summed[0:1, :]

    pl.run_scoped(
        scoped, pltpu.VMEM((256, out_ref.shape[2]), F32), pltpu.VMEM((256, 128), F32)
    )


def pool_back_own_kernel(info, pos_ref, bytes_ref, grads_ref, out_ref, part_ref):
    item = info[0] * 2 + pl.program_id(0)
    pool_back_body(item, info[4 + item], pos_ref, bytes_ref, grads_ref.at[0], out_ref, part_ref)


def pool_back_other_kernel(
    info, pos_ref, bytes_ref, grads_ref, out_held, part_held, out_ref, part_ref
):
    item = (1 - info[0]) * 2 + pl.program_id(0)
    pool_back_body(item, info[4 + item], pos_ref, bytes_ref, grads_ref.at[0], out_ref, part_ref)


def pool_backward(info, positions, byte_states, grads, held, mine):
    items, byte_count, share = byte_states.shape
    half = items // 2

    def place(i, info):
        return (info[0] if mine else 1 - info[0]) * 2 + i

    in_specs = [
        pl.BlockSpec((items, byte_count), lambda i, info: (0, 0)),
        pl.BlockSpec((1, byte_count, share), lambda i, info: (place(i, info), 0, 0)),
        pl.BlockSpec((1, BLOCKS, share), lambda i, info: (i, 0, 0)),
    ]
    args = [info, positions, byte_states, grads]
    if not mine:
        in_specs += [ANY, ANY]
        args += list(held)
    return pl.pallas_call(
        pool_back_own_kernel if mine else pool_back_other_kernel,
        grid_spec=pltpu.PrefetchScalarGridSpec(
            num_scalar_prefetch=1,
            grid=(half,),
            in_specs=in_specs,
            out_specs=[
                pl.BlockSpec((1, byte_count, share), lambda i, info: (place(i, info), 0, 0)),
                pl.BlockSpec((1, 1, byte_count), lambda i, info: (place(i, info), 0, 0)),
            ],
        ),
        out_shape=[
            jax.ShapeDtypeStruct((items, byte_count, share), BF16),
            jax.ShapeDtypeStruct((items, 1, byte_count), F32),
        ],
        input_output_aliases={} if mine else {4: 0, 5: 1},
        compiler_params=params(("arbitrary",)),
        name="pool_back_own" if mine else "pool_back_other",
    )(*args)


def frontier_kernel(info, mine_ref, theirs_ref, pos_ref, frontier_ref, out_ref):
    items, byte_count = frontier_ref.shape
    lane = lax.broadcasted_iota(jnp.int32, (items, byte_count), 1)
    row = lax.broadcasted_iota(jnp.int32, (items, byte_count), 0)
    length = jnp.zeros((items, byte_count), jnp.int32)
    for item in range(items):
        length = jnp.where(row == item, info[4 + item], length)
    valid = lane < length
    total = jnp.sum(jnp.where(valid, frontier_ref[...], 0.0), axis=1, keepdims=True)
    terms = jnp.where(valid, mine_ref[:, 0, :] + theirs_ref[:, 0, :], 0.0)
    weighted = jnp.sum(terms * pos_ref[...], axis=1, keepdims=True)
    step = 1
    while step < byte_count:
        moved = pltpu.roll(terms, byte_count - step, 1)
        terms = terms + jnp.where(lane < byte_count - step, moved, 0.0)
        step *= 2
    count = lax.shift_right_logical(length + 3, 2).astype(F32)
    out_ref[...] = jnp.where(valid, (terms * count - weighted) / total, 0.0)


def frontier_gradient(info, mine, theirs, positions, frontier):
    return pl.pallas_call(
        frontier_kernel,
        grid_spec=pltpu.PrefetchScalarGridSpec(
            num_scalar_prefetch=1,
            grid=(1,),
            in_specs=[
                pl.BlockSpec(x.shape, functools.partial(lambda n, i, info: (0,) * n, x.ndim))
                for x in (mine, theirs, positions, frontier)
            ],
            out_specs=pl.BlockSpec(frontier.shape, lambda i, info: (0, 0)),
        ),
        out_shape=jax.ShapeDtypeStruct(frontier.shape, F32),
        compiler_params=params(("arbitrary",)),
        name="frontier_sum",
    )(info, mine, theirs, positions, frontier)


def build_strips(spread_ref, strips):
    for head in range(strips.shape[0]):
        row = jnp.broadcast_to(spread_ref[head : head + 1, :], (128, WRAP))
        turned = pltpu.roll(row, 384, 1, stride=1, stride_axis=0)
        strips[head] = turned[:, :896]


def gather_halves(info, target, own_ref, other_ref):
    first = pl.multiple_of(info[0] * 256, 256)
    second = pl.multiple_of((1 - info[0]) * 256, 256)
    target[:, pl.ds(first, 256)] = own_ref[0]
    target[:, pl.ds(second, 256)] = other_ref[0]


def layer_kernel(
    info,
    own_ref,
    other_ref,
    cot_own_ref,
    cot_other_ref,
    spread_ref,
    gain_attn_ref,
    gain_mlp_ref,
    w_query,
    w_key,
    w_value,
    w_out,
    w_hidden,
    w_mlp,
    attn_parts,
    out_parts,
    ff_parts,
    blocks_keep,
    blocks_send,
    qkv_ref,
    log_ref,
    grad_att_ref,
    grad_mid_ref,
    joined_ref,
    ff_keep,
    ff_send,
    gain_out,
    w_qkv,
    w_o,
    w_hid,
    w_mid,
    strips,
    pooled,
    top,
    middle,
    attended,
    logs,
    result,
    back,
    acc_hid,
    acc_mid,
    acc_out,
    acc_gain,
    sems,
):
    step = pl.program_id(0)
    mp, core, way, place = info[0], info[1], info[2], info[3]
    length = info[4 + mp * 2 + step]
    count = lax.shift_right_logical(length + 3, 2)

    def copies(first_group):
        early, late = [], []
        near = pl.multiple_of(core * 128, 128)
        far = pl.multiple_of((1 - core) * 128, 128)
        for part, start in ((0, near), (1, far)):
            for index, weight in enumerate((w_query, w_key, w_value)):
                early.append(
                    (weight.at[:, pl.ds(start, 128)], w_qkv.at[:, pl.ds(index * 512 + part * 128, 128)])
                )
            early.append((w_out.at[pl.ds(start, 128), :], w_o.at[pl.ds(part * 128, 128), :]))
        for part, start in (
            (0, pl.multiple_of(core * 512, 512)),
            (1, pl.multiple_of((1 - core) * 512, 512)),
        ):
            late.append((w_hidden.at[:, pl.ds(start, 512)], w_hid.at[part]))
            late.append((w_mlp.at[pl.ds(start, 512), :], w_mid.at[part]))
        for part in range(2):
            for side in range(2):
                turn = way if side == 0 else 1 - way
                rows = pl.multiple_of(turn * 256, 256)
                few = pl.multiple_of(turn * 64, 64)
                source = attn_parts[part * 2 + side]
                for index in range(3):
                    early.append(
                        (
                            source.at[:, pl.ds(index * 128, 128)],
                            w_qkv.at[pl.ds(rows, 256), pl.ds(index * 512 + 256 + part * 128, 128)],
                        )
                    )
                early.append(
                    (
                        out_parts[part * 2 + side],
                        w_o.at[pl.ds(256 + part * 128 + few, 64), :],
                    )
                )
                source = ff_parts[part * 2 + side]
                late.append((source.at[0], w_hid.at[2 + part, pl.ds(rows, 256), :]))
                late.append((source.at[1], w_mid.at[2 + part, pl.ds(rows, 256), :]))
        def make(pairs, first):
            return [
                pltpu.make_async_copy(source, target, sems.at[first + index])
                for index, (source, target) in enumerate(pairs)
            ]

        return make(early, 0) if first_group else make(late, len(early))

    @pl.when(step == 0)
    def _():
        early = copies(True)
        for copy in early + copies(False):
            copy.start()
        build_strips(spread_ref, strips)
        for copy in early:
            copy.wait()
        joined_ref[...] = w_qkv[...]

    gather_halves(info, pooled, own_ref, other_ref)
    gather_halves(info, top, cot_own_ref, cot_other_ref)
    live_rows = lax.broadcasted_iota(jnp.int32, (BLOCKS, 1), 0) < count
    top[...] = jnp.where(live_rows, top[...].astype(F32), 0.0).astype(BF16)

    wide = pooled[...].astype(F32)
    scale = lax.rsqrt(jnp.mean(wide * wide, axis=1, keepdims=True) + EPSILON)
    normed = (wide * scale * gain_attn_ref[...]).astype(BF16)
    qkv_ref[0] = mm(normed, w_qkv[...]).astype(BF16)
    logs[...] = jnp.zeros_like(logs)
    live_keys = lax.broadcasted_iota(jnp.int32, (1, BLOCKS), 1) < count
    lane = lax.broadcasted_iota(jnp.int32, (256, 128), 1)

    def heads_pair(pair, carry):
        off = pl.multiple_of(pair * 128, 128)
        keys = qkv_ref[0, :, pl.ds(512 + off, 128)]
        values = qkv_ref[0, :, pl.ds(1024 + off, 128)]
        for half in range(2):
            span = slice(half * 256, (half + 1) * 256)
            queries = qkv_ref[0, span, pl.ds(off, 128)]
            outs = []
            for side in range(2):
                head = pair * 2 + side
                chosen = jnp.where((lane < 64) == (side == 0), queries, 0).astype(BF16)
                scores = mm(chosen, keys, NT)
                first = (3 - 2 * half) * 128
                second = (2 - 2 * half) * 128
                bias = jnp.concatenate(
                    (
                        strips[head, :, first : first + 512],
                        strips[head, :, second : second + 512],
                    ),
                    axis=0,
                )
                scores = jnp.where(live_keys, scores + bias, MASKED_SCORE)
                most = jnp.max(scores, axis=1, keepdims=True)
                expo = jnp.exp(scores - most)
                total = jnp.sum(expo, axis=1, keepdims=True)
                weights = (expo * (1.0 / total)).astype(BF16)
                outs.append(mm(weights, values))
                logs[span, :] = jnp.where(lane == head, most + jnp.log(total), logs[span, :])
            attended[span, pl.ds(off, 128)] = jnp.where(lane < 64, outs[0], outs[1]).astype(BF16)
        return carry

    lax.fori_loop(0, 4, heads_pair, 0)
    log_ref[0] = jnp.transpose(logs[...])[0:8, :]

    middle[...] = wide + mm(attended[...], w_o[...])
    mid = middle[...]
    scale_mid = lax.rsqrt(jnp.mean(mid * mid, axis=1, keepdims=True) + EPSILON)
    normed_mid = (mid * scale_mid * gain_mlp_ref[...]).astype(BF16)
    turned_mid = jnp.transpose(normed_mid)

    @pl.when(step == 0)
    def _():
        for copy in copies(False):
            copy.wait()

    result[...] = mid
    back[...] = jnp.zeros_like(back)

    def ff_group(group, carry):
        for side in range(2):
            part = group * 2 + side
            hid = w_hid[part]
            out = w_mid[part]
            grads = top[...]
            pre = mm(normed_mid, hid)
            square = pre * pre
            tanh = jnp.tanh(ROOT * pre * (1.0 + CUBIC * square))
            half_up = 0.5 * (1.0 + tanh)
            act = (pre * half_up).astype(BF16)
            slope = half_up + (0.5 * ROOT) * pre * (1.0 - tanh * tanh) * (
                1.0 + (3.0 * CUBIC) * square
            )
            result[...] += mm(act, out)
            grad_pre = (mm(grads, out, NT) * slope).astype(BF16)
            new_mid = mm(act, grads, TN)
            new_hid = mm(turned_mid, grad_pre)
            back[...] += mm(grad_pre, hid, NT)
            target = ff_keep if side == 0 else ff_send

            @pl.when(step == 0)
            def _():
                acc_mid[part] = new_mid
                acc_hid[part] = new_hid

            @pl.when(step == 1)
            def _():
                for shard in range(SHARDS):
                    at = lax.bitwise_xor(place, shard)
                    span = slice(shard * 64, (shard + 1) * 64)
                    target[group, at, 0:64, :] = (acc_hid[part, span, :] + new_hid[span, :]).astype(
                        BF16
                    )
                    target[group, at, 64:128, :] = (
                        acc_mid[part, span, :] + new_mid[span, :]
                    ).astype(BF16)

        return carry

    lax.fori_loop(0, 2, ff_group, 0)

    final = jnp.where(live_rows, result[...], 0.0).astype(BF16)
    pooled[...] = final
    blocks_keep[0] = pooled[:, pl.ds(pl.multiple_of(mp * 256, 256), 256)]
    blocks_send[0] = pooled[:, pl.ds(pl.multiple_of((1 - mp) * 256, 256), 256)]

    mid = middle[...]
    unit = mid * scale_mid
    grad_normed = back[...]
    scaled = grad_normed * gain_mlp_ref[...]
    grad_mid = top[...].astype(F32) + scale_mid * (
        scaled - unit * jnp.mean(scaled * unit, axis=1, keepdims=True)
    )
    grad_mid_ref[0] = grad_mid
    new_gain = jnp.sum(grad_normed * unit, axis=0, keepdims=True)
    branch = grad_mid.astype(BF16)
    grad_att_ref[0] = mm(branch, w_o[...], NT).astype(BF16)
    new_out = mm(attended[...], branch, TN)

    @pl.when(step == 0)
    def _():
        acc_out[...] = new_out
        acc_gain[...] = jnp.broadcast_to(new_gain, acc_gain.shape)

    @pl.when(step == 1)
    def _():
        gain_out[...] = acc_gain[...] + new_gain
        for part in range(4):
            target = ff_keep if part % 2 == 0 else ff_send
            for shard in range(SHARDS):
                at = lax.bitwise_xor(place, shard)
                span = slice(part * 128 + shard * 16, part * 128 + (shard + 1) * 16)
                target[part // 2, at, 128:144, :] = (acc_out[span, :] + new_out[span, :]).astype(
                    BF16
                )


def layer_forward(info, own, other, cot, cot_other, spread, gain_attn, gain_mlp, weights, parts):
    half = own.shape[0]
    attn_parts, out_parts, ff_parts = parts

    def whole(shape):
        return pl.BlockSpec(shape, functools.partial(lambda n, i, info: (0,) * n, len(shape)))

    def item(shape):
        return pl.BlockSpec(
            (1,) + shape, functools.partial(lambda n, i, info: (i,) + (0,) * n, len(shape))
        )

    def kernel(*refs):
        info_ref, refs = refs[0], list(refs[1:])
        head, refs = refs[:13], refs[13:]
        attn, out, ff, refs = refs[:4], refs[4:8], refs[8:12], refs[12:]
        layer_kernel(info_ref, *head, attn, out, ff, *refs)

    packed = (2, SHARDS, 144, 512)
    return pl.pallas_call(
        kernel,
        grid_spec=pltpu.PrefetchScalarGridSpec(
            num_scalar_prefetch=1,
            grid=(half,),
            in_specs=[
                item((BLOCKS, 256)),
                item((BLOCKS, 256)),
                pl.BlockSpec((1, BLOCKS, 256), lambda i, info: (info[0] * 2 + i, 0, 0)),
                item((BLOCKS, 256)),
                whole((8, WRAP)),
                whole((1, 512)),
                whole((1, 512)),
            ]
            + [ANY] * 18,
            out_specs=[
                item((BLOCKS, 256)),
                item((BLOCKS, 256)),
                item((BLOCKS, 1536)),
                item((8, BLOCKS)),
                item((BLOCKS, 512)),
                item((BLOCKS, 512)),
                whole((512, 1536)),
                whole(packed),
                whole(packed),
                whole((8, 512)),
            ],
            scratch_shapes=[
                pltpu.VMEM((512, 1536), BF16),
                pltpu.VMEM((512, 512), BF16),
                pltpu.VMEM((4, 512, 512), BF16),
                pltpu.VMEM((4, 512, 512), BF16),
                pltpu.VMEM((8, 128, 896), F32),
                pltpu.VMEM((BLOCKS, 512), BF16),
                pltpu.VMEM((BLOCKS, 512), BF16),
                pltpu.VMEM((BLOCKS, 512), F32),
                pltpu.VMEM((BLOCKS, 512), BF16),
                pltpu.VMEM((BLOCKS, 128), F32),
                pltpu.VMEM((BLOCKS, 512), F32),
                pltpu.VMEM((BLOCKS, 512), F32),
                pltpu.VMEM((4, 512, 512), F32),
                pltpu.VMEM((4, 512, 512), F32),
                pltpu.VMEM((512, 512), F32),
                pltpu.VMEM((8, 512), F32),
                pltpu.SemaphoreType.DMA((36,)),
            ],
        ),
        out_shape=[
            jax.ShapeDtypeStruct((half, BLOCKS, 256), BF16),
            jax.ShapeDtypeStruct((half, BLOCKS, 256), BF16),
            jax.ShapeDtypeStruct((half, BLOCKS, 1536), BF16),
            jax.ShapeDtypeStruct((half, 8, BLOCKS), F32),
            jax.ShapeDtypeStruct((half, BLOCKS, 512), BF16),
            jax.ShapeDtypeStruct((half, BLOCKS, 512), F32),
            jax.ShapeDtypeStruct((512, 1536), BF16),
            jax.ShapeDtypeStruct(packed, BF16),
            jax.ShapeDtypeStruct(packed, BF16),
            jax.ShapeDtypeStruct((8, 512), F32),
        ],
        compiler_params=params(("arbitrary",)),
        name="layer_forward",
    )(
        info, own, other, cot, cot_other, spread, gain_attn, gain_mlp,
        *weights, *attn_parts, *out_parts, *ff_parts,
    )


def attention_back_kernel(
    info,
    own_ref,
    other_ref,
    qkv_ref,
    log_ref,
    grad_att_ref,
    grad_mid_ref,
    spread_ref,
    collect_ref,
    gain_attn_ref,
    gain_mid_ref,
    joined_ref,
    keep_ref,
    send_ref,
    attn_keep,
    attn_send,
    tiny_ref,
    strips,
    pooled,
    grads,
    sums,
    acc,
    acc_gain,
):
    step = pl.program_id(0)
    mp, core, place = info[0], info[1], info[3]
    length = info[4 + mp * 2 + step]
    count = lax.shift_right_logical(length + 3, 2)

    @pl.when(step == 0)
    def _():
        build_strips(spread_ref, strips)
        sums[...] = jnp.zeros_like(sums)

    gather_halves(info, pooled, own_ref, other_ref)
    live_keys = lax.broadcasted_iota(jnp.int32, (BLOCKS, 256), 0) < count
    lane = lax.broadcasted_iota(jnp.int32, (BLOCKS, 128), 1)

    def heads_pair(pair, carry):
        off = pl.multiple_of(pair * 128, 128)
        keys = qkv_ref[0, :, pl.ds(512 + off, 128)]
        values = qkv_ref[0, :, pl.ds(1024 + off, 128)]
        found = []
        for side in range(2):
            head = pair * 2 + side
            grad_key = jnp.zeros((BLOCKS, 128), F32)
            grad_value = jnp.zeros((BLOCKS, 128), F32)
            grad_query = []
            for half in range(2):
                span = slice(half * 256, (half + 1) * 256)
                own_lane = (lane[:256] < 64) == (side == 0)
                queries = qkv_ref[0, span, pl.ds(off, 128)]
                outer = grad_att_ref[0, span, pl.ds(off, 128)]
                scores = mm(keys, jnp.where(own_lane, queries, 0).astype(BF16), NT)
                bias = jnp.concatenate(
                    [
                        strips[
                            head, :, (3 - row) * 128 + half * 256 : (3 - row) * 128 + half * 256 + 256
                        ]
                        for row in range(4)
                    ],
                    axis=0,
                )
                logs = log_ref[0, pl.ds(head, 1), span]
                probs = jnp.where(live_keys, jnp.exp(scores + bias - logs), 0.0)
                slope = mm(values, jnp.where(own_lane, outer, 0).astype(BF16), NT)
                product = probs * slope
                delta = jnp.sum(product, axis=0, keepdims=True)
                grad_scores = (product - probs * delta).astype(BF16)
                grad_value = grad_value + mm(probs.astype(BF16), outer)
                grad_key = grad_key + mm(grad_scores, queries)
                grad_query.append(mm(grad_scores, keys, TN))
                for row in range(4):
                    first = (3 - row) * 128 + half * 256
                    sums[head, :, first : first + 256] += grad_scores[
                        row * 128 : (row + 1) * 128, :
                    ].astype(F32)
            found.append((jnp.concatenate(grad_query, axis=0), grad_key, grad_value))
        for index in range(3):
            grads[:, pl.ds(index * 512 + off, 128)] = jnp.where(
                lane < 64, found[0][index], found[1][index]
            ).astype(BF16)
        return carry

    lax.fori_loop(0, 4, heads_pair, 0)

    wide = pooled[...].astype(F32)
    scale = lax.rsqrt(jnp.mean(wide * wide, axis=1, keepdims=True) + EPSILON)
    unit = wide * scale
    normed = (unit * gain_attn_ref[...]).astype(BF16)
    grad_normed = mm(grads[...], joined_ref[...], NT)
    scaled = grad_normed * gain_attn_ref[...]
    grad_pooled = grad_mid_ref[0] + scale * (
        scaled - unit * jnp.mean(scaled * unit, axis=1, keepdims=True)
    )
    pooled[...] = grad_pooled.astype(BF16)
    keep_ref[0] = pooled[:, pl.ds(pl.multiple_of(mp * 256, 256), 256)]
    send_ref[0] = pooled[:, pl.ds(pl.multiple_of((1 - mp) * 256, 256), 256)]
    new_gain = jnp.sum(grad_normed * unit, axis=0, keepdims=True)
    turned = jnp.transpose(normed)

    @pl.when(step == 0)
    def _():
        acc[...] = mm(turned, grads[...])
        acc_gain[...] = jnp.broadcast_to(new_gain, acc_gain.shape)

    @pl.when(step == 1)
    def _():
        acc[...] += mm(turned, grads[...])
        for part in range(4):
            target = attn_keep if part % 2 == 0 else attn_send
            for shard in range(SHARDS):
                at = lax.bitwise_xor(place, shard)
                for index in range(3):
                    first = index * 512 + part * 128
                    target[part // 2, at, :, index * 128 : (index + 1) * 128] = acc[
                        shard * 64 : (shard + 1) * 64, first : first + 128
                    ].astype(BF16)
        rows = []
        for head in range(8):
            whole = jnp.concatenate((sums[head], jnp.zeros((128, 128), F32)), axis=1)
            size = 64
            while size >= 1:
                whole = whole[:size] + pltpu.roll(whole[size : 2 * size], WRAP - size, 1)
                size //= 2
            rows.append(whole)
        lines = jnp.concatenate(rows, axis=0)
        found = lax.dot_general(
            lines, collect_ref[...], NN, precision=PRECISE, preferred_element_type=F32
        )
        tiny_ref[...] = jnp.zeros_like(tiny_ref)
        tiny_ref[0:1, :] = acc_gain[0:1, :] + new_gain
        tiny_ref[1:2, :] = gain_mid_ref[0:1, :]
        line = lax.broadcasted_iota(jnp.int32, (8, 128), 0)
        heads = jnp.zeros((8, 128), F32)
        for head in range(8):
            true_head = (
                lax.bitwise_xor(mp, head // 4) * 4
                + lax.bitwise_xor(core, (head // 2) % 2) * 2
                + head % 2
            )
            heads = jnp.where(line == true_head, found[head : head + 1, :], heads)
        tiny_ref[8:16, 0:128] = heads


def attention_back(
    info, own, other, qkv, logs, grad_att, grad_mid, spread, collect, gain_attn, gain_mid, joined
):
    half = own.shape[0]

    def whole(shape):
        return pl.BlockSpec(shape, functools.partial(lambda n, i, info: (0,) * n, len(shape)))

    def item(shape):
        return pl.BlockSpec(
            (1,) + shape, functools.partial(lambda n, i, info: (i,) + (0,) * n, len(shape))
        )

    packed = (2, SHARDS, 64, 384)
    return pl.pallas_call(
        attention_back_kernel,
        grid_spec=pltpu.PrefetchScalarGridSpec(
            num_scalar_prefetch=1,
            grid=(half,),
            in_specs=[
                item((BLOCKS, 256)),
                item((BLOCKS, 256)),
                item((BLOCKS, 1536)),
                item((8, BLOCKS)),
                item((BLOCKS, 512)),
                item((BLOCKS, 512)),
                whole((8, WRAP)),
                whole((WRAP, 128)),
                whole((1, 512)),
                whole((8, 512)),
                whole((512, 1536)),
            ],
            out_specs=[
                item((BLOCKS, 256)),
                item((BLOCKS, 256)),
                whole(packed),
                whole(packed),
                whole((16, 512)),
            ],
            scratch_shapes=[
                pltpu.VMEM((8, 128, 896), F32),
                pltpu.VMEM((BLOCKS, 512), BF16),
                pltpu.VMEM((BLOCKS, 1536), BF16),
                pltpu.VMEM((8, 128, 896), F32),
                pltpu.VMEM((512, 1536), F32),
                pltpu.VMEM((8, 512), F32),
            ],
        ),
        out_shape=[
            jax.ShapeDtypeStruct((half, BLOCKS, 256), BF16),
            jax.ShapeDtypeStruct((half, BLOCKS, 256), BF16),
            jax.ShapeDtypeStruct(packed, BF16),
            jax.ShapeDtypeStruct(packed, BF16),
            jax.ShapeDtypeStruct((16, 512), F32),
        ],
        compiler_params=params(("arbitrary",)),
        name="attention_back",
    )(info, own, other, qkv, logs, grad_att, grad_mid, spread, collect, gain_attn, gain_mid, joined)


def ff_place_kernel(info, near_ref, far_ref, hid_ref, mid_ref, out_ref):
    core, place = info[1], info[3]
    for source, side in ((near_ref, core), (far_ref, 1 - core)):
        for shard in range(SHARDS):
            at = lax.bitwise_xor(place, shard)
            hid_ref[shard * 64 : (shard + 1) * 64, pl.ds(pl.multiple_of(side * 512, 512), 512)] = (
                source[at, 0:64, :].astype(F32)
            )
            mid_ref[pl.ds(pl.multiple_of(side * 512 + shard * 64, 64), 64), :] = source[
                at, 64:128, :
            ].astype(F32)
            out_ref[pl.ds(pl.multiple_of(side * 128 + shard * 16, 16), 16), :] = source[
                at, 128:144, :
            ].astype(F32)


def attn_place_kernel(info, near_ref, far_ref, query_ref, key_ref, value_ref):
    core, place = info[1], info[3]
    for source, side in ((near_ref, core), (far_ref, 1 - core)):
        for shard in range(SHARDS):
            at = lax.bitwise_xor(place, shard)
            for index, target in enumerate((query_ref, key_ref, value_ref)):
                target[
                    shard * 64 : (shard + 1) * 64, pl.ds(pl.multiple_of(side * 128, 128), 128)
                ] = source[at, :, index * 128 : (index + 1) * 128].astype(F32)


def place_weights(kernel, name, info, near, far, shapes):
    def whole(shape):
        return pl.BlockSpec(shape, functools.partial(lambda n, i, info: (0,) * n, len(shape)))

    return pl.pallas_call(
        kernel,
        grid_spec=pltpu.PrefetchScalarGridSpec(
            num_scalar_prefetch=1,
            grid=(1,),
            in_specs=[whole(near.shape), whole(far.shape)],
            out_specs=[whole(shape) for shape in shapes],
        ),
        out_shape=[jax.ShapeDtypeStruct(shape, F32) for shape in shapes],
        compiler_params=params(("arbitrary",)),
        name=name,
    )(info, near, far)


def shards(
    devices,
    byte_states,
    frontier,
    lengths,
    gain_attn,
    w_query,
    w_key,
    w_value,
    w_attn_out,
    rel_bias,
    gain_mlp,
    w_hidden,
    w_mlp_out,
    cotangent,
):
    bits = devices.bit_length() - 1
    mp = lax.axis_index("mp").astype(jnp.int32)
    dp = lax.axis_index("dp").astype(jnp.int32)
    core = dp & 1
    way = (dp >> 1) & 1
    place = (((dp >> 1) & 1) << 2) | (((dp >> 2) & 1) << 1) | ((dp >> 3) & 1)
    info = jnp.concatenate((jnp.stack((mp, core, way, place)), lengths))

    def across(value):
        return lax.ppermute(value, "mp", [(0, 1), (1, 0)])

    def swap(value, bit):
        return lax.ppermute(value, "dp", [(i, i ^ (1 << bit)) for i in range(devices)])

    def added(a, b):
        return (a.astype(F32) + b.astype(F32)).astype(BF16)

    row = way * 256
    attn_piece = jnp.concatenate(
        [
            lax.dynamic_slice(weight, (row, core * 128), (256, 128))
            for weight in (w_query, w_key, w_value)
        ],
        axis=1,
    )
    out_piece = lax.dynamic_slice(w_attn_out, (core * 128 + way * 64, 0), (64, 512))
    ff_piece = jnp.stack(
        (
            lax.dynamic_slice(w_hidden, (row, core * 512), (256, 512)),
            lax.dynamic_slice(w_mlp_out, (core * 512 + row, 0), (256, 512)),
        )
    )

    def spread_out(piece):
        first = across(piece)
        second = swap(first, 1)
        return (first, second, swap(first, 0), swap(second, 0))

    forward, backward, collect = offset_tables()
    tables = jnp.asarray(np.concatenate((forward, backward), axis=0))
    spread_own = jnp.dot(tables, rel_bias, precision=PRECISE).T
    spread_own = jnp.where(core == 0, spread_own, jnp.roll(spread_own, 2, axis=0))
    spread_all = jnp.concatenate((spread_own, across(spread_own)), axis=0)
    spread_forward, spread_backward = spread_all[:, :WRAP], spread_all[:, WRAP:]

    attn_parts = spread_out(attn_piece)
    out_parts = spread_out(out_piece)
    pooled_send, pooled_own, positions = pool_forward(info, frontier, byte_states)
    pooled_other = across(pooled_send)
    ff_parts = spread_out(ff_piece)
    cot_send = lax.dynamic_slice_in_dim(cotangent, (1 - mp) * 2, 2, 0)
    cot_other = across(cot_send)

    gain_attn_row = gain_attn.reshape(1, -1)
    gain_mlp_row = gain_mlp.reshape(1, -1)
    (
        blocks_keep,
        blocks_send,
        qkv,
        logs,
        grad_att,
        grad_mid,
        joined,
        ff_keep,
        ff_send,
        gain_mid,
    ) = layer_forward(
        info,
        pooled_own,
        pooled_other,
        cotangent,
        cot_other,
        spread_forward,
        gain_attn_row,
        gain_mlp_row,
        (w_query, w_key, w_value, w_attn_out, w_hidden, w_mlp_out),
        (attn_parts, out_parts, ff_parts),
    )

    def reduce_all(keep, send):
        got = swap(send, 0)
        other = added(keep[1], got[1])
        value = added(keep[0], got[0])
        value = added(value, across(other))
        halved = min(3, bits - 1)
        for bit in range(1, halved + 1):
            size = value.shape[0] // 2
            value = added(value[:size], swap(value[size:], bit))
        for bit in range(halved + 1, bits):
            value = added(value, swap(value, bit))
        for bit in range(halved, 0, -1):
            value = jnp.concatenate((value, swap(value, bit)), axis=0)
        return value, swap(value, 0)

    ff_near, ff_far = reduce_all(ff_keep, ff_send)
    blocks_other = across(blocks_send)

    grad_keep, grad_send, attn_keep, attn_send, tiny = attention_back(
        info,
        pooled_own,
        pooled_other,
        qkv,
        logs,
        grad_att,
        grad_mid,
        spread_backward,
        jnp.asarray(collect),
        gain_attn_row,
        gain_mid,
        joined,
    )
    grad_other = across(grad_send)
    held = pool_backward(info, positions, byte_states, grad_keep, None, True)
    grad_bytes, part = pool_backward(info, positions, byte_states, grad_other, held, False)
    grad_frontier = frontier_gradient(info, part, across(part), positions, frontier)

    attn_near, attn_far = reduce_all(attn_keep, attn_send)
    tiny = tiny + across(tiny)
    for bit in range(bits):
        tiny = tiny + swap(tiny, bit)

    grad_hidden, grad_mlp, grad_out = place_weights(
        ff_place_kernel,
        "ff_place",
        info,
        ff_near,
        ff_far,
        (w_hidden.shape, w_mlp_out.shape, w_attn_out.shape),
    )
    grad_query, grad_key, grad_value = place_weights(
        attn_place_kernel,
        "attn_place",
        info,
        attn_near,
        attn_far,
        (w_query.shape, w_key.shape, w_value.shape),
    )
    blocks_out = jnp.where(
        mp == 0,
        jnp.concatenate((blocks_keep, blocks_other), axis=0),
        jnp.concatenate((blocks_other, blocks_keep), axis=0),
    )
    grad_rel = lax.dynamic_slice(tiny, (8 + mp * 4, 0), (4, BUCKETS)).T
    return (
        blocks_out,
        grad_bytes,
        grad_frontier,
        tiny[0],
        grad_query,
        grad_key,
        grad_value,
        grad_out,
        grad_rel,
        tiny[1],
        grad_hidden,
        grad_mlp,
    )


def solution(mesh):
    placed = (
        P("dp", None, "mp"),
        P("dp", None),
        P("dp"),
        P(),
        P(None, "mp"),
        P(None, "mp"),
        P(None, "mp"),
        P("mp", None),
        P(None, "mp"),
        P(),
        P(None, "mp"),
        P("mp", None),
        P("dp", None, "mp"),
    )
    return jax.shard_map(
        functools.partial(shards, mesh.shape["dp"]),
        mesh=mesh,
        in_specs=placed,
        out_specs=(
            P("dp", None, "mp"),
            P("dp", None, "mp"),
            P("dp", None),
            P(),
            P(None, "mp"),
            P(None, "mp"),
            P(None, "mp"),
            P("mp", None),
            P(None, "mp"),
            P(),
            P(None, "mp"),
            P("mp", None),
        ),
        check_vma=False,
    )
```

```python
import functools
import math

import jax
import jax.numpy as jnp
import numpy as np
from jax import lax
from jax.experimental import pallas as pl
from jax.experimental.pallas import tpu as pltpu
from jax.sharding import PartitionSpec as P

BUCKETS = 32
REACH = 128
BLOCKS = 512
WRAP = 2 * BLOCKS
SHARDS = 8

EPSILON = 1e-06
SHARPNESS = 2.0
MASKED_SCORE = -1000000000.0
OUTSIDE = -10000.0
REACH_OUT = 8.0
PRECISE = lax.Precision.HIGHEST
ROOT = 0.7978845608028654
CUBIC = 0.044715
VMEM_LIMIT = 60 * 1024 * 1024
ROW_TILE = 16

F32 = jnp.float32
BF16 = jnp.bfloat16
ANY = pl.BlockSpec(memory_space=pl.ANY)
NN = (((1,), (0,)), ((), ()))
NT = (((1,), (1,)), ((), ()))
TN = (((0,), (0,)), ((), ()))


def mm(a, b, dims=NN):
    return lax.dot_general(a, b, dims, preferred_element_type=F32)


def bucket_of(offset):
    half_count = BUCKETS // 2
    exact_count = half_count // 2
    distance = abs(offset)
    if distance < exact_count:
        place = distance
    else:
        place = min(
            half_count - 1,
            exact_count
            + math.floor(
                math.log(distance / exact_count)
                / math.log(REACH / exact_count)
                * (half_count - exact_count)
            ),
        )
    return place + (half_count if offset > 0 else 0)


def offset_tables():
    forward = np.zeros((WRAP, BUCKETS), np.float32)
    backward = np.zeros((WRAP, BUCKETS), np.float32)
    collect = np.zeros((WRAP, 128), np.float32)
    for offset in range(1 - BLOCKS, BLOCKS):
        bucket = bucket_of(offset)
        forward[offset % WRAP, bucket] = 1.0
        backward[(-offset) % WRAP, bucket] = 1.0
        collect[(384 - offset) % WRAP, bucket] = 1.0
    return forward, backward, collect


def params(semantics=None):
    return pltpu.CompilerParams(
        vmem_limit_bytes=VMEM_LIMIT,
        dimension_semantics=semantics,
    )


def cost(micros):
    return pl.CostEstimate(flops=1, bytes_accessed=1, transcendentals=0)


def whole(shape):
    return pl.BlockSpec(shape, functools.partial(lambda n, i, info: (0,) * n, len(shape)))


def item(shape):
    return pl.BlockSpec(
        (1,) + shape, functools.partial(lambda n, i, info: (i,) + (0,) * n, len(shape))
    )


def launch(
    kernel, name, micros, grid, info, args, in_specs, outs, out_specs, scratch=(), after=(),
    through=(), aliases=None,
):
    given, waits, passed, made = 1 + len(args), len(after), len(through), len(outs)

    def body(*refs):
        first = given + waits + passed
        kernel(*refs[:given], *refs[first : first + made], *refs[first + made + passed :])

    aliases = dict(aliases or {})
    for index in range(passed):
        aliases[given + waits + index] = made + index
    return pl.pallas_call(
        body,
        grid_spec=pltpu.PrefetchScalarGridSpec(
            num_scalar_prefetch=1,
            grid=(grid,),
            in_specs=list(in_specs) + [ANY] * (waits + passed),
            out_specs=list(out_specs) + [ANY] * passed,
            scratch_shapes=list(scratch),
        ),
        out_shape=list(outs) + [jax.ShapeDtypeStruct(x.shape, x.dtype) for x in through],
        input_output_aliases=aliases,
        compiler_params=params(("arbitrary",)),
        cost_estimate=cost(micros),
        name=name,
    )(info, *args, *after, *through)


def combine(name, jobs, after=(), through=()):
    args, outs, plan = [], [], []
    for joined, arrays, sizes in jobs:
        first = arrays[0]
        total = sum(x.shape[0] for x in arrays) if joined else first.shape[0]
        sizes = sizes or (total,)
        plan.append((joined, len(arrays), len(sizes)))
        args += list(arrays)
        outs += [jax.ShapeDtypeStruct((size,) + first.shape[1:], first.dtype) for size in sizes]
    given, held, made, passed = len(args), len(args) + len(after), len(outs), len(through)

    def kernel(*refs):
        ins = list(refs[:given])
        results = list(refs[held + passed : held + passed + made])
        for joined, count, parts in plan:
            sources, ins = ins[:count], ins[count:]
            targets, results = results[:parts], results[parts:]
            at = 0
            for target in targets:
                if joined:
                    for source in sources:
                        target[at : at + source.shape[0]] = source[...]
                        at += source.shape[0]
                else:
                    span = slice(at, at + target.shape[0])
                    value = sources[0][span].astype(F32)
                    for source in sources[1:]:
                        value = value + source[span].astype(F32)
                    target[...] = value.astype(target.dtype)
                    at += target.shape[0]

    near = pl.BlockSpec(memory_space=pltpu.VMEM)
    return pl.pallas_call(
        kernel,
        in_specs=[near] * given + [ANY] * (len(after) + passed),
        out_specs=[near] * made + [ANY] * passed,
        out_shape=outs + [jax.ShapeDtypeStruct(x.shape, x.dtype) for x in through],
        input_output_aliases={held + index: made + index for index in range(passed)},
        compiler_params=pltpu.CompilerParams(vmem_limit_bytes=16 * 1024 * 1024),
        cost_estimate=cost(1),
        name=name,
    )(*args, *after, *through)


def pool_rows(item, length, count, pos_ref, bytes_ref, out_ref, acc):
    acc[...] = jnp.zeros_like(acc)
    chunks = bytes_ref.shape[1] // 256
    rows, lows, highs = [], [], []
    for chunk in range(chunks):
        row = pos_ref[pl.ds(item, 1), chunk * 256 : (chunk + 1) * 256]
        rows.append(row)
        lows.append(jnp.min(jnp.where(row < 0.0, 1e6, row)))
        highs.append(jnp.max(row))
    for chunk in range(chunks):
        for tile in range(BLOCKS // 128):
            near = jnp.logical_and(
                highs[chunk] > tile * 128 - REACH_OUT,
                lows[chunk] < tile * 128 + 128 + REACH_OUT,
            )

            @pl.when(jnp.logical_and(near, tile * 128 < count))
            def _():
                centre = (
                    lax.broadcasted_iota(jnp.int32, (128, 256), 0).astype(F32) + tile * 128 + 0.5
                )
                offset = rows[chunk] - centre
                kernel = jnp.exp(-SHARPNESS * offset * offset).astype(BF16)
                acc[tile * 128 : (tile + 1) * 128, :] += mm(
                    kernel, bytes_ref[0, chunk * 256 : (chunk + 1) * 256, :]
                )

    live = lax.broadcasted_iota(jnp.int32, acc.shape, 0) < count
    out_ref[0] = jnp.where(live, acc[...], 0.0).astype(BF16)


def masked_positions(info, frontier_ref, pos_ref):
    items, byte_count = frontier_ref.shape
    lane = lax.broadcasted_iota(jnp.int32, (items, byte_count), 1)
    row = lax.broadcasted_iota(jnp.int32, (items, byte_count), 0)
    length = jnp.zeros((items, byte_count), jnp.int32)
    for item in range(items):
        length = jnp.where(row == item, info[4 + item], length)
    valid = lane < length
    running = jnp.where(valid, frontier_ref[...], 0.0)
    step = 1
    while step < byte_count:
        running = running + jnp.where(lane >= step, pltpu.roll(running, step, 1), 0.0)
        step *= 2
    count = lax.shift_right_logical(length + 3, 2).astype(F32)
    total = running[:, byte_count - 1 :]
    pos_ref[...] = jnp.where(valid, count * running / total, OUTSIDE)


def pool_first_kernel(info, frontier_ref, bytes_ref, out_ref, pos_ref, acc):
    step = pl.program_id(0)

    @pl.when(step == 0)
    def _():
        masked_positions(info, frontier_ref, pos_ref)

    item = (1 - info[0]) * 2 + step
    length = info[4 + item]
    pool_rows(item, length, lax.shift_right_logical(length + 3, 2), pos_ref, bytes_ref, out_ref, acc)


def pool_second_kernel(info, pos_ref, bytes_ref, out_ref, acc):
    item = info[0] * 2 + pl.program_id(0)
    length = info[4 + item]
    pool_rows(item, length, lax.shift_right_logical(length + 3, 2), pos_ref, bytes_ref, out_ref, acc)


def pool_forward(info, frontier, byte_states):
    items, byte_count, share = byte_states.shape
    half = items // 2
    out = jax.ShapeDtypeStruct((half, BLOCKS, share), BF16)
    scratch = [pltpu.VMEM((BLOCKS, share), F32)]
    send, positions = launch(
        pool_first_kernel,
        "pool_send",
        7,
        half,
        info,
        (frontier, byte_states),
        [
            whole((items, byte_count)),
            pl.BlockSpec((1, byte_count, share), lambda i, info: ((1 - info[0]) * 2 + i, 0, 0)),
        ],
        [out, jax.ShapeDtypeStruct((items, byte_count), F32)],
        [item((BLOCKS, share)), whole((items, byte_count))],
        scratch,
    )

    def keep(after, through):
        return launch(
            pool_second_kernel,
            "pool_keep",
            7,
            half,
            info,
            (positions, byte_states),
            [
                whole((items, byte_count)),
                pl.BlockSpec((1, byte_count, share), lambda i, info: (info[0] * 2 + i, 0, 0)),
            ],
            [out],
            [item((BLOCKS, share))],
            scratch,
            after,
            through,
        )

    return send, positions, keep


def pool_back_body(item, length, pos_ref, bytes_ref, grads_ref, out_ref, part_ref):
    count = lax.shift_right_logical(length + 3, 2)
    chunks = bytes_ref.shape[1] // 256
    rows, lows, highs = [], [], []
    for chunk in range(chunks):
        row = pos_ref[pl.ds(item, 1), chunk * 256 : (chunk + 1) * 256]
        rows.append(row)
        lows.append(jnp.min(jnp.where(row < 0.0, 1e6, row)))
        highs.append(jnp.max(row))
    ones = jnp.ones((8, 128), BF16)

    def scoped(acc, terms):
        for chunk in range(chunks):
            span = slice(chunk * 256, (chunk + 1) * 256)

            @pl.when(chunk * 256 >= length)
            def _():
                out_ref[0, span, :] = jnp.zeros((256, out_ref.shape[2]), BF16)
                part_ref[0, :, span] = jnp.zeros((1, 256), F32)

            @pl.when(chunk * 256 < length)
            def _():
                acc[...] = jnp.zeros_like(acc)
                terms[...] = jnp.zeros_like(terms)
                column = jnp.transpose(jnp.broadcast_to(rows[chunk], (128, 256)))
                for tile in range(BLOCKS // 128):
                    near = jnp.logical_and(
                        highs[chunk] > tile * 128 - REACH_OUT,
                        lows[chunk] < tile * 128 + 128 + REACH_OUT,
                    )

                    @pl.when(jnp.logical_and(near, tile * 128 < count))
                    def _():
                        centre = (
                            lax.broadcasted_iota(jnp.int32, (256, 128), 1).astype(F32)
                            + tile * 128
                            + 0.5
                        )
                        offset = column - centre
                        kernel = jnp.exp(-SHARPNESS * offset * offset)
                        grads = grads_ref[tile * 128 : (tile + 1) * 128, :]
                        acc[...] += mm(kernel.astype(BF16), grads)
                        slope = mm(bytes_ref[0, span, :], grads, NT)
                        terms[...] += slope * kernel * offset

                out_ref[0, span, :] = acc[...].astype(BF16)
                term = terms[...]
                high = term.astype(BF16)
                low = (term - high.astype(F32)).astype(BF16)
                summed = mm(ones, high, NT) + mm(ones, low, NT)
                part_ref[0, :, span] = -4.0 * summed[0:1, :]

    pl.run_scoped(
        scoped, pltpu.VMEM((256, out_ref.shape[2]), F32), pltpu.VMEM((256, 128), F32)
    )


def pool_back_kernel(offset, info, pos_ref, bytes_ref, grads_ref, *refs):
    mine, index = offset
    where = info[0] if mine else 1 - info[0]
    out_ref, part_ref = refs[-2:]
    at = where * 2 + index
    pool_back_body(at, info[4 + at], pos_ref, bytes_ref, grads_ref.at[0], out_ref, part_ref)


def pool_backward(info, positions, byte_states, grads, mine, index, held, after, through):
    items, byte_count, share = byte_states.shape

    def place(i, info):
        return ((info[0] if mine else 1 - info[0]) * 2 + index, 0, 0)

    in_specs = [
        whole((items, byte_count)),
        pl.BlockSpec((1, byte_count, share), place),
        pl.BlockSpec((1, BLOCKS, share), lambda i, info: (index, 0, 0)),
    ]
    args = (positions, byte_states, grads) + tuple(held)
    return launch(
        functools.partial(pool_back_kernel, (mine, index)),
        "pool_back",
        5,
        1,
        info,
        args,
        in_specs + [ANY] * len(held),
        [
            jax.ShapeDtypeStruct((items, byte_count, share), BF16),
            jax.ShapeDtypeStruct((items, 1, byte_count), F32),
        ],
        [
            pl.BlockSpec((1, byte_count, share), place),
            pl.BlockSpec((1, 1, byte_count), place),
        ],
        (),
        after,
        through,
        {4: 0, 5: 1} if held else None,
    )


def frontier_kernel(info, mine_ref, theirs_ref, pos_ref, frontier_ref, out_ref):
    items, byte_count = frontier_ref.shape
    lane = lax.broadcasted_iota(jnp.int32, (items, byte_count), 1)
    row = lax.broadcasted_iota(jnp.int32, (items, byte_count), 0)
    length = jnp.zeros((items, byte_count), jnp.int32)
    for item in range(items):
        length = jnp.where(row == item, info[4 + item], length)
    valid = lane < length
    total = jnp.sum(jnp.where(valid, frontier_ref[...], 0.0), axis=1, keepdims=True)
    terms = jnp.where(valid, mine_ref[:, 0, :] + theirs_ref[:, 0, :], 0.0)
    weighted = jnp.sum(terms * pos_ref[...], axis=1, keepdims=True)
    step = 1
    while step < byte_count:
        moved = pltpu.roll(terms, byte_count - step, 1)
        terms = terms + jnp.where(lane < byte_count - step, moved, 0.0)
        step *= 2
    count = lax.shift_right_logical(length + 3, 2).astype(F32)
    out_ref[...] = jnp.where(valid, (terms * count - weighted) / total, 0.0)


def frontier_gradient(info, mine, theirs, positions, frontier, after):
    args = (mine, theirs, positions, frontier)
    return launch(
        frontier_kernel,
        "frontier_sum",
        3,
        1,
        info,
        args,
        [whole(x.shape) for x in args],
        [jax.ShapeDtypeStruct(frontier.shape, F32)],
        [whole(frontier.shape)],
        (),
        after,
    )[0]


def build_strips(spread_ref, strips):
    for head in range(strips.shape[0]):
        row = jnp.broadcast_to(spread_ref[head : head + 1, :], (128, WRAP))
        turned = pltpu.roll(row, 384, 1, stride=1, stride_axis=0)
        strips[head] = turned[:, :896]


def gather_halves(info, target, own_ref, other_ref):
    first = pl.multiple_of(info[0] * 256, 256)
    second = pl.multiple_of((1 - info[0]) * 256, 256)
    target[:, pl.ds(first, 256)] = own_ref[0]
    target[:, pl.ds(second, 256)] = other_ref[0]


def span_of(index, size):
    return slice(index * size, (index + 1) * size)


def tile_at(index, size):
    return pl.ds(pl.multiple_of(index * size, size), size)


def started(pairs, sems):
    return [
        pltpu.make_async_copy(source, target, sems.at[index])
        for index, (source, target) in enumerate(pairs)
    ]


def inverse_rms(values):
    return lax.rsqrt(jnp.mean(values * values, axis=1, keepdims=True) + EPSILON)


def attention_kernel(
    info,
    own_ref,
    other_ref,
    spread_ref,
    gain_attn_ref,
    gain_mlp_ref,
    w_query,
    w_key,
    w_value,
    w_out,
    part_a,
    part_b,
    part_c,
    part_d,
    qkv_ref,
    log_ref,
    att_ref,
    middle_ref,
    normed_ref,
    w_qkv,
    w_o,
    strips,
    pooled,
    sems,
):
    step = pl.program_id(0)
    mp, core, way = info[0], info[1], info[2]
    length = info[4 + mp * 2 + step]
    count = lax.shift_right_logical(length + 3, 2)

    @pl.when(step == 0)
    def _():
        pairs = []
        for part in range(2):
            start = core if part == 0 else 1 - core
            for index, weight in enumerate((w_query, w_key, w_value)):
                pairs.append(
                    (
                        weight.at[:, tile_at(start, 128)],
                        w_qkv.at[:, pl.ds(index * 512 + part * 128, 128)],
                    )
                )
            pairs.append((w_out.at[tile_at(start, 128), :], w_o.at[pl.ds(part * 128, 128), :]))
        for part, sources in enumerate(((part_a, part_b), (part_c, part_d))):
            for side, source in enumerate(sources):
                turn = way if side == 0 else 1 - way
                for index in range(3):
                    pairs.append(
                        (
                            source.at[:, pl.ds(index * 128, 128)],
                            w_qkv.at[
                                tile_at(turn, 256), pl.ds(index * 512 + 256 + part * 128, 128)
                            ],
                        )
                    )
                for lane in range(4):
                    pairs.append(
                        (
                            source.at[pl.ds(lane * 64, 64), pl.ds(384, 128)],
                            w_o.at[
                                pl.ds(
                                    pl.multiple_of(256 + part * 128 + turn * 64, 64),
                                    64,
                                ),
                                pl.ds(lane * 128, 128),
                            ],
                        )
                    )
        copies = started(pairs, sems)
        for copy in copies:
            copy.start()
        build_strips(spread_ref, strips)
        for copy in copies:
            copy.wait()

    gather_halves(info, pooled, own_ref, other_ref)
    wide = pooled[...].astype(F32)
    normed = (wide * inverse_rms(wide) * gain_attn_ref[...]).astype(BF16)
    qkv_ref[0] = mm(normed, w_qkv[...]).astype(BF16)
    lane = lax.broadcasted_iota(jnp.int32, (BLOCKS, 128), 1)
    row = lax.broadcasted_iota(jnp.int32, (BLOCKS, 128), 0)
    dead = jnp.where(row < count, 0.0, MASKED_SCORE).astype(BF16)

    def heads_pair(pair, logs):
        off = pl.multiple_of(pair * 128, 128)
        queries = qkv_ref[0, :, pl.ds(off, 128)]
        keys = qkv_ref[0, :, pl.ds(512 + off, 128)]
        values = qkv_ref[0, :, pl.ds(1024 + off, 128)]
        outs = []
        for side in range(2):
            head = pair * 2 + side
            own = (lane < 64) == (side == 0)
            spare = lane == 64 * (1 - side)
            chosen = jnp.where(own, queries, jnp.where(spare, 1.0, 0.0).astype(BF16))
            masked = jnp.where(spare, dead, keys)
            summing = jnp.where(own, values, jnp.ones_like(values))
            parts, tops = [], []
            for half in range(2):
                scores = mm(chosen[span_of(half, 256), :], masked, NT)
                first = (3 - 2 * half) * 128
                second = (2 - 2 * half) * 128
                bias = jnp.concatenate(
                    (
                        strips[head, :, first : first + 512],
                        strips[head, :, second : second + 512],
                    ),
                    axis=0,
                )
                scores = scores + bias
                most = jnp.max(scores, axis=1, keepdims=True)
                expo = jnp.exp(scores - most).astype(BF16)
                parts.append(mm(expo, summing))
                tops.append(most)
            out = jnp.concatenate(parts, axis=0)
            total = out[:, 64 * (1 - side) : 64 * (1 - side) + 1]
            outs.append(out * (1.0 / total))
            logs = jnp.where(lane == head, jnp.concatenate(tops, axis=0) + jnp.log(total), logs)
        att_ref[0, :, pl.ds(off, 128)] = jnp.where(lane < 64, outs[0], outs[1]).astype(BF16)
        return logs

    logs = jnp.zeros((BLOCKS, 128), F32)
    log_ref[0] = lax.fori_loop(0, 4, heads_pair, logs)

    mid = wide + mm(att_ref[0], w_o[...])
    middle_ref[0] = mid
    normed_ref[0] = (mid * inverse_rms(mid) * gain_mlp_ref[...]).astype(BF16)


def attention_forward(info, own, other, spread, gain_attn, gain_mlp, weights, parts, after):
    half = own.shape[0]
    return launch(
        attention_kernel,
        "attention_forward",
        20,
        half,
        info,
        (own, other, spread, gain_attn, gain_mlp, *weights, *parts),
        [
            item((BLOCKS, 256)),
            item((BLOCKS, 256)),
            whole((8, WRAP)),
            whole((1, 512)),
            whole((1, 512)),
        ]
        + [ANY] * 8,
        [
            jax.ShapeDtypeStruct((half, BLOCKS, 1536), BF16),
            jax.ShapeDtypeStruct((half, BLOCKS, 128), F32),
            jax.ShapeDtypeStruct((half, BLOCKS, 512), BF16),
            jax.ShapeDtypeStruct((half, BLOCKS, 512), F32),
            jax.ShapeDtypeStruct((half, BLOCKS, 512), BF16),
            jax.ShapeDtypeStruct((512, 1536), BF16),
            jax.ShapeDtypeStruct((512, 512), BF16),
        ],
        [
            item((BLOCKS, 1536)),
            item((BLOCKS, 128)),
            item((BLOCKS, 512)),
            item((BLOCKS, 512)),
            item((BLOCKS, 512)),
            whole((512, 1536)),
            whole((512, 512)),
        ],
        [
            pltpu.VMEM((8, 128, 896), F32),
            pltpu.VMEM((BLOCKS, 512), BF16),
            pltpu.SemaphoreType.DMA((36,)),
        ],
        after,
    )


def gelu_and_slope(pre):
    square = pre * pre
    tanh = jnp.tanh(pre * (ROOT + (ROOT * CUBIC) * square))
    up = 0.5 + 0.5 * tanh
    act = pre * up
    slope = up + act * (1.0 - up) * (2.0 * ROOT + (6.0 * ROOT * CUBIC) * square)
    return act, slope


def ff_piece(normed, turned, top, turned_top, hid, mid, acts, grads, result, back, fresh):
    for half in range(2):
        rows = span_of(half, BLOCKS)
        act, slope = gelu_and_slope(mm(normed[rows, :], hid))
        acts[rows, :] = act.astype(BF16)
        grads[rows, :] = (mm(top[rows, :], mid, NT) * slope).astype(BF16)
        new_result = mm(acts[rows, :], mid)
        new_back = mm(grads[rows, :], hid, NT)
        if fresh:
            result[rows, :] = new_result
            back[rows, :] = new_back
        else:
            result[rows, :] += new_result
            back[rows, :] += new_back
    return mm(turned[...], grads[...]), mm(turned_top[...], acts[...])


def store_shards(place, target, first, values):
    rows = values.shape[0] // SHARDS
    for shard in range(SHARDS):
        at = lax.bitwise_xor(place, shard)
        target[at, first : first + rows, :] = values[span_of(shard, rows), :].astype(BF16)


def gather_top(info, top, turned_top, cot_own_ref, cot_other_ref):
    for index in range(2):
        rows = span_of(index, BLOCKS)
        count = lax.shift_right_logical(info[4 + info[0] * 2 + index] + 3, 2)
        live = lax.broadcasted_iota(jnp.int32, (BLOCKS, 256), 0) < count
        zero = jnp.zeros((BLOCKS, 256), BF16)
        top[rows, tile_at(info[0], 256)] = jnp.where(live, cot_own_ref[index], zero)
        top[rows, tile_at(1 - info[0], 256)] = jnp.where(live, cot_other_ref[index], zero)
        turned_top[:, rows] = jnp.transpose(top[rows, :])


def ff_first_kernel(
    info,
    normed_ref,
    cot_own_ref,
    cot_other_ref,
    part_near,
    part_far,
    result,
    back,
    keep_ref,
    send_ref,
    top,
    turned_top,
    turned,
    weights,
    acts,
    grads,
    sems,
):
    place = info[3]
    copies = started(((part_far, weights.at[1]), (part_near, weights.at[0])), sems)
    for copy in copies:
        copy.start()
    gather_top(info, top, turned_top, cot_own_ref, cot_other_ref)
    for index in range(2):
        turned[:, span_of(index, BLOCKS)] = jnp.transpose(normed_ref[span_of(index, BLOCKS), :])
    for part, target in ((1, send_ref), (0, keep_ref)):
        copies[1 - part].wait()
        grad_hid, grad_mid = ff_piece(
            normed_ref,
            turned,
            top,
            turned_top,
            weights[part, 0],
            weights[part, 1],
            acts,
            grads,
            result,
            back,
            part == 1,
        )
        store_shards(place, target, 0, grad_hid)
        store_shards(place, target, 64, grad_mid)


def ff_second_kernel(
    info,
    normed_ref,
    cot_own_ref,
    cot_other_ref,
    w_hidden,
    w_mlp,
    result_ref,
    back_ref,
    middle_ref,
    gain_ref,
    blocks_keep,
    blocks_send,
    grad_mid_ref,
    keep_ref,
    send_ref,
    gain_out,
    top,
    turned_top,
    turned,
    hid,
    mid,
    acts,
    grads,
    result,
    back,
    blocks,
    sems,
):
    mp, core, place = info[0], info[1], info[3]
    pairs = []
    for part in (1, 0):
        start = core if part == 0 else 1 - core
        pairs.append((w_hidden.at[:, tile_at(start, 512)], hid.at[part]))
        pairs.append((w_mlp.at[tile_at(start, 512), :], mid.at[part]))
    pairs.append((result_ref, result))
    pairs.append((back_ref, back))
    copies = started(pairs, sems)
    for copy in copies:
        copy.start()
    gather_top(info, top, turned_top, cot_own_ref, cot_other_ref)
    for index in range(2):
        turned[:, span_of(index, BLOCKS)] = jnp.transpose(normed_ref[span_of(index, BLOCKS), :])
    for copy in copies[:2] + copies[4:]:
        copy.wait()
    for part, target in ((1, send_ref), (0, keep_ref)):
        if part == 0:
            for copy in copies[2:4]:
                copy.wait()
        grad_hid, grad_mid = ff_piece(
            normed_ref,
            turned,
            top,
            turned_top,
            hid[part],
            mid[part],
            acts,
            grads,
            result,
            back,
            False,
        )
        store_shards(place, target, 0, grad_hid)
        store_shards(place, target, 64, grad_mid)

    new_gain = jnp.zeros((1, 512), F32)
    for index in range(2):
        rows = span_of(index, BLOCKS)
        count = lax.shift_right_logical(info[4 + mp * 2 + index] + 3, 2)
        live = lax.broadcasted_iota(jnp.int32, (BLOCKS, 1), 0) < count
        middle = middle_ref[rows, :]
        blocks[...] = jnp.where(live, middle + result[rows, :], 0.0).astype(BF16)
        blocks_keep[index] = blocks[:, tile_at(mp, 256)]
        blocks_send[index] = blocks[:, tile_at(1 - mp, 256)]
        scale = inverse_rms(middle)
        unit = middle * scale
        grad_normed = back[rows, :]
        scaled = grad_normed * gain_ref[...]
        grad_mid_ref[rows, :] = top[rows, :].astype(F32) + scale * (
            scaled - unit * jnp.mean(scaled * unit, axis=1, keepdims=True)
        )
        new_gain = new_gain + jnp.sum(grad_normed * unit, axis=0, keepdims=True)
    gain_out[...] = jnp.broadcast_to(new_gain, gain_out.shape)


def ff_call(info, normed, cot, cot_other, mine, given, after):
    rows = normed.shape[0]
    half = rows // BLOCKS
    packed = (SHARDS, 128, 512)
    wide = jax.ShapeDtypeStruct((rows, 512), F32)
    pack = jax.ShapeDtypeStruct(packed, BF16)
    in_specs = [
        whole((rows, 512)),
        pl.BlockSpec((half, BLOCKS, 256), lambda i, info: (info[0], 0, 0)),
        whole((half, BLOCKS, 256)),
    ]
    turned = [
        pltpu.VMEM((rows, 512), BF16),
        pltpu.VMEM((512, rows), BF16),
        pltpu.VMEM((512, rows), BF16),
    ]
    units = [pltpu.VMEM((rows, 512), BF16), pltpu.VMEM((rows, 512), BF16)]
    if mine:
        share = jax.ShapeDtypeStruct((half, BLOCKS, 256), BF16)
        in_specs += [ANY] * 4 + [whole((rows, 512)), whole((1, 512))]
        outs = [share, share, wide, pack, pack, jax.ShapeDtypeStruct((8, 512), F32)]
        weights = [pltpu.VMEM((2, 512, 512), BF16), pltpu.VMEM((2, 512, 512), BF16)]
        scratch = turned + weights + units
        scratch += [
            pltpu.VMEM((rows, 512), F32),
            pltpu.VMEM((rows, 512), F32),
            pltpu.VMEM((BLOCKS, 512), BF16),
            pltpu.SemaphoreType.DMA((6,)),
        ]
    else:
        in_specs += [ANY] * 2
        outs = [wide, wide, pack, pack]
        scratch = turned + [pltpu.VMEM((2, 2, 512, 512), BF16)] + units
        scratch += [pltpu.SemaphoreType.DMA((2,))]
    return launch(
        ff_second_kernel if mine else ff_first_kernel,
        "ff_own" if mine else "ff_other",
        12,
        1,
        info,
        (normed, cot, cot_other, *given),
        in_specs,
        outs,
        [whole(shape.shape) for shape in outs],
        scratch,
        after,
    )


def triple(values):
    high = values.astype(BF16)
    rest = values - high.astype(F32)
    middle = rest.astype(BF16)
    return high, middle, (rest - middle.astype(F32)).astype(BF16)


def attention_back_body(
    info,
    first_head,
    own_ref,
    other_ref,
    query_ref,
    key_ref,
    value_ref,
    log_ref,
    att_ref,
    grad_mid_ref,
    spread_ref,
    collect_ref,
    gain_attn_ref,
    wq_ref,
    wk_ref,
    wv_ref,
    wo_ref,
    keep_ref,
    send_ref,
    strips,
    pooled,
    outer,
    grads,
    sums,
    acc,
):
    step = pl.program_id(0)
    mp, place = info[0], info[3]
    length = info[4 + mp * 2 + step]
    count = lax.shift_right_logical(length + 3, 2)

    @pl.when(step == 0)
    def _():
        build_strips(spread_ref, strips)
        sums[...] = jnp.zeros_like(sums)

    gather_halves(info, pooled, own_ref, other_ref)
    branch = grad_mid_ref[0].astype(BF16)
    outer[...] = mm(branch, wo_ref[...], NT).astype(BF16)
    lane = lax.broadcasted_iota(jnp.int32, (BLOCKS, 128), 1)
    row = lax.broadcasted_iota(jnp.int32, (BLOCKS, 128), 0)
    dead = jnp.where(row < count, 0.0, MASKED_SCORE).astype(BF16)
    one = jnp.ones((BLOCKS, 128), BF16)
    nought = jnp.zeros((BLOCKS, 128), BF16)

    for pair in range(2):
        span = span_of(pair, 128)
        queries = query_ref[0, :, span]
        keys = key_ref[0, :, span]
        values = value_ref[0, :, span]
        out_grads = outer[:, span]
        overlap = out_grads.astype(F32) * att_ref[0, :, span].astype(F32)
        found = []
        for side in range(2):
            head = pair * 2 + side
            own = (lane < 64) == (side == 0)
            spare = 64 * (1 - side)
            delta = jnp.sum(jnp.where(own, overlap, 0.0), axis=1, keepdims=True)
            logs = jnp.sum(
                jnp.where(lane == first_head + head, log_ref[0], 0.0), axis=1, keepdims=True
            )

            def joined(base, lead, parts):
                filled = jnp.where(own, base, nought)
                filled = jnp.where(lane == spare, lead, filled)
                for index, part in enumerate(parts):
                    filled = jnp.where(lane == spare + 1 + index, part, filled)
                return filled

            chosen = joined(queries, one, triple(-logs))
            masked = joined(keys, dead, (one, one, one))
            drawn = joined(out_grads, nought, triple(-delta))
            weighed = joined(values, nought, (one, one, one))
            grad_key = jnp.zeros((BLOCKS, 128), F32)
            grad_value = jnp.zeros((BLOCKS, 128), F32)
            grad_query = []
            for half in range(2):
                rows = span_of(half, 256)
                scores = mm(masked, chosen[rows, :], NT)
                bias = jnp.concatenate(
                    [
                        strips[head, :, (3 - tile) * 128 + half * 256 : (5 - tile) * 128 + half * 256]
                        for tile in range(4)
                    ],
                    axis=0,
                )
                probs = jnp.exp(scores + bias)
                slope = mm(weighed, drawn[rows, :], NT)
                product = probs * slope
                grad_scores = product.astype(BF16)
                grad_value = grad_value + mm(probs.astype(BF16), out_grads[rows, :])
                grad_key = grad_key + mm(grad_scores, queries[rows, :])
                grad_query.append(mm(grad_scores, keys, TN))
                for line in range(5):
                    first = (3 - line + 1) * 128 + half * 256
                    total = None
                    for tile in range(4):
                        column = tile - line + 1
                        if 0 <= column < 2:
                            block = product[span_of(tile, 128), span_of(column, 128)]
                            total = block if total is None else total + block
                    sums[head, :, first : first + 128] += total
            found.append((jnp.concatenate(grad_query, axis=0), grad_key, grad_value))
        for index in range(3):
            grads[:, index * 256 + pair * 128 : index * 256 + (pair + 1) * 128] = jnp.where(
                lane < 64, found[0][index], found[1][index]
            ).astype(BF16)

    wide = pooled[...].astype(F32)
    scale = inverse_rms(wide)
    unit = wide * scale
    normed = (unit * gain_attn_ref[...]).astype(BF16)
    turned = jnp.transpose(normed)
    turned_branch = jnp.transpose(branch)
    new = mm(turned, grads[...])
    new_out = mm(turned_branch, att_ref[0])

    @pl.when(step == 0)
    def _():
        acc[:, 0:768] = new
        acc[:, 768:1024] = new_out

    @pl.when(step == 1)
    def _():
        acc[:, 0:768] += new
        acc[:, 768:1024] += new_out
        for part, target in ((1, send_ref), (0, keep_ref)):
            for shard in range(SHARDS):
                at = lax.bitwise_xor(place, shard)
                for index in range(4):
                    target[at, :, span_of(index, 128)] = acc[
                        span_of(shard, 64), index * 256 + part * 128 : index * 256 + (part + 1) * 128
                    ].astype(BF16)

    grad_normed = (
        mm(grads[:, 0:256], wq_ref[...], NT)
        + mm(grads[:, 256:512], wk_ref[...], NT)
        + mm(grads[:, 512:768], wv_ref[...], NT)
    )
    return unit, scale, grad_normed


def fold_bias(sums, collect_ref):
    rows = []
    for head in range(4):
        folded = jnp.concatenate((sums[head], jnp.zeros((128, 128), F32)), axis=1)
        size = 64
        while size >= 1:
            folded = folded[:size] + pltpu.roll(folded[size : 2 * size], WRAP - size, 1)
            size //= 2
        rows.append(folded)
    lines = jnp.concatenate(rows + rows, axis=0)
    return lax.dot_general(
        lines, collect_ref[...], NN, precision=PRECISE, preferred_element_type=F32
    )


def attention_back_first_kernel(info, *refs):
    heads, (grad_ref, keep_ref, send_ref, rel_ref), scratch = refs[:15], refs[15:19], refs[19:]
    _, _, grad_normed = attention_back_body(info, 4, *heads, keep_ref, send_ref, *scratch)
    grad_ref[0] = grad_normed

    @pl.when(pl.program_id(0) == 1)
    def _():
        rel_ref[...] = fold_bias(scratch[4], heads[9])


def attention_back_second_kernel(info, *refs):
    heads, (held_ref, rel_ref, gain_mid_ref), refs = refs[:15], refs[15:18], refs[18:]
    (keep_rows, send_rows, keep_ref, send_ref, tiny_ref), scratch = refs[:5], refs[5:]
    scratch, acc_gain = scratch[:-1], scratch[-1]
    unit, scale, grad_normed = attention_back_body(info, 0, *heads, keep_ref, send_ref, *scratch)
    mp, core = info[0], info[1]
    step = pl.program_id(0)
    pooled = scratch[1]
    grad_normed = grad_normed + held_ref[0]
    scaled = grad_normed * heads[10][...]
    grad_pooled = heads[7][0] + scale * (
        scaled - unit * jnp.mean(scaled * unit, axis=1, keepdims=True)
    )
    pooled[...] = grad_pooled.astype(BF16)
    keep_rows[0] = pooled[:, tile_at(mp, 256)]
    send_rows[0] = pooled[:, tile_at(1 - mp, 256)]
    new_gain = jnp.sum(grad_normed * unit, axis=0, keepdims=True)

    @pl.when(step == 0)
    def _():
        acc_gain[...] = jnp.broadcast_to(new_gain, acc_gain.shape)

    @pl.when(step == 1)
    def _():
        found = fold_bias(scratch[4], heads[9])
        line = lax.broadcasted_iota(jnp.int32, (8, 128), 0)
        rows = jnp.zeros((8, 128), F32)
        for head in range(8):
            source = found if head < 4 else rel_ref[...]
            true_head = (
                lax.bitwise_xor(mp, head // 4) * 4
                + lax.bitwise_xor(core, (head // 2) % 2) * 2
                + head % 2
            )
            rows = jnp.where(line == true_head, source[head % 4 : head % 4 + 1, :], rows)
        tiny_ref[...] = jnp.zeros_like(tiny_ref)
        tiny_ref[0:1, :] = acc_gain[0:1, :] + new_gain
        tiny_ref[1:2, :] = gain_mid_ref[0:1, :]
        tiny_ref[8:16, 0:128] = rows


def attention_back(
    info, mine, rows_args, spread, collect, gain_attn, joined, w_o, given, after
):
    own, other, qkv, logs, att, grad_mid = rows_args
    half = own.shape[0]
    where = 0 if mine else 1

    def lanes(index):
        return pl.BlockSpec((1, BLOCKS, 256), lambda i, info: (i, 0, index))

    def columns(index):
        return pl.BlockSpec((512, 256), lambda i, info: (0, index))

    in_specs = [
        item((BLOCKS, 256)),
        item((BLOCKS, 256)),
        lanes(where),
        lanes(2 + where),
        lanes(4 + where),
        item((BLOCKS, 128)),
        lanes(where),
        item((BLOCKS, 512)),
        whole((4, WRAP)),
        whole((WRAP, 128)),
        whole((1, 512)),
        columns(where),
        columns(2 + where),
        columns(4 + where),
        pl.BlockSpec((256, 512), lambda i, info: (where, 0)),
    ]
    args = [own, other, qkv, qkv, qkv, logs, att, grad_mid, spread, collect, gain_attn]
    args += [joined, joined, joined, w_o]
    packed = (SHARDS, 64, 512)
    pack = jax.ShapeDtypeStruct(packed, BF16)
    scratch = [
        pltpu.VMEM((4, 128, 896), F32),
        pltpu.VMEM((BLOCKS, 512), BF16),
        pltpu.VMEM((BLOCKS, 256), BF16),
        pltpu.VMEM((BLOCKS, 768), BF16),
        pltpu.VMEM((4, 128, 896), F32),
        pltpu.VMEM((512, 1024), F32),
    ]
    if mine:
        share = jax.ShapeDtypeStruct((half, BLOCKS, 256), BF16)
        in_specs += [item((BLOCKS, 512)), whole((8, 128)), whole((8, 512))]
        outs = [share, share, pack, pack, jax.ShapeDtypeStruct((16, 512), F32)]
        out_specs = [item((BLOCKS, 256)), item((BLOCKS, 256)), whole(packed), whole(packed)]
        out_specs += [whole((16, 512))]
        scratch += [pltpu.VMEM((8, 512), F32)]
    else:
        outs = [
            jax.ShapeDtypeStruct((half, BLOCKS, 512), F32),
            pack,
            pack,
            jax.ShapeDtypeStruct((8, 128), F32),
        ]
        out_specs = [item((BLOCKS, 512)), whole(packed), whole(packed), whole((8, 128))]
    return launch(
        attention_back_second_kernel if mine else attention_back_first_kernel,
        "attention_back_own" if mine else "attention_back_other",
        17,
        half,
        info,
        (*args, *given),
        in_specs,
        outs,
        out_specs,
        scratch,
        after,
    )


def place_kernel(info, ff_near, ff_far, hid_ref, mid_ref):
    core, place = info[1], info[3]
    for source, side in ((ff_near, core), (ff_far, 1 - core)):
        turned = []
        for shard in range(SHARDS):
            at = lax.bitwise_xor(place, shard)
            hid_ref[span_of(shard, 64), tile_at(side, 512)] = source[at, 0:64, :].astype(F32)
            turned.append(source[at, 64:128, :])
        mid_ref[tile_at(side, 512), :] = jnp.transpose(
            jnp.concatenate(turned, axis=0).astype(F32)
        )


def attn_place_kernel(info, near, far, query_ref, key_ref, value_ref, out_ref):
    core, place = info[1], info[3]
    for source, side in ((near, core), (far, 1 - core)):
        turned = []
        for shard in range(SHARDS):
            at = lax.bitwise_xor(place, shard)
            for index, target in enumerate((query_ref, key_ref, value_ref)):
                target[span_of(shard, 64), tile_at(side, 128)] = source[
                    at, :, span_of(index, 128)
                ].astype(F32)
            turned.append(source[at, :, 384:512])
        out_ref[tile_at(side, 128), :] = jnp.transpose(
            jnp.concatenate(turned, axis=0).astype(F32)
        )


def place_weights(kernel, name, info, near, far, shapes, after):
    return launch(
        kernel,
        name,
        4,
        1,
        info,
        (near, far),
        [whole(near.shape), whole(far.shape)],
        [jax.ShapeDtypeStruct(shape, F32) for shape in shapes],
        [whole(shape) for shape in shapes],
        (),
        after,
    )


def shards(
    devices,
    byte_states,
    frontier,
    lengths,
    gain_attn,
    w_query,
    w_key,
    w_value,
    w_attn_out,
    rel_bias,
    gain_mlp,
    w_hidden,
    w_mlp_out,
    cotangent,
):
    bits = devices.bit_length() - 1
    mp = lax.axis_index("mp").astype(jnp.int32)
    dp = lax.axis_index("dp").astype(jnp.int32)
    core = dp & 1
    way = (dp >> 1) & 1
    place = (((dp >> 1) & 1) << 2) | (((dp >> 2) & 1) << 1) | ((dp >> 3) & 1)
    info = jnp.concatenate((jnp.stack((mp, core, way, place)), lengths))

    def across(value):
        return lax.ppermute(value, "mp", [(0, 1), (1, 0)])

    def swap(value, bit):
        return lax.ppermute(value, "dp", [(i, i ^ (1 << bit)) for i in range(devices)])

    def added(a, b):
        return (a.astype(F32) + b.astype(F32)).astype(BF16)

    row = way * 256
    out_piece = lax.dynamic_slice(w_attn_out, (core * 128 + way * 64, 0), (64, 512))
    attn_piece = jnp.concatenate(
        [
            lax.dynamic_slice(weight, (row, core * 128), (256, 128))
            for weight in (w_query, w_key, w_value)
        ]
        + [jnp.concatenate([out_piece[:, lane * 128 : (lane + 1) * 128] for lane in range(4)], 0)],
        axis=1,
    )
    attn_first = across(attn_piece)
    ff_sent = jnp.stack(
        (
            lax.dynamic_slice(w_hidden, (0, core * 512), (512, 512)),
            lax.dynamic_slice(w_mlp_out, (core * 512, 0), (512, 512)),
        )
    )
    cot_sent = lax.dynamic_slice_in_dim(cotangent, (1 - mp) * 2, 2, 0)

    forward, backward, collect = offset_tables()
    tables = jnp.asarray(np.concatenate((forward, backward), axis=0))
    spread_own = jnp.dot(tables, rel_bias, precision=PRECISE).T
    spread_own = jnp.where(core == 0, spread_own, jnp.roll(spread_own, 2, axis=0))
    spread_other = across(spread_own)
    spread_forward = jnp.concatenate((spread_own[:, :WRAP], spread_other[:, :WRAP]), axis=0)

    def swap_far(value, index):
        turn = ((index >> 1) << 2) | ((index & 1) << 3)
        return lax.ppermute(value, "dp", [(i, i ^ turn) for i in range(devices)])

    pooled_sent, positions, pool_keep = pool_forward(info, frontier, byte_states)
    pooled_other = across(pooled_sent)
    attn_second = swap(attn_first, 1)
    (pooled_own,) = pool_keep((attn_first, spread_forward), ())
    attn_first, attn_second, ff_sent, cot_sent = combine(
        "meet",
        (),
        (pooled_other, attn_second, pooled_own),
        (attn_first, attn_second, ff_sent, cot_sent),
    )
    attn_parts = (attn_first, attn_second, swap(attn_first, 0), swap(attn_second, 0))
    ff_first = across(ff_sent)
    cot_other = across(cot_sent)

    gain_attn_row = gain_attn.reshape(1, -1)
    gain_mlp_row = gain_mlp.reshape(1, -1)
    qkv, logs, att, middle, normed, joined, w_o = attention_forward(
        info,
        pooled_own,
        pooled_other,
        spread_forward,
        gain_attn_row,
        gain_mlp_row,
        (w_query, w_key, w_value, w_attn_out),
        attn_parts,
        (),
    )
    half = pooled_own.shape[0]
    normed = normed.reshape(half * BLOCKS, -1)
    middle = middle.reshape(half * BLOCKS, -1)

    (ff_first,) = combine("meet", (), (normed, cot_other), (ff_first,))
    result, back, far_keep, far_sent = ff_call(
        info, normed, cotangent, cot_other, False, (ff_first, swap(ff_first, 0)), ()
    )
    halves, quarters = (SHARDS // 2, SHARDS // 2), (1, 1, 1, 1)
    far_low, far_high = combine("far_cores", [(False, (far_keep, swap(far_sent, 0)), halves)]
    )
    got = swap(far_high, 1)
    blocks_keep, blocks_sent, grad_mid, near_keep, near_sent, gain_mid = ff_call(
        info,
        normed,
        cotangent,
        cot_other,
        True,
        (w_hidden, w_mlp_out, result, back, middle, gain_mlp_row),
        (far_low,),
    )
    far_ff, near_sent = combine("far_y", [(False, (far_low, got), None)], (gain_mid,), (near_sent,)
    )
    got_far = across(far_ff)
    near_low, near_high = combine("near_cores", [(False, (near_keep, swap(near_sent, 0)), halves)]
    )
    got = swap(near_high, 1)

    grad_mid = grad_mid.reshape(half, BLOCKS, -1)
    rows_args = (pooled_own, pooled_other, qkv, logs, att, grad_mid)
    collect = jnp.asarray(collect)
    grad_normed, far_keep, far_sent, far_rel = attention_back(
        info,
        False,
        rows_args,
        spread_other[:, WRAP:],
        collect,
        gain_attn_row,
        joined,
        w_o,
        (),
        (near_low,),
    )
    *ff_parts, far_sent = combine("near_y", [(False, (near_low, got, got_far), quarters)],
        (grad_normed,),
        (far_sent,),
    )
    more = range(4, bits)
    got_ff = [swap_far(ff_parts[index], index) for index in range(1, 4)]
    (far_attn,) = combine("far_cores", [(False, (far_keep, swap(far_sent, 0)), None)])
    got_attn = across(far_attn)
    grad_keep, grad_sent, near_keep, near_sent, tiny = attention_back(
        info,
        True,
        rows_args,
        spread_own[:, WRAP:],
        collect,
        gain_attn_row,
        joined,
        w_o,
        (grad_normed, far_rel, gain_mid),
        (far_attn, ff_parts[0]),
    )
    grad_other = across(grad_sent)
    near_ff, near_sent = combine("ff_z", [(False, (ff_parts[0], *got_ff), None)],
        (tiny, got_attn),
        (near_sent,),
    )
    for bit in more:
        near_ff = added(near_ff, swap(near_ff, bit))
    got_ff = [swap_far(near_ff, index) for index in range(1, 4)]
    attn_low, attn_high, tiny = combine("near_cores", [
            (False, (near_keep, swap(near_sent, 0), got_attn), halves),
            (False, (tiny, swap(tiny, 0)), None),
        ],
    )
    got_attn, got_tiny = swap(attn_high, 1), swap(tiny, 1)

    def pool_item(mine, index, held, after, through=()):
        grads = grad_keep if mine else grad_other
        return pool_backward(
            info, positions, byte_states, grads, mine, index, held, after, through
        )

    *held, blocks_sent = pool_item(True, 0, (), (attn_low,), (blocks_sent,))
    blocks_other = across(blocks_sent)
    near_ff, *attn_parts, tiny = combine("step_one", [
            (True, (near_ff, *got_ff), None),
            (False, (attn_low, got_attn), quarters),
            (False, (tiny, got_tiny), None),
        ],
        (held[1], grad_other),
    )
    got_ff = swap(near_ff, 1)
    got_attn = [swap_far(attn_parts[index], index) for index in range(1, 4)]
    got_tiny = swap(tiny, 2)

    held = pool_item(True, 1, held, (tiny,))
    near_ff, near_attn, tiny = combine("step_two", [
            (True, (near_ff, got_ff), None),
            (False, (attn_parts[0], *got_attn), None),
            (False, (tiny, got_tiny), None),
        ],
        (held[1],),
    )
    far_ff = swap(near_ff, 0)
    for bit in more:
        near_attn = added(near_attn, swap(near_attn, bit))
        tiny = tiny + swap(tiny, bit)
    got_attn = [swap_far(near_attn, index) for index in range(1, 4)]
    got_tiny = swap(tiny, 3)

    held = pool_item(False, 0, held, (tiny,))
    near_attn, tiny = combine("step_three", [(True, (near_attn, *got_attn), None), (False, (tiny, got_tiny), None)],
        (held[1],),
    )
    got_attn, got_tiny = swap(near_attn, 1), across(tiny)

    held = pool_item(False, 1, held, (tiny,))
    grad_bytes, part = held
    near_attn, tiny = combine("step_four", [(True, (near_attn, got_attn), None), (False, (tiny, got_tiny), None)],
        (part,),
    )
    far_attn = swap(near_attn, 0)
    grad_hidden, grad_mlp = place_weights(
        place_kernel, "ff_place", info, near_ff, far_ff, (w_hidden.shape, w_mlp_out.shape), (part,)
    )
    grad_frontier = frontier_gradient(
        info, part, across(part), positions, frontier, (grad_hidden,)
    )
    grad_query, grad_key, grad_value, grad_out = place_weights(
        attn_place_kernel,
        "attn_place",
        info,
        near_attn,
        far_attn,
        (w_query.shape, w_key.shape, w_value.shape, w_attn_out.shape),
        (grad_frontier,),
    )
    blocks_out = jnp.where(
        mp == 0,
        jnp.concatenate((blocks_keep, blocks_other), axis=0),
        jnp.concatenate((blocks_other, blocks_keep), axis=0),
    )
    grad_rel = lax.dynamic_slice(tiny, (8 + mp * 4, 0), (4, BUCKETS)).T
    return (
        blocks_out,
        grad_bytes,
        grad_frontier,
        tiny[0],
        grad_query,
        grad_key,
        grad_value,
        grad_out,
        grad_rel,
        tiny[1],
        grad_hidden,
        grad_mlp,
    )


def solution(mesh):
    placed = (
        P("dp", None, "mp"),
        P("dp", None),
        P("dp"),
        P(),
        P(None, "mp"),
        P(None, "mp"),
        P(None, "mp"),
        P("mp", None),
        P(None, "mp"),
        P(),
        P(None, "mp"),
        P("mp", None),
        P("dp", None, "mp"),
    )
    return jax.shard_map(
        functools.partial(shards, mesh.shape["dp"]),
        mesh=mesh,
        in_specs=placed,
        out_specs=(
            P("dp", None, "mp"),
            P("dp", None, "mp"),
            P("dp", None),
            P(),
            P(None, "mp"),
            P(None, "mp"),
            P(None, "mp"),
            P("mp", None),
            P(None, "mp"),
            P(),
            P(None, "mp"),
            P("mp", None),
        ),
        check_vma=False,
    )
```

```python
import functools
import math

import jax
import jax.numpy as jnp
import numpy as np
from jax import lax
from jax.experimental import pallas as pl
from jax.experimental.pallas import tpu as pltpu
from jax.sharding import PartitionSpec as P

BUCKETS = 32
REACH = 128
BLOCKS = 512
WRAP = 2 * BLOCKS
SHARDS = 8

EPSILON = 1e-06
SHARPNESS = 2.0
MASKED_SCORE = -1000000000.0
OUTSIDE = -10000.0
REACH_OUT = 8.0
PRECISE = lax.Precision.HIGHEST
ROOT = 0.7978845608028654
CUBIC = 0.044715
VMEM_LIMIT = 24 * 1024 * 1024
VMEM_MOST = 60 * 1024 * 1024
CHUNK = 256

F32 = jnp.float32
BF16 = jnp.bfloat16
ANY = pl.BlockSpec(memory_space=pl.ANY)
HBM = pl.BlockSpec(memory_space=pltpu.HBM)
NEAR = pl.BlockSpec(memory_space=pltpu.VMEM)
NN = (((1,), (0,)), ((), ()))
NT = (((1,), (1,)), ((), ()))
TN = (((0,), (0,)), ((), ()))


def mm(a, b, dims=NN):
    return lax.dot_general(a, b, dims, preferred_element_type=F32)


def bucket_of(offset):
    half_count = BUCKETS // 2
    exact_count = half_count // 2
    distance = abs(offset)
    if distance < exact_count:
        place = distance
    else:
        place = min(
            half_count - 1,
            exact_count
            + math.floor(
                math.log(distance / exact_count)
                / math.log(REACH / exact_count)
                * (half_count - exact_count)
            ),
        )
    return place + (half_count if offset > 0 else 0)


def offset_tables():
    forward = np.zeros((WRAP, BUCKETS), np.float32)
    backward = np.zeros((WRAP, BUCKETS), np.float32)
    collect = np.zeros((WRAP, 128), np.float32)
    for offset in range(1 - BLOCKS, BLOCKS):
        bucket = bucket_of(offset)
        forward[offset % WRAP, bucket] = 1.0
        backward[(-offset) % WRAP, bucket] = 1.0
        collect[(384 - offset) % WRAP, bucket] = 1.0
    return forward.T, backward.T, collect


def cost(micros):
    return pl.CostEstimate(flops=1, bytes_accessed=1, transcendentals=0)


def whole(shape):
    return pl.BlockSpec(shape, functools.partial(lambda n, i, info: (0,) * n, len(shape)))


def item(shape):
    return pl.BlockSpec(
        (1,) + shape, functools.partial(lambda n, i, info: (i,) + (0,) * n, len(shape))
    )


def launch(
    kernel, name, micros, grid, info, args, in_specs, outs, out_specs, scratch=(), after=(),
    through=(), aliases=None, vmem=VMEM_LIMIT,
):
    given, waits, passed, made = 1 + len(args), len(after), len(through), len(outs)

    def body(*refs):
        first = given + waits + passed
        kernel(*refs[:given], *refs[first : first + made], *refs[first + made + passed :])

    aliases = dict(aliases or {})
    for index in range(passed):
        aliases[given + waits + index] = made + index
    return pl.pallas_call(
        body,
        grid_spec=pltpu.PrefetchScalarGridSpec(
            num_scalar_prefetch=1,
            grid=(grid,),
            in_specs=list(in_specs) + [ANY] * (waits + passed),
            out_specs=list(out_specs) + [ANY] * passed,
            scratch_shapes=list(scratch),
        ),
        out_shape=list(outs) + [jax.ShapeDtypeStruct(x.shape, x.dtype) for x in through],
        input_output_aliases=aliases,
        compiler_params=pltpu.CompilerParams(
            vmem_limit_bytes=vmem, dimension_semantics=("arbitrary",)
        ),
        cost_estimate=cost(micros),
        name=name,
    )(info, *args, *after, *through)


def combine(name, work, args=(), outs=(), after=(), through=()):
    given, held, made, passed = len(args), len(args) + len(after), len(outs), len(through)

    def kernel(*refs):
        work(refs[:given], refs[held + passed : held + passed + made])

    near = pl.BlockSpec(memory_space=pltpu.VMEM)
    return pl.pallas_call(
        kernel,
        in_specs=[near] * given + [ANY] * (len(after) + passed),
        out_specs=[near] * made + [ANY] * passed,
        out_shape=[jax.ShapeDtypeStruct(*out) for out in outs]
        + [jax.ShapeDtypeStruct(x.shape, x.dtype) for x in through],
        input_output_aliases={held + index: made + index for index in range(passed)},
        compiler_params=pltpu.CompilerParams(vmem_limit_bytes=16 * 1024 * 1024),
        cost_estimate=cost(1),
        name=name,
    )(*args, *after, *through)


def nothing(ins, outs):
    pass


def sum_into(ins, outs):
    at = 0
    for out in outs:
        rows = slice(at, at + out.shape[0])
        value = ins[0][rows, :].astype(F32)
        for other in ins[1:]:
            value = value + other[rows, :].astype(F32)
        out[...] = value.astype(out.dtype)
        at += out.shape[0]


def join_into(ins, out):
    at = 0
    for source in ins:
        out[at : at + source.shape[0], :] = source[...]
        at += source.shape[0]


def share_out(info):
    lengths = [info[4 + item] for item in range(4)]
    ranks = []
    for item in range(4):
        rank = jnp.int32(0)
        for other in range(4):
            if other != item:
                before = lengths[other] <= lengths[item] if other < item else (
                    lengths[other] < lengths[item]
                )
                rank = rank + jnp.where(before, 1, 0)
        ranks.append(rank)

    def at(wanted):
        found = jnp.int32(0)
        for item in range(1, 4):
            found = jnp.where(ranks[item] == wanted, item, found)
        return found

    sides = ((at(3), at(0)), (at(2), at(1)))
    first = info[0] == 0
    mine = [jnp.where(first, a, b) for a, b in zip(*sides)]
    theirs = [jnp.where(first, b, a) for a, b in zip(*sides)]
    return mine, theirs


def item_count(info, index):
    mine = share_out(info)[0]
    item = mine[index] if isinstance(index, int) else jnp.where(index == 0, mine[0], mine[1])
    return lax.shift_right_logical(info[4 + item] + 3, 2)


def byte_copy(bytes_ref, buffer, sems, item, slot, chunk):
    rows = pl.ds(chunk * CHUNK, CHUNK)
    return pltpu.make_async_copy(
        bytes_ref.at[item, rows, :], buffer.at[slot, rows, :], sems.at[slot, chunk]
    )


def fetch_bytes(bytes_ref, buffer, sems, item, length, slot):
    for chunk in range(bytes_ref.shape[1] // CHUNK):

        @pl.when(chunk * CHUNK < length)
        def _():
            byte_copy(bytes_ref, buffer, sems, item, slot, chunk).start()


def near_blocks(item, pos_ref):
    found = []
    for chunk in range(pos_ref.shape[1] // CHUNK):
        row = pos_ref[pl.ds(item, 1), span_of(chunk, CHUNK)]
        found.append((row, jnp.min(jnp.where(row < 0.0, 1e6, row)), jnp.max(row)))
    return found


def pool_rows(item, slot, info, pos_ref, bytes_ref, buffer, out_ref, acc, sems):
    length = info[4 + item]
    count = lax.shift_right_logical(length + 3, 2)
    acc[...] = jnp.zeros_like(acc)
    for chunk, (row, low, high) in enumerate(near_blocks(item, pos_ref)):

        @pl.when(chunk * CHUNK < length)
        def _():
            byte_copy(bytes_ref, buffer, sems, item, slot, chunk).wait()

        for tile in range(BLOCKS // 128):
            near = jnp.logical_and(
                high > tile * 128 - REACH_OUT, low < tile * 128 + 128 + REACH_OUT
            )

            @pl.when(jnp.logical_and(near, tile * 128 < count))
            def _():
                centre = (
                    lax.broadcasted_iota(jnp.int32, (128, CHUNK), 0).astype(F32) + tile * 128 + 0.5
                )
                offset = row - centre
                kernel = jnp.exp(-SHARPNESS * offset * offset).astype(BF16)
                acc[span_of(tile, 128), :] += mm(kernel, buffer[slot, span_of(chunk, CHUNK), :])

    live = lax.broadcasted_iota(jnp.int32, acc.shape, 0) < count
    out_ref[slot] = jnp.where(live, acc[...], 0.0).astype(BF16)


def masked_positions(info, frontier_ref, pos_ref):
    items, byte_count = frontier_ref.shape
    lane = lax.broadcasted_iota(jnp.int32, (items, byte_count), 1)
    row = lax.broadcasted_iota(jnp.int32, (items, byte_count), 0)
    length = jnp.zeros((items, byte_count), jnp.int32)
    for item in range(items):
        length = jnp.where(row == item, info[4 + item], length)
    valid = lane < length
    running = jnp.where(valid, frontier_ref[...], 0.0)
    step = 1
    while step < byte_count:
        running = running + jnp.where(lane >= step, pltpu.roll(running, step, 1), 0.0)
        step *= 2
    count = lax.shift_right_logical(length + 3, 2).astype(F32)
    total = running[:, byte_count - 1 :]
    pos_ref[...] = jnp.where(valid, count * running / total, OUTSIDE)


def pool_first_kernel(info, frontier_ref, bytes_ref, out_ref, pos_ref, buffer, acc, sems):
    theirs = share_out(info)[1]
    for slot, item in enumerate(theirs):
        fetch_bytes(bytes_ref, buffer, sems, item, info[4 + item], slot)
    masked_positions(info, frontier_ref, pos_ref)
    for slot, item in enumerate(theirs):
        pool_rows(item, slot, info, pos_ref, bytes_ref, buffer, out_ref, acc, sems)


def pool_second_kernel(info, pos_ref, bytes_ref, out_ref, buffer, acc, sems):
    mine = share_out(info)[0]
    for slot, item in enumerate(mine):
        fetch_bytes(bytes_ref, buffer, sems, item, info[4 + item], slot)
    for slot, item in enumerate(mine):
        pool_rows(item, slot, info, pos_ref, bytes_ref, buffer, out_ref, acc, sems)


def pool_forward(info, frontier, byte_states, after):
    items, byte_count, share = byte_states.shape
    half = items // 2
    out = jax.ShapeDtypeStruct((half, BLOCKS, share), BF16)
    scratch = [
        pltpu.VMEM((half, byte_count, share), BF16),
        pltpu.VMEM((BLOCKS, share), F32),
        pltpu.SemaphoreType.DMA((half, byte_count // CHUNK)),
    ]
    send, positions = launch(
        pool_first_kernel,
        "pool_send",
        7,
        1,
        info,
        (frontier, byte_states),
        [whole((items, byte_count)), HBM],
        [out, jax.ShapeDtypeStruct((items, byte_count), F32)],
        [whole(out.shape), whole((items, byte_count))],
        scratch,
        after,
        vmem=VMEM_MOST,
    )

    def keep(after, through):
        return launch(
            pool_second_kernel,
            "pool_keep",
            7,
            1,
            info,
            (positions, byte_states),
            [whole((items, byte_count)), HBM],
            [out],
            [whole(out.shape)],
            scratch,
            after,
            through,
            vmem=VMEM_MOST,
        )

    return send, positions, keep


def pool_back_kernel(mine, index, info, pos_ref, bytes_ref, grads_ref, *refs):
    out_ref, part_ref, buffer, written, acc, terms, sems, out_sems = refs[-8:]
    item = share_out(info)[0 if mine else 1][index]
    length = info[4 + item]
    count = lax.shift_right_logical(length + 3, 2)
    grads = grads_ref.at[index] if mine else grads_ref.at[span_of(index, BLOCKS)]
    fetch_bytes(bytes_ref, buffer, sems, item, length, 0)
    ones = jnp.ones((8, 128), BF16)
    copies = []
    for chunk, (row, low, high) in enumerate(near_blocks(item, pos_ref)):
        span = span_of(chunk, CHUNK)

        @pl.when(chunk * CHUNK >= length)
        def _():
            written[span, :] = jnp.zeros((CHUNK, written.shape[1]), BF16)
            part_ref[0, :, span] = jnp.zeros((1, CHUNK), F32)

        @pl.when(chunk * CHUNK < length)
        def _():
            byte_copy(bytes_ref, buffer, sems, item, 0, chunk).wait()
            acc[...] = jnp.zeros_like(acc)
            terms[...] = jnp.zeros_like(terms)
            column = jnp.transpose(jnp.broadcast_to(row, (128, CHUNK)))
            for tile in range(BLOCKS // 128):
                near = jnp.logical_and(
                    high > tile * 128 - REACH_OUT, low < tile * 128 + 128 + REACH_OUT
                )

                @pl.when(jnp.logical_and(near, tile * 128 < count))
                def _():
                    centre = (
                        lax.broadcasted_iota(jnp.int32, (CHUNK, 128), 1).astype(F32)
                        + tile * 128
                        + 0.5
                    )
                    offset = column - centre
                    kernel = jnp.exp(-SHARPNESS * offset * offset)
                    rows = grads[span_of(tile, 128), :]
                    acc[...] += mm(kernel.astype(BF16), rows)
                    slope = mm(buffer[0, span, :], rows, NT)
                    terms[...] += slope * kernel * offset

            written[span, :] = acc[...].astype(BF16)
            term = terms[...]
            high_part = term.astype(BF16)
            low_part = (term - high_part.astype(F32)).astype(BF16)
            summed = mm(ones, high_part, NT) + mm(ones, low_part, NT)
            part_ref[0, :, span] = -4.0 * summed[0:1, :]

        copy = pltpu.make_async_copy(
            written.at[span, :], out_ref.at[item, span, :], out_sems.at[chunk]
        )
        copy.start()
        copies.append(copy)
    for copy in copies:
        copy.wait()


def pool_backward(info, positions, byte_states, grads, mine, index, held, after, through):
    items, byte_count, share = byte_states.shape
    side = 0 if mine else 1
    return launch(
        functools.partial(pool_back_kernel, mine, index),
        "pool_back",
        5,
        1,
        info,
        (positions, byte_states, grads) + tuple(held),
        [whole((items, byte_count)), HBM, NEAR] + [HBM] * len(held),
        [
            jax.ShapeDtypeStruct((items, byte_count, share), BF16),
            jax.ShapeDtypeStruct((items, 1, byte_count), F32),
        ],
        [
            HBM,
            pl.BlockSpec((1, 1, byte_count), lambda i, info: (share_out(info)[side][index], 0, 0)),
        ],
        [
            pltpu.VMEM((1, byte_count, share), BF16),
            pltpu.VMEM((byte_count, share), BF16),
            pltpu.VMEM((CHUNK, share), F32),
            pltpu.VMEM((CHUNK, 128), F32),
            pltpu.SemaphoreType.DMA((1, byte_count // CHUNK)),
            pltpu.SemaphoreType.DMA((byte_count // CHUNK,)),
        ],
        after,
        through,
        {4: 0, 5: 1} if held else None,
    )


def frontier_kernel(info, mine_ref, theirs_ref, pos_ref, frontier_ref, out_ref):
    items, byte_count = frontier_ref.shape
    lane = lax.broadcasted_iota(jnp.int32, (items, byte_count), 1)
    row = lax.broadcasted_iota(jnp.int32, (items, byte_count), 0)
    length = jnp.zeros((items, byte_count), jnp.int32)
    for item in range(items):
        length = jnp.where(row == item, info[4 + item], length)
    valid = lane < length
    total = jnp.sum(jnp.where(valid, frontier_ref[...], 0.0), axis=1, keepdims=True)
    terms = jnp.where(valid, mine_ref[:, 0, :] + theirs_ref[:, 0, :], 0.0)
    weighted = jnp.sum(terms * pos_ref[...], axis=1, keepdims=True)
    step = 1
    while step < byte_count:
        moved = pltpu.roll(terms, byte_count - step, 1)
        terms = terms + jnp.where(lane < byte_count - step, moved, 0.0)
        step *= 2
    count = lax.shift_right_logical(length + 3, 2).astype(F32)
    out_ref[...] = jnp.where(valid, (terms * count - weighted) / total, 0.0)


def build_strips(core, biases, table_ref, strips):
    rows = []
    for bias in biases:
        values = bias[...]
        turned = jnp.concatenate((values[2:4], values[0:2]), axis=0)
        rows.append(jnp.where(core == 0, values, turned))
    rows = jnp.concatenate(rows * (8 // (4 * len(rows))), axis=0)
    spread = lax.dot_general(
        rows, table_ref[...], NN, precision=PRECISE, preferred_element_type=F32
    )
    for head in range(strips.shape[0]):
        row = jnp.broadcast_to(spread[head : head + 1, :], (128, WRAP))
        turned = pltpu.roll(row, 384, 1, stride=1, stride_axis=0)
        strips[head] = turned[:, :896]


def gather_halves(info, target, own_ref, other_ref):
    first = pl.multiple_of(info[0] * 256, 256)
    second = pl.multiple_of((1 - info[0]) * 256, 256)
    target[:, pl.ds(first, 256)] = own_ref[0]
    target[:, pl.ds(second, 256)] = other_ref[0]


def span_of(index, size):
    return slice(index * size, (index + 1) * size)


def tile_at(index, size):
    return pl.ds(pl.multiple_of(index * size, size), size)


def started(pairs, sems):
    return [
        pltpu.make_async_copy(source, target, sems.at[index])
        for index, (source, target) in enumerate(pairs)
    ]


def inverse_rms(values):
    return lax.rsqrt(jnp.mean(values * values, axis=1, keepdims=True) + EPSILON)


def attention_kernel(
    info,
    own_ref,
    other_ref,
    rel_own_ref,
    rel_other_ref,
    table_ref,
    gain_attn_ref,
    gain_mlp_ref,
    w_query,
    w_key,
    w_value,
    w_out,
    part_a,
    part_b,
    part_c,
    part_d,
    qkv_ref,
    log_ref,
    att_ref,
    middle_ref,
    normed_ref,
    w_qkv,
    w_o,
    strips,
    pooled,
):
    step = pl.program_id(0)
    mp, core, way = info[0], info[1], info[2]
    count = item_count(info, step)

    @pl.when(step == 0)
    def _():
        for part in range(2):
            start = core if part == 0 else 1 - core
            for index, weight in enumerate((w_query, w_key, w_value)):
                first = index * 512 + part * 128
                w_qkv[:, first : first + 128] = weight[:, tile_at(start, 128)]
            w_o[span_of(part, 128), :] = w_out[tile_at(start, 128), :]
        for part, sources in enumerate(((part_a, part_b), (part_c, part_d))):
            for side, source in enumerate(sources):
                turn = way if side == 0 else 1 - way
                for index in range(3):
                    first = index * 512 + 256 + part * 128
                    w_qkv[tile_at(turn, 256), first : first + 128] = source[
                        0:256, span_of(index, 128)
                    ]
                rows = pl.ds(pl.multiple_of(256 + part * 128 + turn * 64, 64), 64)
                for lane in range(4):
                    w_o[rows, span_of(lane, 128)] = source[span_of(lane, 64), 384:512]
        build_strips(core, (rel_own_ref, rel_other_ref), table_ref, strips)

    gather_halves(info, pooled, own_ref, other_ref)
    wide = pooled[...].astype(F32)
    normed = (wide * inverse_rms(wide) * gain_attn_ref[...]).astype(BF16)
    qkv_ref[0] = mm(normed, w_qkv[...]).astype(BF16)
    lane = lax.broadcasted_iota(jnp.int32, (BLOCKS, 128), 1)
    row = lax.broadcasted_iota(jnp.int32, (BLOCKS, 128), 0)
    dead = jnp.where(row < count, 0.0, MASKED_SCORE).astype(BF16)

    def heads_pair(pair, logs):
        off = pl.multiple_of(pair * 128, 128)
        queries = qkv_ref[0, :, pl.ds(off, 128)]
        keys = qkv_ref[0, :, pl.ds(512 + off, 128)]
        values = qkv_ref[0, :, pl.ds(1024 + off, 128)]
        outs = []
        for side in range(2):
            head = pair * 2 + side
            own = (lane < 64) == (side == 0)
            spare = lane == 64 * (1 - side)
            chosen = jnp.where(own, queries, jnp.where(spare, 1.0, 0.0).astype(BF16))
            masked = jnp.where(spare, dead, keys)
            summing = jnp.where(own, values, jnp.ones_like(values))
            parts, tops = [], []
            for half in range(2):
                scores = mm(chosen[span_of(half, 256), :], masked, NT)
                first = (3 - 2 * half) * 128
                second = (2 - 2 * half) * 128
                bias = jnp.concatenate(
                    (
                        strips[head, :, first : first + 512],
                        strips[head, :, second : second + 512],
                    ),
                    axis=0,
                )
                scores = scores + bias
                most = jnp.max(scores, axis=1, keepdims=True)
                expo = jnp.exp(scores - most).astype(BF16)
                parts.append(mm(expo, summing))
                tops.append(most)
            out = jnp.concatenate(parts, axis=0)
            total = out[:, 64 * (1 - side) : 64 * (1 - side) + 1]
            outs.append(out * (1.0 / total))
            logs = jnp.where(lane == head, jnp.concatenate(tops, axis=0) + jnp.log(total), logs)
        att_ref[0, :, pl.ds(off, 128)] = jnp.where(lane < 64, outs[0], outs[1]).astype(BF16)
        return logs

    logs = jnp.zeros((BLOCKS, 128), F32)
    log_ref[0] = lax.fori_loop(0, 4, heads_pair, logs)

    mid = wide + mm(att_ref[0], w_o[...])
    middle_ref[0] = mid
    normed_ref[0] = (mid * inverse_rms(mid) * gain_mlp_ref[...]).astype(BF16)


def attention_forward(info, own, other, rel, table, gain_attn, gain_mlp, weights, parts, after):
    half = own.shape[0]
    return launch(
        attention_kernel,
        "attention_forward",
        20,
        half,
        info,
        (own, other, *rel, table, gain_attn, gain_mlp, *weights, *parts),
        [
            item((BLOCKS, 256)),
            item((BLOCKS, 256)),
            whole((4, BUCKETS)),
            whole((4, BUCKETS)),
            whole((BUCKETS, WRAP)),
            whole((1, 512)),
            whole((1, 512)),
        ]
        + [NEAR] * 8,
        [
            jax.ShapeDtypeStruct((half, BLOCKS, 1536), BF16),
            jax.ShapeDtypeStruct((half, BLOCKS, 128), F32),
            jax.ShapeDtypeStruct((half, BLOCKS, 512), BF16),
            jax.ShapeDtypeStruct((half, BLOCKS, 512), F32),
            jax.ShapeDtypeStruct((half, BLOCKS, 512), BF16),
            jax.ShapeDtypeStruct((512, 1536), BF16),
            jax.ShapeDtypeStruct((512, 512), BF16),
        ],
        [
            item((BLOCKS, 1536)),
            item((BLOCKS, 128)),
            item((BLOCKS, 512)),
            item((BLOCKS, 512)),
            item((BLOCKS, 512)),
            whole((512, 1536)),
            whole((512, 512)),
        ],
        [
            pltpu.VMEM((8, 128, 896), F32),
            pltpu.VMEM((BLOCKS, 512), BF16),
        ],
        after,
    )


def gelu_and_slope(pre):
    square = pre * pre
    tanh = jnp.tanh(pre * (ROOT + (ROOT * CUBIC) * square))
    up = 0.5 + 0.5 * tanh
    act = pre * up
    slope = up + act * (1.0 - up) * (2.0 * ROOT + (6.0 * ROOT * CUBIC) * square)
    return act, slope


def ff_piece(normed, turned, top, turned_top, hid, mid, acts, grads, result, back, start):
    for half in range(2):
        rows = span_of(half, BLOCKS)
        act, slope = gelu_and_slope(mm(normed[rows, :], hid))
        acts[rows, :] = act.astype(BF16)
        grads[rows, :] = (mm(top[rows, :], mid, NT) * slope).astype(BF16)
        new_result = mm(acts[rows, :], mid)
        new_back = mm(grads[rows, :], hid, NT)
        if start is None:
            result[rows, :] += new_result
            back[rows, :] += new_back
        elif start:
            result[rows, :] = start[0][rows, :] + new_result
            back[rows, :] = start[1][rows, :] + new_back
        else:
            result[rows, :] = new_result
            back[rows, :] = new_back
    return mm(turned[...], grads[...]), mm(turned_top[...], acts[...])


def store_shards(place, target, first, values):
    rows = values.shape[0] // SHARDS
    size = target.shape[0] // SHARDS
    for shard in range(SHARDS):
        at = pl.multiple_of(lax.bitwise_xor(place, shard) * size + first, 64)
        target[pl.ds(at, rows), :] = values[span_of(shard, rows), :].astype(BF16)


def gather_top(info, top, turned_top, cot_own_ref, cot_other_ref):
    for index in range(2):
        rows = span_of(index, BLOCKS)
        count = item_count(info, index)
        live = lax.broadcasted_iota(jnp.int32, (BLOCKS, 256), 0) < count
        zero = jnp.zeros((BLOCKS, 256), BF16)
        top[rows, tile_at(info[0], 256)] = jnp.where(live, cot_own_ref[index], zero)
        top[rows, tile_at(1 - info[0], 256)] = jnp.where(live, cot_other_ref[index], zero)
        turned_top[:, rows] = jnp.transpose(top[rows, :])


def ff_first_kernel(
    info,
    normed_ref,
    cot_own_ref,
    cot_other_ref,
    hid_a,
    hid_b,
    hid_c,
    hid_d,
    mid_near,
    mid_far,
    result,
    back,
    keep_ref,
    send_ref,
    top,
    turned_top,
    turned,
    weights,
    acts,
    grads,
):
    way, place = info[2], info[3]
    for part, sources in ((1, (hid_c, hid_d)), (0, (hid_a, hid_b))):
        for side, source in enumerate(sources):
            turn = way if side == 0 else 1 - way
            weights[part, tile_at(turn, 256), :] = source[256:512, :]
    gather_top(info, top, turned_top, cot_own_ref, cot_other_ref)
    for index in range(2):
        turned[:, span_of(index, BLOCKS)] = jnp.transpose(normed_ref[span_of(index, BLOCKS), :])
    for part, target in ((1, send_ref), (0, keep_ref)):
        grad_hid, grad_mid = ff_piece(
            normed_ref,
            turned,
            top,
            turned_top,
            weights[part],
            (mid_far if part == 1 else mid_near)[...],
            acts,
            grads,
            result,
            back,
            () if part == 1 else None,
        )
        store_shards(place, target, 0, grad_hid)
        store_shards(place, target, 64, grad_mid)


def ff_second_kernel(
    info,
    normed_ref,
    cot_own_ref,
    cot_other_ref,
    w_hidden,
    w_mlp,
    result_ref,
    back_ref,
    middle_ref,
    gain_ref,
    blocks_keep,
    blocks_send,
    grad_mid_ref,
    keep_ref,
    send_ref,
    gain_out,
    top,
    turned_top,
    turned,
    acts,
    grads,
    result,
    back,
    blocks,
):
    mp, core, place = info[0], info[1], info[3]
    gather_top(info, top, turned_top, cot_own_ref, cot_other_ref)
    for index in range(2):
        turned[:, span_of(index, BLOCKS)] = jnp.transpose(normed_ref[span_of(index, BLOCKS), :])
    for part, target in ((1, send_ref), (0, keep_ref)):
        start = core if part == 0 else 1 - core
        grad_hid, grad_mid = ff_piece(
            normed_ref,
            turned,
            top,
            turned_top,
            w_hidden[:, tile_at(start, 512)],
            w_mlp[tile_at(start, 512), :],
            acts,
            grads,
            result,
            back,
            (result_ref, back_ref) if part == 1 else None,
        )
        store_shards(place, target, 0, grad_hid)
        store_shards(place, target, 64, grad_mid)

    new_gain = jnp.zeros((1, 512), F32)
    for index in range(2):
        rows = span_of(index, BLOCKS)
        count = item_count(info, index)
        live = lax.broadcasted_iota(jnp.int32, (BLOCKS, 1), 0) < count
        middle = middle_ref[rows, :]
        blocks[...] = jnp.where(live, middle + result[rows, :], 0.0).astype(BF16)
        blocks_keep[index] = blocks[:, tile_at(mp, 256)]
        blocks_send[index] = blocks[:, tile_at(1 - mp, 256)]
        scale = inverse_rms(middle)
        unit = middle * scale
        grad_normed = back[rows, :]
        scaled = grad_normed * gain_ref[...]
        grad_mid_ref[rows, :] = top[rows, :].astype(F32) + scale * (
            scaled - unit * jnp.mean(scaled * unit, axis=1, keepdims=True)
        )
        new_gain = new_gain + jnp.sum(grad_normed * unit, axis=0, keepdims=True)
    gain_out[...] = jnp.broadcast_to(new_gain, gain_out.shape)


def ff_call(info, normed, cot, cot_other, mine, given, after):
    rows = normed.shape[0]
    half = rows // BLOCKS
    packed = (SHARDS * 128, 512)
    wide = jax.ShapeDtypeStruct((rows, 512), F32)
    pack = jax.ShapeDtypeStruct(packed, BF16)
    in_specs = [
        whole((rows, 512)),
        whole((half, BLOCKS, 256)),
        whole((half, BLOCKS, 256)),
    ]
    turned = [
        pltpu.VMEM((rows, 512), BF16),
        pltpu.VMEM((512, rows), BF16),
        pltpu.VMEM((512, rows), BF16),
    ]
    units = [pltpu.VMEM((rows, 512), BF16), pltpu.VMEM((rows, 512), BF16)]
    if mine:
        share = jax.ShapeDtypeStruct((half, BLOCKS, 256), BF16)
        in_specs += [NEAR] * 4 + [whole((rows, 512)), whole((1, 512))]
        outs = [share, share, wide, pack, pack, jax.ShapeDtypeStruct((8, 512), F32)]
        scratch = turned + units
        scratch += [
            pltpu.VMEM((rows, 512), F32),
            pltpu.VMEM((rows, 512), F32),
            pltpu.VMEM((BLOCKS, 512), BF16),
        ]
    else:
        in_specs += [NEAR] * 6
        outs = [wide, wide, pack, pack]
        scratch = turned + [pltpu.VMEM((2, 512, 512), BF16)] + units
    return launch(
        ff_second_kernel if mine else ff_first_kernel,
        "ff_own" if mine else "ff_other",
        12,
        1,
        info,
        (normed, cot, cot_other, *given),
        in_specs,
        outs,
        [whole(x.shape) for x in outs],
        scratch,
        after,
    )


def triple(values):
    high = values.astype(BF16)
    rest = values - high.astype(F32)
    middle = rest.astype(BF16)
    return high, middle, (rest - middle.astype(F32)).astype(BF16)


def attention_back_body(
    info,
    first_head,
    own_ref,
    other_ref,
    query_ref,
    key_ref,
    value_ref,
    log_ref,
    att_ref,
    grad_mid_ref,
    rel_ref,
    table_ref,
    collect_ref,
    gain_attn_ref,
    wq_ref,
    wk_ref,
    wv_ref,
    wo_ref,
    keep_ref,
    send_ref,
    strips,
    pooled,
    outer,
    grads,
    sums,
    acc,
):
    step = pl.program_id(0)
    mp, place = info[0], info[3]
    count = item_count(info, step)

    @pl.when(step == 0)
    def _():
        build_strips(info[1], (rel_ref,), table_ref, strips)
        sums[...] = jnp.zeros_like(sums)

    gather_halves(info, pooled, own_ref, other_ref)
    branch = grad_mid_ref[0].astype(BF16)
    outer[...] = mm(branch, wo_ref[...], NT).astype(BF16)
    lane = lax.broadcasted_iota(jnp.int32, (BLOCKS, 128), 1)
    row = lax.broadcasted_iota(jnp.int32, (BLOCKS, 128), 0)
    dead = jnp.where(row < count, 0.0, MASKED_SCORE).astype(BF16)
    one = jnp.ones((BLOCKS, 128), BF16)
    nought = jnp.zeros((BLOCKS, 128), BF16)

    for pair in range(2):
        span = span_of(pair, 128)
        queries = query_ref[0, :, span]
        keys = key_ref[0, :, span]
        values = value_ref[0, :, span]
        out_grads = outer[:, span]
        overlap = out_grads.astype(F32) * att_ref[0, :, span].astype(F32)
        found = []
        for side in range(2):
            head = pair * 2 + side
            own = (lane < 64) == (side == 0)
            spare = 64 * (1 - side)
            delta = jnp.sum(jnp.where(own, overlap, 0.0), axis=1, keepdims=True)
            logs = jnp.sum(
                jnp.where(lane == first_head + head, log_ref[0], 0.0), axis=1, keepdims=True
            )

            def joined(base, lead, parts):
                filled = jnp.where(own, base, nought)
                filled = jnp.where(lane == spare, lead, filled)
                for index, part in enumerate(parts):
                    filled = jnp.where(lane == spare + 1 + index, part, filled)
                return filled

            chosen = joined(queries, one, triple(-logs))
            masked = joined(keys, dead, (one, one, one))
            drawn = joined(out_grads, nought, triple(-delta))
            weighed = joined(values, nought, (one, one, one))
            grad_key = jnp.zeros((BLOCKS, 128), F32)
            grad_value = jnp.zeros((BLOCKS, 128), F32)
            grad_query = []
            for half in range(2):
                rows = span_of(half, 256)
                scores = mm(masked, chosen[rows, :], NT)
                bias = jnp.concatenate(
                    [
                        strips[head, :, (3 - tile) * 128 + half * 256 : (5 - tile) * 128 + half * 256]
                        for tile in range(4)
                    ],
                    axis=0,
                )
                probs = jnp.exp(scores + bias)
                slope = mm(weighed, drawn[rows, :], NT)
                product = probs * slope
                grad_scores = product.astype(BF16)
                grad_value = grad_value + mm(probs.astype(BF16), out_grads[rows, :])
                grad_key = grad_key + mm(grad_scores, queries[rows, :])
                grad_query.append(mm(grad_scores, keys, TN))
                for line in range(5):
                    first = (3 - line + 1) * 128 + half * 256
                    total = None
                    for tile in range(4):
                        column = tile - line + 1
                        if 0 <= column < 2:
                            block = product[span_of(tile, 128), span_of(column, 128)]
                            total = block if total is None else total + block
                    sums[head, :, first : first + 128] += total
            found.append((jnp.concatenate(grad_query, axis=0), grad_key, grad_value))
        for index in range(3):
            grads[:, index * 256 + pair * 128 : index * 256 + (pair + 1) * 128] = jnp.where(
                lane < 64, found[0][index], found[1][index]
            ).astype(BF16)

    wide = pooled[...].astype(F32)
    scale = inverse_rms(wide)
    unit = wide * scale
    normed = (unit * gain_attn_ref[...]).astype(BF16)
    turned = jnp.transpose(normed)
    turned_branch = jnp.transpose(branch)
    new = mm(turned, grads[...])
    new_out = mm(turned_branch, att_ref[0])

    @pl.when(step == 0)
    def _():
        acc[:, 0:768] = new
        acc[:, 768:1024] = new_out

    @pl.when(step == 1)
    def _():
        acc[:, 0:768] += new
        acc[:, 768:1024] += new_out
        for part, target in ((1, send_ref), (0, keep_ref)):
            for shard in range(SHARDS):
                at = tile_at(lax.bitwise_xor(place, shard), 64)
                for index in range(4):
                    target[at, span_of(index, 128)] = acc[
                        span_of(shard, 64), index * 256 + part * 128 : index * 256 + (part + 1) * 128
                    ].astype(BF16)

    grad_normed = (
        mm(grads[:, 0:256], wq_ref[...], NT)
        + mm(grads[:, 256:512], wk_ref[...], NT)
        + mm(grads[:, 512:768], wv_ref[...], NT)
    )
    return unit, scale, grad_normed


def fold_bias(sums, collect_ref):
    rows = []
    for head in range(4):
        folded = jnp.concatenate((sums[head], jnp.zeros((128, 128), F32)), axis=1)
        size = 64
        while size >= 1:
            folded = folded[:size] + pltpu.roll(folded[size : 2 * size], WRAP - size, 1)
            size //= 2
        rows.append(folded)
    lines = jnp.concatenate(rows + rows, axis=0)
    return lax.dot_general(
        lines, collect_ref[...], NN, precision=PRECISE, preferred_element_type=F32
    )


def attention_back_first_kernel(info, *refs):
    heads, (grad_ref, keep_ref, send_ref, rel_ref), scratch = refs[:16], refs[16:20], refs[20:]
    _, _, grad_normed = attention_back_body(info, 4, *heads, keep_ref, send_ref, *scratch)
    grad_ref[0] = grad_normed

    @pl.when(pl.program_id(0) == 1)
    def _():
        rel_ref[...] = fold_bias(scratch[4], heads[10])


def attention_back_second_kernel(info, *refs):
    heads, (held_ref, rel_ref, gain_mid_ref), refs = refs[:16], refs[16:19], refs[19:]
    (keep_rows, send_rows, keep_ref, send_ref, tiny_ref), scratch = refs[:5], refs[5:]
    scratch, acc_gain = scratch[:-1], scratch[-1]
    unit, scale, grad_normed = attention_back_body(info, 0, *heads, keep_ref, send_ref, *scratch)
    mp, core = info[0], info[1]
    step = pl.program_id(0)
    pooled = scratch[1]
    grad_normed = grad_normed + held_ref[0]
    scaled = grad_normed * heads[11][...]
    grad_pooled = heads[7][0] + scale * (
        scaled - unit * jnp.mean(scaled * unit, axis=1, keepdims=True)
    )
    pooled[...] = grad_pooled.astype(BF16)
    keep_rows[0] = pooled[:, tile_at(mp, 256)]
    send_rows[tile_at(step, BLOCKS), :] = pooled[:, tile_at(1 - mp, 256)]
    new_gain = jnp.sum(grad_normed * unit, axis=0, keepdims=True)

    @pl.when(step == 0)
    def _():
        acc_gain[...] = jnp.broadcast_to(new_gain, acc_gain.shape)

    @pl.when(step == 1)
    def _():
        found = fold_bias(scratch[4], heads[10])
        line = lax.broadcasted_iota(jnp.int32, (8, 128), 0)
        rows = jnp.zeros((8, 128), F32)
        for head in range(8):
            source = found if head < 4 else rel_ref[...]
            true_head = (
                lax.bitwise_xor(mp, head // 4) * 4
                + lax.bitwise_xor(core, (head // 2) % 2) * 2
                + head % 2
            )
            rows = jnp.where(line == true_head, source[head % 4 : head % 4 + 1, :], rows)
        tiny_ref[...] = jnp.zeros_like(tiny_ref)
        tiny_ref[0:1, :] = acc_gain[0:1, :] + new_gain
        tiny_ref[1:2, :] = gain_mid_ref[0:1, :]
        tiny_ref[8:16, 0:128] = rows
        small = tiny_ref[...].astype(BF16)
        send_rows[2 * BLOCKS : 2 * BLOCKS + 16, :] = small[:, 0:256]
        send_rows[2 * BLOCKS + 16 : 2 * BLOCKS + 32, :] = small[:, 256:512]


def attention_back(
    info, mine, rows_args, rel, table, collect, gain_attn, joined, w_o, given, after
):
    own, other, qkv, logs, att, grad_mid = rows_args
    half = own.shape[0]
    where = 0 if mine else 1

    def lanes(index):
        return pl.BlockSpec((1, BLOCKS, 256), lambda i, info: (i, 0, index))

    def columns(index):
        return pl.BlockSpec((512, 256), lambda i, info: (0, index))

    in_specs = [
        item((BLOCKS, 256)),
        item((BLOCKS, 256)),
        lanes(where),
        lanes(2 + where),
        lanes(4 + where),
        item((BLOCKS, 128)),
        lanes(where),
        item((BLOCKS, 512)),
        whole((4, BUCKETS)),
        whole((BUCKETS, WRAP)),
        whole((WRAP, 128)),
        whole((1, 512)),
        columns(where),
        columns(2 + where),
        columns(4 + where),
        pl.BlockSpec((256, 512), lambda i, info: (where, 0)),
    ]
    args = [own, other, qkv, qkv, qkv, logs, att, grad_mid, rel, table, collect, gain_attn]
    args += [joined, joined, joined, w_o]
    packed = (SHARDS * 64, 512)
    pack = jax.ShapeDtypeStruct(packed, BF16)
    scratch = [
        pltpu.VMEM((4, 128, 896), F32),
        pltpu.VMEM((BLOCKS, 512), BF16),
        pltpu.VMEM((BLOCKS, 256), BF16),
        pltpu.VMEM((BLOCKS, 768), BF16),
        pltpu.VMEM((4, 128, 896), F32),
        pltpu.VMEM((512, 1024), F32),
    ]
    if mine:
        share = jax.ShapeDtypeStruct((half, BLOCKS, 256), BF16)
        in_specs += [item((BLOCKS, 512)), whole((8, 128)), whole((8, 512))]
        sent = jax.ShapeDtypeStruct((half * BLOCKS + 32, 256), BF16)
        outs = [share, sent, pack, pack, jax.ShapeDtypeStruct((16, 512), F32)]
        out_specs = [item((BLOCKS, 256)), whole(sent.shape), whole(packed), whole(packed)]
        out_specs += [whole((16, 512))]
        scratch += [pltpu.VMEM((8, 512), F32)]
    else:
        outs = [
            jax.ShapeDtypeStruct((half, BLOCKS, 512), F32),
            pack,
            pack,
            jax.ShapeDtypeStruct((8, 128), F32),
        ]
        out_specs = [item((BLOCKS, 512)), whole(packed), whole(packed), whole((8, 128))]
    return launch(
        attention_back_second_kernel if mine else attention_back_first_kernel,
        "attention_back_own" if mine else "attention_back_other",
        17,
        half,
        info,
        (*args, *given),
        in_specs,
        outs,
        out_specs,
        scratch,
        after,
    )


def place_kernel(info, ff_near, ff_far, hid_ref, mid_ref, mark):
    mark[...] = jnp.zeros_like(mark)
    core, place = info[1], info[3]
    for source, side in ((ff_near, core), (ff_far, 1 - core)):
        turned = []
        for shard in range(SHARDS):
            at = lax.bitwise_xor(place, shard) * 2
            hid_ref[span_of(shard, 64), tile_at(side, 512)] = source[tile_at(at, 64), :].astype(F32)
            turned.append(source[tile_at(at + 1, 64), :])
        mid_ref[tile_at(side, 512), :] = jnp.transpose(
            jnp.concatenate(turned, axis=0).astype(F32)
        )


def pack_kernel(info, wq, wk, wv, wo, wh, rel, out, sems):
    core, way = info[1], info[2]
    rows = tile_at(way, 256)
    pairs = []
    for index, weight in enumerate((wq, wk, wv)):
        lanes = pl.ds(index * 128, 128)
        pairs.append((weight.at[rows, tile_at(core, 128)], out.at[pl.ds(0, 256), lanes]))
    few = pl.ds(pl.multiple_of(core * 128 + way * 64, 64), 64)
    for lane in range(4):
        pairs.append(
            (
                wo.at[few, pl.ds(lane * 128, 128)],
                out.at[pl.ds(lane * 64, 64), pl.ds(384, 128)],
            )
        )
    pairs.append((wh.at[rows, tile_at(core, 512)], out.at[pl.ds(256, 256), :]))
    copies = started(pairs, sems)
    for copy in copies:
        copy.start()
    out[512:528, :] = jnp.zeros((16, 512), BF16)
    for index, part in enumerate(triple(rel[...])):
        out[512:516, index * 128 : index * 128 + BUCKETS] = part
    for copy in copies:
        copy.wait()


def pack(info, weights, rel):
    return launch(
        pack_kernel,
        "pack",
        1,
        1,
        info,
        (*weights[:5], rel),
        [HBM] * 5 + [whole(rel.shape)],
        [jax.ShapeDtypeStruct((528, 512), BF16)],
        [whole((528, 512))],
        [pltpu.SemaphoreType.DMA((8,))],
        vmem=VMEM_MOST,
    )[0]


def pack_more_kernel(info, wm, cot, mid_out, cot_out, cot_own, sems):
    mine, theirs = share_out(info)
    pairs = [(wm.at[tile_at(info[1], 512), :], mid_out)]
    for index in range(2):
        pairs.append((cot.at[theirs[index]], cot_out.at[index]))
        pairs.append((cot.at[mine[index]], cot_own.at[index]))
    copies = started(pairs, sems)
    for copy in copies:
        copy.start()
    for copy in copies:
        copy.wait()


def pack_more(info, w_mlp, cotangent, after):
    half, share = cotangent.shape[0] // 2, cotangent.shape[2]
    outs = [jax.ShapeDtypeStruct((512, 512), BF16)]
    outs += [jax.ShapeDtypeStruct((half, BLOCKS, share), BF16)] * 2
    return launch(
        pack_more_kernel,
        "pack_more",
        1,
        1,
        info,
        (w_mlp, cotangent),
        [HBM] * 2,
        outs,
        [whole(x.shape) for x in outs],
        [pltpu.SemaphoreType.DMA((5,))],
        after,
        vmem=VMEM_MOST,
    )


def final_kernel(
    info,
    near,
    far,
    mine_ref,
    theirs_ref,
    pos_ref,
    frontier_ref,
    blocks_kept,
    blocks_got,
    query_ref,
    key_ref,
    value_ref,
    out_ref,
    front_ref,
    gain_attn_ref,
    gain_mlp_ref,
    rel_ref,
    blocks_ref,
    sems,
):
    mp, core, place = info[0], info[1], info[3]
    pairs = []
    mine, theirs = share_out(info)
    for index in range(2):
        pairs.append((blocks_kept.at[index], blocks_ref.at[mine[index]]))
        pairs.append((blocks_got.at[index], blocks_ref.at[theirs[index]]))
    copies = started(pairs, sems)
    for copy in copies:
        copy.start()
    for source, side in ((near, core), (far, 1 - core)):
        turned = []
        for shard in range(SHARDS):
            at = tile_at(lax.bitwise_xor(place, shard), 64)
            for index, target in enumerate((query_ref, key_ref, value_ref)):
                target[span_of(shard, 64), tile_at(side, 128)] = source[
                    at, span_of(index, 128)
                ].astype(F32)
            turned.append(source[at, 384:512])
        out_ref[tile_at(side, 128), :] = jnp.transpose(
            jnp.concatenate(turned, axis=0).astype(F32)
        )
    tiny = near[512:528, :].astype(F32) + far[512:528, :].astype(F32)
    gain_attn_ref[...] = tiny[0:1, :]
    gain_mlp_ref[...] = tiny[1:2, :]
    heads = jnp.where(mp == 0, tiny[8:12, 0:128], tiny[12:16, 0:128])
    flipped = jnp.transpose(jnp.concatenate((heads, heads), axis=0))
    rel_ref[...] = flipped[0:BUCKETS, 0:4]
    frontier_kernel(info, mine_ref, theirs_ref, pos_ref, frontier_ref, front_ref)
    for copy in copies:
        copy.wait()


def finish(
    info, near, far, mine, theirs, positions, frontier, blocks_kept, blocks_got, after
):
    args = (near, far, mine, theirs, positions, frontier)
    square = jax.ShapeDtypeStruct((512, 256), F32)
    row = jax.ShapeDtypeStruct((1, 512), F32)
    outs = [square, square, square, jax.ShapeDtypeStruct((256, 512), F32)]
    outs += [jax.ShapeDtypeStruct(frontier.shape, F32), row, row]
    outs += [jax.ShapeDtypeStruct((BUCKETS, 4), F32)]
    return launch(
        final_kernel,
        "finish",
        4,
        1,
        info,
        (*args, blocks_kept, blocks_got),
        [whole(x.shape) for x in args] + [ANY] * 2,
        outs + [jax.ShapeDtypeStruct((4,) + blocks_kept.shape[1:], BF16)],
        [whole(x.shape) for x in outs] + [HBM],
        [pltpu.SemaphoreType.DMA((4,))],
        after,
    )


def ff_place(info, near, far, shapes, after):
    return launch(
        place_kernel,
        "ff_place",
        4,
        1,
        info,
        (near, far),
        [whole(near.shape), whole(far.shape)],
        [jax.ShapeDtypeStruct(shape, F32) for shape in shapes],
        [whole(shape) for shape in shapes],
        (),
        after,
    )


def shards(
    devices,
    byte_states,
    frontier,
    lengths,
    gain_attn,
    w_query,
    w_key,
    w_value,
    w_attn_out,
    rel_bias,
    gain_mlp,
    w_hidden,
    w_mlp_out,
    cotangent,
):
    bits = devices.bit_length() - 1
    mp = lax.axis_index("mp").astype(jnp.int32)
    dp = lax.axis_index(("far", "near")).astype(jnp.int32)
    core = dp & 1
    way = (dp >> 1) & 1
    place = (((dp >> 1) & 1) << 2) | (((dp >> 2) & 1) << 1) | ((dp >> 3) & 1)
    info = jnp.concatenate((jnp.stack((mp, core, way, place)), lengths))

    def across(value):
        return lax.ppermute(value, "mp", [(0, 1), (1, 0)])

    def swap(value, bit):
        pairs = [(i, i ^ (1 << bit)) for i in range(devices)]
        return lax.ppermute(value, ("far", "near"), pairs)

    def swap_far(value, index):
        turn = ((index >> 1) << 2) | ((index & 1) << 3)
        return lax.ppermute(value, ("far", "near"), [(i, i ^ turn) for i in range(devices)])

    def rows(count):
        return ((count, 512), BF16)

    weights = (w_query, w_key, w_value, w_attn_out, w_hidden, w_mlp_out)
    rel_own = rel_bias.T
    first_sent = pack(info, weights, rel_own)
    first = across(first_sent)
    forward, backward, collect = (jnp.asarray(table) for table in offset_tables())

    pooled_sent, positions, pool_keep = pool_forward(info, frontier, byte_states, (first_sent,))
    pooled_other = across(pooled_sent)
    mid_sent, cot_sent, cot_own = pack_more(info, w_mlp_out, cotangent, (positions,))
    (first,) = combine("meet", nothing, after=(positions,), through=(first,))
    second = swap(first, 1)
    (pooled_own,) = pool_keep((first, cot_own), ())

    def read_bias(ins, outs):
        parts = [ins[0][512:528, index * 128 : (index + 1) * 128].astype(F32) for index in range(3)]
        outs[0][...] = (parts[0] + parts[1] + parts[2])[0:4, 0:BUCKETS]

    rel_other, second, mid_sent, cot_sent = combine(
        "meet",
        read_bias,
        (first,),
        (((4, BUCKETS), F32),),
        after=(pooled_other, pooled_own),
        through=(second, mid_sent, cot_sent),
    )
    parts = (first, second, swap(first, 0), swap(second, 0))
    cot_other = across(cot_sent)
    mid_first = across(mid_sent)

    gain_attn_row = gain_attn.reshape(1, -1)
    gain_mlp_row = gain_mlp.reshape(1, -1)
    qkv, logs, att, middle, normed, joined, w_o = attention_forward(
        info,
        pooled_own,
        pooled_other,
        (rel_own, rel_other),
        forward,
        gain_attn_row,
        gain_mlp_row,
        weights[:4],
        parts,
        (),
    )
    half = pooled_own.shape[0]
    normed = normed.reshape(half * BLOCKS, -1)
    middle = middle.reshape(half * BLOCKS, -1)

    (mid_first,) = combine("meet", nothing, after=(w_o, cot_other), through=(mid_first,))
    ff_parts = (*parts, mid_first, swap(mid_first, 0))
    result, back, far_keep, far_sent = ff_call(
        info, normed, cot_own, cot_other, False, ff_parts, ()
    )
    far_low, far_high = combine(
        "far_cores", sum_into, (far_keep, swap(far_sent, 0)), (rows(512), rows(512))
    )
    got = swap(far_high, 1)
    blocks_kept, blocks_sent, grad_mid, near_keep, near_sent, gain_mid = ff_call(
        info,
        normed,
        cot_own,
        cot_other,
        True,
        (w_hidden, w_mlp_out, result, back, middle, gain_mlp_row),
        (far_low,),
    )
    far_ff, near_sent = combine(
        "far_y", sum_into, (far_low, got), (rows(512),), (gain_mid,), (near_sent,)
    )
    got_far = across(far_ff)
    near_low, near_high = combine(
        "near_cores", sum_into, (near_keep, swap(near_sent, 0)), (rows(512), rows(512))
    )
    got = swap(near_high, 1)

    grad_mid = grad_mid.reshape(half, BLOCKS, -1)
    rows_args = (pooled_own, pooled_other, qkv, logs, att, grad_mid)
    grad_normed, far_keep, far_sent, far_rel = attention_back(
        info,
        False,
        rows_args,
        rel_other,
        backward,
        collect,
        gain_attn_row,
        joined,
        w_o,
        (),
        (near_low,),
    )
    *ff_parts, far_sent = combine(
        "near_y", sum_into, (near_low, got, got_far), (rows(128),) * 4, (far_rel,), (far_sent,)
    )
    got_ff = [swap_far(ff_parts[index], index) for index in range(1, 4)]
    (far_attn,) = combine("far_cores", sum_into, (far_keep, swap(far_sent, 0)), (rows(512),))
    got_attn = across(far_attn)
    grad_keep, grad_sent, near_keep, near_sent, tiny = attention_back(
        info,
        True,
        rows_args,
        rel_own,
        backward,
        collect,
        gain_attn_row,
        joined,
        w_o,
        (grad_normed, far_rel, gain_mid),
        (far_attn, ff_parts[0]),
    )
    grad_other = across(grad_sent)
    near_ff, near_sent = combine(
        "ff_z", sum_into, (ff_parts[0], *got_ff), (rows(128),), (tiny, got_attn), (near_sent,)
    )
    for bit in range(4, bits):
        near_ff = (near_ff.astype(F32) + swap(near_ff, bit).astype(F32)).astype(BF16)
    got_ff = [swap_far(near_ff, index) for index in range(1, 4)]
    attn_low, attn_high = combine(
        "near_cores",
        sum_into,
        (near_keep, swap(near_sent, 0), got_attn),
        (rows(256), rows(256)),
    )
    got_attn = swap(attn_high, 1)

    def pool_item(mine, index, held, after, through=()):
        grads = grad_keep if mine else grad_other
        return pool_backward(
            info, positions, byte_states, grads, mine, index, held, after, through
        )

    held = pool_item(True, 0, (), (attn_low,))

    def step_one(ins, outs):
        sum_into(ins[:2], outs[:4])
        join_into(ins[2:], outs[4])

    *attn_parts, near_ff, blocks_sent = combine(
        "step_one",
        step_one,
        (attn_low, got_attn, near_ff, *got_ff),
        (rows(64),) * 4 + (rows(512),),
        (held[1],),
        (blocks_sent,),
    )
    got_attn = [swap_far(attn_parts[index], index) for index in range(1, 4)]
    got_ff = swap(near_ff, 1)
    blocks_other = across(blocks_sent)

    def step_two(ins, outs):
        total = ins[0][...].astype(F32)
        for other in ins[1:4]:
            total = total + other[...].astype(F32)
        outs[0][0:64, :] = total.astype(BF16)
        first = 2 * BLOCKS
        small = jnp.concatenate(
            (ins[5][first : first + 16, :], ins[5][first + 16 : first + 32, :]), axis=1
        )
        outs[0][64:80, :] = (ins[4][...] + small.astype(F32)).astype(BF16)
        join_into(ins[6:8], outs[1])

    held = pool_item(True, 1, held, (attn_parts[0],))
    near_attn, near_ff = combine(
        "step_two",
        step_two,
        (attn_parts[0], *got_attn, tiny, grad_other, near_ff, got_ff),
        (rows(80), rows(1024)),
        (held[1],),
    )
    for bit in range(4, bits):
        near_attn = (near_attn.astype(F32) + swap(near_attn, bit).astype(F32)).astype(BF16)
    got_attn = [swap_far(near_attn, index) for index in range(1, 4)]
    far_ff = swap(near_ff, 0)

    def step_three(ins, outs):
        for index, source in enumerate(ins):
            outs[0][span_of(index, 64), :] = source[0:64, :]
        sum_into([source.at[64:80, :] for source in ins], [outs[0].at[256:272, :]])

    held = pool_item(False, 0, held, (near_attn,))
    (near_attn,) = combine(
        "step_three", step_three, (near_attn, *got_attn), (rows(272),), (held[1], blocks_other)
    )
    got_attn = swap(near_attn, 1)

    def step_four(ins, outs):
        join_into([source.at[0:256, :] for source in ins], outs[0])
        sum_into([source.at[256:272, :] for source in ins], [outs[0].at[512:528, :]])

    held = pool_item(False, 1, held, (near_attn,))
    grad_bytes, part = held
    (near_attn,) = combine("step_four", step_four, (near_attn, got_attn), (rows(528),), (part,))
    far_attn = swap(near_attn, 0)
    part_other = across(part)
    grad_hidden, grad_mlp, placed = ff_place(
        info, near_ff, far_ff, (w_hidden.shape, w_mlp_out.shape, (8, 128)), (near_attn,)
    )
    (
        grad_query,
        grad_key,
        grad_value,
        grad_out,
        grad_frontier,
        grad_gain_attn,
        grad_gain_mlp,
        grad_rel,
        blocks_out,
    ) = finish(
        info,
        near_attn,
        far_attn,
        part,
        part_other,
        positions,
        frontier,
        blocks_kept,
        blocks_other,
        (placed,),
    )
    return (
        blocks_out,
        grad_bytes,
        grad_frontier,
        grad_gain_attn.reshape(-1),
        grad_query,
        grad_key,
        grad_value,
        grad_out,
        grad_rel,
        grad_gain_mlp.reshape(-1),
        grad_hidden,
        grad_mlp,
    )


def solution(mesh):
    devices = mesh.shape["dp"]
    split = jax.sharding.Mesh(
        mesh.devices.reshape(devices // 4, 4, mesh.shape["mp"]), ("far", "near", "mp")
    )
    dp = ("far", "near")
    placed = (
        P(dp, None, "mp"),
        P(dp, None),
        P(dp),
        P(),
        P(None, "mp"),
        P(None, "mp"),
        P(None, "mp"),
        P("mp", None),
        P(None, "mp"),
        P(),
        P(None, "mp"),
        P("mp", None),
        P(dp, None, "mp"),
    )
    return jax.shard_map(
        functools.partial(shards, devices),
        mesh=split,
        in_specs=placed,
        out_specs=(
            P(dp, None, "mp"),
            P(dp, None, "mp"),
            P(dp, None),
            P(),
            P(None, "mp"),
            P(None, "mp"),
            P(None, "mp"),
            P("mp", None),
            P(None, "mp"),
            P(),
            P(None, "mp"),
            P("mp", None),
        ),
        check_vma=False,
    )
```

```python
import functools
import math

import jax
import jax.numpy as jnp
import numpy as np
from jax import lax
from jax.experimental import pallas as pl
from jax.experimental.pallas import tpu as pltpu
from jax.sharding import PartitionSpec as P

BUCKETS = 32
REACH = 128
BLOCKS = 512
WRAP = 2 * BLOCKS
SHARDS = 8

EPSILON = 1e-06
SHARPNESS = 2.0
MASKED_SCORE = -1000000000.0
OUTSIDE = -10000.0
REACH_OUT = 8.0
PRECISE = lax.Precision.HIGHEST
ROOT = 0.7978845608028654
CUBIC = 0.044715
VMEM_LIMIT = 24 * 1024 * 1024
VMEM_MOST = 60 * 1024 * 1024
CHUNK = 256
WINDOW = 128

F32 = jnp.float32
BF16 = jnp.bfloat16
ANY = pl.BlockSpec(memory_space=pl.ANY)
HBM = pl.BlockSpec(memory_space=pltpu.HBM)
NEAR = pl.BlockSpec(memory_space=pltpu.VMEM)
SMEM = pl.BlockSpec(memory_space=pltpu.SMEM)
NN = (((1,), (0,)), ((), ()))
NT = (((1,), (1,)), ((), ()))
TN = (((0,), (0,)), ((), ()))


def mm(a, b, dims=NN):
    return lax.dot_general(a, b, dims, preferred_element_type=F32)


def bucket_of(offset):
    half_count = BUCKETS // 2
    exact_count = half_count // 2
    distance = abs(offset)
    if distance < exact_count:
        place = distance
    else:
        place = min(
            half_count - 1,
            exact_count
            + math.floor(
                math.log(distance / exact_count)
                / math.log(REACH / exact_count)
                * (half_count - exact_count)
            ),
        )
    return place + (half_count if offset > 0 else 0)


def offset_tables():
    forward = np.zeros((WRAP, BUCKETS), np.float32)
    backward = np.zeros((WRAP, BUCKETS), np.float32)
    collect = np.zeros((WRAP, 128), np.float32)
    for offset in range(1 - BLOCKS, BLOCKS):
        bucket = bucket_of(offset)
        forward[offset % WRAP, bucket] = 1.0
        backward[(-offset) % WRAP, bucket] = 1.0
        collect[(384 - offset) % WRAP, bucket] = 1.0
    return forward.T, backward.T, collect


def cost(micros):
    return pl.CostEstimate(flops=1, bytes_accessed=1, transcendentals=0)


def whole(shape):
    return pl.BlockSpec(shape, functools.partial(lambda n, i, info: (0,) * n, len(shape)))


def item(shape):
    return pl.BlockSpec(
        (1,) + shape, functools.partial(lambda n, i, info: (i,) + (0,) * n, len(shape))
    )


def launch(
    kernel, name, micros, grid, info, args, in_specs, outs, out_specs, scratch=(), after=(),
    through=(), aliases=None, vmem=VMEM_LIMIT,
):
    given, waits, passed, made = 1 + len(args), len(after), len(through), len(outs)

    def body(*refs):
        first = given + waits + passed
        kernel(*refs[:given], *refs[first : first + made], *refs[first + made + passed :])

    aliases = dict(aliases or {})
    for index in range(passed):
        aliases[given + waits + index] = made + index
    return pl.pallas_call(
        body,
        grid_spec=pltpu.PrefetchScalarGridSpec(
            num_scalar_prefetch=1,
            grid=(grid,),
            in_specs=list(in_specs) + [ANY] * (waits + passed),
            out_specs=list(out_specs) + [ANY] * passed,
            scratch_shapes=list(scratch),
        ),
        out_shape=list(outs) + [jax.ShapeDtypeStruct(x.shape, x.dtype) for x in through],
        input_output_aliases=aliases,
        compiler_params=pltpu.CompilerParams(
            vmem_limit_bytes=vmem, dimension_semantics=("arbitrary",)
        ),
        cost_estimate=cost(micros),
        name=name,
    )(info, *args, *after, *through)


def combine(name, work, args=(), outs=(), after=(), through=()):
    given, held, made, passed = len(args), len(args) + len(after), len(outs), len(through)

    def kernel(*refs):
        work(refs[:given], refs[held + passed : held + passed + made])

    near = pl.BlockSpec(memory_space=pltpu.VMEM)
    return pl.pallas_call(
        kernel,
        in_specs=[near] * given + [ANY] * (len(after) + passed),
        out_specs=[near] * made + [ANY] * passed,
        out_shape=[jax.ShapeDtypeStruct(*out) for out in outs]
        + [jax.ShapeDtypeStruct(x.shape, x.dtype) for x in through],
        input_output_aliases={held + index: made + index for index in range(passed)},
        compiler_params=pltpu.CompilerParams(vmem_limit_bytes=16 * 1024 * 1024),
        cost_estimate=cost(1),
        name=name,
    )(*args, *after, *through)


def nothing(ins, outs):
    pass


def sum_into(ins, outs):
    at = 0
    for out in outs:
        count = min(out.shape[0], ins[0].shape[0] - at)
        rows = slice(at, at + count)
        value = ins[0][rows, :].astype(F32)
        for other in ins[1:]:
            value = value + other[rows, :].astype(F32)
        out[0:count, :] = value.astype(out.dtype)
        if out.shape[0] > count:
            out[count:, :] = jnp.zeros((out.shape[0] - count, out.shape[1]), out.dtype)
        at += count


def join_into(ins, out):
    at = 0
    for source in ins:
        out[at : at + source.shape[0], :] = source[...]
        at += source.shape[0]


def share_out(info):
    lengths = [info[4 + item] for item in range(4)]
    ranks = []
    for item in range(4):
        rank = jnp.int32(0)
        for other in range(4):
            if other != item:
                before = lengths[other] <= lengths[item] if other < item else (
                    lengths[other] < lengths[item]
                )
                rank = rank + jnp.where(before, 1, 0)
        ranks.append(rank)

    def at(wanted):
        found = jnp.int32(0)
        for item in range(1, 4):
            found = jnp.where(ranks[item] == wanted, item, found)
        return found

    sides = ((at(3), at(0)), (at(2), at(1)))
    first = info[0] == 0
    mine = [jnp.where(first, a, b) for a, b in zip(*sides)]
    theirs = [jnp.where(first, b, a) for a, b in zip(*sides)]
    return mine, theirs


def item_count(info, index):
    mine = share_out(info)[0]
    item = mine[index] if isinstance(index, int) else jnp.where(index == 0, mine[0], mine[1])
    return lax.shift_right_logical(info[4 + item] + 3, 2)


def fetch_bytes(bytes_ref, buffer, sems, item, slot):
    return pltpu.make_async_copy(bytes_ref.at[item], buffer.at[slot], sems.at[slot])


def window_kernel(row, first, skipped):
    line = lax.broadcasted_iota(jnp.int32, (WINDOW, CHUNK), 0)
    offset = row - ((line + first).astype(F32) + 0.5)
    kernel = jnp.exp(-SHARPNESS * offset * offset)
    if skipped is not None:
        kernel = jnp.where(line >= skipped, kernel, 0.0)
    return kernel, offset


def chunk_row(pos_ref, item, chunk):
    return pos_ref[pl.ds(item, 1), tile_at(chunk, CHUNK)]


def pool_rows(item, info, meta, pos_ref, buffer, out_ref, acc):
    length = info[4 + item]
    acc[...] = jnp.zeros_like(acc)

    def add(chunk, first, skipped):
        first = pl.multiple_of(first, 16)
        kernel = window_kernel(chunk_row(pos_ref, item, chunk), first, skipped)[0]
        acc[pl.ds(first, WINDOW), :] += mm(
            kernel.astype(BF16), buffer[tile_at(chunk, CHUNK), :]
        )

    def two(pair, carry):
        for chunk in (pair * 2, pair * 2 + 1):
            add(chunk, meta[item, chunk], None)
        for chunk in (pair * 2, pair * 2 + 1):

            @pl.when(meta[4 + item, chunk] > 1)
            def _():
                def more(window, carry):
                    wanted = meta[item, chunk] + window * WINDOW
                    first = jnp.minimum(wanted, BLOCKS - WINDOW)
                    add(chunk, first, wanted - first)
                    return carry

                lax.fori_loop(1, meta[4 + item, chunk], more, 0)

        return carry

    lax.fori_loop(0, lax.div(length + 2 * CHUNK - 1, 2 * CHUNK), two, 0)
    count = lax.shift_right_logical(length + 3, 2)
    live = lax.broadcasted_iota(jnp.int32, acc.shape, 0) < count
    out_ref[...] = jnp.where(live, acc[...], 0.0).astype(BF16)


def find_windows(pos_ref, meta_ref):
    lane = lax.broadcasted_iota(jnp.int32, (4, 128), 1)
    starts = jnp.zeros((4, 128), jnp.int32)
    counts = jnp.ones((4, 128), jnp.int32)
    for chunk in range(pos_ref.shape[1] // CHUNK):
        rows = pos_ref[:, span_of(chunk, CHUNK)]
        low = jnp.min(jnp.where(rows < 0.0, 1e6, rows), axis=1, keepdims=True)
        high = jnp.max(rows, axis=1, keepdims=True)
        start = jnp.clip(low - REACH_OUT, 0.0, float(BLOCKS - WINDOW)).astype(jnp.int32)
        start = lax.shift_left(lax.shift_right_logical(start, 4), 4)
        last = jnp.clip(high + REACH_OUT, 0.0, float(BLOCKS - 1)).astype(jnp.int32)
        count = lax.shift_right_arithmetic(last - start, 7) + 1
        starts = jnp.where(lane == chunk, start, starts)
        counts = jnp.where(lane == chunk, jnp.maximum(count, 1), counts)
    meta_ref[0:4, :] = starts
    meta_ref[4:8, :] = counts


def masked_positions(info, frontier_ref, pos_ref):
    items, byte_count = frontier_ref.shape
    lane = lax.broadcasted_iota(jnp.int32, (items, byte_count), 1)
    row = lax.broadcasted_iota(jnp.int32, (items, byte_count), 0)
    length = jnp.zeros((items, byte_count), jnp.int32)
    for item in range(items):
        length = jnp.where(row == item, info[4 + item], length)
    valid = lane < length
    running = jnp.where(valid, frontier_ref[...], 0.0)
    step = 1
    while step < byte_count:
        running = running + jnp.where(lane >= step, pltpu.roll(running, step, 1), 0.0)
        step *= 2
    count = lax.shift_right_logical(length + 3, 2).astype(F32)
    total = running[:, byte_count - 1 :]
    pos_ref[...] = jnp.where(valid, count * running / total, OUTSIDE)


def pool_own_kernel(
    info, frontier_ref, bytes_ref, out_ref, pos_ref, meta_ref, buffer, acc, meta, sems, meta_sem
):
    mine = share_out(info)[0]
    for slot, item in enumerate(mine):
        fetch_bytes(bytes_ref, buffer, sems, item, slot).start()
    masked_positions(info, frontier_ref, pos_ref)
    find_windows(pos_ref, meta_ref)
    copy = pltpu.make_async_copy(meta_ref, meta, meta_sem)
    copy.start()
    copy.wait()
    for slot, item in enumerate(mine):
        fetch_bytes(bytes_ref, buffer, sems, item, slot).wait()
        pool_rows(item, info, meta, pos_ref, buffer.at[slot], out_ref.at[slot], acc)


def pool_other_kernel(info, meta, pos_ref, bytes_ref, rel, out_ref, buffer, acc, sems):
    theirs = share_out(info)[1]
    out_ref[2 * BLOCKS :, :] = jnp.zeros((32, out_ref.shape[1]), BF16)
    for index, part in enumerate(triple(rel[...])):
        first = 2 * BLOCKS + 16 * (index // 2)
        out_ref[first : first + 4, index % 2 * 128 : index % 2 * 128 + BUCKETS] = part
    for slot, item in enumerate(theirs):
        fetch_bytes(bytes_ref, buffer, sems, item, slot).start()
    for slot, item in enumerate(theirs):
        fetch_bytes(bytes_ref, buffer, sems, item, slot).wait()
        rows = out_ref.at[span_of(slot, BLOCKS), :]
        pool_rows(item, info, meta, pos_ref, buffer.at[slot], rows, acc)


def pool_forward(info, frontier, byte_states, rel, after):
    items, byte_count, share = byte_states.shape
    half = items // 2
    out = jax.ShapeDtypeStruct((half, BLOCKS, share), BF16)
    pos = jax.ShapeDtypeStruct((items, byte_count), F32)
    windows = jax.ShapeDtypeStruct((8, 128), jnp.int32)
    scratch = [pltpu.VMEM((half, byte_count, share), BF16), pltpu.VMEM((BLOCKS, share), F32)]
    own, positions, meta = launch(
        pool_own_kernel,
        "pool_own",
        7,
        1,
        info,
        (frontier, byte_states),
        [whole(pos.shape), HBM],
        [out, pos, windows],
        [whole(out.shape), whole(pos.shape), whole(windows.shape)],
        scratch
        + [
            pltpu.SMEM((8, 128), jnp.int32),
            pltpu.SemaphoreType.DMA((half,)),
            pltpu.SemaphoreType.DMA,
        ],
        after,
        vmem=VMEM_MOST,
    )
    sent = jax.ShapeDtypeStruct((half * BLOCKS + 32, share), BF16)
    (other,) = launch(
        pool_other_kernel,
        "pool_other",
        7,
        1,
        info,
        (meta, positions, byte_states, rel),
        [SMEM, whole(pos.shape), HBM, whole(rel.shape)],
        [sent],
        [whole(sent.shape)],
        scratch + [pltpu.SemaphoreType.DMA((half,))],
        vmem=VMEM_MOST,
    )
    return own, other, positions, meta


def pool_back_kernel(mine, index, info, meta, pos_ref, bytes_ref, grads_ref, *refs):
    out_ref, part_ref, buffer, written, acc, sems, out_sems = refs[-7:]
    item = share_out(info)[0 if mine else 1][index]
    length = info[4 + item]
    grads = grads_ref.at[index] if mine else grads_ref.at[span_of(index, BLOCKS)]
    fetch = fetch_bytes(bytes_ref, buffer, sems, item, 0)
    fetch.start()
    pairs = lax.div(length + 2 * CHUNK - 1, 2 * CHUNK)
    size = 2 * CHUNK

    def written_copy(pair):
        rows = tile_at(pair, size)
        return pltpu.make_async_copy(
            written.at[rows, :], out_ref.at[item, rows, :], out_sems.at[pair]
        )

    def window(chunk, first, skipped):
        first = pl.multiple_of(first, 16)
        kernel, offset = window_kernel(chunk_row(pos_ref, item, chunk), first, skipped)
        rows = grads[pl.ds(first, WINDOW), :]
        slope = mm(rows, buffer[0, tile_at(chunk, CHUNK), :], NT)
        back = mm(kernel.astype(BF16), rows, TN)
        return back, jnp.sum(slope * kernel * offset, axis=0, keepdims=True)

    def two(pair, carry):
        for chunk in (pair * 2, pair * 2 + 1):
            back, terms = window(chunk, meta[item, chunk], None)
            written[tile_at(chunk, CHUNK), :] = back.astype(BF16)
            part_ref[0, :, tile_at(chunk, CHUNK)] = -4.0 * terms
        for chunk in (pair * 2, pair * 2 + 1):

            @pl.when(meta[4 + item, chunk] > 1)
            def _():
                acc[...] = jnp.zeros_like(acc)

                def more(number, total):
                    wanted = meta[item, chunk] + number * WINDOW
                    first = jnp.minimum(wanted, BLOCKS - WINDOW)
                    back, terms = window(chunk, first, wanted - first)
                    acc[...] += back
                    return total + terms

                total = lax.fori_loop(
                    0, meta[4 + item, chunk], more, jnp.zeros((1, CHUNK), F32)
                )
                written[tile_at(chunk, CHUNK), :] = acc[...].astype(BF16)
                part_ref[0, :, tile_at(chunk, CHUNK)] = -4.0 * total

        written_copy(pair).start()
        return carry

    def empty(pair, carry):
        written[tile_at(pair, size), :] = jnp.zeros((size, written.shape[1]), BF16)
        part_ref[0, :, tile_at(pair, size)] = jnp.zeros((1, size), F32)
        written_copy(pair).start()
        return carry

    every = written.shape[0] // size
    lax.fori_loop(pairs, every, empty, 0)
    fetch.wait()
    lax.fori_loop(0, pairs, two, 0)
    for pair in range(every):
        written_copy(pair).wait()


def pool_backward(info, meta, positions, byte_states, grads, mine, index, held, after, through):
    items, byte_count, share = byte_states.shape
    side = 0 if mine else 1
    return launch(
        functools.partial(pool_back_kernel, mine, index),
        "pool_back",
        5,
        1,
        info,
        (meta, positions, byte_states, grads) + tuple(held),
        [SMEM, whole((items, byte_count)), HBM, NEAR] + [HBM] * len(held),
        [
            jax.ShapeDtypeStruct((items, byte_count, share), BF16),
            jax.ShapeDtypeStruct((items, 1, byte_count), F32),
        ],
        [
            HBM,
            pl.BlockSpec((1, 1, byte_count), lambda i, info: (share_out(info)[side][index], 0, 0)),
        ],
        [
            pltpu.VMEM((1, byte_count, share), BF16),
            pltpu.VMEM((byte_count, share), BF16),
            pltpu.VMEM((CHUNK, share), F32),
            pltpu.SemaphoreType.DMA((1,)),
            pltpu.SemaphoreType.DMA((byte_count // (2 * CHUNK),)),
        ],
        after,
        through,
        {5: 0, 6: 1} if held else None,
    )


def frontier_kernel(info, mine_ref, theirs_ref, pos_ref, frontier_ref, out_ref):
    items, byte_count = frontier_ref.shape
    lane = lax.broadcasted_iota(jnp.int32, (items, byte_count), 1)
    row = lax.broadcasted_iota(jnp.int32, (items, byte_count), 0)
    length = jnp.zeros((items, byte_count), jnp.int32)
    for item in range(items):
        length = jnp.where(row == item, info[4 + item], length)
    valid = lane < length
    total = jnp.sum(jnp.where(valid, frontier_ref[...], 0.0), axis=1, keepdims=True)
    terms = jnp.where(valid, mine_ref[:, 0, :] + theirs_ref[:, 0, :], 0.0)
    weighted = jnp.sum(terms * pos_ref[...], axis=1, keepdims=True)
    step = 1
    while step < byte_count:
        moved = pltpu.roll(terms, byte_count - step, 1)
        terms = terms + jnp.where(lane < byte_count - step, moved, 0.0)
        step *= 2
    count = lax.shift_right_logical(length + 3, 2).astype(F32)
    out_ref[...] = jnp.where(valid, (terms * count - weighted) / total, 0.0)


def build_strips(core, biases, table_ref, strips):
    rows = []
    for bias in biases:
        values = bias[...]
        turned = jnp.concatenate((values[2:4], values[0:2]), axis=0)
        rows.append(jnp.where(core == 0, values, turned))
    rows = jnp.concatenate(rows * (8 // (4 * len(rows))), axis=0)
    spread = lax.dot_general(
        rows, table_ref[...], NN, precision=PRECISE, preferred_element_type=F32
    )
    for head in range(strips.shape[0]):
        row = jnp.broadcast_to(spread[head : head + 1, :], (128, WRAP))
        turned = pltpu.roll(row, 384, 1, stride=1, stride_axis=0)
        strips[head] = turned[:, :896]


def gather_halves(info, target, own_ref, other_ref):
    target[:, tile_at(info[0], 256)] = own_ref[0]
    target[:, tile_at(1 - info[0], 256)] = other_ref[...]


def span_of(index, size):
    return slice(index * size, (index + 1) * size)


def tile_at(index, size):
    return pl.ds(pl.multiple_of(index * size, size), size)


def started(pairs, sems):
    return [
        pltpu.make_async_copy(source, target, sems.at[index])
        for index, (source, target) in enumerate(pairs)
    ]


def inverse_rms(values):
    return lax.rsqrt(jnp.mean(values * values, axis=1, keepdims=True) + EPSILON)


def attention_kernel(
    info,
    own_ref,
    other_ref,
    rel_own_ref,
    rel_other_ref,
    table_ref,
    gain_attn_ref,
    gain_mlp_ref,
    w_query,
    w_key,
    w_value,
    w_out,
    part_a,
    part_b,
    part_c,
    part_d,
    qkv_ref,
    log_ref,
    att_ref,
    middle_ref,
    normed_ref,
    w_qkv,
    w_o,
    strips,
    pooled,
):
    step = pl.program_id(0)
    mp, core, way = info[0], info[1], info[2]
    count = item_count(info, step)

    @pl.when(step == 0)
    def _():
        for part in range(2):
            start = core if part == 0 else 1 - core
            for index, weight in enumerate((w_query, w_key, w_value)):
                first = index * 512 + part * 128
                w_qkv[:, first : first + 128] = weight[:, tile_at(start, 128)]
            w_o[span_of(part, 128), :] = w_out[tile_at(start, 128), :]
        for part, sources in enumerate(((part_a, part_b), (part_c, part_d))):
            for side, source in enumerate(sources):
                turn = way if side == 0 else 1 - way
                for index in range(3):
                    first = index * 512 + 256 + part * 128
                    w_qkv[tile_at(turn, 256), first : first + 128] = source[
                        0:256, span_of(index, 128)
                    ]
                rows = pl.ds(pl.multiple_of(256 + part * 128 + turn * 64, 64), 64)
                for lane in range(4):
                    w_o[rows, span_of(lane, 128)] = source[span_of(lane, 64), 384:512]
        build_strips(core, (rel_own_ref, rel_other_ref), table_ref, strips)

    gather_halves(info, pooled, own_ref, other_ref)
    wide = pooled[...].astype(F32)
    normed = (wide * inverse_rms(wide) * gain_attn_ref[...]).astype(BF16)
    qkv_ref[0] = mm(normed, w_qkv[...]).astype(BF16)
    lane = lax.broadcasted_iota(jnp.int32, (BLOCKS, 128), 1)
    row = lax.broadcasted_iota(jnp.int32, (BLOCKS, 128), 0)
    dead = jnp.where(row < count, 0.0, MASKED_SCORE).astype(BF16)

    def heads_pair(pair, logs):
        off = pl.multiple_of(pair * 128, 128)
        queries = qkv_ref[0, :, pl.ds(off, 128)]
        keys = qkv_ref[0, :, pl.ds(512 + off, 128)]
        values = qkv_ref[0, :, pl.ds(1024 + off, 128)]
        outs = []
        for side in range(2):
            head = pair * 2 + side
            own = (lane < 64) == (side == 0)
            spare = lane == 64 * (1 - side)
            chosen = jnp.where(own, queries, jnp.where(spare, 1.0, 0.0).astype(BF16))
            masked = jnp.where(spare, dead, keys)
            summing = jnp.where(own, values, jnp.ones_like(values))
            parts, tops = [], []
            for half in range(2):
                scores = mm(chosen[span_of(half, 256), :], masked, NT)
                first = (3 - 2 * half) * 128
                second = (2 - 2 * half) * 128
                bias = jnp.concatenate(
                    (
                        strips[head, :, first : first + 512],
                        strips[head, :, second : second + 512],
                    ),
                    axis=0,
                )
                scores = scores + bias
                most = jnp.max(scores, axis=1, keepdims=True)
                expo = jnp.exp(scores - most).astype(BF16)
                parts.append(mm(expo, summing))
                tops.append(most)
            out = jnp.concatenate(parts, axis=0)
            total = out[:, 64 * (1 - side) : 64 * (1 - side) + 1]
            outs.append(out * (1.0 / total))
            logs = jnp.where(lane == head, jnp.concatenate(tops, axis=0) + jnp.log(total), logs)
        att_ref[0, :, pl.ds(off, 128)] = jnp.where(lane < 64, outs[0], outs[1]).astype(BF16)
        return logs

    logs = jnp.zeros((BLOCKS, 128), F32)
    log_ref[0] = lax.fori_loop(0, 4, heads_pair, logs)

    mid = wide + mm(att_ref[0], w_o[...])
    middle_ref[0] = mid
    normed_ref[0] = (mid * inverse_rms(mid) * gain_mlp_ref[...]).astype(BF16)


def attention_forward(info, own, other, rel, table, gain_attn, gain_mlp, weights, parts, after):
    half = own.shape[0]
    return launch(
        attention_kernel,
        "attention_forward",
        20,
        half,
        info,
        (own, other, *rel, table, gain_attn, gain_mlp, *weights, *parts),
        [
            item((BLOCKS, 256)),
            pl.BlockSpec((BLOCKS, 256), lambda i, info: (i, 0)),
            whole((4, BUCKETS)),
            whole((4, BUCKETS)),
            whole((BUCKETS, WRAP)),
            whole((1, 512)),
            whole((1, 512)),
        ]
        + [NEAR] * 8,
        [
            jax.ShapeDtypeStruct((half, BLOCKS, 1536), BF16),
            jax.ShapeDtypeStruct((half, BLOCKS, 128), F32),
            jax.ShapeDtypeStruct((half, BLOCKS, 512), BF16),
            jax.ShapeDtypeStruct((half, BLOCKS, 512), F32),
            jax.ShapeDtypeStruct((half, BLOCKS, 512), BF16),
            jax.ShapeDtypeStruct((512, 1536), BF16),
            jax.ShapeDtypeStruct((512, 512), BF16),
        ],
        [
            item((BLOCKS, 1536)),
            item((BLOCKS, 128)),
            item((BLOCKS, 512)),
            item((BLOCKS, 512)),
            item((BLOCKS, 512)),
            whole((512, 1536)),
            whole((512, 512)),
        ],
        [
            pltpu.VMEM((8, 128, 896), F32),
            pltpu.VMEM((BLOCKS, 512), BF16),
        ],
        after,
    )


def gelu_and_slope(pre):
    square = pre * pre
    tanh = jnp.tanh(pre * (ROOT + (ROOT * CUBIC) * square))
    up = 0.5 + 0.5 * tanh
    act = pre * up
    slope = up + act * (1.0 - up) * (2.0 * ROOT + (6.0 * ROOT * CUBIC) * square)
    return act, slope


def ff_piece(normed, turned, top, turned_top, hid, mid, acts, grads, result, back, start):
    for half in range(2):
        rows = span_of(half, BLOCKS)
        act, slope = gelu_and_slope(mm(normed[rows, :], hid))
        acts[rows, :] = act.astype(BF16)
        grads[rows, :] = (mm(top[rows, :], mid, NT) * slope).astype(BF16)
        new_result = mm(acts[rows, :], mid)
        new_back = mm(grads[rows, :], hid, NT)
        if start is None:
            result[rows, :] += new_result
            back[rows, :] += new_back
        elif start:
            result[rows, :] = start[0][rows, :] + new_result
            back[rows, :] = start[1][rows, :] + new_back
        else:
            result[rows, :] = new_result
            back[rows, :] = new_back
    return mm(turned[...], grads[...]), mm(turned_top[...], acts[...])


def store_shards(place, target, first, values):
    rows = values.shape[0] // SHARDS
    size = target.shape[0] // SHARDS
    for shard in range(SHARDS):
        at = pl.multiple_of(lax.bitwise_xor(place, shard) * size + first, 64)
        target[pl.ds(at, rows), :] = values[span_of(shard, rows), :].astype(BF16)


def gather_top(info, top, turned_top, cot_own_ref, cot_other_ref):
    for index in range(2):
        rows = span_of(index, BLOCKS)
        count = item_count(info, index)
        live = lax.broadcasted_iota(jnp.int32, (BLOCKS, 256), 0) < count
        zero = jnp.zeros((BLOCKS, 256), BF16)
        top[rows, tile_at(info[0], 256)] = jnp.where(live, cot_own_ref[index], zero)
        top[rows, tile_at(1 - info[0], 256)] = jnp.where(live, cot_other_ref[index], zero)
        turned_top[:, rows] = jnp.transpose(top[rows, :])


def ff_own_kernel(
    info,
    normed_ref,
    cot_own_ref,
    cot_other_ref,
    w_hidden,
    w_mlp,
    result,
    back,
    keep_ref,
    send_ref,
    mark,
    top,
    turned_top,
    turned,
    acts,
    grads,
):
    core, place = info[1], info[3]
    mark[...] = jnp.zeros_like(mark)
    gather_top(info, top, turned_top, cot_own_ref, cot_other_ref)
    for index in range(2):
        turned[:, span_of(index, BLOCKS)] = jnp.transpose(normed_ref[span_of(index, BLOCKS), :])
    for part, target in ((1, send_ref), (0, keep_ref)):
        start = core if part == 0 else 1 - core
        grad_hid, grad_mid = ff_piece(
            normed_ref,
            turned,
            top,
            turned_top,
            w_hidden[:, tile_at(start, 512)],
            w_mlp[tile_at(start, 512), :],
            acts,
            grads,
            result,
            back,
            () if part == 1 else None,
        )
        store_shards(place, target, 0, grad_hid)
        store_shards(place, target, 64, grad_mid)


def ff_other_kernel(
    info,
    normed_ref,
    cot_own_ref,
    cot_other_ref,
    hid_a,
    hid_b,
    hid_c,
    hid_d,
    mid_near,
    mid_far,
    result_ref,
    back_ref,
    middle_ref,
    gain_ref,
    blocks_keep,
    blocks_send,
    grad_mid_ref,
    keep_ref,
    send_ref,
    gain_out,
    top,
    turned_top,
    turned,
    acts,
    grads,
    weights,
    result,
    back,
    blocks,
):
    mp, way, place = info[0], info[2], info[3]
    for part, sources in ((1, (hid_c, hid_d)), (0, (hid_a, hid_b))):
        for side, source in enumerate(sources):
            turn = way if side == 0 else 1 - way
            weights[part, tile_at(turn, 256), :] = source[256:512, :]
    gather_top(info, top, turned_top, cot_own_ref, cot_other_ref)
    for index in range(2):
        turned[:, span_of(index, BLOCKS)] = jnp.transpose(normed_ref[span_of(index, BLOCKS), :])
    for part, target in ((1, send_ref), (0, keep_ref)):
        grad_hid, grad_mid = ff_piece(
            normed_ref,
            turned,
            top,
            turned_top,
            weights[part],
            (mid_far if part == 1 else mid_near)[...],
            acts,
            grads,
            result,
            back,
            (result_ref, back_ref) if part == 1 else None,
        )
        store_shards(place, target, 0, grad_hid)
        store_shards(place, target, 64, grad_mid)

    new_gain = jnp.zeros((1, 512), F32)
    for index in range(2):
        rows = span_of(index, BLOCKS)
        count = item_count(info, index)
        live = lax.broadcasted_iota(jnp.int32, (BLOCKS, 1), 0) < count
        middle = middle_ref[rows, :]
        blocks[...] = jnp.where(live, middle + result[rows, :], 0.0).astype(BF16)
        blocks_keep[index] = blocks[:, tile_at(mp, 256)]
        blocks_send[index] = blocks[:, tile_at(1 - mp, 256)]
        scale = inverse_rms(middle)
        unit = middle * scale
        grad_normed = back[rows, :]
        scaled = grad_normed * gain_ref[...]
        grad_mid_ref[rows, :] = top[rows, :].astype(F32) + scale * (
            scaled - unit * jnp.mean(scaled * unit, axis=1, keepdims=True)
        )
        new_gain = new_gain + jnp.sum(grad_normed * unit, axis=0, keepdims=True)
    gain_out[...] = jnp.broadcast_to(new_gain, gain_out.shape)


def ff_call(info, normed, cot, cot_other, mine, given, after):
    rows = normed.shape[0]
    half = rows // BLOCKS
    packed = (SHARDS * 128, 512)
    wide = jax.ShapeDtypeStruct((rows, 512), F32)
    pack = jax.ShapeDtypeStruct(packed, BF16)
    share = jax.ShapeDtypeStruct((half, BLOCKS, 256), BF16)
    in_specs = [whole((rows, 512)), whole(share.shape), whole(share.shape)]
    scratch = [
        pltpu.VMEM((rows, 512), BF16),
        pltpu.VMEM((512, rows), BF16),
        pltpu.VMEM((512, rows), BF16),
        pltpu.VMEM((rows, 512), BF16),
        pltpu.VMEM((rows, 512), BF16),
    ]
    if mine:
        in_specs += [NEAR] * 2
        outs = [wide, wide, pack, pack, jax.ShapeDtypeStruct((8, 128), F32)]
    else:
        in_specs += [NEAR] * 8 + [whole((rows, 512)), whole((1, 512))]
        outs = [share, share, wide, pack, pack, jax.ShapeDtypeStruct((8, 512), F32)]
        scratch += [
            pltpu.VMEM((2, 512, 512), BF16),
            pltpu.VMEM((rows, 512), F32),
            pltpu.VMEM((rows, 512), F32),
            pltpu.VMEM((BLOCKS, 512), BF16),
        ]
    return launch(
        ff_own_kernel if mine else ff_other_kernel,
        "ff_own" if mine else "ff_other",
        12,
        1,
        info,
        (normed, cot, cot_other, *given),
        in_specs,
        outs,
        [whole(x.shape) for x in outs],
        scratch,
        after,
    )


def triple(values):
    high = values.astype(BF16)
    rest = values - high.astype(F32)
    middle = rest.astype(BF16)
    return high, middle, (rest - middle.astype(F32)).astype(BF16)


def attention_back_body(
    info,
    first_head,
    own_ref,
    other_ref,
    query_ref,
    key_ref,
    value_ref,
    log_ref,
    att_ref,
    grad_mid_ref,
    rel_ref,
    table_ref,
    collect_ref,
    gain_attn_ref,
    wq_ref,
    wk_ref,
    wv_ref,
    wo_ref,
    keep_ref,
    send_ref,
    strips,
    pooled,
    outer,
    grads,
    sums,
    acc,
):
    step = pl.program_id(0)
    mp, place = info[0], info[3]
    count = item_count(info, step)

    @pl.when(step == 0)
    def _():
        build_strips(info[1], (rel_ref,), table_ref, strips)
        sums[...] = jnp.zeros_like(sums)

    gather_halves(info, pooled, own_ref, other_ref)
    branch = grad_mid_ref[0].astype(BF16)
    outer[...] = mm(branch, wo_ref[...], NT).astype(BF16)
    lane = lax.broadcasted_iota(jnp.int32, (BLOCKS, 128), 1)
    row = lax.broadcasted_iota(jnp.int32, (BLOCKS, 128), 0)
    dead = jnp.where(row < count, 0.0, MASKED_SCORE).astype(BF16)
    one = jnp.ones((BLOCKS, 128), BF16)
    nought = jnp.zeros((BLOCKS, 128), BF16)

    for pair in range(2):
        span = span_of(pair, 128)
        queries = query_ref[0, :, span]
        keys = key_ref[0, :, span]
        values = value_ref[0, :, span]
        out_grads = outer[:, span]
        overlap = out_grads.astype(F32) * att_ref[0, :, span].astype(F32)
        found = []
        for side in range(2):
            head = pair * 2 + side
            own = (lane < 64) == (side == 0)
            spare = 64 * (1 - side)
            delta = jnp.sum(jnp.where(own, overlap, 0.0), axis=1, keepdims=True)
            logs = jnp.sum(
                jnp.where(lane == first_head + head, log_ref[0], 0.0), axis=1, keepdims=True
            )

            def joined(base, lead, parts):
                filled = jnp.where(own, base, nought)
                filled = jnp.where(lane == spare, lead, filled)
                for index, part in enumerate(parts):
                    filled = jnp.where(lane == spare + 1 + index, part, filled)
                return filled

            chosen = joined(queries, one, triple(-logs))
            masked = joined(keys, dead, (one, one, one))
            drawn = joined(out_grads, nought, triple(-delta))
            weighed = joined(values, nought, (one, one, one))
            grad_key = jnp.zeros((BLOCKS, 128), F32)
            grad_value = jnp.zeros((BLOCKS, 128), F32)
            grad_query = []
            for half in range(2):
                rows = span_of(half, 256)
                scores = mm(masked, chosen[rows, :], NT)
                bias = jnp.concatenate(
                    [
                        strips[head, :, (3 - tile) * 128 + half * 256 : (5 - tile) * 128 + half * 256]
                        for tile in range(4)
                    ],
                    axis=0,
                )
                probs = jnp.exp(scores + bias)
                slope = mm(weighed, drawn[rows, :], NT)
                product = probs * slope
                grad_scores = product.astype(BF16)
                grad_value = grad_value + mm(probs.astype(BF16), out_grads[rows, :])
                grad_key = grad_key + mm(grad_scores, queries[rows, :])
                grad_query.append(mm(grad_scores, keys, TN))
                for line in range(5):
                    first = (3 - line + 1) * 128 + half * 256
                    total = None
                    for tile in range(4):
                        column = tile - line + 1
                        if 0 <= column < 2:
                            block = product[span_of(tile, 128), span_of(column, 128)]
                            total = block if total is None else total + block
                    sums[head, :, first : first + 128] += total
            found.append((jnp.concatenate(grad_query, axis=0), grad_key, grad_value))
        for index in range(3):
            grads[:, index * 256 + pair * 128 : index * 256 + (pair + 1) * 128] = jnp.where(
                lane < 64, found[0][index], found[1][index]
            ).astype(BF16)

    wide = pooled[...].astype(F32)
    scale = inverse_rms(wide)
    unit = wide * scale
    normed = (unit * gain_attn_ref[...]).astype(BF16)
    turned = jnp.transpose(normed)
    turned_branch = jnp.transpose(branch)
    new = mm(turned, grads[...])
    new_out = mm(turned_branch, att_ref[0])

    @pl.when(step == 0)
    def _():
        acc[:, 0:768] = new
        acc[:, 768:1024] = new_out

    @pl.when(step == 1)
    def _():
        acc[:, 0:768] += new
        acc[:, 768:1024] += new_out
        for part, target in ((1, send_ref), (0, keep_ref)):
            for shard in range(SHARDS):
                at = tile_at(lax.bitwise_xor(place, shard), 64)
                for index in range(4):
                    target[at, span_of(index, 128)] = acc[
                        span_of(shard, 64), index * 256 + part * 128 : index * 256 + (part + 1) * 128
                    ].astype(BF16)

    grad_normed = (
        mm(grads[:, 0:256], wq_ref[...], NT)
        + mm(grads[:, 256:512], wk_ref[...], NT)
        + mm(grads[:, 512:768], wv_ref[...], NT)
    )
    return unit, scale, grad_normed


def fold_bias(sums, collect_ref):
    rows = []
    for head in range(4):
        folded = jnp.concatenate((sums[head], jnp.zeros((128, 128), F32)), axis=1)
        size = 64
        while size >= 1:
            folded = folded[:size] + pltpu.roll(folded[size : 2 * size], WRAP - size, 1)
            size //= 2
        rows.append(folded)
    lines = jnp.concatenate(rows + rows, axis=0)
    return lax.dot_general(
        lines, collect_ref[...], NN, precision=PRECISE, preferred_element_type=F32
    )


def attention_back_first_kernel(info, *refs):
    heads, (grad_ref, keep_ref, send_ref, rel_ref), scratch = refs[:16], refs[16:20], refs[20:]
    _, _, grad_normed = attention_back_body(info, 4, *heads, keep_ref, send_ref, *scratch)
    grad_ref[0] = grad_normed

    @pl.when(pl.program_id(0) == 1)
    def _():
        rel_ref[...] = fold_bias(scratch[4], heads[10])


def attention_back_second_kernel(info, *refs):
    heads, (held_ref, rel_ref, gain_mid_ref), refs = refs[:16], refs[16:19], refs[19:]
    (keep_rows, send_rows, keep_ref, send_ref, tiny_ref), scratch = refs[:5], refs[5:]
    scratch, acc_gain = scratch[:-1], scratch[-1]
    unit, scale, grad_normed = attention_back_body(info, 0, *heads, keep_ref, send_ref, *scratch)
    mp, core = info[0], info[1]
    step = pl.program_id(0)
    pooled = scratch[1]
    grad_normed = grad_normed + held_ref[0]
    scaled = grad_normed * heads[11][...]
    grad_pooled = heads[7][0] + scale * (
        scaled - unit * jnp.mean(scaled * unit, axis=1, keepdims=True)
    )
    pooled[...] = grad_pooled.astype(BF16)
    keep_rows[0] = pooled[:, tile_at(mp, 256)]
    send_rows[tile_at(step, BLOCKS), :] = pooled[:, tile_at(1 - mp, 256)]
    new_gain = jnp.sum(grad_normed * unit, axis=0, keepdims=True)

    @pl.when(step == 0)
    def _():
        acc_gain[...] = jnp.broadcast_to(new_gain, acc_gain.shape)

    @pl.when(step == 1)
    def _():
        found = fold_bias(scratch[4], heads[10])
        line = lax.broadcasted_iota(jnp.int32, (8, 128), 0)
        rows = jnp.zeros((8, 128), F32)
        for head in range(8):
            source = found if head < 4 else rel_ref[...]
            true_head = (
                lax.bitwise_xor(mp, head // 4) * 4
                + lax.bitwise_xor(core, (head // 2) % 2) * 2
                + head % 2
            )
            rows = jnp.where(line == true_head, source[head % 4 : head % 4 + 1, :], rows)
        tiny_ref[...] = jnp.zeros_like(tiny_ref)
        tiny_ref[0:1, :] = acc_gain[0:1, :] + new_gain
        tiny_ref[1:2, :] = gain_mid_ref[0:1, :]
        tiny_ref[8:16, 0:128] = rows


def attention_back(
    info, mine, rows_args, rel, table, collect, gain_attn, joined, w_o, given, after
):
    own, other, qkv, logs, att, grad_mid = rows_args
    half = own.shape[0]
    where = 0 if mine else 1

    def lanes(index):
        return pl.BlockSpec((1, BLOCKS, 256), lambda i, info: (i, 0, index))

    def columns(index):
        return pl.BlockSpec((512, 256), lambda i, info: (0, index))

    in_specs = [
        item((BLOCKS, 256)),
        pl.BlockSpec((BLOCKS, 256), lambda i, info: (i, 0)),
        lanes(where),
        lanes(2 + where),
        lanes(4 + where),
        item((BLOCKS, 128)),
        lanes(where),
        item((BLOCKS, 512)),
        whole((4, BUCKETS)),
        whole((BUCKETS, WRAP)),
        whole((WRAP, 128)),
        whole((1, 512)),
        columns(where),
        columns(2 + where),
        columns(4 + where),
        pl.BlockSpec((256, 512), lambda i, info: (where, 0)),
    ]
    args = [own, other, qkv, qkv, qkv, logs, att, grad_mid, rel, table, collect, gain_attn]
    args += [joined, joined, joined, w_o]
    packed = (SHARDS * 64, 512)
    pack = jax.ShapeDtypeStruct(packed, BF16)
    scratch = [
        pltpu.VMEM((4, 128, 896), F32),
        pltpu.VMEM((BLOCKS, 512), BF16),
        pltpu.VMEM((BLOCKS, 256), BF16),
        pltpu.VMEM((BLOCKS, 768), BF16),
        pltpu.VMEM((4, 128, 896), F32),
        pltpu.VMEM((512, 1024), F32),
    ]
    if mine:
        share = jax.ShapeDtypeStruct((half, BLOCKS, 256), BF16)
        in_specs += [item((BLOCKS, 512)), whole((8, 128)), whole((8, 512))]
        sent = jax.ShapeDtypeStruct((half * BLOCKS, 256), BF16)
        outs = [share, sent, pack, pack, jax.ShapeDtypeStruct((16, 512), F32)]
        out_specs = [item((BLOCKS, 256)), whole(sent.shape), whole(packed), whole(packed)]
        out_specs += [whole((16, 512))]
        scratch += [pltpu.VMEM((8, 512), F32)]
    else:
        outs = [
            jax.ShapeDtypeStruct((half, BLOCKS, 512), F32),
            pack,
            pack,
            jax.ShapeDtypeStruct((8, 128), F32),
        ]
        out_specs = [item((BLOCKS, 512)), whole(packed), whole(packed), whole((8, 128))]
    return launch(
        attention_back_second_kernel if mine else attention_back_first_kernel,
        "attention_back_own" if mine else "attention_back_other",
        17,
        half,
        info,
        (*args, *given),
        in_specs,
        outs,
        out_specs,
        scratch,
        after,
    )


def place_kernel(info, ff_near, ff_far, hid_ref, mid_ref, mark):
    mark[...] = jnp.zeros_like(mark)
    core, place = info[1], info[3]
    for source, side in ((ff_near, core), (ff_far, 1 - core)):
        turned = []
        for shard in range(SHARDS):
            at = lax.bitwise_xor(place, shard)
            at = at * 2
            hid_ref[span_of(shard, 64), tile_at(side, 512)] = source[tile_at(at, 64), :].astype(F32)
            turned.append(source[tile_at(at + 1, 64), :])
        mid_ref[tile_at(side, 512), :] = jnp.transpose(
            jnp.concatenate(turned, axis=0).astype(F32)
        )


def pack_kernel(info, wq, wk, wv, wo, wh, out, sems):
    core, way = info[1], info[2]
    rows = tile_at(way, 256)
    pairs = []
    for index, weight in enumerate((wq, wk, wv)):
        lanes = pl.ds(index * 128, 128)
        pairs.append((weight.at[rows, tile_at(core, 128)], out.at[pl.ds(0, 256), lanes]))
    few = pl.ds(pl.multiple_of(core * 128 + way * 64, 64), 64)
    for lane in range(4):
        pairs.append(
            (
                wo.at[few, pl.ds(lane * 128, 128)],
                out.at[pl.ds(lane * 64, 64), pl.ds(384, 128)],
            )
        )
    pairs.append((wh.at[rows, tile_at(core, 512)], out.at[pl.ds(256, 256), :]))
    copies = started(pairs, sems)
    for copy in copies:
        copy.start()
    for copy in copies:
        copy.wait()


def pack(info, weights):
    return launch(
        pack_kernel,
        "pack",
        1,
        1,
        info,
        weights[:5],
        [HBM] * 5,
        [jax.ShapeDtypeStruct((512, 512), BF16)],
        [whole((512, 512))],
        [pltpu.SemaphoreType.DMA((8,))],
        vmem=VMEM_MOST,
    )[0]


def pack_more_kernel(info, wm, cot, mid_out, cot_out, cot_own, sems):
    mine, theirs = share_out(info)
    pairs = [(wm.at[tile_at(info[1], 512), :], mid_out)]
    for index in range(2):
        pairs.append((cot.at[theirs[index]], cot_out.at[index]))
        pairs.append((cot.at[mine[index]], cot_own.at[index]))
    copies = started(pairs, sems)
    for copy in copies:
        copy.start()
    for copy in copies:
        copy.wait()


def pack_more(info, w_mlp, cotangent, after):
    half, share = cotangent.shape[0] // 2, cotangent.shape[2]
    outs = [jax.ShapeDtypeStruct((512, 512), BF16)]
    outs += [jax.ShapeDtypeStruct((half, BLOCKS, share), BF16)] * 2
    return launch(
        pack_more_kernel,
        "pack_more",
        1,
        1,
        info,
        (w_mlp, cotangent),
        [HBM] * 2,
        outs,
        [whole(x.shape) for x in outs],
        [pltpu.SemaphoreType.DMA((5,))],
        after,
        vmem=VMEM_MOST,
    )


def final_kernel(
    info,
    near,
    far,
    mine_ref,
    theirs_ref,
    pos_ref,
    frontier_ref,
    blocks_kept,
    blocks_got,
    query_ref,
    key_ref,
    value_ref,
    out_ref,
    front_ref,
    gain_attn_ref,
    gain_mlp_ref,
    rel_ref,
    blocks_ref,
    sems,
):
    mp, core, place = info[0], info[1], info[3]
    pairs = []
    mine, theirs = share_out(info)
    for index in range(2):
        pairs.append((blocks_kept.at[index], blocks_ref.at[mine[index]]))
        pairs.append((blocks_got.at[index], blocks_ref.at[theirs[index]]))
    copies = started(pairs, sems)
    for copy in copies:
        copy.start()
    for source, side in ((near, core), (far, 1 - core)):
        turned = []
        for shard in range(SHARDS):
            at = tile_at(lax.bitwise_xor(place, shard), 64)
            for index, target in enumerate((query_ref, key_ref, value_ref)):
                target[span_of(shard, 64), tile_at(side, 128)] = source[
                    at, span_of(index, 128)
                ].astype(F32)
            turned.append(source[at, 384:512])
        out_ref[tile_at(side, 128), :] = jnp.transpose(
            jnp.concatenate(turned, axis=0).astype(F32)
        )
    tiny = near[512:528, :].astype(F32) + far[512:528, :].astype(F32)
    gain_attn_ref[...] = tiny[0:1, :]
    gain_mlp_ref[...] = tiny[1:2, :]
    heads = jnp.where(mp == 0, tiny[8:12, 0:128], tiny[12:16, 0:128])
    flipped = jnp.transpose(jnp.concatenate((heads, heads), axis=0))
    rel_ref[...] = flipped[0:BUCKETS, 0:4]
    frontier_kernel(info, mine_ref, theirs_ref, pos_ref, frontier_ref, front_ref)
    for copy in copies:
        copy.wait()


def finish(
    info, near, far, mine, theirs, positions, frontier, blocks_kept, blocks_got, after
):
    args = (near, far, mine, theirs, positions, frontier)
    square = jax.ShapeDtypeStruct((512, 256), F32)
    row = jax.ShapeDtypeStruct((1, 512), F32)
    outs = [square, square, square, jax.ShapeDtypeStruct((256, 512), F32)]
    outs += [jax.ShapeDtypeStruct(frontier.shape, F32), row, row]
    outs += [jax.ShapeDtypeStruct((BUCKETS, 4), F32)]
    return launch(
        final_kernel,
        "finish",
        4,
        1,
        info,
        (*args, blocks_kept, blocks_got),
        [whole(x.shape) for x in args] + [ANY] * 2,
        outs + [jax.ShapeDtypeStruct((4,) + blocks_kept.shape[1:], BF16)],
        [whole(x.shape) for x in outs] + [HBM],
        [pltpu.SemaphoreType.DMA((4,))],
        after,
    )


def ff_place(info, near, far, shapes, after):
    return launch(
        place_kernel,
        "ff_place",
        4,
        1,
        info,
        (near, far),
        [whole(near.shape), whole(far.shape)],
        [jax.ShapeDtypeStruct(shape, F32) for shape in shapes],
        [whole(shape) for shape in shapes],
        (),
        after,
    )


def shards(
    devices,
    byte_states,
    frontier,
    lengths,
    gain_attn,
    w_query,
    w_key,
    w_value,
    w_attn_out,
    rel_bias,
    gain_mlp,
    w_hidden,
    w_mlp_out,
    cotangent,
):
    bits = devices.bit_length() - 1
    mp = lax.axis_index("mp").astype(jnp.int32)
    dp = lax.axis_index(("far", "near")).astype(jnp.int32)
    core = dp & 1
    way = (dp >> 1) & 1
    place = (((dp >> 1) & 1) << 2) | (((dp >> 2) & 1) << 1)
    info = jnp.concatenate((jnp.stack((mp, core, way, place)), lengths))

    def across(value):
        return lax.ppermute(value, "mp", [(0, 1), (1, 0)])

    def swap(value, bit):
        pairs = [(i, i ^ (1 << bit)) for i in range(devices)]
        return lax.ppermute(value, ("far", "near"), pairs)

    def swap_four(value, index):
        turn = ((index & 1) << 2) | ((index >> 1) << 1)
        return lax.ppermute(value, ("far", "near"), [(i, i ^ turn) for i in range(devices)])

    def rows(count):
        return ((count, 512), BF16)

    weights = (w_query, w_key, w_value, w_attn_out, w_hidden, w_mlp_out)
    rel_own = rel_bias.T
    first_sent = pack(info, weights)
    first = across(first_sent)
    forward, backward, collect = (jnp.asarray(table) for table in offset_tables())

    pooled_own, pooled_sent, positions, meta = pool_forward(
        info, frontier, byte_states, rel_own, (first_sent,)
    )
    pooled_other = across(pooled_sent)
    (first,) = combine("meet", nothing, after=(pooled_sent,), through=(first,))
    second = swap(first, 1)
    mid_sent, cot_sent, cot_own = pack_more(info, w_mlp_out, cotangent, (pooled_sent,))

    def read_bias(ins, outs):
        total = jnp.zeros((16, 128), F32)
        for index in range(3):
            first = 2 * BLOCKS + 16 * (index // 2)
            lanes = slice(index % 2 * 128, (index % 2 + 1) * 128)
            total = total + ins[0][first : first + 16, lanes].astype(F32)
        outs[0][...] = total[0:4, 0:BUCKETS]

    rel_other, second, mid_sent, cot_sent = combine(
        "meet",
        read_bias,
        (pooled_other,),
        (((4, BUCKETS), F32),),
        after=(cot_own,),
        through=(second, mid_sent, cot_sent),
    )
    parts = (first, second, swap(first, 0), swap(second, 0))
    cot_other = across(cot_sent)
    mid_first = across(mid_sent)

    gain_attn_row = gain_attn.reshape(1, -1)
    gain_mlp_row = gain_mlp.reshape(1, -1)
    qkv, logs, att, middle, normed, joined, w_o = attention_forward(
        info,
        pooled_own,
        pooled_other,
        (rel_own, rel_other),
        forward,
        gain_attn_row,
        gain_mlp_row,
        weights[:4],
        parts,
        (),
    )
    half = pooled_own.shape[0]
    normed = normed.reshape(half * BLOCKS, -1)
    middle = middle.reshape(half * BLOCKS, -1)

    result, back, near_keep, near_sent, mark = ff_call(
        info, normed, cot_own, cot_other, True, (w_hidden, w_mlp_out), ()
    )
    got_near = swap(near_sent, 0)
    (mid_first,) = combine("meet", nothing, after=(mark,), through=(mid_first,))
    blocks_kept, blocks_sent, grad_mid, far_keep, far_sent, gain_mid = ff_call(
        info,
        normed,
        cot_own,
        cot_other,
        False,
        (*parts, mid_first, swap(mid_first, 0), result, back, middle, gain_mlp_row),
        (),
    )
    near_low, near_high, far_sent = combine(
        "near_cores",
        sum_into,
        (near_keep, got_near),
        (rows(512), rows(528)),
        (gain_mid,),
        (far_sent,),
    )
    far_low, far_high, near_high = combine(
        "far_cores",
        sum_into,
        (far_keep, swap(far_sent, 0)),
        (rows(512), rows(512)),
        (),
        (near_high,),
    )
    got_far = swap(far_high, 1)
    blocks_other = across(blocks_sent)

    grad_mid = grad_mid.reshape(half, BLOCKS, -1)
    rows_args = (pooled_own, pooled_other, qkv, logs, att, grad_mid)
    grad_normed, far_keep, far_sent, far_rel = attention_back(
        info,
        False,
        rows_args,
        rel_other,
        backward,
        collect,
        gain_attn_row,
        joined,
        w_o,
        (),
        (far_low,),
    )
    far_ff, far_sent, near_high = combine(
        "far_y", sum_into, (far_low, got_far), (rows(544),), (far_rel, blocks_other), (far_sent, near_high)
    )
    got_near = swap(near_high, 1)
    far_attn, far_ff = combine(
        "far_cores", sum_into, (far_keep, swap(far_sent, 0)), (rows(528),), (), (far_ff,)
    )
    got_attn = across(far_attn)
    got_far = across(far_ff)
    grad_keep, grad_sent, near_keep, near_sent, tiny = attention_back(
        info,
        True,
        rows_args,
        rel_own,
        backward,
        collect,
        gain_attn_row,
        joined,
        w_o,
        (grad_normed, far_rel, gain_mid),
        (far_attn,),
    )
    grad_other = across(grad_sent)
    ff_low, ff_high, near_sent = combine(
        "ff_sum",
        sum_into,
        (near_low, got_near, got_far),
        (rows(256), rows(272)),
        (tiny,),
        (near_sent,),
    )
    got_ff = swap(ff_high, 2)
    got_sent = swap(near_sent, 0)

    def pool_item(mine, index, held, after, through=()):
        grads = grad_keep if mine else grad_other
        return pool_backward(
            info, meta, positions, byte_states, grads, mine, index, held, after, through
        )

    held = pool_item(True, 0, (), (ff_low,))

    def step_one(ins, outs):
        for index in range(4):
            at = span_of(index, 128)
            total = ins[0][at, :].astype(F32) + ins[1][at, :].astype(F32)
            outs[index][0:128, :] = (total + ins[2][at, :].astype(F32)).astype(BF16)
            outs[index][128:144, :] = ins[3][...].astype(BF16)
        sum_into(ins[4:], outs[4:])

    *attn_parts, near_ff = combine(
        "step_one",
        step_one,
        (near_keep, got_sent, got_attn, tiny, ff_low, got_ff),
        (rows(144),) * 4 + (rows(256),),
        (held[1],),
    )
    got_ff = swap(near_ff, 3)
    got_attn = [swap_four(attn_parts[index], index) for index in range(1, 4)]

    held = pool_item(True, 1, held, (attn_parts[0],))

    def step_two(ins, outs):
        sum_into(ins[:4], outs[:1])
        sum_into(ins[4:], outs[1:])

    attn, near_ff = combine(
        "step_two",
        step_two,
        (attn_parts[0], *got_attn, near_ff, got_ff),
        (rows(144), rows(256)),
        (held[1],),
    )
    for bit in range(4, bits):
        near_ff = (near_ff.astype(F32) + swap(near_ff, bit).astype(F32)).astype(BF16)
        attn = (attn.astype(F32) + swap(attn, bit).astype(F32)).astype(BF16)
    got_attn = swap(attn, 3)
    got_ff = [swap_four(near_ff, index) for index in range(1, 4)]

    def step_three(ins, outs):
        outs[0][...] = (ins[0][0:128, :].astype(F32) + ins[1][0:128, :].astype(F32)).astype(BF16)
        outs[1][...] = (
            ins[0][128:144, :].astype(F32) + ins[1][128:144, :].astype(F32)
        ).astype(BF16)

    held = pool_item(False, 0, held, (attn,))
    attn, tiny = combine(
        "step_three", step_three, (attn, got_attn), (rows(128), rows(16)), (held[1],)
    )
    got_attn = [swap_four(attn, index) for index in range(1, 4)]
    got_tiny = across(tiny)

    def step_four(ins, outs):
        join_into(ins[:4], outs[0])
        sum_into(ins[4:6], [outs[0].at[512:528, :]])
        join_into(ins[6:], outs[1])

    held = pool_item(False, 1, held, (attn,))
    grad_bytes, part = held
    near_attn, near_ff = combine(
        "step_four",
        step_four,
        (attn, *got_attn, tiny, got_tiny, near_ff, *got_ff),
        (rows(528), rows(1024)),
        (part,),
    )
    far_attn, far_ff = swap(near_attn, 0), swap(near_ff, 0)
    part_other = across(part)
    (
        grad_query,
        grad_key,
        grad_value,
        grad_out,
        grad_frontier,
        grad_gain_attn,
        grad_gain_mlp,
        grad_rel,
        blocks_out,
    ) = finish(
        info,
        near_attn,
        far_attn,
        part,
        part_other,
        positions,
        frontier,
        blocks_kept,
        blocks_other,
        (),
    )
    grad_hidden, grad_mlp, _ = ff_place(
        info, near_ff, far_ff, (w_hidden.shape, w_mlp_out.shape, (8, 128)), (grad_gain_attn,)
    )
    return (
        blocks_out,
        grad_bytes,
        grad_frontier,
        grad_gain_attn.reshape(-1),
        grad_query,
        grad_key,
        grad_value,
        grad_out,
        grad_rel,
        grad_gain_mlp.reshape(-1),
        grad_hidden,
        grad_mlp,
    )


def solution(mesh):
    devices = mesh.shape["dp"]
    split = jax.sharding.Mesh(
        mesh.devices.reshape(devices // 4, 4, mesh.shape["mp"]), ("far", "near", "mp")
    )
    dp = ("far", "near")
    placed = (
        P(dp, None, "mp"),
        P(dp, None),
        P(dp),
        P(),
        P(None, "mp"),
        P(None, "mp"),
        P(None, "mp"),
        P("mp", None),
        P(None, "mp"),
        P(),
        P(None, "mp"),
        P("mp", None),
        P(dp, None, "mp"),
    )
    return jax.shard_map(
        functools.partial(shards, devices),
        mesh=split,
        in_specs=placed,
        out_specs=(
            P(dp, None, "mp"),
            P(dp, None, "mp"),
            P(dp, None),
            P(),
            P(None, "mp"),
            P(None, "mp"),
            P(None, "mp"),
            P("mp", None),
            P(None, "mp"),
            P(),
            P(None, "mp"),
            P("mp", None),
        ),
        check_vma=False,
    )
```

```python
import functools
import math

import jax
import jax.numpy as jnp
import numpy as np
from jax import lax
from jax.experimental import pallas as pl
from jax.experimental.pallas import tpu as pltpu
from jax.sharding import PartitionSpec as P

BUCKETS = 32
REACH = 128
BLOCKS = 512
WRAP = 2 * BLOCKS
SHARDS = 8

EPSILON = 1e-06
SHARPNESS = 2.0
MASKED_SCORE = -1000000000.0
OUTSIDE = -10000.0
REACH_OUT = 8.0
PRECISE = lax.Precision.HIGHEST
ROOT = 0.7978845608028654
CUBIC = 0.044715
VMEM_LIMIT = 24 * 1024 * 1024
VMEM_MOST = 60 * 1024 * 1024
CHUNK = 256
WINDOW = 128
SLOTS = 3

F32 = jnp.float32
BF16 = jnp.bfloat16
ANY = pl.BlockSpec(memory_space=pl.ANY)
HBM = pl.BlockSpec(memory_space=pltpu.HBM)
NEAR = pl.BlockSpec(memory_space=pltpu.VMEM)
SMEM = pl.BlockSpec(memory_space=pltpu.SMEM)
NN = (((1,), (0,)), ((), ()))
NT = (((1,), (1,)), ((), ()))
TN = (((0,), (0,)), ((), ()))


def mm(a, b, dims=NN):
    return lax.dot_general(a, b, dims, preferred_element_type=F32)


def bucket_of(offset):
    half_count = BUCKETS // 2
    exact_count = half_count // 2
    distance = abs(offset)
    if distance < exact_count:
        place = distance
    else:
        place = min(
            half_count - 1,
            exact_count
            + math.floor(
                math.log(distance / exact_count)
                / math.log(REACH / exact_count)
                * (half_count - exact_count)
            ),
        )
    return place + (half_count if offset > 0 else 0)


def offset_tables():
    backward = np.zeros((WRAP, BUCKETS), np.float32)
    collect = np.zeros((WRAP, BUCKETS), np.float32)
    for offset in range(1 - BLOCKS, BLOCKS):
        bucket = bucket_of(offset)
        backward[(-offset) % WRAP, bucket] = 1.0
        collect[(384 - offset) % WRAP, bucket] = 1.0
    collect = np.concatenate([np.roll(collect, turn, axis=0) for turn in range(8)], axis=1)
    return backward.T, collect


def cost(micros):
    return pl.CostEstimate(flops=1, bytes_accessed=1, transcendentals=0)


def whole(shape):
    return pl.BlockSpec(shape, functools.partial(lambda n, i, info: (0,) * n, len(shape)))


def item(shape):
    return pl.BlockSpec(
        (1,) + shape, functools.partial(lambda n, i, info: (i,) + (0,) * n, len(shape))
    )


def launch(
    kernel, name, micros, grid, info, args, in_specs, outs, out_specs, scratch=(), after=(),
    through=(), aliases=None, vmem=VMEM_LIMIT,
):
    given, waits, passed, made = 1 + len(args), len(after), len(through), len(outs)

    def body(*refs):
        first = given + waits + passed
        kernel(*refs[:given], *refs[first : first + made], *refs[first + made + passed :])

    aliases = dict(aliases or {})
    for index in range(passed):
        aliases[given + waits + index] = made + index
    return pl.pallas_call(
        body,
        grid_spec=pltpu.PrefetchScalarGridSpec(
            num_scalar_prefetch=1,
            grid=(grid,),
            in_specs=list(in_specs) + [ANY] * (waits + passed),
            out_specs=list(out_specs) + [ANY] * passed,
            scratch_shapes=list(scratch),
        ),
        out_shape=list(outs) + [jax.ShapeDtypeStruct(x.shape, x.dtype) for x in through],
        input_output_aliases=aliases,
        compiler_params=pltpu.CompilerParams(
            vmem_limit_bytes=vmem, dimension_semantics=("arbitrary",)
        ),
        cost_estimate=cost(micros),
        name=name,
    )(info, *args, *after, *through)


def combine(name, work, args=(), outs=(), after=(), through=()):
    given, held, made, passed = len(args), len(args) + len(after), len(outs), len(through)

    def kernel(*refs):
        work(refs[:given], refs[held + passed : held + passed + made])

    near = pl.BlockSpec(memory_space=pltpu.VMEM)
    return pl.pallas_call(
        kernel,
        in_specs=[near] * given + [ANY] * (len(after) + passed),
        out_specs=[near] * made + [ANY] * passed,
        out_shape=[jax.ShapeDtypeStruct(*out) for out in outs]
        + [jax.ShapeDtypeStruct(x.shape, x.dtype) for x in through],
        input_output_aliases={held + index: made + index for index in range(passed)},
        compiler_params=pltpu.CompilerParams(vmem_limit_bytes=16 * 1024 * 1024),
        cost_estimate=cost(1),
        name=name,
    )(*args, *after, *through)


def nothing(ins, outs):
    pass


def sum_into(ins, outs):
    at = 0
    for out in outs:
        count = min(out.shape[0], ins[0].shape[0] - at)
        rows = slice(at, at + count)
        value = ins[0][rows, :].astype(F32)
        for other in ins[1:]:
            value = value + other[rows, :].astype(F32)
        out[0:count, :] = value.astype(out.dtype)
        if out.shape[0] > count:
            out[count:, :] = jnp.zeros((out.shape[0] - count, out.shape[1]), out.dtype)
        at += count


def join_into(ins, out):
    at = 0
    for source in ins:
        out[at : at + source.shape[0], :] = source[...]
        at += source.shape[0]


def share_out(info):
    lengths = [info[4 + item] for item in range(4)]
    ranks = []
    for item in range(4):
        rank = jnp.int32(0)
        for other in range(4):
            if other != item:
                before = lengths[other] <= lengths[item] if other < item else (
                    lengths[other] < lengths[item]
                )
                rank = rank + jnp.where(before, 1, 0)
        ranks.append(rank)

    def at(wanted):
        found = jnp.int32(0)
        for item in range(1, 4):
            found = jnp.where(ranks[item] == wanted, item, found)
        return found

    sides = ((at(3), at(0)), (at(2), at(1)))
    first = info[0] == 0
    mine = [jnp.where(first, a, b) for a, b in zip(*sides)]
    theirs = [jnp.where(first, b, a) for a, b in zip(*sides)]
    return mine, theirs


def item_count(info, index):
    mine = share_out(info)[0]
    item = mine[index] if isinstance(index, int) else jnp.where(index == 0, mine[0], mine[1])
    return lax.shift_right_logical(info[4 + item] + 3, 2)


def fetch_bytes(bytes_ref, buffer, sems, item, slot):
    return pltpu.make_async_copy(bytes_ref.at[item], buffer.at[slot], sems.at[slot])


def window_kernel(row, first, skipped):
    line = lax.broadcasted_iota(jnp.int32, (WINDOW, CHUNK), 0)
    offset = row - ((line + first).astype(F32) + 0.5)
    kernel = jnp.exp(-SHARPNESS * offset * offset)
    if skipped is not None:
        kernel = jnp.where(line >= skipped, kernel, 0.0)
    return kernel, offset


def chunk_row(pos_ref, item, chunk):
    return pos_ref[pl.ds(item, 1), tile_at(chunk, CHUNK)]


def pool_rows(item, info, meta, pos_ref, buffer, out_ref, acc):
    length = info[4 + item]
    acc[...] = jnp.zeros_like(acc)

    def add(chunk, first, skipped):
        first = pl.multiple_of(first, 16)
        kernel = window_kernel(chunk_row(pos_ref, item, chunk), first, skipped)[0]
        acc[pl.ds(first, WINDOW), :] += mm(
            kernel.astype(BF16), buffer[tile_at(chunk, CHUNK), :]
        )

    def two(pair, carry):
        for chunk in (pair * 2, pair * 2 + 1):
            add(chunk, meta[item, chunk], None)
        for chunk in (pair * 2, pair * 2 + 1):

            @pl.when(meta[4 + item, chunk] > 1)
            def _():
                def more(window, carry):
                    wanted = meta[item, chunk] + window * WINDOW
                    first = jnp.minimum(wanted, BLOCKS - WINDOW)
                    add(chunk, first, wanted - first)
                    return carry

                lax.fori_loop(1, meta[4 + item, chunk], more, 0)

        return carry

    lax.fori_loop(0, lax.div(length + 2 * CHUNK - 1, 2 * CHUNK), two, 0)
    count = lax.shift_right_logical(length + 3, 2)
    live = lax.broadcasted_iota(jnp.int32, acc.shape, 0) < count
    out_ref[...] = jnp.where(live, acc[...], 0.0).astype(BF16)


def find_windows(pos_ref, meta_ref):
    lane = lax.broadcasted_iota(jnp.int32, (4, 128), 1)
    starts = jnp.zeros((4, 128), jnp.int32)
    counts = jnp.ones((4, 128), jnp.int32)
    for chunk in range(pos_ref.shape[1] // CHUNK):
        rows = pos_ref[:, span_of(chunk, CHUNK)]
        low = jnp.min(jnp.where(rows < 0.0, 1e6, rows), axis=1, keepdims=True)
        high = jnp.max(rows, axis=1, keepdims=True)
        start = jnp.clip(low - REACH_OUT, 0.0, float(BLOCKS - WINDOW)).astype(jnp.int32)
        start = lax.shift_left(lax.shift_right_logical(start, 4), 4)
        last = jnp.clip(high + REACH_OUT, 0.0, float(BLOCKS - 1)).astype(jnp.int32)
        count = lax.shift_right_arithmetic(last - start, 7) + 1
        starts = jnp.where(lane == chunk, start, starts)
        counts = jnp.where(lane == chunk, jnp.maximum(count, 1), counts)
    meta_ref[0:4, :] = starts
    meta_ref[4:8, :] = counts


def masked_positions(info, frontier_ref, pos_ref):
    items, byte_count = frontier_ref.shape
    lane = lax.broadcasted_iota(jnp.int32, (items, byte_count), 1)
    row = lax.broadcasted_iota(jnp.int32, (items, byte_count), 0)
    length = jnp.zeros((items, byte_count), jnp.int32)
    for item in range(items):
        length = jnp.where(row == item, info[4 + item], length)
    valid = lane < length
    running = jnp.where(valid, frontier_ref[...], 0.0)
    step = 1
    while step < byte_count:
        running = running + jnp.where(lane >= step, pltpu.roll(running, step, 1), 0.0)
        step *= 2
    count = lax.shift_right_logical(length + 3, 2).astype(F32)
    total = running[:, byte_count - 1 :]
    pos_ref[...] = jnp.where(valid, count * running / total, OUTSIDE)


def pool_own_kernel(
    info, frontier_ref, bytes_ref, out_ref, pos_ref, meta_ref, buffer, acc, meta, sems, meta_sem
):
    mine = share_out(info)[0]
    for slot, item in enumerate(mine):
        fetch_bytes(bytes_ref, buffer, sems, item, slot).start()
    masked_positions(info, frontier_ref, pos_ref)
    find_windows(pos_ref, meta_ref)
    copy = pltpu.make_async_copy(meta_ref, meta, meta_sem)
    copy.start()
    copy.wait()
    for slot, item in enumerate(mine):
        fetch_bytes(bytes_ref, buffer, sems, item, slot).wait()
        pool_rows(item, info, meta, pos_ref, buffer.at[slot], out_ref.at[slot], acc)


def pool_other_kernel(info, meta, pos_ref, bytes_ref, out_ref, buffer, acc, sems):
    theirs = share_out(info)[1]
    out_ref[2 * BLOCKS :, :] = jnp.zeros((64, out_ref.shape[1]), BF16)
    for slot, item in enumerate(theirs):
        fetch_bytes(bytes_ref, buffer, sems, item, slot).start()
    for slot, item in enumerate(theirs):
        fetch_bytes(bytes_ref, buffer, sems, item, slot).wait()
        rows = out_ref.at[span_of(slot, BLOCKS), :]
        pool_rows(item, info, meta, pos_ref, buffer.at[slot], rows, acc)


def pool_forward(info, frontier, byte_states, after):
    items, byte_count, share = byte_states.shape
    half = items // 2
    out = jax.ShapeDtypeStruct((half, BLOCKS, share), BF16)
    pos = jax.ShapeDtypeStruct((items, byte_count), F32)
    windows = jax.ShapeDtypeStruct((8, 128), jnp.int32)
    scratch = [pltpu.VMEM((half, byte_count, share), BF16), pltpu.VMEM((BLOCKS, share), F32)]
    own, positions, meta = launch(
        pool_own_kernel,
        "pool_own",
        7,
        1,
        info,
        (frontier, byte_states),
        [whole(pos.shape), HBM],
        [out, pos, windows],
        [whole(out.shape), whole(pos.shape), whole(windows.shape)],
        scratch
        + [
            pltpu.SMEM((8, 128), jnp.int32),
            pltpu.SemaphoreType.DMA((half,)),
            pltpu.SemaphoreType.DMA,
        ],
        after,
        vmem=VMEM_MOST,
    )
    sent = jax.ShapeDtypeStruct((half * BLOCKS + 64, share), BF16)
    (other,) = launch(
        pool_other_kernel,
        "pool_other",
        7,
        1,
        info,
        (meta, positions, byte_states),
        [SMEM, whole(pos.shape), HBM],
        [sent],
        [whole(sent.shape)],
        scratch + [pltpu.SemaphoreType.DMA((half,))],
        vmem=VMEM_MOST,
    )
    return own, other, positions, meta


def pool_back_kernel(mine, index, info, meta, pos_ref, bytes_ref, grads_ref, *refs):
    out_ref, part_ref, buffer, written, acc, sems, out_sems = refs[-7:]
    item = share_out(info)[0 if mine else 1][index]
    length = info[4 + item]
    grads = grads_ref.at[index] if mine else grads_ref.at[span_of(index, BLOCKS)]
    fetch = fetch_bytes(bytes_ref, buffer, sems, item, 0)
    fetch.start()
    pairs = lax.div(length + 2 * CHUNK - 1, 2 * CHUNK)
    size = 2 * CHUNK

    def written_copy(pair):
        rows = tile_at(pair, size)
        return pltpu.make_async_copy(
            written.at[rows, :], out_ref.at[item, rows, :], out_sems.at[pair]
        )

    def window(chunk, first, skipped):
        first = pl.multiple_of(first, 16)
        kernel, offset = window_kernel(chunk_row(pos_ref, item, chunk), first, skipped)
        rows = grads[pl.ds(first, WINDOW), :]
        slope = mm(rows, buffer[0, tile_at(chunk, CHUNK), :], NT)
        back = mm(kernel.astype(BF16), rows, TN)
        return back, jnp.sum(slope * kernel * offset, axis=0, keepdims=True)

    def two(pair, carry):
        for chunk in (pair * 2, pair * 2 + 1):
            back, terms = window(chunk, meta[item, chunk], None)
            written[tile_at(chunk, CHUNK), :] = back.astype(BF16)
            part_ref[0, :, tile_at(chunk, CHUNK)] = -4.0 * terms
        for chunk in (pair * 2, pair * 2 + 1):

            @pl.when(meta[4 + item, chunk] > 1)
            def _():
                acc[...] = jnp.zeros_like(acc)

                def more(number, total):
                    wanted = meta[item, chunk] + number * WINDOW
                    first = jnp.minimum(wanted, BLOCKS - WINDOW)
                    back, terms = window(chunk, first, wanted - first)
                    acc[...] += back
                    return total + terms

                total = lax.fori_loop(
                    0, meta[4 + item, chunk], more, jnp.zeros((1, CHUNK), F32)
                )
                written[tile_at(chunk, CHUNK), :] = acc[...].astype(BF16)
                part_ref[0, :, tile_at(chunk, CHUNK)] = -4.0 * total

        written_copy(pair).start()
        return carry

    def empty(pair, carry):
        written[tile_at(pair, size), :] = jnp.zeros((size, written.shape[1]), BF16)
        part_ref[0, :, tile_at(pair, size)] = jnp.zeros((1, size), F32)
        written_copy(pair).start()
        return carry

    every = written.shape[0] // size
    lax.fori_loop(pairs, every, empty, 0)
    fetch.wait()
    lax.fori_loop(0, pairs, two, 0)
    for pair in range(every):
        written_copy(pair).wait()


def pool_backward(info, meta, positions, byte_states, grads, mine, index, held, after, through):
    items, byte_count, share = byte_states.shape
    side = 0 if mine else 1
    return launch(
        functools.partial(pool_back_kernel, mine, index),
        "pool_back",
        5,
        1,
        info,
        (meta, positions, byte_states, grads) + tuple(held),
        [SMEM, whole((items, byte_count)), HBM, NEAR] + [HBM] * len(held),
        [
            jax.ShapeDtypeStruct((items, byte_count, share), BF16),
            jax.ShapeDtypeStruct((items, 1, byte_count), F32),
        ],
        [
            HBM,
            pl.BlockSpec((1, 1, byte_count), lambda i, info: (share_out(info)[side][index], 0, 0)),
        ],
        [
            pltpu.VMEM((1, byte_count, share), BF16),
            pltpu.VMEM((byte_count, share), BF16),
            pltpu.VMEM((CHUNK, share), F32),
            pltpu.SemaphoreType.DMA((1,)),
            pltpu.SemaphoreType.DMA((byte_count // (2 * CHUNK),)),
        ],
        after,
        through,
        {5: 0, 6: 1} if held else None,
    )


def frontier_kernel(info, mine_ref, theirs_ref, pos_ref, frontier_ref, out_ref):
    items, byte_count = frontier_ref.shape
    lane = lax.broadcasted_iota(jnp.int32, (items, byte_count), 1)
    row = lax.broadcasted_iota(jnp.int32, (items, byte_count), 0)
    length = jnp.zeros((items, byte_count), jnp.int32)
    for item in range(items):
        length = jnp.where(row == item, info[4 + item], length)
    valid = lane < length
    total = jnp.sum(jnp.where(valid, frontier_ref[...], 0.0), axis=1, keepdims=True)
    terms = jnp.where(valid, mine_ref[:, 0, :] + theirs_ref[:, 0, :], 0.0)
    weighted = jnp.sum(terms * pos_ref[...], axis=1, keepdims=True)
    step = 1
    while step < byte_count:
        moved = pltpu.roll(terms, byte_count - step, 1)
        terms = terms + jnp.where(lane < byte_count - step, moved, 0.0)
        step *= 2
    count = lax.shift_right_logical(length + 3, 2).astype(F32)
    out_ref[...] = jnp.where(valid, (terms * count - weighted) / total, 0.0)


def strips_kernel(info, rel_ref, first_ref, table_ref, strips):
    core = info[1]
    parts = [first_ref[512:528, span_of(index, 128)].astype(F32) for index in range(3)]
    other = (parts[0] + parts[1] + parts[2])[0:4, 0:BUCKETS]
    rows = []
    for values in (rel_ref[...], other):
        turned = jnp.concatenate((values[2:4], values[0:2]), axis=0)
        rows.append(jnp.where(core == 0, values, turned))
    spread = lax.dot_general(
        jnp.concatenate(rows, axis=0),
        table_ref[...],
        NN,
        precision=PRECISE,
        preferred_element_type=F32,
    )
    for head in range(strips.shape[0]):
        row = jnp.broadcast_to(spread[head : head + 1, :], (8, WRAP))
        eight = pltpu.roll(row, 384, 1, stride=1, stride_axis=0)
        for group in range(16):
            turned = pltpu.roll(eight, 8 * group, 1) if group else eight
            strips[head, span_of(group, 8), :] = turned[:, :896]


def bias_strips(info, rel, first, table, after):
    return launch(
        strips_kernel,
        "bias_strips",
        2,
        1,
        info,
        (rel, first, table),
        [NEAR, NEAR, NEAR],
        [jax.ShapeDtypeStruct((8, 128, 896), F32)],
        [NEAR],
        (),
        after,
    )[0]


def gather_halves(info, target, own_ref, other_ref):
    target[:, tile_at(info[0], 256)] = own_ref[0]
    target[:, tile_at(1 - info[0], 256)] = other_ref[...]


def span_of(index, size):
    return slice(index * size, (index + 1) * size)


def tile_at(index, size):
    return pl.ds(pl.multiple_of(index * size, size), size)


def started(pairs, sems):
    return [
        pltpu.make_async_copy(source, target, sems.at[index])
        for index, (source, target) in enumerate(pairs)
    ]


def inverse_rms(values):
    return lax.rsqrt(jnp.mean(values * values, axis=1, keepdims=True) + EPSILON)


def triple(values):
    high = values.astype(BF16)
    rest = values - high.astype(F32)
    middle = rest.astype(BF16)
    return high, middle, (rest - middle.astype(F32)).astype(BF16)


def spare_lane(head):
    return (head // 2) * 4 + 64 * (1 - head % 2)


def strip_tiles(strips, head, half):
    return jnp.concatenate(
        [
            strips[head, :, (3 - tile) * 128 + half * 256 : (5 - tile) * 128 + half * 256]
            for tile in range(4)
        ],
        axis=0,
    )


def parts_by_lane(values, lead):
    spot = lax.broadcasted_iota(jnp.int32, values.shape, 1) & 3
    parts = [part.astype(F32) for part in triple(values)]
    found = jnp.where(spot == 1, parts[0], jnp.where(spot == 2, parts[1], parts[2]))
    return jnp.where(spot == 0, lead, found).astype(BF16)


def attention_kernel(
    info,
    own_ref,
    other_ref,
    strips,
    gain_attn_ref,
    gain_mlp_ref,
    w_query,
    w_key,
    w_value,
    w_out,
    part_a,
    part_b,
    part_c,
    part_d,
    qkv_ref,
    log_ref,
    att_ref,
    middle_ref,
    normed_ref,
    w_qkv,
    w_o,
    pooled,
    logs,
    scores,
):
    step = pl.program_id(0)
    mp, core, way = info[0], info[1], info[2]
    count = item_count(info, step)

    @pl.when(step == 0)
    def _():
        for part in range(2):
            start = core if part == 0 else 1 - core
            for index, weight in enumerate((w_query, w_key, w_value)):
                first = index * 512 + part * 128
                w_qkv[:, first : first + 128] = weight[:, tile_at(start, 128)]
            w_o[span_of(part, 128), :] = w_out[tile_at(start, 128), :]
        for part, sources in enumerate(((part_a, part_b), (part_c, part_d))):
            for side, source in enumerate(sources):
                turn = way if side == 0 else 1 - way
                for index in range(3):
                    first = index * 512 + 256 + part * 128
                    w_qkv[tile_at(turn, 256), first : first + 128] = source[
                        0:256, span_of(index, 128)
                    ]
                rows = pl.ds(pl.multiple_of(256 + part * 128 + turn * 64, 64), 64)
                for lane in range(4):
                    w_o[rows, span_of(lane, 128)] = source[span_of(lane, 64), 384:512]
        logs[...] = jnp.zeros_like(logs)

    gather_halves(info, pooled, own_ref, other_ref)
    wide = pooled[...].astype(F32)
    normed = (wide * inverse_rms(wide) * gain_attn_ref[...]).astype(BF16)
    qkv_ref[0] = mm(normed, w_qkv[...]).astype(BF16)
    lane = lax.broadcasted_iota(jnp.int32, (BLOCKS, 128), 1)
    row = lax.broadcasted_iota(jnp.int32, (BLOCKS, 128), 0)
    dead = jnp.where(row < count, 0.0, MASKED_SCORE).astype(BF16)

    ready, found, tops = {}, {}, {}

    def prepare(pair):
        queries = qkv_ref[0, :, span_of(pair, 128)]
        keys = qkv_ref[0, :, span_of(pair + 4, 128)]
        values = qkv_ref[0, :, span_of(pair + 8, 128)]
        for side in range(2):
            own = (lane < 64) == (side == 0)
            spare = lane == 64 * (1 - side)
            chosen = jnp.where(own, queries, jnp.where(spare, 1.0, 0.0).astype(BF16))
            masked = jnp.where(spare, dead, keys)
            summing = jnp.transpose(jnp.where(own, values, jnp.ones_like(values)))
            ready[pair, side] = (chosen, masked, summing)

    def first_pass(slot, pair, half, side):
        chosen, masked, _ = ready[pair, side]
        held = scores.at[slot]
        raw = mm(masked, chosen[span_of(half, 256), :], NT)
        most = None
        for tile in range(4):
            first = (3 - tile) * 128 + half * 256
            part = raw[span_of(tile, 128), :] + strips[pair * 2 + side, :, first : first + 256]
            held[span_of(tile, 128), :] = part
            part = jnp.max(part.reshape(16, 8, 256), axis=0)
            most = part if most is None else jnp.maximum(most, part)
        tops[slot] = jnp.max(most, axis=0, keepdims=True)

    def second_pass(slot, pair, half, side):
        held = scores.at[slot]
        most = tops[slot]
        expo = jnp.concatenate(
            [jnp.exp(held[span_of(tile, 128), :] - most).astype(BF16) for tile in range(4)],
            axis=0,
        )
        out = mm(ready[pair, side][2], expo)
        other = 64 * (1 - side)
        total = out[other : other + 1, :]
        found[side] = (out * (1.0 / total))[64 * side : 64 * side + 64, :]
        place = pair * 4 + other
        logs[place : place + 4, span_of(half, 256)] = jnp.broadcast_to(
            most + jnp.log(total), (4, 256)
        )
        if side == 1:
            both = jnp.concatenate((found[0], found[1]), axis=0).astype(BF16)
            att_ref[0, span_of(half, 256), span_of(pair, 128)] = jnp.transpose(both)

    chains = [(pair, half, side) for pair in range(4) for half in range(2) for side in range(2)]
    for index, chain in enumerate(chains):
        if index % 4 == 0:
            prepare(chain[0])
        first_pass(index % SLOTS, *chain)
        if index >= SLOTS - 1:
            last = index - SLOTS + 1
            second_pass(last % SLOTS, *chains[last])
    for last in range(len(chains) - SLOTS + 1, len(chains)):
        second_pass(last % SLOTS, *chains[last])
    log_ref[0] = parts_by_lane(-jnp.transpose(logs[...]), 1.0)

    mid = wide + mm(att_ref[0], w_o[...])
    middle_ref[0] = mid
    normed_ref[0] = (mid * inverse_rms(mid) * gain_mlp_ref[...]).astype(BF16)


def attention_forward(info, own, other, strips, gain_attn, gain_mlp, weights, parts, after):
    half = own.shape[0]
    return launch(
        attention_kernel,
        "attention_forward",
        20,
        half,
        info,
        (own, other, strips, gain_attn, gain_mlp, *weights, *parts),
        [
            item((BLOCKS, 256)),
            pl.BlockSpec((BLOCKS, 256), lambda i, info: (i, 0)),
            NEAR,
            whole((1, 512)),
            whole((1, 512)),
        ]
        + [NEAR] * 8,
        [
            jax.ShapeDtypeStruct((half, BLOCKS, 1536), BF16),
            jax.ShapeDtypeStruct((half, BLOCKS, 128), BF16),
            jax.ShapeDtypeStruct((half, BLOCKS, 512), BF16),
            jax.ShapeDtypeStruct((half, BLOCKS, 512), F32),
            jax.ShapeDtypeStruct((half, BLOCKS, 512), BF16),
            jax.ShapeDtypeStruct((512, 1536), BF16),
            jax.ShapeDtypeStruct((512, 512), BF16),
        ],
        [
            item((BLOCKS, 1536)),
            item((BLOCKS, 128)),
            item((BLOCKS, 512)),
            item((BLOCKS, 512)),
            item((BLOCKS, 512)),
            whole((512, 1536)),
            whole((512, 512)),
        ],
        [
            pltpu.VMEM((BLOCKS, 512), BF16),
            pltpu.VMEM((128, BLOCKS), F32),
            pltpu.VMEM((SLOTS, BLOCKS, 256), F32),
        ],
        after,
    )


def gelu_and_slope(pre):
    square = pre * pre
    tanh = jnp.tanh(pre * (ROOT + (ROOT * CUBIC) * square))
    up = 0.5 + 0.5 * tanh
    act = pre * up
    slope = up + act * (1.0 - up) * (2.0 * ROOT + (6.0 * ROOT * CUBIC) * square)
    return act, slope


def ff_piece(normed, turned, top, turned_top, hid, mid, acts, grads, result, back, start):
    for half in range(2):
        rows = span_of(half, BLOCKS)
        act, slope = gelu_and_slope(mm(normed[rows, :], hid))
        acts[rows, :] = act.astype(BF16)
        grads[rows, :] = (mm(top[rows, :], mid, NT) * slope).astype(BF16)
        new_result = mm(acts[rows, :], mid)
        new_back = mm(grads[rows, :], hid, NT)
        if start is None:
            result[rows, :] += new_result
            back[rows, :] += new_back
        elif start:
            result[rows, :] = start[0][rows, :] + new_result
            back[rows, :] = start[1][rows, :] + new_back
        else:
            result[rows, :] = new_result
            back[rows, :] = new_back
    return mm(turned[...], grads[...]), mm(turned_top[...], acts[...])


def store_shards(place, target, first, values):
    rows = values.shape[0] // SHARDS
    size = target.shape[0] // SHARDS
    for shard in range(SHARDS):
        at = pl.multiple_of(lax.bitwise_xor(place, shard) * size + first, 64)
        target[pl.ds(at, rows), :] = values[span_of(shard, rows), :].astype(BF16)


def gather_top(info, top, turned_top, cot_own_ref, cot_other_ref):
    for index in range(2):
        rows = span_of(index, BLOCKS)
        count = item_count(info, index)
        live = lax.broadcasted_iota(jnp.int32, (BLOCKS, 256), 0) < count
        zero = jnp.zeros((BLOCKS, 256), BF16)
        top[rows, tile_at(info[0], 256)] = jnp.where(live, cot_own_ref[index], zero)
        top[rows, tile_at(1 - info[0], 256)] = jnp.where(live, cot_other_ref[index], zero)
        turned_top[:, rows] = jnp.transpose(top[rows, :])


def ff_own_kernel(
    info,
    normed_ref,
    cot_own_ref,
    cot_other_ref,
    w_hidden,
    w_mlp,
    result,
    back,
    keep_ref,
    send_ref,
    mark,
    top,
    turned_top,
    turned,
    acts,
    grads,
):
    core, place = info[1], info[3]
    mark[...] = jnp.zeros_like(mark)
    gather_top(info, top, turned_top, cot_own_ref, cot_other_ref)
    for index in range(2):
        turned[:, span_of(index, BLOCKS)] = jnp.transpose(normed_ref[span_of(index, BLOCKS), :])
    for part, target in ((1, send_ref), (0, keep_ref)):
        start = core if part == 0 else 1 - core
        grad_hid, grad_mid = ff_piece(
            normed_ref,
            turned,
            top,
            turned_top,
            w_hidden[:, tile_at(start, 512)],
            w_mlp[tile_at(start, 512), :],
            acts,
            grads,
            result,
            back,
            () if part == 1 else None,
        )
        store_shards(place, target, 0, grad_hid)
        store_shards(place, target, 64, grad_mid)


def ff_other_kernel(
    info,
    normed_ref,
    cot_own_ref,
    cot_other_ref,
    hid_a,
    hid_b,
    hid_c,
    hid_d,
    mid_near,
    mid_far,
    result_ref,
    back_ref,
    middle_ref,
    gain_ref,
    blocks_keep,
    blocks_send,
    grad_mid_ref,
    keep_ref,
    send_ref,
    gain_out,
    top,
    turned_top,
    turned,
    acts,
    grads,
    weights,
    result,
    back,
    blocks,
):
    mp, way, place = info[0], info[2], info[3]
    for part, sources in ((1, (hid_c, hid_d)), (0, (hid_a, hid_b))):
        for side, source in enumerate(sources):
            turn = way if side == 0 else 1 - way
            weights[part, tile_at(turn, 256), :] = source[256:512, :]
    gather_top(info, top, turned_top, cot_own_ref, cot_other_ref)
    for index in range(2):
        turned[:, span_of(index, BLOCKS)] = jnp.transpose(normed_ref[span_of(index, BLOCKS), :])
    for part, target in ((1, send_ref), (0, keep_ref)):
        grad_hid, grad_mid = ff_piece(
            normed_ref,
            turned,
            top,
            turned_top,
            weights[part],
            (mid_far if part == 1 else mid_near)[...],
            acts,
            grads,
            result,
            back,
            (result_ref, back_ref) if part == 1 else None,
        )
        store_shards(place, target, 0, grad_hid)
        store_shards(place, target, 64, grad_mid)

    new_gain = jnp.zeros((1, 512), F32)
    for index in range(2):
        rows = span_of(index, BLOCKS)
        count = item_count(info, index)
        live = lax.broadcasted_iota(jnp.int32, (BLOCKS, 1), 0) < count
        middle = middle_ref[rows, :]
        blocks[...] = jnp.where(live, middle + result[rows, :], 0.0).astype(BF16)
        blocks_keep[index] = blocks[:, tile_at(mp, 256)]
        blocks_send[index] = blocks[:, tile_at(1 - mp, 256)]
        scale = inverse_rms(middle)
        unit = middle * scale
        grad_normed = back[rows, :]
        scaled = grad_normed * gain_ref[...]
        grad_mid_ref[rows, :] = top[rows, :].astype(F32) + scale * (
            scaled - unit * jnp.mean(scaled * unit, axis=1, keepdims=True)
        )
        new_gain = new_gain + jnp.sum(grad_normed * unit, axis=0, keepdims=True)
    gain_out[...] = jnp.broadcast_to(new_gain, gain_out.shape)


def ff_call(info, normed, cot, cot_other, mine, given, after):
    rows = normed.shape[0]
    half = rows // BLOCKS
    packed = (SHARDS * 128, 512)
    wide = jax.ShapeDtypeStruct((rows, 512), F32)
    pack = jax.ShapeDtypeStruct(packed, BF16)
    share = jax.ShapeDtypeStruct((half, BLOCKS, 256), BF16)
    in_specs = [whole((rows, 512)), whole(share.shape), whole(share.shape)]
    scratch = [
        pltpu.VMEM((rows, 512), BF16),
        pltpu.VMEM((512, rows), BF16),
        pltpu.VMEM((512, rows), BF16),
        pltpu.VMEM((rows, 512), BF16),
        pltpu.VMEM((rows, 512), BF16),
    ]
    if mine:
        in_specs += [NEAR] * 2
        outs = [wide, wide, pack, pack, jax.ShapeDtypeStruct((8, 128), F32)]
    else:
        in_specs += [NEAR] * 8 + [whole((rows, 512)), whole((1, 512))]
        outs = [share, share, wide, pack, pack, jax.ShapeDtypeStruct((8, 512), F32)]
        scratch += [
            pltpu.VMEM((2, 512, 512), BF16),
            pltpu.VMEM((rows, 512), F32),
            pltpu.VMEM((rows, 512), F32),
            pltpu.VMEM((BLOCKS, 512), BF16),
        ]
    return launch(
        ff_own_kernel if mine else ff_other_kernel,
        "ff_own" if mine else "ff_other",
        12,
        1,
        info,
        (normed, cot, cot_other, *given),
        in_specs,
        outs,
        [whole(x.shape) for x in outs],
        scratch,
        after,
    )


def attention_back_body(
    info,
    first_head,
    own_ref,
    other_ref,
    query_ref,
    key_ref,
    value_ref,
    log_ref,
    att_ref,
    grad_mid_ref,
    strips,
    collect_ref,
    gain_attn_ref,
    wq_ref,
    wk_ref,
    wv_ref,
    wo_ref,
    keep_ref,
    send_ref,
    pooled,
    outer,
    grads,
    sums,
    turned,
    turned_branch,
    atts,
    probs,
    weights,
    scored,
):
    step = pl.program_id(0)
    mp, place = info[0], info[3]
    count = item_count(info, step)

    @pl.when(step == 0)
    def _():
        sums[...] = jnp.zeros_like(sums)

    gather_halves(info, pooled, own_ref, other_ref)
    here = tile_at(step, BLOCKS)
    branch = grad_mid_ref[0].astype(BF16)
    outer[...] = mm(branch, wo_ref[...], NT).astype(BF16)
    lane = lax.broadcasted_iota(jnp.int32, (BLOCKS, 128), 1)
    row = lax.broadcasted_iota(jnp.int32, (BLOCKS, 128), 0)
    dead = jnp.where(row < count, 0.0, MASKED_SCORE).astype(BF16)
    line = lax.broadcasted_iota(jnp.int32, (1, 128), 1)
    deltas = jnp.zeros((BLOCKS, 128), F32)
    for pair in range(2):
        span = span_of(pair, 128)
        overlap = outer[:, span].astype(F32) * att_ref[0, :, span].astype(F32)
        for side in range(2):
            own = (lane < 64) == (side == 0)
            delta = jnp.sum(jnp.where(own, overlap, 0.0), axis=1, keepdims=True)
            spare = spare_lane(first_head + pair * 2 + side)
            mine = jnp.logical_and(lane >= spare, lane < spare + 4)
            deltas = jnp.where(mine, delta, deltas)
    deltas = parts_by_lane(-deltas, 0.0)

    ready, found = {}, {}

    def prepare(pair):
        span = span_of(pair, 128)
        queries = query_ref[0, :, span]
        keys = key_ref[0, :, span]
        values = value_ref[0, :, span]
        out_grads = outer[:, span]
        for side in range(2):
            own = (lane < 64) == (side == 0)
            spare = spare_lane(first_head + pair * 2 + side)
            added = jnp.logical_and(line > spare, line < spare + 4)
            ones = jnp.where(added, 1.0, 0.0).astype(BF16)
            chosen = jnp.where(own, queries, log_ref[0])
            masked = jnp.where(own, keys, jnp.where(lane == spare, dead, ones))
            drawn = jnp.where(own, out_grads, deltas)
            weighed = jnp.where(own, values, ones)
            ready[pair, side] = (chosen, masked, drawn, weighed)

    def first_pass(slot, pair, side, half):
        chosen, masked, _, _ = ready[pair, side]
        raw = mm(masked, chosen[span_of(half, 256), :], NT)
        for tile in range(4):
            first = (3 - tile) * 128 + half * 256
            rows = span_of(tile, 128)
            part = jnp.exp(
                raw[rows, :] + strips[first_head + pair * 2 + side, :, first : first + 256]
            )
            probs[slot, rows, :] = part
            weights[slot, rows, :] = part.astype(BF16)

    def second_pass(slot, pair, side, half):
        _, _, drawn, weighed = ready[pair, side]
        head = pair * 2 + side
        slope = mm(weighed, drawn[span_of(half, 256), :], NT)
        product = [probs[slot, span_of(tile, 128), :] * slope[span_of(tile, 128), :] for tile in range(4)]
        for tile in range(4):
            scored[slot, span_of(tile, 128), :] = product[tile].astype(BF16)
        for diagonal in range(5):
            first = (3 - diagonal + 1) * 128 + half * 256
            total = None
            for tile in range(4):
                column = tile - diagonal + 1
                if 0 <= column < 2:
                    block = product[tile][:, span_of(column, 128)]
                    total = block if total is None else total + block
            sums[head, :, first : first + 128] += total

    def third_pass(slots, pair, side):
        span = span_of(pair, 128)
        halves = [(slots[half], span_of(half, 256)) for half in range(2)]
        keys = key_ref[0, :, span]
        grad_query = jnp.concatenate([mm(scored[slot], keys, TN) for slot, _ in halves], axis=0)
        grad_key = sum(mm(scored[slot], query_ref[0, rows, span]) for slot, rows in halves)
        grad_value = sum(mm(weights[slot], outer[rows, span]) for slot, rows in halves)
        found[side] = (grad_query, grad_key, grad_value)
        if side == 1:
            for index in range(3):
                first = index * 256 + pair * 128
                grads[here, first : first + 128] = jnp.where(
                    lane < 64, found[0][index], found[1][index]
                ).astype(BF16)

    units = [(pair, side, half) for pair in range(2) for side in range(2) for half in range(2)]
    for index in range(len(units) + 2):
        if index < len(units):
            if index % 4 == 0:
                prepare(units[index][0])
            first_pass(index % 4, *units[index])
        if 1 <= index <= len(units):
            second_pass((index - 1) % 4, *units[index - 1])
        if index >= 2 and units[index - 2][2] == 1:
            third_pass(((index - 3) % 4, (index - 2) % 4), *units[index - 2][:2])

    wide = pooled[...].astype(F32)
    scale = inverse_rms(wide)
    unit = wide * scale
    normed = (unit * gain_attn_ref[...]).astype(BF16)
    turned[:, here] = jnp.transpose(normed)
    turned_branch[:, here] = jnp.transpose(branch)
    atts[here, :] = att_ref[0]

    @pl.when(step == 1)
    def _():
        new = mm(turned[...], grads[...])
        new_out = mm(turned_branch[...], atts[...])
        for part, target in ((1, send_ref), (0, keep_ref)):
            for shard in range(SHARDS):
                at = tile_at(lax.bitwise_xor(place, shard), 64)
                here_rows = span_of(shard, 64)
                for index in range(3):
                    first = index * 256 + part * 128
                    target[at, span_of(index, 128)] = new[here_rows, first : first + 128].astype(
                        BF16
                    )
                target[at, 384:512] = new_out[here_rows, span_of(part, 128)].astype(BF16)

    grad_normed = (
        mm(grads[here, 0:256], wq_ref[...], NT)
        + mm(grads[here, 256:512], wk_ref[...], NT)
        + mm(grads[here, 512:768], wv_ref[...], NT)
    )
    return unit, scale, grad_normed


def fold_bias(sums, collect_ref):
    rows = []
    for head in range(4):
        folded = jnp.concatenate((sums[head], jnp.zeros((128, 128), F32)), axis=1)
        size = 64
        while size >= 8:
            folded = folded[:size] + pltpu.roll(folded[size : 2 * size], WRAP - size, 1)
            size //= 2
        rows.append(folded)
    lines = jnp.concatenate(triple(jnp.concatenate(rows, axis=0)), axis=0)
    found = mm(lines, collect_ref[...])
    found = found[0:32] + found[32:64] + found[64:96]
    row = lax.broadcasted_iota(jnp.int32, found.shape, 0) & 7
    spot = lax.shift_right_logical(lax.broadcasted_iota(jnp.int32, found.shape, 1), 5)
    found = jnp.where(row == spot, found, 0.0)
    rows = []
    for head in range(4):
        total = jnp.sum(found[span_of(head, 8), :], axis=0, keepdims=True)
        total = total[:, 0:128] + total[:, 128:256]
        total = total + pltpu.roll(total, 64, 1)
        rows.append(total + pltpu.roll(total, 32, 1))
    return jnp.concatenate(rows + rows, axis=0)


def attention_back_first_kernel(info, *refs):
    heads, (grad_ref, keep_ref, send_ref, rel_ref), scratch = refs[:15], refs[15:19], refs[19:]
    _, _, grad_normed = attention_back_body(info, 4, *heads, keep_ref, send_ref, *scratch)
    grad_ref[0] = grad_normed

    @pl.when(pl.program_id(0) == 1)
    def _():
        rel_ref[...] = fold_bias(scratch[3], heads[9])


def attention_back_second_kernel(info, *refs):
    heads, (held_ref, rel_ref, gain_mid_ref), refs = refs[:15], refs[15:18], refs[18:]
    (keep_rows, send_rows, keep_ref, send_ref, tiny_ref), scratch = refs[:5], refs[5:]
    scratch, acc_gain = scratch[:-1], scratch[-1]
    unit, scale, grad_normed = attention_back_body(info, 0, *heads, keep_ref, send_ref, *scratch)
    mp, core = info[0], info[1]
    step = pl.program_id(0)
    pooled = scratch[0]
    grad_normed = grad_normed + held_ref[0]
    scaled = grad_normed * heads[10][...]
    grad_pooled = heads[7][0] + scale * (
        scaled - unit * jnp.mean(scaled * unit, axis=1, keepdims=True)
    )
    pooled[...] = grad_pooled.astype(BF16)
    keep_rows[0] = pooled[:, tile_at(mp, 256)]
    send_rows[tile_at(step, BLOCKS), :] = pooled[:, tile_at(1 - mp, 256)]
    new_gain = jnp.sum(grad_normed * unit, axis=0, keepdims=True)

    @pl.when(step == 0)
    def _():
        acc_gain[...] = jnp.broadcast_to(new_gain, acc_gain.shape)

    @pl.when(step == 1)
    def _():
        found = fold_bias(scratch[3], heads[9])
        line = lax.broadcasted_iota(jnp.int32, (8, 128), 0)
        rows = jnp.zeros((8, 128), F32)
        for head in range(8):
            source = found if head < 4 else rel_ref[...]
            true_head = (
                lax.bitwise_xor(mp, head // 4) * 4
                + lax.bitwise_xor(core, (head // 2) % 2) * 2
                + head % 2
            )
            rows = jnp.where(line == true_head, source[head % 4 : head % 4 + 1, :], rows)
        tiny_ref[...] = jnp.zeros_like(tiny_ref)
        tiny_ref[0:1, :] = acc_gain[0:1, :] + new_gain
        tiny_ref[1:2, :] = gain_mid_ref[0:1, :]
        tiny_ref[8:16, 0:128] = rows


def attention_back(
    info, mine, rows_args, strips, collect, gain_attn, joined, w_o, given, after
):
    own, other, qkv, logs, att, grad_mid = rows_args
    half = own.shape[0]
    where = 0 if mine else 1

    def lanes(index):
        return pl.BlockSpec((1, BLOCKS, 256), lambda i, info: (i, 0, index))

    def columns(index):
        return pl.BlockSpec((512, 256), lambda i, info: (0, index))

    in_specs = [
        item((BLOCKS, 256)),
        pl.BlockSpec((BLOCKS, 256), lambda i, info: (i, 0)),
        lanes(where),
        lanes(2 + where),
        lanes(4 + where),
        item((BLOCKS, 128)),
        lanes(where),
        item((BLOCKS, 512)),
        NEAR,
        whole((WRAP, 256)),
        whole((1, 512)),
        columns(where),
        columns(2 + where),
        columns(4 + where),
        pl.BlockSpec((256, 512), lambda i, info: (where, 0)),
    ]
    args = [own, other, qkv, qkv, qkv, logs, att, grad_mid, strips, collect, gain_attn]
    args += [joined, joined, joined, w_o]
    packed = (SHARDS * 64, 512)
    pack = jax.ShapeDtypeStruct(packed, BF16)
    scratch = [
        pltpu.VMEM((BLOCKS, 512), BF16),
        pltpu.VMEM((BLOCKS, 256), BF16),
        pltpu.VMEM((half * BLOCKS, 768), BF16),
        pltpu.VMEM((4, 128, 896), F32),
        pltpu.VMEM((512, half * BLOCKS), BF16),
        pltpu.VMEM((512, half * BLOCKS), BF16),
        pltpu.VMEM((half * BLOCKS, 256), BF16),
        pltpu.VMEM((4, BLOCKS, 256), F32),
        pltpu.VMEM((4, BLOCKS, 256), BF16),
        pltpu.VMEM((4, BLOCKS, 256), BF16),
    ]
    if mine:
        share = jax.ShapeDtypeStruct((half, BLOCKS, 256), BF16)
        in_specs += [item((BLOCKS, 512)), whole((8, 128)), whole((8, 512))]
        sent = jax.ShapeDtypeStruct((half * BLOCKS, 256), BF16)
        outs = [share, sent, pack, pack, jax.ShapeDtypeStruct((16, 512), F32)]
        out_specs = [item((BLOCKS, 256)), whole(sent.shape), whole(packed), whole(packed)]
        out_specs += [whole((16, 512))]
        scratch += [pltpu.VMEM((8, 512), F32)]
    else:
        outs = [
            jax.ShapeDtypeStruct((half, BLOCKS, 512), F32),
            pack,
            pack,
            jax.ShapeDtypeStruct((8, 128), F32),
        ]
        out_specs = [item((BLOCKS, 512)), whole(packed), whole(packed), whole((8, 128))]
    return launch(
        attention_back_second_kernel if mine else attention_back_first_kernel,
        "attention_back_own" if mine else "attention_back_other",
        17,
        half,
        info,
        (*args, *given),
        in_specs,
        outs,
        out_specs,
        scratch,
        after,
    )


def place_kernel(info, ff_near, ff_far, hid_ref, mid_ref, mark):
    mark[...] = jnp.zeros_like(mark)
    core, place = info[1], info[3]
    for source, side in ((ff_near, core), (ff_far, 1 - core)):
        turned = []
        for shard in range(SHARDS):
            at = lax.bitwise_xor(place, shard)
            at = at * 2
            hid_ref[span_of(shard, 64), tile_at(side, 512)] = source[tile_at(at, 64), :].astype(F32)
            turned.append(source[tile_at(at + 1, 64), :])
        mid_ref[tile_at(side, 512), :] = jnp.transpose(
            jnp.concatenate(turned, axis=0).astype(F32)
        )


def pack_kernel(info, wq, wk, wv, wo, wh, rel, out, sems):
    core, way = info[1], info[2]
    rows = tile_at(way, 256)
    pairs = []
    for index, weight in enumerate((wq, wk, wv)):
        lanes = pl.ds(index * 128, 128)
        pairs.append((weight.at[rows, tile_at(core, 128)], out.at[pl.ds(0, 256), lanes]))
    few = pl.ds(pl.multiple_of(core * 128 + way * 64, 64), 64)
    for lane in range(4):
        pairs.append(
            (
                wo.at[few, pl.ds(lane * 128, 128)],
                out.at[pl.ds(lane * 64, 64), pl.ds(384, 128)],
            )
        )
    pairs.append((wh.at[rows, tile_at(core, 512)], out.at[pl.ds(256, 256), :]))
    copies = started(pairs, sems)
    for copy in copies:
        copy.start()
    out[512:528, :] = jnp.zeros((16, 512), BF16)
    for index, part in enumerate(triple(rel[...])):
        out[512:516, index * 128 : index * 128 + BUCKETS] = part
    for copy in copies:
        copy.wait()


def pack(info, weights, rel):
    return launch(
        pack_kernel,
        "pack",
        1,
        1,
        info,
        (*weights[:5], rel),
        [HBM] * 5 + [whole(rel.shape)],
        [jax.ShapeDtypeStruct((528, 512), BF16)],
        [whole((528, 512))],
        [pltpu.SemaphoreType.DMA((8,))],
        vmem=VMEM_MOST,
    )[0]


def pack_more_kernel(info, wm, cot, mid_out, cot_out, cot_own, sems):
    mine, theirs = share_out(info)
    pairs = [(wm.at[tile_at(info[1], 512), :], mid_out)]
    for index in range(2):
        pairs.append((cot.at[theirs[index]], cot_out.at[index, pl.ds(0, BLOCKS), :]))
        pairs.append((cot.at[mine[index]], cot_own.at[index]))
    copies = started(pairs, sems)
    for copy in copies:
        copy.start()
    cot_out[:, BLOCKS:, :] = jnp.zeros((2, 32, cot_out.shape[2]), BF16)
    for copy in copies:
        copy.wait()


def pack_more(info, w_mlp, cotangent, after):
    half, share = cotangent.shape[0] // 2, cotangent.shape[2]
    outs = [jax.ShapeDtypeStruct((512, 512), BF16)]
    outs += [jax.ShapeDtypeStruct((half, rows, share), BF16) for rows in (BLOCKS + 32, BLOCKS)]
    return launch(
        pack_more_kernel,
        "pack_more",
        1,
        1,
        info,
        (w_mlp, cotangent),
        [HBM] * 2,
        outs,
        [whole(x.shape) for x in outs],
        [pltpu.SemaphoreType.DMA((5,))],
        after,
        vmem=VMEM_MOST,
    )


def final_kernel(
    info,
    near,
    far,
    mine_ref,
    theirs_ref,
    pos_ref,
    frontier_ref,
    blocks_kept,
    blocks_got,
    query_ref,
    key_ref,
    value_ref,
    out_ref,
    front_ref,
    gain_attn_ref,
    gain_mlp_ref,
    rel_ref,
    blocks_ref,
    sems,
):
    mp, core, place = info[0], info[1], info[3]
    pairs = []
    mine, theirs = share_out(info)
    for index in range(2):
        pairs.append((blocks_kept.at[index], blocks_ref.at[mine[index]]))
        pairs.append((blocks_got.at[index], blocks_ref.at[theirs[index]]))
    copies = started(pairs, sems)
    for copy in copies:
        copy.start()
    for source, side in ((near, core), (far, 1 - core)):
        turned = []
        for shard in range(SHARDS):
            at = tile_at(lax.bitwise_xor(place, shard), 64)
            for index, target in enumerate((query_ref, key_ref, value_ref)):
                target[span_of(shard, 64), tile_at(side, 128)] = source[
                    at, span_of(index, 128)
                ].astype(F32)
            turned.append(source[at, 384:512])
        out_ref[tile_at(side, 128), :] = jnp.transpose(
            jnp.concatenate(turned, axis=0).astype(F32)
        )
    tiny = near[512:528, :].astype(F32) + far[512:528, :].astype(F32)
    gain_attn_ref[...] = tiny[0:1, :]
    gain_mlp_ref[...] = tiny[1:2, :]
    heads = jnp.where(mp == 0, tiny[8:12, 0:128], tiny[12:16, 0:128])
    flipped = jnp.transpose(jnp.concatenate((heads, heads), axis=0))
    rel_ref[...] = flipped[0:BUCKETS, 0:4]
    frontier_kernel(info, mine_ref, theirs_ref, pos_ref, frontier_ref, front_ref)
    for copy in copies:
        copy.wait()


def finish(
    info, near, far, mine, theirs, positions, frontier, blocks_kept, blocks_got, after
):
    args = (near, far, mine, theirs, positions, frontier)
    square = jax.ShapeDtypeStruct((512, 256), F32)
    row = jax.ShapeDtypeStruct((1, 512), F32)
    outs = [square, square, square, jax.ShapeDtypeStruct((256, 512), F32)]
    outs += [jax.ShapeDtypeStruct(frontier.shape, F32), row, row]
    outs += [jax.ShapeDtypeStruct((BUCKETS, 4), F32)]
    return launch(
        final_kernel,
        "finish",
        4,
        1,
        info,
        (*args, blocks_kept, blocks_got),
        [whole(x.shape) for x in args] + [ANY] * 2,
        outs + [jax.ShapeDtypeStruct((4,) + blocks_kept.shape[1:], BF16)],
        [whole(x.shape) for x in outs] + [HBM],
        [pltpu.SemaphoreType.DMA((4,))],
        after,
    )


def ff_place(info, near, far, shapes, after):
    return launch(
        place_kernel,
        "ff_place",
        4,
        1,
        info,
        (near, far),
        [whole(near.shape), whole(far.shape)],
        [jax.ShapeDtypeStruct(shape, F32) for shape in shapes],
        [whole(shape) for shape in shapes],
        (),
        after,
    )


def shards(
    devices,
    byte_states,
    frontier,
    lengths,
    gain_attn,
    w_query,
    w_key,
    w_value,
    w_attn_out,
    rel_bias,
    gain_mlp,
    w_hidden,
    w_mlp_out,
    cotangent,
):
    bits = devices.bit_length() - 1
    mp = lax.axis_index("mp").astype(jnp.int32)
    dp = lax.axis_index(("far", "near")).astype(jnp.int32)
    core = dp & 1
    way = (dp >> 1) & 1
    place = (((dp >> 1) & 1) << 2) | (((dp >> 2) & 1) << 1)
    info = jnp.concatenate((jnp.stack((mp, core, way, place)), lengths))

    def across(value):
        return lax.ppermute(value, "mp", [(0, 1), (1, 0)])

    def swap(value, bit):
        pairs = [(i, i ^ (1 << bit)) for i in range(devices)]
        return lax.ppermute(value, ("far", "near"), pairs)

    def swap_four(value, index):
        turn = ((index & 1) << 2) | ((index >> 1) << 1)
        return lax.ppermute(value, ("far", "near"), [(i, i ^ turn) for i in range(devices)])

    def rows(count):
        return ((count, 512), BF16)

    weights = (w_query, w_key, w_value, w_attn_out, w_hidden, w_mlp_out)
    rel_own = rel_bias.T
    first_sent = pack(info, weights, rel_own)
    first = across(first_sent)
    backward, collect = offset_tables()
    backward, collect = jnp.asarray(backward), jnp.asarray(collect, BF16)

    pooled_own, pooled_sent, positions, meta = pool_forward(
        info, frontier, byte_states, (first_sent,)
    )
    pooled_other = across(pooled_sent)
    (first,) = combine("meet", nothing, after=(pooled_sent,), through=(first,))
    second = swap(first, 1)
    mid_sent, cot_sent, cot_own = pack_more(info, w_mlp_out, cotangent, (pooled_sent,))

    strips = bias_strips(info, rel_own, first, backward, (cot_own,))
    second, mid_sent = combine(
        "meet", nothing, after=(pooled_other, strips), through=(second, mid_sent)
    )
    parts = (first, second, swap(first, 0), swap(second, 0))
    cot_other = across(cot_sent)
    mid_first = across(mid_sent)

    gain_attn_row = gain_attn.reshape(1, -1)
    gain_mlp_row = gain_mlp.reshape(1, -1)
    qkv, logs, att, middle, normed, joined, w_o = attention_forward(
        info,
        pooled_own,
        pooled_other,
        strips,
        gain_attn_row,
        gain_mlp_row,
        weights[:4],
        parts,
        (),
    )
    half = pooled_own.shape[0]
    normed = normed.reshape(half * BLOCKS, -1)
    middle = middle.reshape(half * BLOCKS, -1)

    result, back, near_keep, near_sent, mark = ff_call(
        info, normed, cot_own, cot_other, True, (w_hidden, w_mlp_out), ()
    )
    got_near = swap(near_sent, 0)
    (mid_first,) = combine("meet", nothing, after=(mark,), through=(mid_first,))
    blocks_kept, blocks_sent, grad_mid, far_keep, far_sent, gain_mid = ff_call(
        info,
        normed,
        cot_own,
        cot_other,
        False,
        (*parts, mid_first, swap(mid_first, 0), result, back, middle, gain_mlp_row),
        (),
    )
    near_low, near_high, far_sent = combine(
        "near_cores",
        sum_into,
        (near_keep, got_near),
        (rows(512), rows(528)),
        (gain_mid,),
        (far_sent,),
    )
    far_low, far_high, near_high = combine(
        "far_cores",
        sum_into,
        (far_keep, swap(far_sent, 0)),
        (rows(512), rows(512)),
        (),
        (near_high,),
    )
    got_far = swap(far_high, 1)
    blocks_other = across(blocks_sent)

    grad_mid = grad_mid.reshape(half, BLOCKS, -1)
    rows_args = (pooled_own, pooled_other, qkv, logs, att, grad_mid)
    grad_normed, far_keep, far_sent, far_rel = attention_back(
        info,
        False,
        rows_args,
        strips,
        collect,
        gain_attn_row,
        joined,
        w_o,
        (),
        (far_low,),
    )
    far_ff, far_sent, near_high = combine(
        "far_y", sum_into, (far_low, got_far), (rows(528),), (far_rel, blocks_other), (far_sent, near_high)
    )
    got_near = swap(near_high, 1)
    far_attn, far_ff = combine(
        "far_cores", sum_into, (far_keep, swap(far_sent, 0)), (rows(544),), (), (far_ff,)
    )
    got_attn = across(far_attn)
    got_far = across(far_ff)
    grad_keep, grad_sent, near_keep, near_sent, tiny = attention_back(
        info,
        True,
        rows_args,
        strips,
        collect,
        gain_attn_row,
        joined,
        w_o,
        (grad_normed, far_rel, gain_mid),
        (far_attn,),
    )
    grad_other = across(grad_sent)

    def step_zero(ins, outs):
        for index in range(4):
            at = span_of(index, 128)
            total = ins[0][at, :].astype(F32) + ins[1][at, :].astype(F32)
            outs[index][0:128, :] = (total + ins[2][at, :].astype(F32)).astype(BF16)
            outs[index][128:144, :] = ins[3][...].astype(BF16)

    attn_parts = combine(
        "step_zero",
        step_zero,
        (near_keep, swap(near_sent, 0), got_attn, tiny),
        (rows(144),) * 4,
        (got_near,),
    )
    got_attn = [swap_four(attn_parts[index], index) for index in range(1, 4)]

    def pool_item(mine, index, held, after, through=()):
        grads = grad_keep if mine else grad_other
        return pool_backward(
            info, meta, positions, byte_states, grads, mine, index, held, after, through
        )

    held = pool_item(True, 0, (), (attn_parts[0],))

    def step_one(ins, outs):
        sum_into(ins[:4], outs[:1])
        sum_into(ins[4:], outs[1:])

    attn, ff_low, ff_high = combine(
        "step_one",
        step_one,
        (attn_parts[0], *got_attn, near_low, got_near, got_far),
        (rows(144), rows(256), rows(256)),
        (held[1],),
    )
    for bit in range(4, bits):
        attn = (attn.astype(F32) + swap(attn, bit).astype(F32)).astype(BF16)
    got_attn, got_ff = swap(attn, 3), swap(ff_high, 2)

    def step_two(ins, outs):
        total = ins[0][...].astype(F32) + ins[1][...].astype(F32)
        outs[0][...] = total[0:128, :].astype(BF16)
        outs[1][...] = total[128:144, :].astype(BF16)
        sum_into(ins[2:], outs[2:])

    held = pool_item(True, 1, held, (attn,))
    attn, tiny, near_ff = combine(
        "step_two",
        step_two,
        (attn, got_attn, ff_low, got_ff),
        (rows(128), rows(16), rows(256)),
        (held[1],),
    )
    got_ff = swap(near_ff, 3)
    got_attn = [swap_four(attn, index) for index in range(1, 4)]
    got_tiny = across(tiny)

    def step_three(ins, outs):
        join_into(ins[:4], outs[0])
        sum_into(ins[4:6], [outs[0].at[512:528, :]])
        sum_into(ins[6:], outs[1:])

    held = pool_item(False, 0, held, (attn,))
    near_attn, near_ff = combine(
        "step_three",
        step_three,
        (attn, *got_attn, tiny, got_tiny, near_ff, got_ff),
        (rows(528), rows(256)),
        (held[1],),
    )
    for bit in range(4, bits):
        near_ff = (near_ff.astype(F32) + swap(near_ff, bit).astype(F32)).astype(BF16)
    got_ff = [swap_four(near_ff, index) for index in range(1, 4)]
    far_attn = swap(near_attn, 0)

    held = pool_item(False, 1, held, (near_attn, near_ff))
    grad_bytes, part = held
    part_other = across(part)
    (
        grad_query,
        grad_key,
        grad_value,
        grad_out,
        grad_frontier,
        grad_gain_attn,
        grad_gain_mlp,
        grad_rel,
        blocks_out,
    ) = finish(
        info,
        near_attn,
        far_attn,
        part,
        part_other,
        positions,
        frontier,
        blocks_kept,
        blocks_other,
        (),
    )

    def join(ins, outs):
        join_into(ins, outs[0])

    (near_ff,) = combine("step_four", join, (near_ff, *got_ff), (rows(1024),), (grad_gain_attn,))
    far_ff = swap(near_ff, 0)
    grad_hidden, grad_mlp, _ = ff_place(
        info, near_ff, far_ff, (w_hidden.shape, w_mlp_out.shape, (8, 128)), ()
    )
    return (
        blocks_out,
        grad_bytes,
        grad_frontier,
        grad_gain_attn.reshape(-1),
        grad_query,
        grad_key,
        grad_value,
        grad_out,
        grad_rel,
        grad_gain_mlp.reshape(-1),
        grad_hidden,
        grad_mlp,
    )


def solution(mesh):
    devices = mesh.shape["dp"]
    split = jax.sharding.Mesh(
        mesh.devices.reshape(devices // 4, 4, mesh.shape["mp"]), ("far", "near", "mp")
    )
    dp = ("far", "near")
    placed = (
        P(dp, None, "mp"),
        P(dp, None),
        P(dp),
        P(),
        P(None, "mp"),
        P(None, "mp"),
        P(None, "mp"),
        P("mp", None),
        P(None, "mp"),
        P(),
        P(None, "mp"),
        P("mp", None),
        P(dp, None, "mp"),
    )
    return jax.shard_map(
        functools.partial(shards, devices),
        mesh=split,
        in_specs=placed,
        out_specs=(
            P(dp, None, "mp"),
            P(dp, None, "mp"),
            P(dp, None),
            P(),
            P(None, "mp"),
            P(None, "mp"),
            P(None, "mp"),
            P("mp", None),
            P(None, "mp"),
            P(),
            P(None, "mp"),
            P("mp", None),
        ),
        check_vma=False,
    )
```

```python
import functools
import math

import jax
import jax.numpy as jnp
import numpy as np
from jax import lax
from jax.experimental import pallas as pl
from jax.experimental.pallas import tpu as pltpu
from jax.sharding import PartitionSpec as P

BUCKETS = 32
REACH = 128
BLOCKS = 512
WRAP = 2 * BLOCKS
SHARDS = 8

EPSILON = 1e-06
SHARPNESS = 2.0
MASKED_SCORE = -1000000000.0
OUTSIDE = -10000.0
REACH_OUT = 8.0
PRECISE = lax.Precision.HIGHEST
ROOT = 0.7978845608028654
CUBIC = 0.044715
VMEM_LIMIT = 24 * 1024 * 1024
VMEM_MOST = 60 * 1024 * 1024
CHUNK = 256
WINDOW = 128
SLOTS = 3

F32 = jnp.float32
BF16 = jnp.bfloat16
ANY = pl.BlockSpec(memory_space=pl.ANY)
HBM = pl.BlockSpec(memory_space=pltpu.HBM)
NEAR = pl.BlockSpec(memory_space=pltpu.VMEM)
SMEM = pl.BlockSpec(memory_space=pltpu.SMEM)
NN = (((1,), (0,)), ((), ()))
NT = (((1,), (1,)), ((), ()))
TN = (((0,), (0,)), ((), ()))


def mm(a, b, dims=NN):
    return lax.dot_general(a, b, dims, preferred_element_type=F32)


def bucket_of(offset):
    half_count = BUCKETS // 2
    exact_count = half_count // 2
    distance = abs(offset)
    if distance < exact_count:
        place = distance
    else:
        place = min(
            half_count - 1,
            exact_count
            + math.floor(
                math.log(distance / exact_count)
                / math.log(REACH / exact_count)
                * (half_count - exact_count)
            ),
        )
    return place + (half_count if offset > 0 else 0)


def offset_tables():
    backward = np.zeros((WRAP, BUCKETS), np.float32)
    collect = np.zeros((WRAP, BUCKETS), np.float32)
    for offset in range(1 - BLOCKS, BLOCKS):
        bucket = bucket_of(offset)
        backward[(-offset) % WRAP, bucket] = 1.0
        collect[(384 - offset) % WRAP, bucket] = 1.0
    collect = np.concatenate([np.roll(collect, turn, axis=0) for turn in range(8)], axis=1)
    return backward.T, collect


def cost(micros):
    return pl.CostEstimate(flops=1, bytes_accessed=1, transcendentals=0)


def whole(shape):
    return pl.BlockSpec(shape, functools.partial(lambda n, i, info: (0,) * n, len(shape)))


def item(shape):
    return pl.BlockSpec(
        (1,) + shape, functools.partial(lambda n, i, info: (i,) + (0,) * n, len(shape))
    )


def launch(
    kernel, name, micros, grid, info, args, in_specs, outs, out_specs, scratch=(), after=(),
    through=(), aliases=None, vmem=VMEM_LIMIT,
):
    given, waits, passed, made = 1 + len(args), len(after), len(through), len(outs)

    def body(*refs):
        first = given + waits + passed
        kernel(*refs[:given], *refs[first : first + made], *refs[first + made + passed :])

    aliases = dict(aliases or {})
    for index in range(passed):
        aliases[given + waits + index] = made + index
    return pl.pallas_call(
        body,
        grid_spec=pltpu.PrefetchScalarGridSpec(
            num_scalar_prefetch=1,
            grid=(grid,),
            in_specs=list(in_specs) + [ANY] * (waits + passed),
            out_specs=list(out_specs) + [ANY] * passed,
            scratch_shapes=list(scratch),
        ),
        out_shape=list(outs) + [jax.ShapeDtypeStruct(x.shape, x.dtype) for x in through],
        input_output_aliases=aliases,
        compiler_params=pltpu.CompilerParams(
            vmem_limit_bytes=vmem, dimension_semantics=("arbitrary",)
        ),
        cost_estimate=cost(micros),
        name=name,
    )(info, *args, *after, *through)


def combine(name, work, args=(), outs=(), after=(), through=()):
    given, held, made, passed = len(args), len(args) + len(after), len(outs), len(through)

    def kernel(*refs):
        work(refs[:given], refs[held + passed : held + passed + made])

    near = pl.BlockSpec(memory_space=pltpu.VMEM)
    return pl.pallas_call(
        kernel,
        in_specs=[near] * given + [ANY] * (len(after) + passed),
        out_specs=[near] * made + [ANY] * passed,
        out_shape=[jax.ShapeDtypeStruct(*out) for out in outs]
        + [jax.ShapeDtypeStruct(x.shape, x.dtype) for x in through],
        input_output_aliases={held + index: made + index for index in range(passed)},
        compiler_params=pltpu.CompilerParams(vmem_limit_bytes=16 * 1024 * 1024),
        cost_estimate=cost(1),
        name=name,
    )(*args, *after, *through)


def nothing(ins, outs):
    pass


def sum_into(ins, outs):
    at = 0
    for out in outs:
        count = min(out.shape[0], ins[0].shape[0] - at)
        rows = slice(at, at + count)
        value = ins[0][rows, :].astype(F32)
        for other in ins[1:]:
            value = value + other[rows, :].astype(F32)
        out[0:count, :] = value.astype(out.dtype)
        if out.shape[0] > count:
            out[count:, :] = jnp.zeros((out.shape[0] - count, out.shape[1]), out.dtype)
        at += count


def join_into(ins, out):
    at = 0
    for source in ins:
        out[at : at + source.shape[0], :] = source[...]
        at += source.shape[0]


def share_out(info):
    lengths = [info[4 + item] for item in range(4)]
    ranks = []
    for item in range(4):
        rank = jnp.int32(0)
        for other in range(4):
            if other != item:
                before = lengths[other] <= lengths[item] if other < item else (
                    lengths[other] < lengths[item]
                )
                rank = rank + jnp.where(before, 1, 0)
        ranks.append(rank)

    def at(wanted):
        found = jnp.int32(0)
        for item in range(1, 4):
            found = jnp.where(ranks[item] == wanted, item, found)
        return found

    sides = ((at(3), at(0)), (at(2), at(1)))
    first = info[0] == 0
    mine = [jnp.where(first, a, b) for a, b in zip(*sides)]
    theirs = [jnp.where(first, b, a) for a, b in zip(*sides)]
    return mine, theirs


def item_count(info, index):
    mine = share_out(info)[0]
    item = mine[index] if isinstance(index, int) else jnp.where(index == 0, mine[0], mine[1])
    return lax.shift_right_logical(info[4 + item] + 3, 2)


def fetch_bytes(bytes_ref, buffer, sems, item, slot):
    return pltpu.make_async_copy(bytes_ref.at[item], buffer.at[slot], sems.at[slot])


def window_kernel(row, first, skipped):
    line = lax.broadcasted_iota(jnp.int32, (WINDOW, CHUNK), 0)
    offset = row - ((line + first).astype(F32) + 0.5)
    kernel = jnp.exp(-SHARPNESS * offset * offset)
    if skipped is not None:
        kernel = jnp.where(line >= skipped, kernel, 0.0)
    return kernel, offset


def chunk_row(pos_ref, item, chunk):
    return pos_ref[pl.ds(item, 1), tile_at(chunk, CHUNK)]


def pool_rows(item, info, meta, pos_ref, buffer, out_ref, acc):
    length = info[4 + item]
    acc[...] = jnp.zeros_like(acc)

    def add(chunk, first, skipped):
        first = pl.multiple_of(first, 16)
        kernel = window_kernel(chunk_row(pos_ref, item, chunk), first, skipped)[0]
        acc[pl.ds(first, WINDOW), :] += mm(
            kernel.astype(BF16), buffer[tile_at(chunk, CHUNK), :]
        )

    def two(pair, carry):
        for chunk in (pair * 2, pair * 2 + 1):
            add(chunk, meta[item, chunk], None)
        for chunk in (pair * 2, pair * 2 + 1):

            @pl.when(meta[4 + item, chunk] > 1)
            def _():
                def more(window, carry):
                    wanted = meta[item, chunk] + window * WINDOW
                    first = jnp.minimum(wanted, BLOCKS - WINDOW)
                    add(chunk, first, wanted - first)
                    return carry

                lax.fori_loop(1, meta[4 + item, chunk], more, 0)

        return carry

    lax.fori_loop(0, lax.div(length + 2 * CHUNK - 1, 2 * CHUNK), two, 0)
    count = lax.shift_right_logical(length + 3, 2)
    live = lax.broadcasted_iota(jnp.int32, acc.shape, 0) < count
    out_ref[...] = jnp.where(live, acc[...], 0.0).astype(BF16)


def find_windows(pos_ref, meta_ref):
    lane = lax.broadcasted_iota(jnp.int32, (4, 128), 1)
    starts = jnp.zeros((4, 128), jnp.int32)
    counts = jnp.ones((4, 128), jnp.int32)
    for chunk in range(pos_ref.shape[1] // CHUNK):
        rows = pos_ref[:, span_of(chunk, CHUNK)]
        low = jnp.min(jnp.where(rows < 0.0, 1e6, rows), axis=1, keepdims=True)
        high = jnp.max(rows, axis=1, keepdims=True)
        start = jnp.clip(low - REACH_OUT, 0.0, float(BLOCKS - WINDOW)).astype(jnp.int32)
        start = lax.shift_left(lax.shift_right_logical(start, 4), 4)
        last = jnp.clip(high + REACH_OUT, 0.0, float(BLOCKS - 1)).astype(jnp.int32)
        count = lax.shift_right_arithmetic(last - start, 7) + 1
        starts = jnp.where(lane == chunk, start, starts)
        counts = jnp.where(lane == chunk, jnp.maximum(count, 1), counts)
    meta_ref[0:4, :] = starts
    meta_ref[4:8, :] = counts


def masked_positions(info, frontier_ref, pos_ref):
    items, byte_count = frontier_ref.shape
    lane = lax.broadcasted_iota(jnp.int32, (items, byte_count), 1)
    row = lax.broadcasted_iota(jnp.int32, (items, byte_count), 0)
    length = jnp.zeros((items, byte_count), jnp.int32)
    for item in range(items):
        length = jnp.where(row == item, info[4 + item], length)
    valid = lane < length
    running = jnp.where(valid, frontier_ref[...], 0.0)
    step = 1
    while step < byte_count:
        running = running + jnp.where(lane >= step, pltpu.roll(running, step, 1), 0.0)
        step *= 2
    count = lax.shift_right_logical(length + 3, 2).astype(F32)
    total = running[:, byte_count - 1 :]
    pos_ref[...] = jnp.where(valid, count * running / total, OUTSIDE)


def pool_own_kernel(
    info, frontier_ref, bytes_ref, out_ref, pos_ref, meta_ref, buffer, acc, meta, sems, meta_sem
):
    mine = share_out(info)[0]
    for slot, item in enumerate(mine):
        fetch_bytes(bytes_ref, buffer, sems, item, slot).start()
    masked_positions(info, frontier_ref, pos_ref)
    find_windows(pos_ref, meta_ref)
    copy = pltpu.make_async_copy(meta_ref, meta, meta_sem)
    copy.start()
    copy.wait()
    for slot, item in enumerate(mine):
        fetch_bytes(bytes_ref, buffer, sems, item, slot).wait()
        pool_rows(item, info, meta, pos_ref, buffer.at[slot], out_ref.at[slot], acc)


def pool_other_kernel(info, meta, pos_ref, bytes_ref, out_ref, buffer, acc, sems):
    theirs = share_out(info)[1]
    out_ref[2 * BLOCKS :, :] = jnp.zeros((64, out_ref.shape[1]), BF16)
    for slot, item in enumerate(theirs):
        fetch_bytes(bytes_ref, buffer, sems, item, slot).start()
    for slot, item in enumerate(theirs):
        fetch_bytes(bytes_ref, buffer, sems, item, slot).wait()
        rows = out_ref.at[span_of(slot, BLOCKS), :]
        pool_rows(item, info, meta, pos_ref, buffer.at[slot], rows, acc)


def pool_forward(info, frontier, byte_states, after):
    items, byte_count, share = byte_states.shape
    half = items // 2
    out = jax.ShapeDtypeStruct((half, BLOCKS, share), BF16)
    pos = jax.ShapeDtypeStruct((items, byte_count), F32)
    windows = jax.ShapeDtypeStruct((8, 128), jnp.int32)
    scratch = [pltpu.VMEM((half, byte_count, share), BF16), pltpu.VMEM((BLOCKS, share), F32)]
    own, positions, meta = launch(
        pool_own_kernel,
        "pool_own",
        7,
        1,
        info,
        (frontier, byte_states),
        [whole(pos.shape), HBM],
        [out, pos, windows],
        [whole(out.shape), whole(pos.shape), whole(windows.shape)],
        scratch
        + [
            pltpu.SMEM((8, 128), jnp.int32),
            pltpu.SemaphoreType.DMA((half,)),
            pltpu.SemaphoreType.DMA,
        ],
        after,
        vmem=VMEM_MOST,
    )
    sent = jax.ShapeDtypeStruct((half * BLOCKS + 64, share), BF16)
    (other,) = launch(
        pool_other_kernel,
        "pool_other",
        7,
        1,
        info,
        (meta, positions, byte_states),
        [SMEM, whole(pos.shape), HBM],
        [sent],
        [whole(sent.shape)],
        scratch + [pltpu.SemaphoreType.DMA((half,))],
        vmem=VMEM_MOST,
    )
    return own, other, positions, meta


def pool_back_kernel(mine, index, info, meta, pos_ref, bytes_ref, grads_ref, *refs):
    out_ref, part_ref, buffer, written, acc, sems, out_sems = refs[-7:]
    item = share_out(info)[0 if mine else 1][index]
    length = info[4 + item]
    grads = grads_ref.at[index] if mine else grads_ref.at[span_of(index, BLOCKS)]
    fetch = fetch_bytes(bytes_ref, buffer, sems, item, 0)
    fetch.start()
    pairs = lax.div(length + 2 * CHUNK - 1, 2 * CHUNK)
    size = 2 * CHUNK

    def written_copy(pair):
        rows = tile_at(pair, size)
        return pltpu.make_async_copy(
            written.at[rows, :], out_ref.at[item, rows, :], out_sems.at[pair]
        )

    def window(chunk, first, skipped):
        first = pl.multiple_of(first, 16)
        kernel, offset = window_kernel(chunk_row(pos_ref, item, chunk), first, skipped)
        rows = grads[pl.ds(first, WINDOW), :]
        slope = mm(rows, buffer[0, tile_at(chunk, CHUNK), :], NT)
        back = mm(kernel.astype(BF16), rows, TN)
        return back, jnp.sum(slope * kernel * offset, axis=0, keepdims=True)

    def two(pair, carry):
        for chunk in (pair * 2, pair * 2 + 1):
            back, terms = window(chunk, meta[item, chunk], None)
            written[tile_at(chunk, CHUNK), :] = back.astype(BF16)
            part_ref[0, :, tile_at(chunk, CHUNK)] = -4.0 * terms
        for chunk in (pair * 2, pair * 2 + 1):

            @pl.when(meta[4 + item, chunk] > 1)
            def _():
                acc[...] = jnp.zeros_like(acc)

                def more(number, total):
                    wanted = meta[item, chunk] + number * WINDOW
                    first = jnp.minimum(wanted, BLOCKS - WINDOW)
                    back, terms = window(chunk, first, wanted - first)
                    acc[...] += back
                    return total + terms

                total = lax.fori_loop(
                    0, meta[4 + item, chunk], more, jnp.zeros((1, CHUNK), F32)
                )
                written[tile_at(chunk, CHUNK), :] = acc[...].astype(BF16)
                part_ref[0, :, tile_at(chunk, CHUNK)] = -4.0 * total

        written_copy(pair).start()
        return carry

    def empty(pair, carry):
        written[tile_at(pair, size), :] = jnp.zeros((size, written.shape[1]), BF16)
        part_ref[0, :, tile_at(pair, size)] = jnp.zeros((1, size), F32)
        written_copy(pair).start()
        return carry

    every = written.shape[0] // size
    lax.fori_loop(pairs, every, empty, 0)
    fetch.wait()
    lax.fori_loop(0, pairs, two, 0)
    for pair in range(every):
        written_copy(pair).wait()


def pool_backward(info, meta, positions, byte_states, grads, mine, index, held, after, through):
    items, byte_count, share = byte_states.shape
    side = 0 if mine else 1
    return launch(
        functools.partial(pool_back_kernel, mine, index),
        "pool_back",
        5,
        1,
        info,
        (meta, positions, byte_states, grads) + tuple(held),
        [SMEM, whole((items, byte_count)), HBM, NEAR] + [HBM] * len(held),
        [
            jax.ShapeDtypeStruct((items, byte_count, share), BF16),
            jax.ShapeDtypeStruct((items, 1, byte_count), F32),
        ],
        [
            HBM,
            pl.BlockSpec((1, 1, byte_count), lambda i, info: (share_out(info)[side][index], 0, 0)),
        ],
        [
            pltpu.VMEM((1, byte_count, share), BF16),
            pltpu.VMEM((byte_count, share), BF16),
            pltpu.VMEM((CHUNK, share), F32),
            pltpu.SemaphoreType.DMA((1,)),
            pltpu.SemaphoreType.DMA((byte_count // (2 * CHUNK),)),
        ],
        after,
        through,
        {5: 0, 6: 1} if held else None,
    )


def frontier_kernel(info, mine_ref, theirs_ref, pos_ref, frontier_ref, out_ref):
    items, byte_count = frontier_ref.shape
    lane = lax.broadcasted_iota(jnp.int32, (items, byte_count), 1)
    row = lax.broadcasted_iota(jnp.int32, (items, byte_count), 0)
    length = jnp.zeros((items, byte_count), jnp.int32)
    for item in range(items):
        length = jnp.where(row == item, info[4 + item], length)
    valid = lane < length
    total = jnp.sum(jnp.where(valid, frontier_ref[...], 0.0), axis=1, keepdims=True)
    terms = jnp.where(valid, mine_ref[:, 0, :] + theirs_ref[:, 0, :], 0.0)
    weighted = jnp.sum(terms * pos_ref[...], axis=1, keepdims=True)
    step = 1
    while step < byte_count:
        moved = pltpu.roll(terms, byte_count - step, 1)
        terms = terms + jnp.where(lane < byte_count - step, moved, 0.0)
        step *= 2
    count = lax.shift_right_logical(length + 3, 2).astype(F32)
    out_ref[...] = jnp.where(valid, (terms * count - weighted) / total, 0.0)


def strips_kernel(info, rel_ref, first_ref, table_ref, strips):
    core = info[1]
    parts = [first_ref[512:528, span_of(index, 128)].astype(F32) for index in range(3)]
    other = (parts[0] + parts[1] + parts[2])[0:4, 0:BUCKETS]
    rows = []
    for values in (rel_ref[...], other):
        turned = jnp.concatenate((values[2:4], values[0:2]), axis=0)
        rows.append(jnp.where(core == 0, values, turned))
    spread = lax.dot_general(
        jnp.concatenate(rows, axis=0),
        table_ref[...],
        NN,
        precision=PRECISE,
        preferred_element_type=F32,
    )
    for head in range(strips.shape[0]):
        row = jnp.broadcast_to(spread[head : head + 1, :], (8, WRAP))
        eight = pltpu.roll(row, 384, 1, stride=1, stride_axis=0)
        for group in range(16):
            turned = pltpu.roll(eight, 8 * group, 1) if group else eight
            strips[head, span_of(group, 8), :] = turned[:, :896]


def bias_strips(info, rel, first, table, after):
    return launch(
        strips_kernel,
        "bias_strips",
        2,
        1,
        info,
        (rel, first, table),
        [NEAR, NEAR, NEAR],
        [jax.ShapeDtypeStruct((8, 128, 896), F32)],
        [NEAR],
        (),
        after,
    )[0]


def gather_halves(info, target, own_ref, other_ref):
    target[:, tile_at(info[0], 256)] = own_ref[0]
    target[:, tile_at(1 - info[0], 256)] = other_ref[...]


def span_of(index, size):
    return slice(index * size, (index + 1) * size)


def tile_at(index, size):
    return pl.ds(pl.multiple_of(index * size, size), size)


def started(pairs, sems):
    return [
        pltpu.make_async_copy(source, target, sems.at[index])
        for index, (source, target) in enumerate(pairs)
    ]


def inverse_rms(values):
    return lax.rsqrt(jnp.mean(values * values, axis=1, keepdims=True) + EPSILON)


def triple(values):
    high = values.astype(BF16)
    rest = values - high.astype(F32)
    middle = rest.astype(BF16)
    return high, middle, (rest - middle.astype(F32)).astype(BF16)


def spare_lane(head):
    return (head // 2) * 4 + 64 * (1 - head % 2)


def strip_tiles(strips, head, half):
    return jnp.concatenate(
        [
            strips[head, :, (3 - tile) * 128 + half * 256 : (5 - tile) * 128 + half * 256]
            for tile in range(4)
        ],
        axis=0,
    )


def parts_by_lane(values, lead):
    spot = lax.broadcasted_iota(jnp.int32, values.shape, 1) & 3
    parts = [part.astype(F32) for part in triple(values)]
    found = jnp.where(spot == 1, parts[0], jnp.where(spot == 2, parts[1], parts[2]))
    return jnp.where(spot == 0, lead, found).astype(BF16)


def attention_kernel(
    info,
    own_ref,
    other_ref,
    strips,
    gain_attn_ref,
    gain_mlp_ref,
    w_query,
    w_key,
    w_value,
    w_out,
    part_a,
    part_b,
    part_c,
    part_d,
    qkv_ref,
    log_ref,
    att_ref,
    middle_ref,
    normed_ref,
    w_qkv,
    w_o,
    pooled,
    logs,
    scores,
):
    step = pl.program_id(0)
    mp, core, way = info[0], info[1], info[2]
    count = item_count(info, step)

    @pl.when(step == 0)
    def _():
        for part in range(2):
            start = core if part == 0 else 1 - core
            for index, weight in enumerate((w_query, w_key, w_value)):
                first = index * 512 + part * 128
                w_qkv[:, first : first + 128] = weight[:, tile_at(start, 128)]
            w_o[span_of(part, 128), :] = w_out[tile_at(start, 128), :]
        for part, sources in enumerate(((part_a, part_b), (part_c, part_d))):
            for side, source in enumerate(sources):
                turn = way if side == 0 else 1 - way
                for index in range(3):
                    first = index * 512 + 256 + part * 128
                    w_qkv[tile_at(turn, 256), first : first + 128] = source[
                        0:256, span_of(index, 128)
                    ]
                rows = pl.ds(pl.multiple_of(256 + part * 128 + turn * 64, 64), 64)
                for lane in range(4):
                    w_o[rows, span_of(lane, 128)] = source[span_of(lane, 64), 384:512]
        logs[...] = jnp.zeros_like(logs)

    gather_halves(info, pooled, own_ref, other_ref)
    wide = pooled[...].astype(F32)
    normed = (wide * inverse_rms(wide) * gain_attn_ref[...]).astype(BF16)
    qkv_ref[0] = mm(normed, w_qkv[...]).astype(BF16)
    lane = lax.broadcasted_iota(jnp.int32, (BLOCKS, 128), 1)
    row = lax.broadcasted_iota(jnp.int32, (BLOCKS, 128), 0)
    dead = jnp.where(row < count, 0.0, MASKED_SCORE).astype(BF16)

    ready, found, tops = {}, {}, {}

    def prepare(pair):
        queries = qkv_ref[0, :, span_of(pair, 128)]
        keys = qkv_ref[0, :, span_of(pair + 4, 128)]
        values = qkv_ref[0, :, span_of(pair + 8, 128)]
        for side in range(2):
            own = (lane < 64) == (side == 0)
            spare = lane == 64 * (1 - side)
            chosen = jnp.where(own, queries, jnp.where(spare, 1.0, 0.0).astype(BF16))
            masked = jnp.where(spare, dead, keys)
            summing = jnp.transpose(jnp.where(own, values, jnp.ones_like(values)))
            ready[pair, side] = (chosen, masked, summing)

    def first_pass(slot, pair, half, side):
        chosen, masked, _ = ready[pair, side]
        held = scores.at[slot]
        raw = mm(masked, chosen[span_of(half, 256), :], NT)
        most = None
        for tile in range(4):
            first = (3 - tile) * 128 + half * 256
            part = raw[span_of(tile, 128), :] + strips[pair * 2 + side, :, first : first + 256]
            held[span_of(tile, 128), :] = part
            part = jnp.max(part.reshape(16, 8, 256), axis=0)
            most = part if most is None else jnp.maximum(most, part)
        tops[slot] = jnp.max(most, axis=0, keepdims=True)

    def second_pass(slot, pair, half, side):
        held = scores.at[slot]
        most = tops[slot]
        expo = jnp.concatenate(
            [jnp.exp(held[span_of(tile, 128), :] - most).astype(BF16) for tile in range(4)],
            axis=0,
        )
        out = mm(ready[pair, side][2], expo)
        other = 64 * (1 - side)
        total = out[other : other + 1, :]
        found[side] = (out * (1.0 / total))[64 * side : 64 * side + 64, :]
        place = pair * 4 + other
        logs[place : place + 4, span_of(half, 256)] = jnp.broadcast_to(
            most + jnp.log(total), (4, 256)
        )
        if side == 1:
            both = jnp.concatenate((found[0], found[1]), axis=0).astype(BF16)
            att_ref[0, span_of(half, 256), span_of(pair, 128)] = jnp.transpose(both)

    chains = [(pair, half, side) for pair in range(4) for half in range(2) for side in range(2)]
    for index, chain in enumerate(chains):
        if index % 4 == 0:
            prepare(chain[0])
        first_pass(index % SLOTS, *chain)
        if index >= SLOTS - 1:
            last = index - SLOTS + 1
            second_pass(last % SLOTS, *chains[last])
    for last in range(len(chains) - SLOTS + 1, len(chains)):
        second_pass(last % SLOTS, *chains[last])
    log_ref[0] = parts_by_lane(-jnp.transpose(logs[...]), 1.0)

    mid = wide + mm(att_ref[0], w_o[...])
    middle_ref[0] = mid
    normed_ref[0] = (mid * inverse_rms(mid) * gain_mlp_ref[...]).astype(BF16)


def attention_forward(info, own, other, strips, gain_attn, gain_mlp, weights, parts, after):
    half = own.shape[0]
    return launch(
        attention_kernel,
        "attention_forward",
        20,
        half,
        info,
        (own, other, strips, gain_attn, gain_mlp, *weights, *parts),
        [
            item((BLOCKS, 256)),
            pl.BlockSpec((BLOCKS, 256), lambda i, info: (i, 0)),
            NEAR,
            whole((1, 512)),
            whole((1, 512)),
        ]
        + [NEAR] * 8,
        [
            jax.ShapeDtypeStruct((half, BLOCKS, 1536), BF16),
            jax.ShapeDtypeStruct((half, BLOCKS, 128), BF16),
            jax.ShapeDtypeStruct((half, BLOCKS, 512), BF16),
            jax.ShapeDtypeStruct((half, BLOCKS, 512), F32),
            jax.ShapeDtypeStruct((half, BLOCKS, 512), BF16),
            jax.ShapeDtypeStruct((512, 1536), BF16),
            jax.ShapeDtypeStruct((512, 512), BF16),
        ],
        [
            item((BLOCKS, 1536)),
            item((BLOCKS, 128)),
            item((BLOCKS, 512)),
            item((BLOCKS, 512)),
            item((BLOCKS, 512)),
            whole((512, 1536)),
            whole((512, 512)),
        ],
        [
            pltpu.VMEM((BLOCKS, 512), BF16),
            pltpu.VMEM((128, BLOCKS), F32),
            pltpu.VMEM((SLOTS, BLOCKS, 256), F32),
        ],
        after,
    )


def gelu_and_slope(pre):
    square = pre * pre
    tanh = jnp.tanh(pre * (ROOT + (ROOT * CUBIC) * square))
    up = 0.5 + 0.5 * tanh
    act = pre * up
    slope = up + act * (1.0 - up) * (2.0 * ROOT + (6.0 * ROOT * CUBIC) * square)
    return act, slope


def ff_piece(normed, turned, top, turned_top, hid, mid, acts, grads, result, back, start):
    for half in range(2):
        rows = span_of(half, BLOCKS)
        act, slope = gelu_and_slope(mm(normed[rows, :], hid))
        acts[rows, :] = act.astype(BF16)
        grads[rows, :] = (mm(top[rows, :], mid, NT) * slope).astype(BF16)
        new_result = mm(acts[rows, :], mid)
        new_back = mm(grads[rows, :], hid, NT)
        if start is None:
            result[rows, :] += new_result
            back[rows, :] += new_back
        elif start:
            result[rows, :] = start[0][rows, :] + new_result
            back[rows, :] = start[1][rows, :] + new_back
        else:
            result[rows, :] = new_result
            back[rows, :] = new_back
    return mm(turned[...], grads[...]), mm(turned_top[...], acts[...])


def store_shards(place, target, first, values):
    rows = values.shape[0] // SHARDS
    size = target.shape[0] // SHARDS
    for shard in range(SHARDS):
        at = pl.multiple_of(lax.bitwise_xor(place, shard) * size + first, 64)
        target[pl.ds(at, rows), :] = values[span_of(shard, rows), :].astype(BF16)


def gather_top(info, top, turned_top, cot_own_ref, cot_other_ref):
    for index in range(2):
        rows = span_of(index, BLOCKS)
        count = item_count(info, index)
        live = lax.broadcasted_iota(jnp.int32, (BLOCKS, 256), 0) < count
        zero = jnp.zeros((BLOCKS, 256), BF16)
        top[rows, tile_at(info[0], 256)] = jnp.where(live, cot_own_ref[index], zero)
        top[rows, tile_at(1 - info[0], 256)] = jnp.where(live, cot_other_ref[index], zero)
        turned_top[:, rows] = jnp.transpose(top[rows, :])


def ff_own_kernel(
    info,
    normed_ref,
    cot_own_ref,
    cot_other_ref,
    w_hidden,
    w_mlp,
    result,
    back,
    keep_ref,
    send_ref,
    mark,
    top,
    turned_top,
    turned,
    acts,
    grads,
):
    core, place = info[1], info[3]
    mark[...] = jnp.zeros_like(mark)
    gather_top(info, top, turned_top, cot_own_ref, cot_other_ref)
    for index in range(2):
        turned[:, span_of(index, BLOCKS)] = jnp.transpose(normed_ref[span_of(index, BLOCKS), :])
    for part, target in ((1, send_ref), (0, keep_ref)):
        start = core if part == 0 else 1 - core
        grad_hid, grad_mid = ff_piece(
            normed_ref,
            turned,
            top,
            turned_top,
            w_hidden[:, tile_at(start, 512)],
            w_mlp[tile_at(start, 512), :],
            acts,
            grads,
            result,
            back,
            () if part == 1 else None,
        )
        store_shards(place, target, 0, grad_hid)
        store_shards(place, target, 64, grad_mid)


def ff_other_kernel(
    info,
    normed_ref,
    cot_own_ref,
    cot_other_ref,
    hid_a,
    hid_b,
    hid_c,
    hid_d,
    mid_near,
    mid_far,
    result_ref,
    back_ref,
    middle_ref,
    gain_ref,
    blocks_keep,
    blocks_send,
    grad_mid_ref,
    keep_ref,
    send_ref,
    gain_out,
    top,
    turned_top,
    turned,
    acts,
    grads,
    weights,
    result,
    back,
    blocks,
):
    mp, way, place = info[0], info[2], info[3]
    for part, sources in ((1, (hid_c, hid_d)), (0, (hid_a, hid_b))):
        for side, source in enumerate(sources):
            turn = way if side == 0 else 1 - way
            weights[part, tile_at(turn, 256), :] = source[256:512, :]
    gather_top(info, top, turned_top, cot_own_ref, cot_other_ref)
    for index in range(2):
        turned[:, span_of(index, BLOCKS)] = jnp.transpose(normed_ref[span_of(index, BLOCKS), :])
    for part, target in ((1, send_ref), (0, keep_ref)):
        grad_hid, grad_mid = ff_piece(
            normed_ref,
            turned,
            top,
            turned_top,
            weights[part],
            (mid_far if part == 1 else mid_near)[...],
            acts,
            grads,
            result,
            back,
            (result_ref, back_ref) if part == 1 else None,
        )
        store_shards(place, target, 0, grad_hid)
        store_shards(place, target, 64, grad_mid)

    new_gain = jnp.zeros((1, 512), F32)
    for index in range(2):
        rows = span_of(index, BLOCKS)
        count = item_count(info, index)
        live = lax.broadcasted_iota(jnp.int32, (BLOCKS, 1), 0) < count
        middle = middle_ref[rows, :]
        blocks[...] = jnp.where(live, middle + result[rows, :], 0.0).astype(BF16)
        blocks_keep[index] = blocks[:, tile_at(mp, 256)]
        blocks_send[index] = blocks[:, tile_at(1 - mp, 256)]
        scale = inverse_rms(middle)
        unit = middle * scale
        grad_normed = back[rows, :]
        scaled = grad_normed * gain_ref[...]
        grad_mid_ref[rows, :] = top[rows, :].astype(F32) + scale * (
            scaled - unit * jnp.mean(scaled * unit, axis=1, keepdims=True)
        )
        new_gain = new_gain + jnp.sum(grad_normed * unit, axis=0, keepdims=True)
    gain_out[...] = jnp.broadcast_to(new_gain, gain_out.shape)


def ff_call(info, normed, cot, cot_other, mine, given, after):
    rows = normed.shape[0]
    half = rows // BLOCKS
    packed = (SHARDS * 128, 512)
    wide = jax.ShapeDtypeStruct((rows, 512), F32)
    pack = jax.ShapeDtypeStruct(packed, BF16)
    share = jax.ShapeDtypeStruct((half, BLOCKS, 256), BF16)
    in_specs = [whole((rows, 512)), whole(share.shape), whole(share.shape)]
    scratch = [
        pltpu.VMEM((rows, 512), BF16),
        pltpu.VMEM((512, rows), BF16),
        pltpu.VMEM((512, rows), BF16),
        pltpu.VMEM((rows, 512), BF16),
        pltpu.VMEM((rows, 512), BF16),
    ]
    if mine:
        in_specs += [NEAR] * 2
        outs = [wide, wide, pack, pack, jax.ShapeDtypeStruct((8, 128), F32)]
    else:
        in_specs += [NEAR] * 8 + [whole((rows, 512)), whole((1, 512))]
        outs = [share, share, wide, pack, pack, jax.ShapeDtypeStruct((8, 512), F32)]
        scratch += [
            pltpu.VMEM((2, 512, 512), BF16),
            pltpu.VMEM((rows, 512), F32),
            pltpu.VMEM((rows, 512), F32),
            pltpu.VMEM((BLOCKS, 512), BF16),
        ]
    return launch(
        ff_own_kernel if mine else ff_other_kernel,
        "ff_own" if mine else "ff_other",
        12,
        1,
        info,
        (normed, cot, cot_other, *given),
        in_specs,
        outs,
        [whole(x.shape) for x in outs],
        scratch,
        after,
    )


def attention_back_body(
    info,
    first_head,
    own_ref,
    other_ref,
    query_ref,
    key_ref,
    value_ref,
    log_ref,
    att_ref,
    grad_mid_ref,
    strips,
    collect_ref,
    gain_attn_ref,
    wq_ref,
    wk_ref,
    wv_ref,
    wo_ref,
    keep_ref,
    send_ref,
    pooled,
    outer,
    grads,
    sums,
    turned,
    turned_branch,
    atts,
    probs,
    weights,
    scored,
):
    step = pl.program_id(0)
    mp, place = info[0], info[3]
    count = item_count(info, step)

    @pl.when(step == 0)
    def _():
        sums[...] = jnp.zeros_like(sums)

    gather_halves(info, pooled, own_ref, other_ref)
    here = tile_at(step, BLOCKS)
    branch = grad_mid_ref[0].astype(BF16)
    outer[...] = mm(branch, wo_ref[...], NT).astype(BF16)
    lane = lax.broadcasted_iota(jnp.int32, (BLOCKS, 128), 1)
    row = lax.broadcasted_iota(jnp.int32, (BLOCKS, 128), 0)
    dead = jnp.where(row < count, 0.0, MASKED_SCORE).astype(BF16)
    line = lax.broadcasted_iota(jnp.int32, (1, 128), 1)
    deltas = jnp.zeros((BLOCKS, 128), F32)
    for pair in range(2):
        span = span_of(pair, 128)
        overlap = outer[:, span].astype(F32) * att_ref[0, :, span].astype(F32)
        for side in range(2):
            own = (lane < 64) == (side == 0)
            delta = jnp.sum(jnp.where(own, overlap, 0.0), axis=1, keepdims=True)
            spare = spare_lane(first_head + pair * 2 + side)
            mine = jnp.logical_and(lane >= spare, lane < spare + 4)
            deltas = jnp.where(mine, delta, deltas)
    deltas = parts_by_lane(-deltas, 0.0)

    ready, found = {}, {}

    def prepare(pair):
        span = span_of(pair, 128)
        queries = query_ref[0, :, span]
        keys = key_ref[0, :, span]
        values = value_ref[0, :, span]
        out_grads = outer[:, span]
        ready[pair] = jnp.transpose(keys)
        for side in range(2):
            own = (lane < 64) == (side == 0)
            spare = spare_lane(first_head + pair * 2 + side)
            added = jnp.logical_and(line > spare, line < spare + 4)
            ones = jnp.where(added, 1.0, 0.0).astype(BF16)
            chosen = jnp.where(own, queries, log_ref[0])
            masked = jnp.where(own, keys, jnp.where(lane == spare, dead, ones))
            drawn = jnp.where(own, out_grads, deltas)
            weighed = jnp.where(own, values, ones)
            ready[pair, side] = (chosen, masked, drawn, weighed)

    def first_pass(slot, pair, side, half):
        chosen, masked, _, _ = ready[pair, side]
        raw = mm(masked, chosen[span_of(half, 256), :], NT)
        for tile in range(4):
            first = (3 - tile) * 128 + half * 256
            rows = span_of(tile, 128)
            part = jnp.exp(
                raw[rows, :] + strips[first_head + pair * 2 + side, :, first : first + 256]
            )
            probs[slot, rows, :] = part
            weights[slot, rows, :] = part.astype(BF16)

    def second_pass(slot, pair, side, half):
        _, _, drawn, weighed = ready[pair, side]
        head = pair * 2 + side
        slope = mm(weighed, drawn[span_of(half, 256), :], NT)
        product = [probs[slot, span_of(tile, 128), :] * slope[span_of(tile, 128), :] for tile in range(4)]
        for tile in range(4):
            scored[slot, span_of(tile, 128), :] = product[tile].astype(BF16)
        for diagonal in range(5):
            first = (3 - diagonal + 1) * 128 + half * 256
            total = None
            for tile in range(4):
                column = tile - diagonal + 1
                if 0 <= column < 2:
                    block = product[tile][:, span_of(column, 128)]
                    total = block if total is None else total + block
            sums[head, :, first : first + 128] += total

    def third_pass(slot, pair, side, half):
        span = span_of(pair, 128)
        rows = span_of(half, 256)
        turned_query = mm(ready[pair], scored[slot])
        grad_key = mm(scored[slot], query_ref[0, rows, span])
        grad_value = mm(weights[slot], outer[rows, span])
        if half == 0:
            found[side] = ([turned_query], grad_key, grad_value)
        else:
            before = found[side]
            found[side] = (
                before[0] + [turned_query],
                before[1] + grad_key,
                before[2] + grad_value,
            )
        if side == 1 and half == 1:
            for index in range(2):
                both = jnp.concatenate(
                    (found[0][0][index][0:64, :], found[1][0][index][64:128, :]), axis=0
                ).astype(BF16)
                grads[
                    pl.ds(pl.multiple_of(step * BLOCKS + index * 256, 256), 256), span
                ] = jnp.transpose(both)
            for index in range(1, 3):
                first = index * 256 + pair * 128
                grads[here, first : first + 128] = jnp.where(
                    lane < 64, found[0][index], found[1][index]
                ).astype(BF16)

    units = [(pair, side, half) for pair in range(2) for side in range(2) for half in range(2)]
    for index in range(len(units) + 2):
        if index < len(units):
            if index % 4 == 0:
                prepare(units[index][0])
            first_pass(index % 4, *units[index])
        if 1 <= index <= len(units):
            second_pass((index - 1) % 4, *units[index - 1])
        if index >= 2:
            third_pass((index - 2) % 4, *units[index - 2])

    wide = pooled[...].astype(F32)
    scale = inverse_rms(wide)
    unit = wide * scale
    normed = (unit * gain_attn_ref[...]).astype(BF16)
    turned[:, here] = jnp.transpose(normed)
    turned_branch[:, here] = jnp.transpose(branch)
    atts[here, :] = att_ref[0]

    @pl.when(step == 1)
    def _():
        new = mm(turned[...], grads[...])
        new_out = mm(turned_branch[...], atts[...])
        for part, target in ((1, send_ref), (0, keep_ref)):
            for shard in range(SHARDS):
                at = tile_at(lax.bitwise_xor(place, shard), 64)
                here_rows = span_of(shard, 64)
                for index in range(3):
                    first = index * 256 + part * 128
                    target[at, span_of(index, 128)] = new[here_rows, first : first + 128].astype(
                        BF16
                    )
                target[at, 384:512] = new_out[here_rows, span_of(part, 128)].astype(BF16)

    grad_normed = (
        mm(grads[here, 0:256], wq_ref[...], NT)
        + mm(grads[here, 256:512], wk_ref[...], NT)
        + mm(grads[here, 512:768], wv_ref[...], NT)
    )
    return unit, scale, grad_normed


def fold_bias(sums, collect_ref):
    rows = []
    for head in range(4):
        folded = jnp.concatenate((sums[head], jnp.zeros((128, 128), F32)), axis=1)
        size = 64
        while size >= 8:
            folded = folded[:size] + pltpu.roll(folded[size : 2 * size], WRAP - size, 1)
            size //= 2
        rows.append(folded)
    lines = jnp.concatenate(triple(jnp.concatenate(rows, axis=0)), axis=0)
    found = mm(lines, collect_ref[...])
    found = found[0:32] + found[32:64] + found[64:96]
    row = lax.broadcasted_iota(jnp.int32, found.shape, 0) & 7
    spot = lax.shift_right_logical(lax.broadcasted_iota(jnp.int32, found.shape, 1), 5)
    found = jnp.where(row == spot, found, 0.0)
    rows = []
    for head in range(4):
        total = jnp.sum(found[span_of(head, 8), :], axis=0, keepdims=True)
        total = total[:, 0:128] + total[:, 128:256]
        total = total + pltpu.roll(total, 64, 1)
        rows.append(total + pltpu.roll(total, 32, 1))
    return jnp.concatenate(rows + rows, axis=0)


def attention_back_first_kernel(info, *refs):
    heads, (grad_ref, keep_ref, send_ref, rel_ref), scratch = refs[:15], refs[15:19], refs[19:]
    _, _, grad_normed = attention_back_body(info, 4, *heads, keep_ref, send_ref, *scratch)
    grad_ref[0] = grad_normed

    @pl.when(pl.program_id(0) == 1)
    def _():
        rel_ref[...] = fold_bias(scratch[3], heads[9])


def attention_back_second_kernel(info, *refs):
    heads, (held_ref, rel_ref, gain_mid_ref), refs = refs[:15], refs[15:18], refs[18:]
    (keep_rows, send_rows, keep_ref, send_ref, tiny_ref), scratch = refs[:5], refs[5:]
    scratch, acc_gain = scratch[:-1], scratch[-1]
    unit, scale, grad_normed = attention_back_body(info, 0, *heads, keep_ref, send_ref, *scratch)
    mp, core = info[0], info[1]
    step = pl.program_id(0)
    pooled = scratch[0]
    grad_normed = grad_normed + held_ref[0]
    scaled = grad_normed * heads[10][...]
    grad_pooled = heads[7][0] + scale * (
        scaled - unit * jnp.mean(scaled * unit, axis=1, keepdims=True)
    )
    pooled[...] = grad_pooled.astype(BF16)
    keep_rows[0] = pooled[:, tile_at(mp, 256)]
    send_rows[tile_at(step, BLOCKS), :] = pooled[:, tile_at(1 - mp, 256)]
    new_gain = jnp.sum(grad_normed * unit, axis=0, keepdims=True)

    @pl.when(step == 0)
    def _():
        acc_gain[...] = jnp.broadcast_to(new_gain, acc_gain.shape)

    @pl.when(step == 1)
    def _():
        found = fold_bias(scratch[3], heads[9])
        line = lax.broadcasted_iota(jnp.int32, (8, 128), 0)
        rows = jnp.zeros((8, 128), F32)
        for head in range(8):
            source = found if head < 4 else rel_ref[...]
            true_head = (
                lax.bitwise_xor(mp, head // 4) * 4
                + lax.bitwise_xor(core, (head // 2) % 2) * 2
                + head % 2
            )
            rows = jnp.where(line == true_head, source[head % 4 : head % 4 + 1, :], rows)
        tiny_ref[...] = jnp.zeros_like(tiny_ref)
        tiny_ref[0:1, :] = acc_gain[0:1, :] + new_gain
        tiny_ref[1:2, :] = gain_mid_ref[0:1, :]
        tiny_ref[8:16, 0:128] = rows


def attention_back(
    info, mine, rows_args, strips, collect, gain_attn, joined, w_o, given, after
):
    own, other, qkv, logs, att, grad_mid = rows_args
    half = own.shape[0]
    where = 0 if mine else 1

    def lanes(index):
        return pl.BlockSpec((1, BLOCKS, 256), lambda i, info: (i, 0, index))

    def columns(index):
        return pl.BlockSpec((512, 256), lambda i, info: (0, index))

    in_specs = [
        item((BLOCKS, 256)),
        pl.BlockSpec((BLOCKS, 256), lambda i, info: (i, 0)),
        lanes(where),
        lanes(2 + where),
        lanes(4 + where),
        item((BLOCKS, 128)),
        lanes(where),
        item((BLOCKS, 512)),
        NEAR,
        whole((WRAP, 256)),
        whole((1, 512)),
        columns(where),
        columns(2 + where),
        columns(4 + where),
        pl.BlockSpec((256, 512), lambda i, info: (where, 0)),
    ]
    args = [own, other, qkv, qkv, qkv, logs, att, grad_mid, strips, collect, gain_attn]
    args += [joined, joined, joined, w_o]
    packed = (SHARDS * 64, 512)
    pack = jax.ShapeDtypeStruct(packed, BF16)
    scratch = [
        pltpu.VMEM((BLOCKS, 512), BF16),
        pltpu.VMEM((BLOCKS, 256), BF16),
        pltpu.VMEM((half * BLOCKS, 768), BF16),
        pltpu.VMEM((4, 128, 896), F32),
        pltpu.VMEM((512, half * BLOCKS), BF16),
        pltpu.VMEM((512, half * BLOCKS), BF16),
        pltpu.VMEM((half * BLOCKS, 256), BF16),
        pltpu.VMEM((4, BLOCKS, 256), F32),
        pltpu.VMEM((4, BLOCKS, 256), BF16),
        pltpu.VMEM((4, BLOCKS, 256), BF16),
    ]
    if mine:
        share = jax.ShapeDtypeStruct((half, BLOCKS, 256), BF16)
        in_specs += [item((BLOCKS, 512)), whole((8, 128)), whole((8, 512))]
        sent = jax.ShapeDtypeStruct((half * BLOCKS, 256), BF16)
        outs = [share, sent, pack, pack, jax.ShapeDtypeStruct((16, 512), F32)]
        out_specs = [item((BLOCKS, 256)), whole(sent.shape), whole(packed), whole(packed)]
        out_specs += [whole((16, 512))]
        scratch += [pltpu.VMEM((8, 512), F32)]
    else:
        outs = [
            jax.ShapeDtypeStruct((half, BLOCKS, 512), F32),
            pack,
            pack,
            jax.ShapeDtypeStruct((8, 128), F32),
        ]
        out_specs = [item((BLOCKS, 512)), whole(packed), whole(packed), whole((8, 128))]
    return launch(
        attention_back_second_kernel if mine else attention_back_first_kernel,
        "attention_back_own" if mine else "attention_back_other",
        17,
        half,
        info,
        (*args, *given),
        in_specs,
        outs,
        out_specs,
        scratch,
        after,
    )


def place_kernel(info, ff_near, ff_far, hid_ref, mid_ref, mark):
    mark[...] = jnp.zeros_like(mark)
    core, place = info[1], info[3]
    for source, side in ((ff_near, core), (ff_far, 1 - core)):
        turned = []
        for shard in range(SHARDS):
            at = lax.bitwise_xor(place, shard)
            at = at * 2
            hid_ref[span_of(shard, 64), tile_at(side, 512)] = source[tile_at(at, 64), :].astype(F32)
            turned.append(source[tile_at(at + 1, 64), :])
        mid_ref[tile_at(side, 512), :] = jnp.transpose(
            jnp.concatenate(turned, axis=0).astype(F32)
        )


def pack_kernel(wq, wk, wv, wo, wh, rel, out, sems):
    near = lax.axis_index("near")
    core, way = lax.rem(near, 2), lax.div(near, 2)
    rows = tile_at(way, 256)
    pairs = []
    for index, weight in enumerate((wq, wk, wv)):
        lanes = pl.ds(index * 128, 128)
        pairs.append((weight.at[rows, tile_at(core, 128)], out.at[pl.ds(0, 256), lanes]))
    few = pl.ds(pl.multiple_of(core * 128 + way * 64, 64), 64)
    for lane in range(4):
        pairs.append(
            (
                wo.at[few, pl.ds(lane * 128, 128)],
                out.at[pl.ds(lane * 64, 64), pl.ds(384, 128)],
            )
        )
    pairs.append((wh.at[rows, tile_at(core, 512)], out.at[pl.ds(256, 256), :]))
    copies = started(pairs, sems)
    for copy in copies:
        copy.start()
    out[512:528, :] = jnp.zeros((16, 512), BF16)
    for index, part in enumerate(triple(rel[...])):
        out[512:516, index * 128 : index * 128 + BUCKETS] = part
    for copy in copies:
        copy.wait()


def pack(weights, rel):
    return pl.pallas_call(
        pack_kernel,
        grid=(1,),
        in_specs=[HBM] * 5 + [pl.BlockSpec(rel.shape, lambda i: (0, 0))],
        out_specs=pl.BlockSpec((528, 512), lambda i: (0, 0)),
        out_shape=jax.ShapeDtypeStruct((528, 512), BF16),
        scratch_shapes=[pltpu.SemaphoreType.DMA((8,))],
        compiler_params=pltpu.CompilerParams(
            vmem_limit_bytes=VMEM_MOST, dimension_semantics=("arbitrary",)
        ),
        cost_estimate=cost(1),
        name="pack",
    )(*weights[:5], rel)


def pack_more_kernel(info, wm, cot, mid_out, cot_out, cot_own, sems):
    mine, theirs = share_out(info)
    pairs = [(wm.at[tile_at(info[1], 512), :], mid_out)]
    for index in range(2):
        pairs.append((cot.at[theirs[index]], cot_out.at[index, pl.ds(0, BLOCKS), :]))
        pairs.append((cot.at[mine[index]], cot_own.at[index]))
    copies = started(pairs, sems)
    for copy in copies:
        copy.start()
    cot_out[:, BLOCKS:, :] = jnp.zeros((2, 32, cot_out.shape[2]), BF16)
    for copy in copies:
        copy.wait()


def pack_more(info, w_mlp, cotangent, after):
    half, share = cotangent.shape[0] // 2, cotangent.shape[2]
    outs = [jax.ShapeDtypeStruct((512, 512), BF16)]
    outs += [jax.ShapeDtypeStruct((half, rows, share), BF16) for rows in (BLOCKS + 32, BLOCKS)]
    return launch(
        pack_more_kernel,
        "pack_more",
        1,
        1,
        info,
        (w_mlp, cotangent),
        [HBM] * 2,
        outs,
        [whole(x.shape) for x in outs],
        [pltpu.SemaphoreType.DMA((5,))],
        after,
        vmem=VMEM_MOST,
    )


def final_kernel(
    info,
    near,
    far,
    mine_ref,
    theirs_ref,
    pos_ref,
    frontier_ref,
    blocks_kept,
    blocks_got,
    query_ref,
    key_ref,
    value_ref,
    out_ref,
    front_ref,
    gain_attn_ref,
    gain_mlp_ref,
    rel_ref,
    blocks_ref,
    sems,
):
    mp, core, place = info[0], info[1], info[3]
    pairs = []
    mine, theirs = share_out(info)
    for index in range(2):
        pairs.append((blocks_kept.at[index], blocks_ref.at[mine[index]]))
        pairs.append((blocks_got.at[index], blocks_ref.at[theirs[index]]))
    copies = started(pairs, sems)
    for copy in copies:
        copy.start()
    for source, side in ((near, core), (far, 1 - core)):
        turned = []
        for shard in range(SHARDS):
            at = tile_at(lax.bitwise_xor(place, shard), 64)
            for index, target in enumerate((query_ref, key_ref, value_ref)):
                target[span_of(shard, 64), tile_at(side, 128)] = source[
                    at, span_of(index, 128)
                ].astype(F32)
            turned.append(source[at, 384:512])
        out_ref[tile_at(side, 128), :] = jnp.transpose(
            jnp.concatenate(turned, axis=0).astype(F32)
        )
    tiny = near[512:528, :].astype(F32) + far[512:528, :].astype(F32)
    gain_attn_ref[...] = tiny[0:1, :]
    gain_mlp_ref[...] = tiny[1:2, :]
    heads = jnp.where(mp == 0, tiny[8:12, 0:128], tiny[12:16, 0:128])
    rel_ref[...] = heads[:, 0:BUCKETS]
    frontier_kernel(info, mine_ref, theirs_ref, pos_ref, frontier_ref, front_ref)
    for copy in copies:
        copy.wait()


def finish(
    info, near, far, mine, theirs, positions, frontier, blocks_kept, blocks_got, after
):
    args = (near, far, mine, theirs, positions, frontier)
    square = jax.ShapeDtypeStruct((512, 256), F32)
    row = jax.ShapeDtypeStruct((1, 512), F32)
    outs = [square, square, square, jax.ShapeDtypeStruct((256, 512), F32)]
    outs += [jax.ShapeDtypeStruct(frontier.shape, F32), row, row]
    outs += [jax.ShapeDtypeStruct((4, BUCKETS), F32)]
    return launch(
        final_kernel,
        "finish",
        4,
        1,
        info,
        (*args, blocks_kept, blocks_got),
        [whole(x.shape) for x in args] + [ANY] * 2,
        outs + [jax.ShapeDtypeStruct((4,) + blocks_kept.shape[1:], BF16)],
        [whole(x.shape) for x in outs] + [HBM],
        [pltpu.SemaphoreType.DMA((4,))],
        after,
    )


def ff_place(info, near, far, shapes, after):
    return launch(
        place_kernel,
        "ff_place",
        4,
        1,
        info,
        (near, far),
        [whole(near.shape), whole(far.shape)],
        [jax.ShapeDtypeStruct(shape, F32) for shape in shapes],
        [whole(shape) for shape in shapes],
        (),
        after,
    )


def shards(
    devices,
    byte_states,
    frontier,
    lengths,
    gain_attn,
    w_query,
    w_key,
    w_value,
    w_attn_out,
    rel_bias,
    gain_mlp,
    w_hidden,
    w_mlp_out,
    cotangent,
):
    bits = devices.bit_length() - 1
    mp = lax.axis_index("mp").astype(jnp.int32)
    dp = lax.axis_index(("far", "near")).astype(jnp.int32)
    core = dp & 1
    way = (dp >> 1) & 1
    place = (((dp >> 1) & 1) << 2) | (((dp >> 2) & 1) << 1)
    info = jnp.concatenate((jnp.stack((mp, core, way, place)), lengths))

    def across(value):
        return lax.ppermute(value, "mp", [(0, 1), (1, 0)])

    def swap(value, bit):
        pairs = [(i, i ^ (1 << bit)) for i in range(devices)]
        return lax.ppermute(value, ("far", "near"), pairs)

    def swap_four(value, index):
        turn = ((index & 1) << 2) | ((index >> 1) << 1)
        return lax.ppermute(value, ("far", "near"), [(i, i ^ turn) for i in range(devices)])

    def rows(count):
        return ((count, 512), BF16)

    weights = (w_query, w_key, w_value, w_attn_out, w_hidden, w_mlp_out)
    rel_own = rel_bias.T
    first_sent = pack(weights, rel_own)
    first = across(first_sent)
    backward, collect = offset_tables()
    backward, collect = jnp.asarray(backward), jnp.asarray(collect, BF16)

    pooled_own, pooled_sent, positions, meta = pool_forward(
        info, frontier, byte_states, (first_sent,)
    )
    pooled_other = across(pooled_sent)
    (first,) = combine("meet", nothing, after=(pooled_sent,), through=(first,))
    second = swap(first, 1)
    mid_sent, cot_sent, cot_own = pack_more(info, w_mlp_out, cotangent, (pooled_sent,))

    strips = bias_strips(info, rel_own, first, backward, (cot_own,))
    second, mid_sent = combine(
        "meet", nothing, after=(pooled_other, strips), through=(second, mid_sent)
    )
    parts = (first, second, swap(first, 0), swap(second, 0))
    cot_other = across(cot_sent)
    mid_first = across(mid_sent)

    gain_attn_row = gain_attn.reshape(1, -1)
    gain_mlp_row = gain_mlp.reshape(1, -1)
    qkv, logs, att, middle, normed, joined, w_o = attention_forward(
        info,
        pooled_own,
        pooled_other,
        strips,
        gain_attn_row,
        gain_mlp_row,
        weights[:4],
        parts,
        (),
    )
    half = pooled_own.shape[0]
    normed = normed.reshape(half * BLOCKS, -1)
    middle = middle.reshape(half * BLOCKS, -1)

    result, back, near_keep, near_sent, mark = ff_call(
        info, normed, cot_own, cot_other, True, (w_hidden, w_mlp_out), ()
    )
    got_near = swap(near_sent, 0)
    (mid_first,) = combine("meet", nothing, after=(mark,), through=(mid_first,))
    blocks_kept, blocks_sent, grad_mid, far_keep, far_sent, gain_mid = ff_call(
        info,
        normed,
        cot_own,
        cot_other,
        False,
        (*parts, mid_first, swap(mid_first, 0), result, back, middle, gain_mlp_row),
        (),
    )
    near_low, near_high, far_sent = combine(
        "near_cores",
        sum_into,
        (near_keep, got_near),
        (rows(512), rows(528)),
        (gain_mid,),
        (far_sent,),
    )
    far_low, far_high, near_high = combine(
        "far_cores",
        sum_into,
        (far_keep, swap(far_sent, 0)),
        (rows(512), rows(512)),
        (),
        (near_high,),
    )
    got_far = swap(far_high, 1)
    blocks_other = across(blocks_sent)

    grad_mid = grad_mid.reshape(half, BLOCKS, -1)
    rows_args = (pooled_own, pooled_other, qkv, logs, att, grad_mid)
    grad_normed, far_keep, far_sent, far_rel = attention_back(
        info,
        False,
        rows_args,
        strips,
        collect,
        gain_attn_row,
        joined,
        w_o,
        (),
        (far_low,),
    )
    far_ff, far_sent, near_high = combine(
        "far_y", sum_into, (far_low, got_far), (rows(528),), (far_rel, blocks_other), (far_sent, near_high)
    )
    got_near = swap(near_high, 1)
    far_attn, far_ff = combine(
        "far_cores", sum_into, (far_keep, swap(far_sent, 0)), (rows(544),), (), (far_ff,)
    )
    got_attn = across(far_attn)
    got_far = across(far_ff)
    grad_keep, grad_sent, near_keep, near_sent, tiny = attention_back(
        info,
        True,
        rows_args,
        strips,
        collect,
        gain_attn_row,
        joined,
        w_o,
        (grad_normed, far_rel, gain_mid),
        (far_attn,),
    )
    grad_other = across(grad_sent)

    def step_zero(ins, outs):
        for index in range(4):
            at = span_of(index, 128)
            total = ins[0][at, :].astype(F32) + ins[1][at, :].astype(F32)
            outs[index][0:128, :] = (total + ins[2][at, :].astype(F32)).astype(BF16)
            outs[index][128:144, :] = ins[3][...].astype(BF16)

    attn_parts = combine(
        "step_zero",
        step_zero,
        (near_keep, swap(near_sent, 0), got_attn, tiny),
        (rows(144),) * 4,
        (got_near,),
    )
    got_attn = [swap_four(attn_parts[index], index) for index in range(1, 4)]

    def pool_item(mine, index, held, after, through=()):
        grads = grad_keep if mine else grad_other
        return pool_backward(
            info, meta, positions, byte_states, grads, mine, index, held, after, through
        )

    held = pool_item(True, 0, (), (attn_parts[0],))

    def step_one(ins, outs):
        sum_into(ins[:4], outs[:1])
        sum_into(ins[4:], outs[1:])

    attn, ff_low, ff_high = combine(
        "step_one",
        step_one,
        (attn_parts[0], *got_attn, near_low, got_near, got_far),
        (rows(144), rows(256), rows(256)),
        (held[1],),
    )
    for bit in range(4, bits):
        attn = (attn.astype(F32) + swap(attn, bit).astype(F32)).astype(BF16)
    got_attn, got_ff = swap(attn, 3), swap(ff_high, 2)

    def step_two(ins, outs):
        total = ins[0][...].astype(F32) + ins[1][...].astype(F32)
        outs[0][...] = total[0:128, :].astype(BF16)
        outs[1][...] = total[128:144, :].astype(BF16)
        sum_into(ins[2:], outs[2:])

    held = pool_item(True, 1, held, (attn,))
    attn, tiny, near_ff = combine(
        "step_two",
        step_two,
        (attn, got_attn, ff_low, got_ff),
        (rows(128), rows(16), rows(256)),
        (held[1],),
    )
    got_ff = swap(near_ff, 3)
    got_attn = [swap_four(attn, index) for index in range(1, 4)]
    got_tiny = across(tiny)

    def step_three(ins, outs):
        join_into(ins[:4], outs[0])
        sum_into(ins[4:6], [outs[0].at[512:528, :]])
        sum_into(ins[6:], outs[1:])

    held = pool_item(False, 0, held, (attn,))
    near_attn, near_ff = combine(
        "step_three",
        step_three,
        (attn, *got_attn, tiny, got_tiny, near_ff, got_ff),
        (rows(528), rows(256)),
        (held[1],),
    )
    for bit in range(4, bits):
        near_ff = (near_ff.astype(F32) + swap(near_ff, bit).astype(F32)).astype(BF16)
    got_ff = [swap_four(near_ff, index) for index in range(1, 4)]
    far_attn = swap(near_attn, 0)

    held = pool_item(False, 1, held, (near_attn, near_ff))
    grad_bytes, part = held
    part_other = across(part)
    (
        grad_query,
        grad_key,
        grad_value,
        grad_out,
        grad_frontier,
        grad_gain_attn,
        grad_gain_mlp,
        grad_rel,
        blocks_out,
    ) = finish(
        info,
        near_attn,
        far_attn,
        part,
        part_other,
        positions,
        frontier,
        blocks_kept,
        blocks_other,
        (),
    )

    def join(ins, outs):
        join_into(ins, outs[0])

    (near_ff,) = combine("step_four", join, (near_ff, *got_ff), (rows(1024),), (grad_gain_attn,))
    far_ff = swap(near_ff, 0)
    grad_hidden, grad_mlp, _ = ff_place(
        info, near_ff, far_ff, (w_hidden.shape, w_mlp_out.shape, (8, 128)), ()
    )
    return (
        blocks_out,
        grad_bytes,
        grad_frontier,
        grad_gain_attn.reshape(-1),
        grad_query,
        grad_key,
        grad_value,
        grad_out,
        grad_rel.T,
        grad_gain_mlp.reshape(-1),
        grad_hidden,
        grad_mlp,
    )


def solution(mesh):
    devices = mesh.shape["dp"]
    split = jax.sharding.Mesh(
        mesh.devices.reshape(devices // 4, 4, mesh.shape["mp"]), ("far", "near", "mp")
    )
    dp = ("far", "near")
    placed = (
        P(dp, None, "mp"),
        P(dp, None),
        P(dp),
        P(),
        P(None, "mp"),
        P(None, "mp"),
        P(None, "mp"),
        P("mp", None),
        P(None, "mp"),
        P(),
        P(None, "mp"),
        P("mp", None),
        P(dp, None, "mp"),
    )
    return jax.shard_map(
        functools.partial(shards, devices),
        mesh=split,
        in_specs=placed,
        out_specs=(
            P(dp, None, "mp"),
            P(dp, None, "mp"),
            P(dp, None),
            P(),
            P(None, "mp"),
            P(None, "mp"),
            P(None, "mp"),
            P("mp", None),
            P(None, "mp"),
            P(),
            P(None, "mp"),
            P("mp", None),
        ),
        check_vma=False,
    )
```

```python
import functools
import math

import jax
import jax.numpy as jnp
import numpy as np
from jax import lax
from jax.experimental import pallas as pl
from jax.experimental.pallas import tpu as pltpu
from jax.sharding import PartitionSpec as P

BUCKETS = 32
REACH = 128
BLOCKS = 512
WRAP = 2 * BLOCKS
SHARDS = 8

EPSILON = 1e-06
SHARPNESS = 2.0
MASKED_SCORE = -1000000000.0
OUTSIDE = -10000.0
REACH_OUT = 8.0
PRECISE = lax.Precision.HIGHEST
ROOT = 0.7978845608028654
CUBIC = 0.044715
VMEM_LIMIT = 24 * 1024 * 1024
VMEM_MOST = 60 * 1024 * 1024
CHUNK = 256
WINDOW = 128
SLOTS = 3

F32 = jnp.float32
BF16 = jnp.bfloat16
ANY = pl.BlockSpec(memory_space=pl.ANY)
HBM = pl.BlockSpec(memory_space=pltpu.HBM)
NEAR = pl.BlockSpec(memory_space=pltpu.VMEM)
SMEM = pl.BlockSpec(memory_space=pltpu.SMEM)
NN = (((1,), (0,)), ((), ()))
NT = (((1,), (1,)), ((), ()))
TN = (((0,), (0,)), ((), ()))


def mm(a, b, dims=NN):
    return lax.dot_general(a, b, dims, preferred_element_type=F32)


def bucket_of(offset):
    half_count = BUCKETS // 2
    exact_count = half_count // 2
    distance = abs(offset)
    if distance < exact_count:
        place = distance
    else:
        place = min(
            half_count - 1,
            exact_count
            + math.floor(
                math.log(distance / exact_count)
                / math.log(REACH / exact_count)
                * (half_count - exact_count)
            ),
        )
    return place + (half_count if offset > 0 else 0)


def offset_tables():
    backward = np.zeros((WRAP, BUCKETS), np.float32)
    collect = np.zeros((WRAP, BUCKETS), np.float32)
    for offset in range(1 - BLOCKS, BLOCKS):
        bucket = bucket_of(offset)
        backward[(-offset) % WRAP, bucket] = 1.0
        collect[(384 - offset) % WRAP, bucket] = 1.0
    collect = np.concatenate([np.roll(collect, turn, axis=0) for turn in range(8)], axis=1)
    return backward.T, collect


def cost(micros):
    return pl.CostEstimate(flops=1, bytes_accessed=1, transcendentals=0)


def whole(shape):
    return pl.BlockSpec(shape, functools.partial(lambda n, i, info: (0,) * n, len(shape)))


def item(shape):
    return pl.BlockSpec(
        (1,) + shape, functools.partial(lambda n, i, info: (i,) + (0,) * n, len(shape))
    )


def launch(
    kernel, name, micros, grid, info, args, in_specs, outs, out_specs, scratch=(), after=(),
    through=(), aliases=None, vmem=VMEM_LIMIT,
):
    given, waits, passed, made = 1 + len(args), len(after), len(through), len(outs)

    def body(*refs):
        first = given + waits + passed
        kernel(*refs[:given], *refs[first : first + made], *refs[first + made + passed :])

    aliases = dict(aliases or {})
    for index in range(passed):
        aliases[given + waits + index] = made + index
    return pl.pallas_call(
        body,
        grid_spec=pltpu.PrefetchScalarGridSpec(
            num_scalar_prefetch=1,
            grid=(grid,),
            in_specs=list(in_specs) + [ANY] * (waits + passed),
            out_specs=list(out_specs) + [ANY] * passed,
            scratch_shapes=list(scratch),
        ),
        out_shape=list(outs) + [jax.ShapeDtypeStruct(x.shape, x.dtype) for x in through],
        input_output_aliases=aliases,
        compiler_params=pltpu.CompilerParams(
            vmem_limit_bytes=vmem, dimension_semantics=("arbitrary",)
        ),
        cost_estimate=cost(micros),
        name=name,
    )(info, *args, *after, *through)


def combine(name, work, args=(), outs=(), after=(), through=()):
    given, held, made, passed = len(args), len(args) + len(after), len(outs), len(through)

    def kernel(*refs):
        work(refs[:given], refs[held + passed : held + passed + made])

    near = pl.BlockSpec(memory_space=pltpu.VMEM)
    return pl.pallas_call(
        kernel,
        in_specs=[near] * given + [ANY] * (len(after) + passed),
        out_specs=[near] * made + [ANY] * passed,
        out_shape=[jax.ShapeDtypeStruct(*out) for out in outs]
        + [jax.ShapeDtypeStruct(x.shape, x.dtype) for x in through],
        input_output_aliases={held + index: made + index for index in range(passed)},
        compiler_params=pltpu.CompilerParams(vmem_limit_bytes=16 * 1024 * 1024),
        cost_estimate=cost(1),
        name=name,
    )(*args, *after, *through)


def nothing(ins, outs):
    pass


def sum_into(ins, outs):
    at = 0
    for out in outs:
        count = min(out.shape[0], ins[0].shape[0] - at)
        rows = slice(at, at + count)
        value = ins[0][rows, :].astype(F32)
        for other in ins[1:]:
            value = value + other[rows, :].astype(F32)
        out[0:count, :] = value.astype(out.dtype)
        if out.shape[0] > count:
            out[count:, :] = jnp.zeros((out.shape[0] - count, out.shape[1]), out.dtype)
        at += count


def join_into(ins, out):
    at = 0
    for source in ins:
        out[at : at + source.shape[0], :] = source[...]
        at += source.shape[0]


def share_out(info):
    lengths = [info[4 + item] for item in range(4)]
    ranks = []
    for item in range(4):
        rank = jnp.int32(0)
        for other in range(4):
            if other != item:
                before = lengths[other] <= lengths[item] if other < item else (
                    lengths[other] < lengths[item]
                )
                rank = rank + jnp.where(before, 1, 0)
        ranks.append(rank)

    def at(wanted):
        found = jnp.int32(0)
        for item in range(1, 4):
            found = jnp.where(ranks[item] == wanted, item, found)
        return found

    sides = ((at(3), at(0)), (at(2), at(1)))
    first = info[0] == 0
    mine = [jnp.where(first, a, b) for a, b in zip(*sides)]
    theirs = [jnp.where(first, b, a) for a, b in zip(*sides)]
    return mine, theirs


def item_count(info, index):
    mine = share_out(info)[0]
    item = mine[index] if isinstance(index, int) else jnp.where(index == 0, mine[0], mine[1])
    return lax.shift_right_logical(info[4 + item] + 3, 2)


def fetch_bytes(bytes_ref, buffer, sems, item, slot):
    return pltpu.make_async_copy(bytes_ref.at[item], buffer.at[slot], sems.at[slot])


def window_kernel(row, first, skipped):
    line = lax.broadcasted_iota(jnp.int32, (WINDOW, CHUNK), 0)
    offset = row - ((line + first).astype(F32) + 0.5)
    kernel = jnp.exp(-SHARPNESS * offset * offset)
    if skipped is not None:
        kernel = jnp.where(line >= skipped, kernel, 0.0)
    return kernel, offset


def chunk_row(pos_ref, item, chunk):
    return pos_ref[pl.ds(item, 1), tile_at(chunk, CHUNK)]


def pool_rows(item, info, meta, pos_ref, buffer, out_ref, acc):
    length = info[4 + item]
    acc[...] = jnp.zeros_like(acc)

    def add(chunk, first, skipped):
        first = pl.multiple_of(first, 16)
        kernel = window_kernel(chunk_row(pos_ref, item, chunk), first, skipped)[0]
        acc[pl.ds(first, WINDOW), :] += mm(
            kernel.astype(BF16), buffer[tile_at(chunk, CHUNK), :]
        )

    def two(pair, carry):
        for chunk in (pair * 2, pair * 2 + 1):
            add(chunk, meta[item, chunk], None)
        for chunk in (pair * 2, pair * 2 + 1):

            @pl.when(meta[4 + item, chunk] > 1)
            def _():
                def more(window, carry):
                    wanted = meta[item, chunk] + window * WINDOW
                    first = jnp.minimum(wanted, BLOCKS - WINDOW)
                    add(chunk, first, wanted - first)
                    return carry

                lax.fori_loop(1, meta[4 + item, chunk], more, 0)

        return carry

    lax.fori_loop(0, lax.div(length + 2 * CHUNK - 1, 2 * CHUNK), two, 0)
    count = lax.shift_right_logical(length + 3, 2)
    live = lax.broadcasted_iota(jnp.int32, acc.shape, 0) < count
    out_ref[...] = jnp.where(live, acc[...], 0.0).astype(BF16)


def find_windows(pos_ref, meta_ref):
    lane = lax.broadcasted_iota(jnp.int32, (4, 128), 1)
    starts = jnp.zeros((4, 128), jnp.int32)
    counts = jnp.ones((4, 128), jnp.int32)
    for chunk in range(pos_ref.shape[1] // CHUNK):
        rows = pos_ref[:, span_of(chunk, CHUNK)]
        low = jnp.min(jnp.where(rows < 0.0, 1e6, rows), axis=1, keepdims=True)
        high = jnp.max(rows, axis=1, keepdims=True)
        start = jnp.clip(low - REACH_OUT, 0.0, float(BLOCKS - WINDOW)).astype(jnp.int32)
        start = lax.shift_left(lax.shift_right_logical(start, 4), 4)
        last = jnp.clip(high + REACH_OUT, 0.0, float(BLOCKS - 1)).astype(jnp.int32)
        count = lax.shift_right_arithmetic(last - start, 7) + 1
        starts = jnp.where(lane == chunk, start, starts)
        counts = jnp.where(lane == chunk, jnp.maximum(count, 1), counts)
    meta_ref[0:4, :] = starts
    meta_ref[4:8, :] = counts


def masked_positions(info, frontier_ref, pos_ref):
    items, byte_count = frontier_ref.shape
    lane = lax.broadcasted_iota(jnp.int32, (items, byte_count), 1)
    row = lax.broadcasted_iota(jnp.int32, (items, byte_count), 0)
    length = jnp.zeros((items, byte_count), jnp.int32)
    for item in range(items):
        length = jnp.where(row == item, info[4 + item], length)
    valid = lane < length
    running = jnp.where(valid, frontier_ref[...], 0.0)
    step = 1
    while step < byte_count:
        running = running + jnp.where(lane >= step, pltpu.roll(running, step, 1), 0.0)
        step *= 2
    count = lax.shift_right_logical(length + 3, 2).astype(F32)
    total = running[:, byte_count - 1 :]
    pos_ref[...] = jnp.where(valid, count * running / total, OUTSIDE)


def pool_own_kernel(
    info, frontier_ref, bytes_ref, out_ref, pos_ref, meta_ref, buffer, acc, meta, sems, meta_sem
):
    mine = share_out(info)[0]
    for slot, item in enumerate(mine):
        fetch_bytes(bytes_ref, buffer, sems, item, slot).start()
    masked_positions(info, frontier_ref, pos_ref)
    find_windows(pos_ref, meta_ref)
    copy = pltpu.make_async_copy(meta_ref, meta, meta_sem)
    copy.start()
    copy.wait()
    for slot, item in enumerate(mine):
        fetch_bytes(bytes_ref, buffer, sems, item, slot).wait()
        pool_rows(item, info, meta, pos_ref, buffer.at[slot], out_ref.at[slot], acc)


def pool_other_kernel(info, meta, pos_ref, bytes_ref, out_ref, buffer, acc, sems):
    theirs = share_out(info)[1]
    out_ref[2 * BLOCKS :, :] = jnp.zeros((64, out_ref.shape[1]), BF16)
    for slot, item in enumerate(theirs):
        fetch_bytes(bytes_ref, buffer, sems, item, slot).start()
    for slot, item in enumerate(theirs):
        fetch_bytes(bytes_ref, buffer, sems, item, slot).wait()
        rows = out_ref.at[span_of(slot, BLOCKS), :]
        pool_rows(item, info, meta, pos_ref, buffer.at[slot], rows, acc)


def pool_forward(info, frontier, byte_states, after):
    items, byte_count, share = byte_states.shape
    half = items // 2
    out = jax.ShapeDtypeStruct((half, BLOCKS, share), BF16)
    pos = jax.ShapeDtypeStruct((items, byte_count), F32)
    windows = jax.ShapeDtypeStruct((8, 128), jnp.int32)
    scratch = [pltpu.VMEM((half, byte_count, share), BF16), pltpu.VMEM((BLOCKS, share), F32)]
    own, positions, meta = launch(
        pool_own_kernel,
        "pool_own",
        7,
        1,
        info,
        (frontier, byte_states),
        [whole(pos.shape), HBM],
        [out, pos, windows],
        [whole(out.shape), whole(pos.shape), whole(windows.shape)],
        scratch
        + [
            pltpu.SMEM((8, 128), jnp.int32),
            pltpu.SemaphoreType.DMA((half,)),
            pltpu.SemaphoreType.DMA,
        ],
        after,
        vmem=VMEM_MOST,
    )
    sent = jax.ShapeDtypeStruct((half * BLOCKS + 64, share), BF16)
    (other,) = launch(
        pool_other_kernel,
        "pool_other",
        7,
        1,
        info,
        (meta, positions, byte_states),
        [SMEM, whole(pos.shape), HBM],
        [sent],
        [whole(sent.shape)],
        scratch + [pltpu.SemaphoreType.DMA((half,))],
        vmem=VMEM_MOST,
    )
    return own, other, positions, meta


def pool_back_kernel(mine, index, info, meta, pos_ref, bytes_ref, grads_ref, *refs):
    out_ref, part_ref, buffer, written, acc, sems, out_sems = refs[-7:]
    item = share_out(info)[0 if mine else 1][index]
    length = info[4 + item]
    grads = grads_ref.at[index] if mine else grads_ref.at[span_of(index, BLOCKS)]
    fetch = fetch_bytes(bytes_ref, buffer, sems, item, 0)
    fetch.start()
    pairs = lax.div(length + 2 * CHUNK - 1, 2 * CHUNK)
    size = 2 * CHUNK

    def written_copy(pair):
        rows = tile_at(pair, size)
        return pltpu.make_async_copy(
            written.at[rows, :], out_ref.at[item, rows, :], out_sems.at[pair]
        )

    def window(chunk, first, skipped):
        first = pl.multiple_of(first, 16)
        kernel, offset = window_kernel(chunk_row(pos_ref, item, chunk), first, skipped)
        rows = grads[pl.ds(first, WINDOW), :]
        slope = mm(rows, buffer[0, tile_at(chunk, CHUNK), :], NT)
        back = mm(kernel.astype(BF16), rows, TN)
        return back, jnp.sum(slope * kernel * offset, axis=0, keepdims=True)

    def two(pair, carry):
        for chunk in (pair * 2, pair * 2 + 1):
            back, terms = window(chunk, meta[item, chunk], None)
            written[tile_at(chunk, CHUNK), :] = back.astype(BF16)
            part_ref[0, :, tile_at(chunk, CHUNK)] = -4.0 * terms
        for chunk in (pair * 2, pair * 2 + 1):

            @pl.when(meta[4 + item, chunk] > 1)
            def _():
                acc[...] = jnp.zeros_like(acc)

                def more(number, total):
                    wanted = meta[item, chunk] + number * WINDOW
                    first = jnp.minimum(wanted, BLOCKS - WINDOW)
                    back, terms = window(chunk, first, wanted - first)
                    acc[...] += back
                    return total + terms

                total = lax.fori_loop(
                    0, meta[4 + item, chunk], more, jnp.zeros((1, CHUNK), F32)
                )
                written[tile_at(chunk, CHUNK), :] = acc[...].astype(BF16)
                part_ref[0, :, tile_at(chunk, CHUNK)] = -4.0 * total

        written_copy(pair).start()
        return carry

    def empty(pair, carry):
        written[tile_at(pair, size), :] = jnp.zeros((size, written.shape[1]), BF16)
        part_ref[0, :, tile_at(pair, size)] = jnp.zeros((1, size), F32)
        written_copy(pair).start()
        return carry

    every = written.shape[0] // size
    lax.fori_loop(pairs, every, empty, 0)
    fetch.wait()
    lax.fori_loop(0, pairs, two, 0)
    for pair in range(every):
        written_copy(pair).wait()


def pool_backward(info, meta, positions, byte_states, grads, mine, index, held, after, through):
    items, byte_count, share = byte_states.shape
    side = 0 if mine else 1
    return launch(
        functools.partial(pool_back_kernel, mine, index),
        "pool_back",
        5,
        1,
        info,
        (meta, positions, byte_states, grads) + tuple(held),
        [SMEM, whole((items, byte_count)), HBM, NEAR] + [HBM] * len(held),
        [
            jax.ShapeDtypeStruct((items, byte_count, share), BF16),
            jax.ShapeDtypeStruct((items, 1, byte_count), F32),
        ],
        [
            HBM,
            pl.BlockSpec((1, 1, byte_count), lambda i, info: (share_out(info)[side][index], 0, 0)),
        ],
        [
            pltpu.VMEM((1, byte_count, share), BF16),
            pltpu.VMEM((byte_count, share), BF16),
            pltpu.VMEM((CHUNK, share), F32),
            pltpu.SemaphoreType.DMA((1,)),
            pltpu.SemaphoreType.DMA((byte_count // (2 * CHUNK),)),
        ],
        after,
        through,
        {5: 0, 6: 1} if held else None,
    )


def frontier_kernel(info, mine_ref, theirs_ref, pos_ref, frontier_ref, out_ref):
    items, byte_count = frontier_ref.shape
    lane = lax.broadcasted_iota(jnp.int32, (items, byte_count), 1)
    row = lax.broadcasted_iota(jnp.int32, (items, byte_count), 0)
    length = jnp.zeros((items, byte_count), jnp.int32)
    for item in range(items):
        length = jnp.where(row == item, info[4 + item], length)
    valid = lane < length
    total = jnp.sum(jnp.where(valid, frontier_ref[...], 0.0), axis=1, keepdims=True)
    terms = jnp.where(valid, mine_ref[:, 0, :] + theirs_ref[:, 0, :], 0.0)
    weighted = jnp.sum(terms * pos_ref[...], axis=1, keepdims=True)
    step = 1
    while step < byte_count:
        moved = pltpu.roll(terms, byte_count - step, 1)
        terms = terms + jnp.where(lane < byte_count - step, moved, 0.0)
        step *= 2
    count = lax.shift_right_logical(length + 3, 2).astype(F32)
    out_ref[...] = jnp.where(valid, (terms * count - weighted) / total, 0.0)


def strips_kernel(info, rel_ref, first_ref, table_ref, strips):
    core = info[1]
    parts = [first_ref[512:528, span_of(index, 128)].astype(F32) for index in range(3)]
    other = (parts[0] + parts[1] + parts[2])[0:4, 0:BUCKETS]
    rows = []
    for values in (rel_ref[...], other):
        turned = jnp.concatenate((values[2:4], values[0:2]), axis=0)
        rows.append(jnp.where(core == 0, values, turned))
    spread = lax.dot_general(
        jnp.concatenate(rows, axis=0),
        table_ref[...],
        NN,
        precision=PRECISE,
        preferred_element_type=F32,
    )
    for head in range(strips.shape[0]):
        row = jnp.broadcast_to(spread[head : head + 1, :], (8, WRAP))
        eight = pltpu.roll(row, 384, 1, stride=1, stride_axis=0)
        for group in range(16):
            turned = pltpu.roll(eight, 8 * group, 1) if group else eight
            strips[head, span_of(group, 8), :] = turned[:, :896]


def bias_strips(info, rel, first, table, after):
    return launch(
        strips_kernel,
        "bias_strips",
        2,
        1,
        info,
        (rel, first, table),
        [NEAR, NEAR, NEAR],
        [jax.ShapeDtypeStruct((8, 128, 896), F32)],
        [NEAR],
        (),
        after,
    )[0]


def gather_halves(info, target, own_ref, other_ref):
    target[:, tile_at(info[0], 256)] = own_ref[0]
    target[:, tile_at(1 - info[0], 256)] = other_ref[...]


def span_of(index, size):
    return slice(index * size, (index + 1) * size)


def tile_at(index, size):
    return pl.ds(pl.multiple_of(index * size, size), size)


def started(pairs, sems):
    return [
        pltpu.make_async_copy(source, target, sems.at[index])
        for index, (source, target) in enumerate(pairs)
    ]


def inverse_rms(values):
    return lax.rsqrt(jnp.mean(values * values, axis=1, keepdims=True) + EPSILON)


def triple(values):
    high = values.astype(BF16)
    rest = values - high.astype(F32)
    middle = rest.astype(BF16)
    return high, middle, (rest - middle.astype(F32)).astype(BF16)


def spare_lane(head):
    return (head // 2) * 4 + 64 * (1 - head % 2)


def strip_tiles(strips, head, half):
    return jnp.concatenate(
        [
            strips[head, :, (3 - tile) * 128 + half * 256 : (5 - tile) * 128 + half * 256]
            for tile in range(4)
        ],
        axis=0,
    )


def parts_by_lane(values, lead):
    spot = lax.broadcasted_iota(jnp.int32, values.shape, 1) & 3
    parts = [part.astype(F32) for part in triple(values)]
    found = jnp.where(spot == 1, parts[0], jnp.where(spot == 2, parts[1], parts[2]))
    return jnp.where(spot == 0, lead, found).astype(BF16)


def attention_kernel(
    info,
    own_ref,
    other_ref,
    strips,
    gain_attn_ref,
    gain_mlp_ref,
    w_query,
    w_key,
    w_value,
    w_out,
    part_a,
    part_b,
    part_c,
    part_d,
    qkv_ref,
    log_ref,
    att_ref,
    middle_ref,
    normed_ref,
    w_qkv,
    w_o,
    pooled,
    logs,
    scores,
):
    step = pl.program_id(0)
    mp, core, way = info[0], info[1], info[2]
    count = item_count(info, step)

    @pl.when(step == 0)
    def _():
        for part in range(2):
            start = core if part == 0 else 1 - core
            for index, weight in enumerate((w_query, w_key, w_value)):
                first = index * 512 + part * 128
                w_qkv[:, first : first + 128] = weight[:, tile_at(start, 128)]
            w_o[span_of(part, 128), :] = w_out[tile_at(start, 128), :]
        for part, sources in enumerate(((part_a, part_b), (part_c, part_d))):
            for side, source in enumerate(sources):
                turn = way if side == 0 else 1 - way
                for index in range(3):
                    first = index * 512 + 256 + part * 128
                    w_qkv[tile_at(turn, 256), first : first + 128] = source[
                        0:256, span_of(index, 128)
                    ]
                rows = pl.ds(pl.multiple_of(256 + part * 128 + turn * 64, 64), 64)
                for lane in range(4):
                    w_o[rows, span_of(lane, 128)] = source[span_of(lane, 64), 384:512]
        logs[...] = jnp.zeros_like(logs)

    gather_halves(info, pooled, own_ref, other_ref)
    wide = pooled[...].astype(F32)
    normed = (wide * inverse_rms(wide) * gain_attn_ref[...]).astype(BF16)
    qkv_ref[0] = mm(normed, w_qkv[...]).astype(BF16)
    lane = lax.broadcasted_iota(jnp.int32, (BLOCKS, 128), 1)
    row = lax.broadcasted_iota(jnp.int32, (BLOCKS, 128), 0)
    dead = jnp.where(row < count, 0.0, MASKED_SCORE).astype(BF16)

    ready, found, tops = {}, {}, {}

    def prepare(pair):
        queries = qkv_ref[0, :, span_of(pair, 128)]
        keys = qkv_ref[0, :, span_of(pair + 4, 128)]
        values = qkv_ref[0, :, span_of(pair + 8, 128)]
        for side in range(2):
            own = (lane < 64) == (side == 0)
            spare = lane == 64 * (1 - side)
            chosen = jnp.where(own, queries, jnp.where(spare, 1.0, 0.0).astype(BF16))
            masked = jnp.where(spare, dead, keys)
            summing = jnp.transpose(jnp.where(own, values, jnp.ones_like(values)))
            ready[pair, side] = (chosen, masked, summing)

    def first_pass(slot, pair, half, side):
        chosen, masked, _ = ready[pair, side]
        held = scores.at[slot]
        raw = mm(masked, chosen[span_of(half, 256), :], NT)
        most = None
        for tile in range(4):
            first = (3 - tile) * 128 + half * 256
            part = raw[span_of(tile, 128), :] + strips[pair * 2 + side, :, first : first + 256]
            held[span_of(tile, 128), :] = part
            part = jnp.max(part.reshape(16, 8, 256), axis=0)
            most = part if most is None else jnp.maximum(most, part)
        tops[slot] = jnp.max(most, axis=0, keepdims=True)

    def second_pass(slot, pair, half, side):
        held = scores.at[slot]
        most = tops[slot]
        expo = jnp.concatenate(
            [jnp.exp(held[span_of(tile, 128), :] - most).astype(BF16) for tile in range(4)],
            axis=0,
        )
        out = mm(ready[pair, side][2], expo)
        other = 64 * (1 - side)
        total = out[other : other + 1, :]
        found[side] = (out * (1.0 / total))[64 * side : 64 * side + 64, :]
        place = pair * 4 + other
        logs[place : place + 4, span_of(half, 256)] = jnp.broadcast_to(
            most + jnp.log(total), (4, 256)
        )
        if side == 1:
            both = jnp.concatenate((found[0], found[1]), axis=0).astype(BF16)
            att_ref[0, span_of(half, 256), span_of(pair, 128)] = jnp.transpose(both)

    chains = [(pair, half, side) for pair in range(4) for half in range(2) for side in range(2)]
    for index, chain in enumerate(chains):
        if index % 4 == 0:
            prepare(chain[0])
        first_pass(index % SLOTS, *chain)
        if index >= SLOTS - 1:
            last = index - SLOTS + 1
            second_pass(last % SLOTS, *chains[last])
    for last in range(len(chains) - SLOTS + 1, len(chains)):
        second_pass(last % SLOTS, *chains[last])
    log_ref[0] = parts_by_lane(-jnp.transpose(logs[...]), 1.0)

    mid = wide + mm(att_ref[0], w_o[...])
    middle_ref[0] = mid
    normed_ref[0] = (mid * inverse_rms(mid) * gain_mlp_ref[...]).astype(BF16)


def attention_forward(info, own, other, strips, gain_attn, gain_mlp, weights, parts, after):
    half = own.shape[0]
    return launch(
        attention_kernel,
        "attention_forward",
        20,
        half,
        info,
        (own, other, strips, gain_attn, gain_mlp, *weights, *parts),
        [
            item((BLOCKS, 256)),
            pl.BlockSpec((BLOCKS, 256), lambda i, info: (i, 0)),
            NEAR,
            whole((1, 512)),
            whole((1, 512)),
        ]
        + [NEAR] * 8,
        [
            jax.ShapeDtypeStruct((half, BLOCKS, 1536), BF16),
            jax.ShapeDtypeStruct((half, BLOCKS, 128), BF16),
            jax.ShapeDtypeStruct((half, BLOCKS, 512), BF16),
            jax.ShapeDtypeStruct((half, BLOCKS, 512), F32),
            jax.ShapeDtypeStruct((half, BLOCKS, 512), BF16),
            jax.ShapeDtypeStruct((512, 1536), BF16),
            jax.ShapeDtypeStruct((512, 512), BF16),
        ],
        [
            item((BLOCKS, 1536)),
            item((BLOCKS, 128)),
            item((BLOCKS, 512)),
            item((BLOCKS, 512)),
            item((BLOCKS, 512)),
            whole((512, 1536)),
            whole((512, 512)),
        ],
        [
            pltpu.VMEM((BLOCKS, 512), BF16),
            pltpu.VMEM((128, BLOCKS), F32),
            pltpu.VMEM((SLOTS, BLOCKS, 256), F32),
        ],
        after,
    )


def gelu_and_slope(pre):
    square = pre * pre
    tanh = jnp.tanh(pre * (ROOT + (ROOT * CUBIC) * square))
    up = 0.5 + 0.5 * tanh
    act = pre * up
    slope = up + act * (1.0 - up) * (2.0 * ROOT + (6.0 * ROOT * CUBIC) * square)
    return act, slope


def ff_piece(normed, turned, top, turned_top, hid, mid, acts, grads, result, back, start):
    for half in range(2):
        rows = span_of(half, BLOCKS)
        act, slope = gelu_and_slope(mm(normed[rows, :], hid))
        acts[rows, :] = act.astype(BF16)
        grads[rows, :] = (mm(top[rows, :], mid, NT) * slope).astype(BF16)
        new_result = mm(acts[rows, :], mid)
        new_back = mm(grads[rows, :], hid, NT)
        if start is None:
            result[rows, :] += new_result
            back[rows, :] += new_back
        elif start:
            result[rows, :] = start[0][rows, :] + new_result
            back[rows, :] = start[1][rows, :] + new_back
        else:
            result[rows, :] = new_result
            back[rows, :] = new_back
    return mm(turned[...], grads[...]), mm(turned_top[...], acts[...])


def store_shards(place, target, first, values):
    rows = values.shape[0] // SHARDS
    size = target.shape[0] // SHARDS
    for shard in range(SHARDS):
        at = pl.multiple_of(lax.bitwise_xor(place, shard) * size + first, 64)
        target[pl.ds(at, rows), :] = values[span_of(shard, rows), :].astype(BF16)


def gather_top(info, top, turned_top, cot_own_ref, cot_other_ref):
    for index in range(2):
        rows = span_of(index, BLOCKS)
        count = item_count(info, index)
        live = lax.broadcasted_iota(jnp.int32, (BLOCKS, 256), 0) < count
        zero = jnp.zeros((BLOCKS, 256), BF16)
        top[rows, tile_at(info[0], 256)] = jnp.where(live, cot_own_ref[index], zero)
        top[rows, tile_at(1 - info[0], 256)] = jnp.where(live, cot_other_ref[index], zero)
        turned_top[:, rows] = jnp.transpose(top[rows, :])


def ff_own_kernel(
    info,
    normed_ref,
    cot_own_ref,
    cot_other_ref,
    w_hidden,
    w_mlp,
    result,
    back,
    keep_ref,
    send_ref,
    mark,
    top,
    turned_top,
    turned,
    acts,
    grads,
):
    core, place = info[1], info[3]
    mark[...] = jnp.zeros_like(mark)
    gather_top(info, top, turned_top, cot_own_ref, cot_other_ref)
    for index in range(2):
        turned[:, span_of(index, BLOCKS)] = jnp.transpose(normed_ref[span_of(index, BLOCKS), :])
    for part, target in ((1, send_ref), (0, keep_ref)):
        start = core if part == 0 else 1 - core
        grad_hid, grad_mid = ff_piece(
            normed_ref,
            turned,
            top,
            turned_top,
            w_hidden[:, tile_at(start, 512)],
            w_mlp[tile_at(start, 512), :],
            acts,
            grads,
            result,
            back,
            () if part == 1 else None,
        )
        store_shards(place, target, 0, grad_hid)
        store_shards(place, target, 64, grad_mid)


def ff_other_kernel(
    info,
    normed_ref,
    cot_own_ref,
    cot_other_ref,
    hid_a,
    hid_b,
    hid_c,
    hid_d,
    mid_near,
    mid_far,
    result_ref,
    back_ref,
    middle_ref,
    gain_ref,
    blocks_keep,
    blocks_send,
    grad_mid_ref,
    keep_ref,
    send_ref,
    gain_out,
    top,
    turned_top,
    turned,
    acts,
    grads,
    weights,
    result,
    back,
    blocks,
):
    mp, way, place = info[0], info[2], info[3]
    for part, sources in ((1, (hid_c, hid_d)), (0, (hid_a, hid_b))):
        for side, source in enumerate(sources):
            turn = way if side == 0 else 1 - way
            weights[part, tile_at(turn, 256), :] = source[256:512, :]
    gather_top(info, top, turned_top, cot_own_ref, cot_other_ref)
    for index in range(2):
        turned[:, span_of(index, BLOCKS)] = jnp.transpose(normed_ref[span_of(index, BLOCKS), :])
    for part, target in ((1, send_ref), (0, keep_ref)):
        grad_hid, grad_mid = ff_piece(
            normed_ref,
            turned,
            top,
            turned_top,
            weights[part],
            (mid_far if part == 1 else mid_near)[...],
            acts,
            grads,
            result,
            back,
            (result_ref, back_ref) if part == 1 else None,
        )
        store_shards(place, target, 0, grad_hid)
        store_shards(place, target, 64, grad_mid)

    new_gain = jnp.zeros((1, 512), F32)
    for index in range(2):
        rows = span_of(index, BLOCKS)
        count = item_count(info, index)
        live = lax.broadcasted_iota(jnp.int32, (BLOCKS, 1), 0) < count
        middle = middle_ref[rows, :]
        blocks[...] = jnp.where(live, middle + result[rows, :], 0.0).astype(BF16)
        blocks_keep[index] = blocks[:, tile_at(mp, 256)]
        blocks_send[index] = blocks[:, tile_at(1 - mp, 256)]
        scale = inverse_rms(middle)
        unit = middle * scale
        grad_normed = back[rows, :]
        scaled = grad_normed * gain_ref[...]
        grad_mid_ref[rows, :] = top[rows, :].astype(F32) + scale * (
            scaled - unit * jnp.mean(scaled * unit, axis=1, keepdims=True)
        )
        new_gain = new_gain + jnp.sum(grad_normed * unit, axis=0, keepdims=True)
    gain_out[...] = jnp.broadcast_to(new_gain, gain_out.shape)


def ff_call(info, normed, cot, cot_other, mine, given, after):
    rows = normed.shape[0]
    half = rows // BLOCKS
    packed = (SHARDS * 128, 512)
    wide = jax.ShapeDtypeStruct((rows, 512), F32)
    pack = jax.ShapeDtypeStruct(packed, BF16)
    share = jax.ShapeDtypeStruct((half, BLOCKS, 256), BF16)
    in_specs = [whole((rows, 512)), whole(share.shape), whole(share.shape)]
    scratch = [
        pltpu.VMEM((rows, 512), BF16),
        pltpu.VMEM((512, rows), BF16),
        pltpu.VMEM((512, rows), BF16),
        pltpu.VMEM((rows, 512), BF16),
        pltpu.VMEM((rows, 512), BF16),
    ]
    if mine:
        in_specs += [NEAR] * 2
        outs = [wide, wide, pack, pack, jax.ShapeDtypeStruct((8, 128), F32)]
    else:
        in_specs += [NEAR] * 8 + [whole((rows, 512)), whole((1, 512))]
        outs = [share, share, wide, pack, pack, jax.ShapeDtypeStruct((8, 512), F32)]
        scratch += [
            pltpu.VMEM((2, 512, 512), BF16),
            pltpu.VMEM((rows, 512), F32),
            pltpu.VMEM((rows, 512), F32),
            pltpu.VMEM((BLOCKS, 512), BF16),
        ]
    return launch(
        ff_own_kernel if mine else ff_other_kernel,
        "ff_own" if mine else "ff_other",
        12,
        1,
        info,
        (normed, cot, cot_other, *given),
        in_specs,
        outs,
        [whole(x.shape) for x in outs],
        scratch,
        after,
    )


def attention_back_body(
    info,
    first_head,
    own_ref,
    other_ref,
    query_ref,
    key_ref,
    value_ref,
    log_ref,
    att_ref,
    grad_mid_ref,
    strips,
    collect_ref,
    gain_attn_ref,
    wq_ref,
    wk_ref,
    wv_ref,
    wo_ref,
    keep_ref,
    send_ref,
    pooled,
    outer,
    grads,
    sums,
    turned,
    turned_branch,
    atts,
    probs,
    weights,
    scored,
):
    step = pl.program_id(0)
    mp, place = info[0], info[3]
    count = item_count(info, step)

    @pl.when(step == 0)
    def _():
        sums[...] = jnp.zeros_like(sums)

    gather_halves(info, pooled, own_ref, other_ref)
    here = tile_at(step, BLOCKS)
    branch = grad_mid_ref[0].astype(BF16)
    outer[...] = mm(branch, wo_ref[...], NT).astype(BF16)
    lane = lax.broadcasted_iota(jnp.int32, (BLOCKS, 128), 1)
    row = lax.broadcasted_iota(jnp.int32, (BLOCKS, 128), 0)
    dead = jnp.where(row < count, 0.0, MASKED_SCORE).astype(BF16)
    line = lax.broadcasted_iota(jnp.int32, (1, 128), 1)
    deltas = jnp.zeros((BLOCKS, 128), F32)
    for pair in range(2):
        span = span_of(pair, 128)
        overlap = outer[:, span].astype(F32) * att_ref[0, :, span].astype(F32)
        for side in range(2):
            own = (lane < 64) == (side == 0)
            delta = jnp.sum(jnp.where(own, overlap, 0.0), axis=1, keepdims=True)
            spare = spare_lane(first_head + pair * 2 + side)
            mine = jnp.logical_and(lane >= spare, lane < spare + 4)
            deltas = jnp.where(mine, delta, deltas)
    deltas = parts_by_lane(-deltas, 0.0)

    ready, found = {}, {}

    def prepare(pair):
        span = span_of(pair, 128)
        queries = query_ref[0, :, span]
        keys = key_ref[0, :, span]
        values = value_ref[0, :, span]
        out_grads = outer[:, span]
        ready[pair] = jnp.transpose(keys)
        for side in range(2):
            own = (lane < 64) == (side == 0)
            spare = spare_lane(first_head + pair * 2 + side)
            added = jnp.logical_and(line > spare, line < spare + 4)
            ones = jnp.where(added, 1.0, 0.0).astype(BF16)
            chosen = jnp.where(own, queries, log_ref[0])
            masked = jnp.where(own, keys, jnp.where(lane == spare, dead, ones))
            drawn = jnp.where(own, out_grads, deltas)
            weighed = jnp.where(own, values, ones)
            ready[pair, side] = (chosen, masked, drawn, weighed)

    def first_pass(slot, pair, side, half):
        chosen, masked, _, _ = ready[pair, side]
        raw = mm(masked, chosen[span_of(half, 256), :], NT)
        for tile in range(4):
            first = (3 - tile) * 128 + half * 256
            rows = span_of(tile, 128)
            part = jnp.exp(
                raw[rows, :] + strips[first_head + pair * 2 + side, :, first : first + 256]
            )
            probs[slot, rows, :] = part
            weights[slot, rows, :] = part.astype(BF16)

    def second_pass(slot, pair, side, half):
        _, _, drawn, weighed = ready[pair, side]
        head = pair * 2 + side
        slope = mm(weighed, drawn[span_of(half, 256), :], NT)
        product = [probs[slot, span_of(tile, 128), :] * slope[span_of(tile, 128), :] for tile in range(4)]
        for tile in range(4):
            scored[slot, span_of(tile, 128), :] = product[tile].astype(BF16)
        for diagonal in range(5):
            first = (3 - diagonal + 1) * 128 + half * 256
            total = None
            for tile in range(4):
                column = tile - diagonal + 1
                if 0 <= column < 2:
                    block = product[tile][:, span_of(column, 128)]
                    total = block if total is None else total + block
            sums[head, :, first : first + 128] += total

    def third_pass(slot, pair, side, half):
        span = span_of(pair, 128)
        rows = span_of(half, 256)
        turned_query = mm(ready[pair], scored[slot])
        grad_key = mm(scored[slot], query_ref[0, rows, span])
        grad_value = mm(weights[slot], outer[rows, span])
        if half == 0:
            found[side] = ([turned_query], grad_key, grad_value)
        else:
            before = found[side]
            found[side] = (
                before[0] + [turned_query],
                before[1] + grad_key,
                before[2] + grad_value,
            )
        if side == 1 and half == 1:
            for index in range(2):
                both = jnp.concatenate(
                    (found[0][0][index][0:64, :], found[1][0][index][64:128, :]), axis=0
                ).astype(BF16)
                grads[
                    pl.ds(pl.multiple_of(step * BLOCKS + index * 256, 256), 256), span
                ] = jnp.transpose(both)
            for index in range(1, 3):
                first = index * 256 + pair * 128
                grads[here, first : first + 128] = jnp.where(
                    lane < 64, found[0][index], found[1][index]
                ).astype(BF16)

    units = [(pair, side, half) for pair in range(2) for side in range(2) for half in range(2)]
    for index in range(len(units) + 2):
        if index < len(units):
            if index % 4 == 0:
                prepare(units[index][0])
            first_pass(index % 4, *units[index])
        if 1 <= index <= len(units):
            second_pass((index - 1) % 4, *units[index - 1])
        if index >= 2:
            third_pass((index - 2) % 4, *units[index - 2])

    wide = pooled[...].astype(F32)
    scale = inverse_rms(wide)
    unit = wide * scale
    normed = (unit * gain_attn_ref[...]).astype(BF16)
    turned[:, here] = jnp.transpose(normed)
    turned_branch[:, here] = jnp.transpose(branch)
    atts[here, :] = att_ref[0]

    @pl.when(step == 1)
    def _():
        new = mm(turned[...], grads[...])
        new_out = mm(turned_branch[...], atts[...])
        for part, targets in ((1, send_ref), (0, keep_ref)):
            for shard in range(SHARDS):
                at = lax.bitwise_xor(place, shard)
                if isinstance(targets, tuple):
                    target, at = targets[shard % 2], lax.shift_right_logical(at, 1)
                else:
                    target = targets
                at = tile_at(at, 64)
                here_rows = span_of(shard, 64)
                for index in range(3):
                    first = index * 256 + part * 128
                    target[at, span_of(index, 128)] = new[here_rows, first : first + 128].astype(
                        BF16
                    )
                target[at, 384:512] = new_out[here_rows, span_of(part, 128)].astype(BF16)

    grad_normed = (
        mm(grads[here, 0:256], wq_ref[...], NT)
        + mm(grads[here, 256:512], wk_ref[...], NT)
        + mm(grads[here, 512:768], wv_ref[...], NT)
    )
    return unit, scale, grad_normed


def fold_bias(sums, collect_ref):
    rows = []
    for head in range(4):
        folded = jnp.concatenate((sums[head], jnp.zeros((128, 128), F32)), axis=1)
        size = 64
        while size >= 8:
            folded = folded[:size] + pltpu.roll(folded[size : 2 * size], WRAP - size, 1)
            size //= 2
        rows.append(folded)
    lines = jnp.concatenate(triple(jnp.concatenate(rows, axis=0)), axis=0)
    found = mm(lines, collect_ref[...])
    found = found[0:32] + found[32:64] + found[64:96]
    row = lax.broadcasted_iota(jnp.int32, found.shape, 0) & 7
    spot = lax.shift_right_logical(lax.broadcasted_iota(jnp.int32, found.shape, 1), 5)
    found = jnp.where(row == spot, found, 0.0)
    rows = []
    for head in range(4):
        total = jnp.sum(found[span_of(head, 8), :], axis=0, keepdims=True)
        total = total[:, 0:128] + total[:, 128:256]
        total = total + pltpu.roll(total, 64, 1)
        rows.append(total + pltpu.roll(total, 32, 1))
    return jnp.concatenate(rows + rows, axis=0)


def attention_back_first_kernel(info, *refs):
    heads, (grad_ref, keep_ref, send_ref, rel_ref), scratch = refs[:15], refs[15:19], refs[19:]
    _, _, grad_normed = attention_back_body(info, 4, *heads, keep_ref, send_ref, *scratch)
    grad_ref[0] = grad_normed

    @pl.when(pl.program_id(0) == 1)
    def _():
        rel_ref[...] = fold_bias(scratch[3], heads[9])


def attention_back_second_kernel(info, *refs):
    heads, (held_ref, rel_ref, gain_mid_ref), refs = refs[:15], refs[15:18], refs[18:]
    (keep_rows, send_rows, keep_ref, even_ref, odd_ref, tiny_ref), scratch = refs[:6], refs[6:]
    send_ref = (even_ref, odd_ref)
    scratch, acc_gain = scratch[:-1], scratch[-1]
    unit, scale, grad_normed = attention_back_body(info, 0, *heads, keep_ref, send_ref, *scratch)
    mp, core = info[0], info[1]
    step = pl.program_id(0)
    pooled = scratch[0]
    grad_normed = grad_normed + held_ref[0]
    scaled = grad_normed * heads[10][...]
    grad_pooled = heads[7][0] + scale * (
        scaled - unit * jnp.mean(scaled * unit, axis=1, keepdims=True)
    )
    pooled[...] = grad_pooled.astype(BF16)
    keep_rows[0] = pooled[:, tile_at(mp, 256)]
    send_rows[tile_at(step, BLOCKS), :] = pooled[:, tile_at(1 - mp, 256)]
    new_gain = jnp.sum(grad_normed * unit, axis=0, keepdims=True)

    @pl.when(step == 0)
    def _():
        acc_gain[...] = jnp.broadcast_to(new_gain, acc_gain.shape)

    @pl.when(step == 1)
    def _():
        found = fold_bias(scratch[3], heads[9])
        line = lax.broadcasted_iota(jnp.int32, (8, 128), 0)
        rows = jnp.zeros((8, 128), F32)
        for head in range(8):
            source = found if head < 4 else rel_ref[...]
            true_head = (
                lax.bitwise_xor(mp, head // 4) * 4
                + lax.bitwise_xor(core, (head // 2) % 2) * 2
                + head % 2
            )
            rows = jnp.where(line == true_head, source[head % 4 : head % 4 + 1, :], rows)
        tiny_ref[...] = jnp.zeros_like(tiny_ref)
        tiny_ref[0:1, :] = acc_gain[0:1, :] + new_gain
        tiny_ref[1:2, :] = gain_mid_ref[0:1, :]
        tiny_ref[8:16, 0:128] = rows


def attention_back(
    info, mine, rows_args, strips, collect, gain_attn, joined, w_o, given, after
):
    own, other, qkv, logs, att, grad_mid = rows_args
    half = own.shape[0]
    where = 0 if mine else 1

    def lanes(index):
        return pl.BlockSpec((1, BLOCKS, 256), lambda i, info: (i, 0, index))

    def columns(index):
        return pl.BlockSpec((512, 256), lambda i, info: (0, index))

    in_specs = [
        item((BLOCKS, 256)),
        pl.BlockSpec((BLOCKS, 256), lambda i, info: (i, 0)),
        lanes(where),
        lanes(2 + where),
        lanes(4 + where),
        item((BLOCKS, 128)),
        lanes(where),
        item((BLOCKS, 512)),
        NEAR,
        whole((WRAP, 256)),
        whole((1, 512)),
        columns(where),
        columns(2 + where),
        columns(4 + where),
        pl.BlockSpec((256, 512), lambda i, info: (where, 0)),
    ]
    args = [own, other, qkv, qkv, qkv, logs, att, grad_mid, strips, collect, gain_attn]
    args += [joined, joined, joined, w_o]
    packed = (SHARDS * 64, 512)
    pack = jax.ShapeDtypeStruct(packed, BF16)
    scratch = [
        pltpu.VMEM((BLOCKS, 512), BF16),
        pltpu.VMEM((BLOCKS, 256), BF16),
        pltpu.VMEM((half * BLOCKS, 768), BF16),
        pltpu.VMEM((4, 128, 896), F32),
        pltpu.VMEM((512, half * BLOCKS), BF16),
        pltpu.VMEM((512, half * BLOCKS), BF16),
        pltpu.VMEM((half * BLOCKS, 256), BF16),
        pltpu.VMEM((4, BLOCKS, 256), F32),
        pltpu.VMEM((4, BLOCKS, 256), BF16),
        pltpu.VMEM((4, BLOCKS, 256), BF16),
    ]
    if mine:
        share = jax.ShapeDtypeStruct((half, BLOCKS, 256), BF16)
        in_specs += [item((BLOCKS, 512)), whole((8, 128)), whole((8, 512))]
        sent = jax.ShapeDtypeStruct((half * BLOCKS, 256), BF16)
        few = (SHARDS * 32, 512)
        packs = [pack, jax.ShapeDtypeStruct(few, BF16), jax.ShapeDtypeStruct(few, BF16)]
        outs = [share, sent, *packs, jax.ShapeDtypeStruct((16, 512), F32)]
        out_specs = [item((BLOCKS, 256)), whole(sent.shape), whole(packed), whole(few), whole(few)]
        out_specs += [whole((16, 512))]
        scratch += [pltpu.VMEM((8, 512), F32)]
    else:
        outs = [
            jax.ShapeDtypeStruct((half, BLOCKS, 512), F32),
            pack,
            pack,
            jax.ShapeDtypeStruct((8, 128), F32),
        ]
        out_specs = [item((BLOCKS, 512)), whole(packed), whole(packed), whole((8, 128))]
    return launch(
        attention_back_second_kernel if mine else attention_back_first_kernel,
        "attention_back_own" if mine else "attention_back_other",
        17,
        half,
        info,
        (*args, *given),
        in_specs,
        outs,
        out_specs,
        scratch,
        after,
    )


def place_kernel(info, ff_near, ff_far, hid_ref, mid_ref, mark):
    mark[...] = jnp.zeros_like(mark)
    core, place = info[1], info[3]
    for source, side in ((ff_near, core), (ff_far, 1 - core)):
        turned = []
        for shard in range(SHARDS):
            at = lax.bitwise_xor(place, shard)
            at = at * 2
            hid_ref[span_of(shard, 64), tile_at(side, 512)] = source[tile_at(at, 64), :].astype(F32)
            turned.append(source[tile_at(at + 1, 64), :])
        mid_ref[tile_at(side, 512), :] = jnp.transpose(
            jnp.concatenate(turned, axis=0).astype(F32)
        )


def pack_kernel(wq, wk, wv, wo, wh, rel, out, sems):
    near = lax.axis_index("near")
    core, way = lax.rem(near, 2), lax.div(near, 2)
    rows = tile_at(way, 256)
    pairs = []
    for index, weight in enumerate((wq, wk, wv)):
        lanes = pl.ds(index * 128, 128)
        pairs.append((weight.at[rows, tile_at(core, 128)], out.at[pl.ds(0, 256), lanes]))
    few = pl.ds(pl.multiple_of(core * 128 + way * 64, 64), 64)
    for lane in range(4):
        pairs.append(
            (
                wo.at[few, pl.ds(lane * 128, 128)],
                out.at[pl.ds(lane * 64, 64), pl.ds(384, 128)],
            )
        )
    pairs.append((wh.at[rows, tile_at(core, 512)], out.at[pl.ds(256, 256), :]))
    copies = started(pairs, sems)
    for copy in copies:
        copy.start()
    out[512:528, :] = jnp.zeros((16, 512), BF16)
    for index, part in enumerate(triple(rel[...])):
        out[512:516, index * 128 : index * 128 + BUCKETS] = part
    for copy in copies:
        copy.wait()


def pack(weights, rel):
    return pl.pallas_call(
        pack_kernel,
        grid=(1,),
        in_specs=[HBM] * 5 + [pl.BlockSpec(rel.shape, lambda i: (0, 0))],
        out_specs=pl.BlockSpec((528, 512), lambda i: (0, 0)),
        out_shape=jax.ShapeDtypeStruct((528, 512), BF16),
        scratch_shapes=[pltpu.SemaphoreType.DMA((8,))],
        compiler_params=pltpu.CompilerParams(
            vmem_limit_bytes=VMEM_MOST, dimension_semantics=("arbitrary",)
        ),
        cost_estimate=cost(1),
        name="pack",
    )(*weights[:5], rel)


def pack_more_kernel(info, wm, cot, mid_out, cot_out, cot_own, sems):
    mine, theirs = share_out(info)
    pairs = [(wm.at[tile_at(info[1], 512), :], mid_out)]
    for index in range(2):
        pairs.append((cot.at[theirs[index]], cot_out.at[index, pl.ds(0, BLOCKS), :]))
        pairs.append((cot.at[mine[index]], cot_own.at[index]))
    copies = started(pairs, sems)
    for copy in copies:
        copy.start()
    cot_out[:, BLOCKS:, :] = jnp.zeros((2, 32, cot_out.shape[2]), BF16)
    for copy in copies:
        copy.wait()


def pack_more(info, w_mlp, cotangent, after):
    half, share = cotangent.shape[0] // 2, cotangent.shape[2]
    outs = [jax.ShapeDtypeStruct((512, 512), BF16)]
    outs += [jax.ShapeDtypeStruct((half, rows, share), BF16) for rows in (BLOCKS + 32, BLOCKS)]
    return launch(
        pack_more_kernel,
        "pack_more",
        1,
        1,
        info,
        (w_mlp, cotangent),
        [HBM] * 2,
        outs,
        [whole(x.shape) for x in outs],
        [pltpu.SemaphoreType.DMA((5,))],
        after,
        vmem=VMEM_MOST,
    )


def final_kernel(
    info,
    near,
    far,
    mine_ref,
    theirs_ref,
    pos_ref,
    frontier_ref,
    blocks_kept,
    blocks_got,
    query_ref,
    key_ref,
    value_ref,
    out_ref,
    front_ref,
    gain_attn_ref,
    gain_mlp_ref,
    rel_ref,
    blocks_ref,
    sems,
):
    mp, core, place = info[0], info[1], info[3]
    pairs = []
    mine, theirs = share_out(info)
    for index in range(2):
        pairs.append((blocks_kept.at[index], blocks_ref.at[mine[index]]))
        pairs.append((blocks_got.at[index], blocks_ref.at[theirs[index]]))
    copies = started(pairs, sems)
    for copy in copies:
        copy.start()
    for source, side in ((near, core), (far, 1 - core)):
        turned = []
        for shard in range(SHARDS):
            at = tile_at(lax.bitwise_xor(place, shard), 64)
            for index, target in enumerate((query_ref, key_ref, value_ref)):
                target[span_of(shard, 64), tile_at(side, 128)] = source[
                    at, span_of(index, 128)
                ].astype(F32)
            turned.append(source[at, 384:512])
        out_ref[tile_at(side, 128), :] = jnp.transpose(
            jnp.concatenate(turned, axis=0).astype(F32)
        )
    tiny = near[512:528, :].astype(F32) + far[512:528, :].astype(F32)
    gain_attn_ref[...] = tiny[0:1, :]
    gain_mlp_ref[...] = tiny[1:2, :]
    heads = jnp.where(mp == 0, tiny[8:12, 0:128], tiny[12:16, 0:128])
    rel_ref[...] = heads[:, 0:BUCKETS]
    frontier_kernel(info, mine_ref, theirs_ref, pos_ref, frontier_ref, front_ref)
    for copy in copies:
        copy.wait()


def finish(
    info, near, far, mine, theirs, positions, frontier, blocks_kept, blocks_got, after
):
    args = (near, far, mine, theirs, positions, frontier)
    square = jax.ShapeDtypeStruct((512, 256), F32)
    row = jax.ShapeDtypeStruct((1, 512), F32)
    outs = [square, square, square, jax.ShapeDtypeStruct((256, 512), F32)]
    outs += [jax.ShapeDtypeStruct(frontier.shape, F32), row, row]
    outs += [jax.ShapeDtypeStruct((4, BUCKETS), F32)]
    return launch(
        final_kernel,
        "finish",
        4,
        1,
        info,
        (*args, blocks_kept, blocks_got),
        [whole(x.shape) for x in args] + [ANY] * 2,
        outs + [jax.ShapeDtypeStruct((4,) + blocks_kept.shape[1:], BF16)],
        [whole(x.shape) for x in outs] + [HBM],
        [pltpu.SemaphoreType.DMA((4,))],
        after,
    )


def ff_place(info, near, far, shapes, after):
    return launch(
        place_kernel,
        "ff_place",
        4,
        1,
        info,
        (near, far),
        [whole(near.shape), whole(far.shape)],
        [jax.ShapeDtypeStruct(shape, F32) for shape in shapes],
        [whole(shape) for shape in shapes],
        (),
        after,
    )


def shards(
    devices,
    byte_states,
    frontier,
    lengths,
    gain_attn,
    w_query,
    w_key,
    w_value,
    w_attn_out,
    rel_bias,
    gain_mlp,
    w_hidden,
    w_mlp_out,
    cotangent,
):
    bits = devices.bit_length() - 1
    mp = lax.axis_index("mp").astype(jnp.int32)
    dp = lax.axis_index(("far", "near")).astype(jnp.int32)
    core = dp & 1
    way = (dp >> 1) & 1
    place = (((dp >> 1) & 1) << 2) | (((dp >> 2) & 1) << 1)
    info = jnp.concatenate((jnp.stack((mp, core, way, place)), lengths))

    def across(value):
        return lax.ppermute(value, "mp", [(0, 1), (1, 0)])

    def swap(value, bit):
        pairs = [(i, i ^ (1 << bit)) for i in range(devices)]
        return lax.ppermute(value, ("far", "near"), pairs)

    def swap_four(value, index):
        turn = ((index & 1) << 2) | ((index >> 1) << 1)
        return lax.ppermute(value, ("far", "near"), [(i, i ^ turn) for i in range(devices)])

    def rows(count):
        return ((count, 512), BF16)

    weights = (w_query, w_key, w_value, w_attn_out, w_hidden, w_mlp_out)
    rel_own = rel_bias.T
    first_sent = pack(weights, rel_own)
    first = across(first_sent)
    backward, collect = offset_tables()
    backward, collect = jnp.asarray(backward), jnp.asarray(collect, BF16)

    pooled_own, pooled_sent, positions, meta = pool_forward(
        info, frontier, byte_states, (first_sent,)
    )
    pooled_other = across(pooled_sent)
    (first,) = combine("meet", nothing, after=(pooled_sent,), through=(first,))
    second = swap(first, 1)
    mid_sent, cot_sent, cot_own = pack_more(info, w_mlp_out, cotangent, (pooled_sent,))

    strips = bias_strips(info, rel_own, first, backward, (cot_own,))
    second, mid_sent = combine(
        "meet", nothing, after=(pooled_other, strips), through=(second, mid_sent)
    )
    parts = (first, second, swap(first, 0), swap(second, 0))
    cot_other = across(cot_sent)
    mid_first = across(mid_sent)

    gain_attn_row = gain_attn.reshape(1, -1)
    gain_mlp_row = gain_mlp.reshape(1, -1)
    qkv, logs, att, middle, normed, joined, w_o = attention_forward(
        info,
        pooled_own,
        pooled_other,
        strips,
        gain_attn_row,
        gain_mlp_row,
        weights[:4],
        parts,
        (),
    )
    half = pooled_own.shape[0]
    normed = normed.reshape(half * BLOCKS, -1)
    middle = middle.reshape(half * BLOCKS, -1)

    result, back, near_keep, near_sent, mark = ff_call(
        info, normed, cot_own, cot_other, True, (w_hidden, w_mlp_out), ()
    )
    got_near = swap(near_sent, 0)
    (mid_first,) = combine("meet", nothing, after=(mark,), through=(mid_first,))
    blocks_kept, blocks_sent, grad_mid, far_keep, far_sent, gain_mid = ff_call(
        info,
        normed,
        cot_own,
        cot_other,
        False,
        (*parts, mid_first, swap(mid_first, 0), result, back, middle, gain_mlp_row),
        (),
    )
    near_low, near_high, far_sent = combine(
        "near_cores",
        sum_into,
        (near_keep, got_near),
        (rows(512), rows(528)),
        (gain_mid,),
        (far_sent,),
    )
    far_low, far_high, near_high = combine(
        "far_cores",
        sum_into,
        (far_keep, swap(far_sent, 0)),
        (rows(512), rows(512)),
        (),
        (near_high,),
    )
    got_far = swap(far_high, 1)
    blocks_other = across(blocks_sent)

    grad_mid = grad_mid.reshape(half, BLOCKS, -1)
    rows_args = (pooled_own, pooled_other, qkv, logs, att, grad_mid)
    grad_normed, far_keep, far_sent, far_rel = attention_back(
        info,
        False,
        rows_args,
        strips,
        collect,
        gain_attn_row,
        joined,
        w_o,
        (),
        (far_low,),
    )
    far_ff, far_sent, near_high = combine(
        "far_y", sum_into, (far_low, got_far), (rows(528),), (far_rel, blocks_other), (far_sent, near_high)
    )
    got_near = swap(near_high, 1)
    far_attn, far_ff = combine(
        "far_cores", sum_into, (far_keep, swap(far_sent, 0)), (rows(544),), (), (far_ff,)
    )
    got_attn = across(far_attn)
    got_far = across(far_ff)
    grad_keep, grad_sent, near_keep, near_even, near_odd, tiny = attention_back(
        info,
        True,
        rows_args,
        strips,
        collect,
        gain_attn_row,
        joined,
        w_o,
        (grad_normed, far_rel, gain_mid),
        (far_attn,),
    )
    grad_other = across(grad_sent)

    def step_zero(ins, outs):
        for index in range(4):
            for odd in range(2):
                at = span_of(index * 2 + odd, 64)
                total = ins[0][at, :].astype(F32) + ins[1 + odd][span_of(index, 64), :].astype(F32)
                outs[index][span_of(odd, 64), :] = (total + ins[3][at, :].astype(F32)).astype(BF16)
            outs[index][128:144, :] = ins[4][...].astype(BF16)

    attn_parts = combine(
        "step_zero",
        step_zero,
        (near_keep, swap(near_even, 0), swap(near_odd, 0), got_attn, tiny),
        (rows(144),) * 4,
        (got_near,),
    )
    got_attn = [swap_four(attn_parts[index], index) for index in range(1, 4)]

    def pool_item(mine, index, held, after, through=()):
        grads = grad_keep if mine else grad_other
        return pool_backward(
            info, meta, positions, byte_states, grads, mine, index, held, after, through
        )

    held = pool_item(True, 0, (), (attn_parts[0],))

    def step_one(ins, outs):
        sum_into(ins[:4], outs[:1])
        sum_into(ins[4:], outs[1:])

    attn, ff_low, ff_high = combine(
        "step_one",
        step_one,
        (attn_parts[0], *got_attn, near_low, got_near, got_far),
        (rows(144), rows(256), rows(256)),
        (held[1],),
    )
    for bit in range(4, bits):
        attn = (attn.astype(F32) + swap(attn, bit).astype(F32)).astype(BF16)
    got_attn, got_ff = swap(attn, 3), swap(ff_high, 2)

    def step_two(ins, outs):
        total = ins[0][...].astype(F32) + ins[1][...].astype(F32)
        outs[0][...] = total[0:128, :].astype(BF16)
        outs[1][...] = total[128:144, :].astype(BF16)
        sum_into(ins[2:], outs[2:])

    held = pool_item(True, 1, held, (attn,))
    attn, tiny, near_ff = combine(
        "step_two",
        step_two,
        (attn, got_attn, ff_low, got_ff),
        (rows(128), rows(16), rows(256)),
        (held[1],),
    )
    got_ff = swap(near_ff, 3)
    got_attn = [swap_four(attn, index) for index in range(1, 4)]
    got_tiny = across(tiny)

    def step_three(ins, outs):
        join_into(ins[:4], outs[0])
        sum_into(ins[4:6], [outs[0].at[512:528, :]])
        sum_into(ins[6:], outs[1:])

    held = pool_item(False, 0, held, (attn,))
    near_attn, near_ff = combine(
        "step_three",
        step_three,
        (attn, *got_attn, tiny, got_tiny, near_ff, got_ff),
        (rows(528), rows(256)),
        (held[1],),
    )
    for bit in range(4, bits):
        near_ff = (near_ff.astype(F32) + swap(near_ff, bit).astype(F32)).astype(BF16)
    got_ff = [swap_four(near_ff, index) for index in range(1, 4)]
    far_attn = swap(near_attn, 0)

    held = pool_item(False, 1, held, (near_attn, near_ff))
    grad_bytes, part = held
    part_other = across(part)
    (
        grad_query,
        grad_key,
        grad_value,
        grad_out,
        grad_frontier,
        grad_gain_attn,
        grad_gain_mlp,
        grad_rel,
        blocks_out,
    ) = finish(
        info,
        near_attn,
        far_attn,
        part,
        part_other,
        positions,
        frontier,
        blocks_kept,
        blocks_other,
        (),
    )

    def join(ins, outs):
        join_into(ins, outs[0])

    (near_ff,) = combine("step_four", join, (near_ff, *got_ff), (rows(1024),), (grad_gain_attn,))
    far_ff = swap(near_ff, 0)
    grad_hidden, grad_mlp, _ = ff_place(
        info, near_ff, far_ff, (w_hidden.shape, w_mlp_out.shape, (8, 128)), ()
    )
    return (
        blocks_out,
        grad_bytes,
        grad_frontier,
        grad_gain_attn.reshape(-1),
        grad_query,
        grad_key,
        grad_value,
        grad_out,
        grad_rel.T,
        grad_gain_mlp.reshape(-1),
        grad_hidden,
        grad_mlp,
    )


def solution(mesh):
    devices = mesh.shape["dp"]
    split = jax.sharding.Mesh(
        mesh.devices.reshape(devices // 4, 4, mesh.shape["mp"]), ("far", "near", "mp")
    )
    dp = ("far", "near")
    placed = (
        P(dp, None, "mp"),
        P(dp, None),
        P(dp),
        P(),
        P(None, "mp"),
        P(None, "mp"),
        P(None, "mp"),
        P("mp", None),
        P(None, "mp"),
        P(),
        P(None, "mp"),
        P("mp", None),
        P(dp, None, "mp"),
    )
    return jax.shard_map(
        functools.partial(shards, devices),
        mesh=split,
        in_specs=placed,
        out_specs=(
            P(dp, None, "mp"),
            P(dp, None, "mp"),
            P(dp, None),
            P(),
            P(None, "mp"),
            P(None, "mp"),
            P(None, "mp"),
            P("mp", None),
            P(None, "mp"),
            P(),
            P(None, "mp"),
            P("mp", None),
        ),
        check_vma=False,
    )
```

```python
import functools
import math

import jax
import jax.numpy as jnp
import numpy as np
from jax import lax
from jax.experimental import pallas as pl
from jax.experimental.pallas import tpu as pltpu
from jax.sharding import PartitionSpec as P

BUCKETS = 32
REACH = 128
BLOCKS = 512
WRAP = 2 * BLOCKS
SHARDS = 8

EPSILON = 1e-06
SHARPNESS = 2.0
MASKED_SCORE = -1000000000.0
OUTSIDE = -10000.0
REACH_OUT = 8.0
PRECISE = lax.Precision.HIGHEST
ROOT = 0.7978845608028654
CUBIC = 0.044715
VMEM_LIMIT = 24 * 1024 * 1024
VMEM_MOST = 60 * 1024 * 1024
CHUNK = 256
WINDOW = 128
SLOTS = 3

F32 = jnp.float32
BF16 = jnp.bfloat16
ANY = pl.BlockSpec(memory_space=pl.ANY)
HBM = pl.BlockSpec(memory_space=pltpu.HBM)
NEAR = pl.BlockSpec(memory_space=pltpu.VMEM)
SMEM = pl.BlockSpec(memory_space=pltpu.SMEM)
NN = (((1,), (0,)), ((), ()))
NT = (((1,), (1,)), ((), ()))
TN = (((0,), (0,)), ((), ()))


def mm(a, b, dims=NN):
    return lax.dot_general(a, b, dims, preferred_element_type=F32)


def bucket_of(offset):
    half_count = BUCKETS // 2
    exact_count = half_count // 2
    distance = abs(offset)
    if distance < exact_count:
        place = distance
    else:
        place = min(
            half_count - 1,
            exact_count
            + math.floor(
                math.log(distance / exact_count)
                / math.log(REACH / exact_count)
                * (half_count - exact_count)
            ),
        )
    return place + (half_count if offset > 0 else 0)


def offset_tables():
    backward = np.zeros((WRAP, BUCKETS), np.float32)
    collect = np.zeros((WRAP, BUCKETS), np.float32)
    for offset in range(1 - BLOCKS, BLOCKS):
        bucket = bucket_of(offset)
        backward[(-offset) % WRAP, bucket] = 1.0
        collect[(384 - offset) % WRAP, bucket] = 1.0
    collect = np.concatenate([np.roll(collect, turn, axis=0) for turn in range(8)], axis=1)
    return backward.T, collect


def cost(micros):
    return pl.CostEstimate(flops=1, bytes_accessed=1, transcendentals=0)


def whole(shape):
    return pl.BlockSpec(shape, functools.partial(lambda n, i, info: (0,) * n, len(shape)))


def item(shape):
    return pl.BlockSpec(
        (1,) + shape, functools.partial(lambda n, i, info: (i,) + (0,) * n, len(shape))
    )


def launch(
    kernel, name, micros, grid, info, args, in_specs, outs, out_specs, scratch=(), after=(),
    through=(), aliases=None, vmem=VMEM_LIMIT,
):
    given, waits, passed, made = 1 + len(args), len(after), len(through), len(outs)

    def body(*refs):
        first = given + waits + passed
        kernel(*refs[:given], *refs[first : first + made], *refs[first + made + passed :])

    aliases = dict(aliases or {})
    for index in range(passed):
        aliases[given + waits + index] = made + index
    return pl.pallas_call(
        body,
        grid_spec=pltpu.PrefetchScalarGridSpec(
            num_scalar_prefetch=1,
            grid=(grid,),
            in_specs=list(in_specs) + [ANY] * (waits + passed),
            out_specs=list(out_specs) + [ANY] * passed,
            scratch_shapes=list(scratch),
        ),
        out_shape=list(outs) + [jax.ShapeDtypeStruct(x.shape, x.dtype) for x in through],
        input_output_aliases=aliases,
        compiler_params=pltpu.CompilerParams(
            vmem_limit_bytes=vmem, dimension_semantics=("arbitrary",)
        ),
        cost_estimate=cost(micros),
        name=name,
    )(info, *args, *after, *through)


def combine(name, work, args=(), outs=(), after=(), through=()):
    given, held, made, passed = len(args), len(args) + len(after), len(outs), len(through)

    def kernel(*refs):
        work(refs[:given], refs[held + passed : held + passed + made])

    near = pl.BlockSpec(memory_space=pltpu.VMEM)
    return pl.pallas_call(
        kernel,
        in_specs=[near] * given + [ANY] * (len(after) + passed),
        out_specs=[near] * made + [ANY] * passed,
        out_shape=[jax.ShapeDtypeStruct(*out) for out in outs]
        + [jax.ShapeDtypeStruct(x.shape, x.dtype) for x in through],
        input_output_aliases={held + index: made + index for index in range(passed)},
        compiler_params=pltpu.CompilerParams(vmem_limit_bytes=16 * 1024 * 1024),
        cost_estimate=cost(1),
        name=name,
    )(*args, *after, *through)


def nothing(ins, outs):
    pass


def sum_into(ins, outs):
    at = 0
    for out in outs:
        count = min(out.shape[0], ins[0].shape[0] - at)
        rows = slice(at, at + count)
        value = ins[0][rows, :].astype(F32)
        for other in ins[1:]:
            value = value + other[rows, :].astype(F32)
        out[0:count, :] = value.astype(out.dtype)
        if out.shape[0] > count:
            out[count:, :] = jnp.zeros((out.shape[0] - count, out.shape[1]), out.dtype)
        at += count


def join_into(ins, out):
    at = 0
    for source in ins:
        out[at : at + source.shape[0], :] = source[...]
        at += source.shape[0]


def share_out(info):
    lengths = [info[4 + item] for item in range(4)]
    ranks = []
    for item in range(4):
        rank = jnp.int32(0)
        for other in range(4):
            if other != item:
                before = lengths[other] <= lengths[item] if other < item else (
                    lengths[other] < lengths[item]
                )
                rank = rank + jnp.where(before, 1, 0)
        ranks.append(rank)

    def at(wanted):
        found = jnp.int32(0)
        for item in range(1, 4):
            found = jnp.where(ranks[item] == wanted, item, found)
        return found

    sides = ((at(3), at(0)), (at(2), at(1)))
    first = info[0] == 0
    mine = [jnp.where(first, a, b) for a, b in zip(*sides)]
    theirs = [jnp.where(first, b, a) for a, b in zip(*sides)]
    return mine, theirs


def item_count(info, index):
    mine = share_out(info)[0]
    item = mine[index] if isinstance(index, int) else jnp.where(index == 0, mine[0], mine[1])
    return lax.shift_right_logical(info[4 + item] + 3, 2)


def fetch_bytes(bytes_ref, buffer, sems, item, slot):
    return pltpu.make_async_copy(bytes_ref.at[item], buffer.at[slot], sems.at[slot])


def window_kernel(row, first, skipped):
    line = lax.broadcasted_iota(jnp.int32, (WINDOW, CHUNK), 0)
    offset = row - ((line + first).astype(F32) + 0.5)
    kernel = jnp.exp(-SHARPNESS * offset * offset)
    if skipped is not None:
        kernel = jnp.where(line >= skipped, kernel, 0.0)
    return kernel, offset


def chunk_row(pos_ref, item, chunk):
    return pos_ref[pl.ds(item, 1), tile_at(chunk, CHUNK)]


def pool_rows(item, info, meta, pos_ref, buffer, out_ref, acc):
    length = info[4 + item]
    acc[...] = jnp.zeros_like(acc)

    def add(chunk, first, skipped):
        first = pl.multiple_of(first, 16)
        kernel = window_kernel(chunk_row(pos_ref, item, chunk), first, skipped)[0]
        acc[pl.ds(first, WINDOW), :] += mm(
            kernel.astype(BF16), buffer[tile_at(chunk, CHUNK), :]
        )

    def two(pair, carry):
        for chunk in (pair * 2, pair * 2 + 1):
            add(chunk, meta[item, chunk], None)
        for chunk in (pair * 2, pair * 2 + 1):

            @pl.when(meta[4 + item, chunk] > 1)
            def _():
                def more(window, carry):
                    wanted = meta[item, chunk] + window * WINDOW
                    first = jnp.minimum(wanted, BLOCKS - WINDOW)
                    add(chunk, first, wanted - first)
                    return carry

                lax.fori_loop(1, meta[4 + item, chunk], more, 0)

        return carry

    lax.fori_loop(0, lax.div(length + 2 * CHUNK - 1, 2 * CHUNK), two, 0)
    count = lax.shift_right_logical(length + 3, 2)
    live = lax.broadcasted_iota(jnp.int32, acc.shape, 0) < count
    out_ref[...] = jnp.where(live, acc[...], 0.0).astype(BF16)


def find_windows(pos_ref, meta_ref):
    lane = lax.broadcasted_iota(jnp.int32, (4, 128), 1)
    starts = jnp.zeros((4, 128), jnp.int32)
    counts = jnp.ones((4, 128), jnp.int32)
    for chunk in range(pos_ref.shape[1] // CHUNK):
        rows = pos_ref[:, span_of(chunk, CHUNK)]
        low = jnp.min(jnp.where(rows < 0.0, 1e6, rows), axis=1, keepdims=True)
        high = jnp.max(rows, axis=1, keepdims=True)
        start = jnp.clip(low - REACH_OUT, 0.0, float(BLOCKS - WINDOW)).astype(jnp.int32)
        start = lax.shift_left(lax.shift_right_logical(start, 4), 4)
        last = jnp.clip(high + REACH_OUT, 0.0, float(BLOCKS - 1)).astype(jnp.int32)
        count = lax.shift_right_arithmetic(last - start, 7) + 1
        starts = jnp.where(lane == chunk, start, starts)
        counts = jnp.where(lane == chunk, jnp.maximum(count, 1), counts)
    meta_ref[0:4, :] = starts
    meta_ref[4:8, :] = counts


def masked_positions(info, frontier_ref, pos_ref):
    items, byte_count = frontier_ref.shape
    lane = lax.broadcasted_iota(jnp.int32, (items, byte_count), 1)
    row = lax.broadcasted_iota(jnp.int32, (items, byte_count), 0)
    length = jnp.zeros((items, byte_count), jnp.int32)
    for item in range(items):
        length = jnp.where(row == item, info[4 + item], length)
    valid = lane < length
    running = jnp.where(valid, frontier_ref[...], 0.0)
    step = 1
    while step < byte_count:
        running = running + jnp.where(lane >= step, pltpu.roll(running, step, 1), 0.0)
        step *= 2
    count = lax.shift_right_logical(length + 3, 2).astype(F32)
    total = running[:, byte_count - 1 :]
    pos_ref[...] = jnp.where(valid, count * running / total, OUTSIDE)


def pool_own_kernel(
    info, frontier_ref, bytes_ref, out_ref, pos_ref, meta_ref, buffer, acc, meta, sems, meta_sem
):
    mine = share_out(info)[0]
    for slot, item in enumerate(mine):
        fetch_bytes(bytes_ref, buffer, sems, item, slot).start()
    masked_positions(info, frontier_ref, pos_ref)
    find_windows(pos_ref, meta_ref)
    copy = pltpu.make_async_copy(meta_ref, meta, meta_sem)
    copy.start()
    copy.wait()
    for slot, item in enumerate(mine):
        fetch_bytes(bytes_ref, buffer, sems, item, slot).wait()
        pool_rows(item, info, meta, pos_ref, buffer.at[slot], out_ref.at[slot], acc)


def pool_other_kernel(info, meta, pos_ref, bytes_ref, out_ref, buffer, acc, sems):
    theirs = share_out(info)[1]
    out_ref[2 * BLOCKS :, :] = jnp.zeros((64, out_ref.shape[1]), BF16)
    for slot, item in enumerate(theirs):
        fetch_bytes(bytes_ref, buffer, sems, item, slot).start()
    for slot, item in enumerate(theirs):
        fetch_bytes(bytes_ref, buffer, sems, item, slot).wait()
        rows = out_ref.at[span_of(slot, BLOCKS), :]
        pool_rows(item, info, meta, pos_ref, buffer.at[slot], rows, acc)


def pool_forward(info, frontier, byte_states, after):
    items, byte_count, share = byte_states.shape
    half = items // 2
    out = jax.ShapeDtypeStruct((half, BLOCKS, share), BF16)
    pos = jax.ShapeDtypeStruct((items, byte_count), F32)
    windows = jax.ShapeDtypeStruct((8, 128), jnp.int32)
    scratch = [pltpu.VMEM((half, byte_count, share), BF16), pltpu.VMEM((BLOCKS, share), F32)]
    own, positions, meta = launch(
        pool_own_kernel,
        "pool_own",
        7,
        1,
        info,
        (frontier, byte_states),
        [whole(pos.shape), HBM],
        [out, pos, windows],
        [whole(out.shape), whole(pos.shape), whole(windows.shape)],
        scratch
        + [
            pltpu.SMEM((8, 128), jnp.int32),
            pltpu.SemaphoreType.DMA((half,)),
            pltpu.SemaphoreType.DMA,
        ],
        after,
        vmem=VMEM_MOST,
    )
    sent = jax.ShapeDtypeStruct((half * BLOCKS + 64, share), BF16)
    (other,) = launch(
        pool_other_kernel,
        "pool_other",
        7,
        1,
        info,
        (meta, positions, byte_states),
        [SMEM, whole(pos.shape), HBM],
        [sent],
        [whole(sent.shape)],
        scratch + [pltpu.SemaphoreType.DMA((half,))],
        vmem=VMEM_MOST,
    )
    return own, other, positions, meta


def pool_back_kernel(mine, index, info, meta, pos_ref, bytes_ref, grads_ref, *refs):
    out_ref, part_ref, buffer, written, acc, sems, out_sems = refs[-7:]
    item = share_out(info)[0 if mine else 1][index]
    length = info[4 + item]
    grads = grads_ref.at[index] if mine else grads_ref.at[span_of(index, BLOCKS)]
    fetch = fetch_bytes(bytes_ref, buffer, sems, item, 0)
    fetch.start()
    pairs = lax.div(length + 2 * CHUNK - 1, 2 * CHUNK)
    size = 2 * CHUNK

    def written_copy(pair):
        rows = tile_at(pair, size)
        return pltpu.make_async_copy(
            written.at[rows, :], out_ref.at[item, rows, :], out_sems.at[pair]
        )

    def window(chunk, first, skipped):
        first = pl.multiple_of(first, 16)
        kernel, offset = window_kernel(chunk_row(pos_ref, item, chunk), first, skipped)
        rows = grads[pl.ds(first, WINDOW), :]
        slope = mm(rows, buffer[0, tile_at(chunk, CHUNK), :], NT)
        back = mm(kernel.astype(BF16), rows, TN)
        return back, jnp.sum(slope * kernel * offset, axis=0, keepdims=True)

    def two(pair, carry):
        for chunk in (pair * 2, pair * 2 + 1):
            back, terms = window(chunk, meta[item, chunk], None)
            written[tile_at(chunk, CHUNK), :] = back.astype(BF16)
            part_ref[0, :, tile_at(chunk, CHUNK)] = -4.0 * terms
        for chunk in (pair * 2, pair * 2 + 1):

            @pl.when(meta[4 + item, chunk] > 1)
            def _():
                acc[...] = jnp.zeros_like(acc)

                def more(number, total):
                    wanted = meta[item, chunk] + number * WINDOW
                    first = jnp.minimum(wanted, BLOCKS - WINDOW)
                    back, terms = window(chunk, first, wanted - first)
                    acc[...] += back
                    return total + terms

                total = lax.fori_loop(
                    0, meta[4 + item, chunk], more, jnp.zeros((1, CHUNK), F32)
                )
                written[tile_at(chunk, CHUNK), :] = acc[...].astype(BF16)
                part_ref[0, :, tile_at(chunk, CHUNK)] = -4.0 * total

        written_copy(pair).start()
        return carry

    def empty(pair, carry):
        written[tile_at(pair, size), :] = jnp.zeros((size, written.shape[1]), BF16)
        part_ref[0, :, tile_at(pair, size)] = jnp.zeros((1, size), F32)
        written_copy(pair).start()
        return carry

    every = written.shape[0] // size
    lax.fori_loop(pairs, every, empty, 0)
    fetch.wait()
    lax.fori_loop(0, pairs, two, 0)
    for pair in range(every):
        written_copy(pair).wait()


def pool_backward(info, meta, positions, byte_states, grads, mine, index, held, after, through):
    items, byte_count, share = byte_states.shape
    side = 0 if mine else 1
    return launch(
        functools.partial(pool_back_kernel, mine, index),
        "pool_back",
        5,
        1,
        info,
        (meta, positions, byte_states, grads) + tuple(held),
        [SMEM, whole((items, byte_count)), HBM, NEAR] + [HBM] * len(held),
        [
            jax.ShapeDtypeStruct((items, byte_count, share), BF16),
            jax.ShapeDtypeStruct((items, 1, byte_count), F32),
        ],
        [
            HBM,
            pl.BlockSpec((1, 1, byte_count), lambda i, info: (share_out(info)[side][index], 0, 0)),
        ],
        [
            pltpu.VMEM((1, byte_count, share), BF16),
            pltpu.VMEM((byte_count, share), BF16),
            pltpu.VMEM((CHUNK, share), F32),
            pltpu.SemaphoreType.DMA((1,)),
            pltpu.SemaphoreType.DMA((byte_count // (2 * CHUNK),)),
        ],
        after,
        through,
        {5: 0, 6: 1} if held else None,
    )


def frontier_kernel(info, mine_ref, theirs_ref, pos_ref, frontier_ref, out_ref):
    items, byte_count = frontier_ref.shape
    lane = lax.broadcasted_iota(jnp.int32, (items, byte_count), 1)
    row = lax.broadcasted_iota(jnp.int32, (items, byte_count), 0)
    length = jnp.zeros((items, byte_count), jnp.int32)
    for item in range(items):
        length = jnp.where(row == item, info[4 + item], length)
    valid = lane < length
    total = jnp.sum(jnp.where(valid, frontier_ref[...], 0.0), axis=1, keepdims=True)
    terms = jnp.where(valid, mine_ref[:, 0, :] + theirs_ref[:, 0, :], 0.0)
    weighted = jnp.sum(terms * pos_ref[...], axis=1, keepdims=True)
    step = 1
    while step < byte_count:
        moved = pltpu.roll(terms, byte_count - step, 1)
        terms = terms + jnp.where(lane < byte_count - step, moved, 0.0)
        step *= 2
    count = lax.shift_right_logical(length + 3, 2).astype(F32)
    out_ref[...] = jnp.where(valid, (terms * count - weighted) / total, 0.0)


def strips_kernel(info, rel_ref, first_ref, table_ref, strips):
    core = info[1]
    parts = [first_ref[512:528, span_of(index, 128)].astype(F32) for index in range(3)]
    other = (parts[0] + parts[1] + parts[2])[0:4, 0:BUCKETS]
    rows = []
    for values in (rel_ref[...], other):
        turned = jnp.concatenate((values[2:4], values[0:2]), axis=0)
        rows.append(jnp.where(core == 0, values, turned))
    spread = lax.dot_general(
        jnp.concatenate(rows, axis=0),
        table_ref[...],
        NN,
        precision=PRECISE,
        preferred_element_type=F32,
    )
    for head in range(strips.shape[0]):
        row = jnp.broadcast_to(spread[head : head + 1, :], (8, WRAP))
        eight = pltpu.roll(row, 384, 1, stride=1, stride_axis=0)
        for group in range(16):
            turned = pltpu.roll(eight, 8 * group, 1) if group else eight
            strips[head, span_of(group, 8), :] = turned[:, :896]


def bias_strips(info, rel, first, table, after):
    return launch(
        strips_kernel,
        "bias_strips",
        2,
        1,
        info,
        (rel, first, table),
        [NEAR, NEAR, NEAR],
        [jax.ShapeDtypeStruct((8, 128, 896), F32)],
        [NEAR],
        (),
        after,
    )[0]


def gather_halves(info, target, own_ref, other_ref):
    target[:, tile_at(info[0], 256)] = own_ref[0]
    target[:, tile_at(1 - info[0], 256)] = other_ref[...]


def span_of(index, size):
    return slice(index * size, (index + 1) * size)


def tile_at(index, size):
    return pl.ds(pl.multiple_of(index * size, size), size)


def started(pairs, sems):
    return [
        pltpu.make_async_copy(source, target, sems.at[index])
        for index, (source, target) in enumerate(pairs)
    ]


def inverse_rms(values):
    return lax.rsqrt(jnp.mean(values * values, axis=1, keepdims=True) + EPSILON)


def triple(values):
    high = values.astype(BF16)
    rest = values - high.astype(F32)
    middle = rest.astype(BF16)
    return high, middle, (rest - middle.astype(F32)).astype(BF16)


def spare_lane(head):
    return (head // 2) * 4 + 64 * (1 - head % 2)


def strip_tiles(strips, head, half):
    return jnp.concatenate(
        [
            strips[head, :, (3 - tile) * 128 + half * 256 : (5 - tile) * 128 + half * 256]
            for tile in range(4)
        ],
        axis=0,
    )


def parts_by_lane(values, lead):
    spot = lax.broadcasted_iota(jnp.int32, values.shape, 1) & 3
    parts = [part.astype(F32) for part in triple(values)]
    found = jnp.where(spot == 1, parts[0], jnp.where(spot == 2, parts[1], parts[2]))
    return jnp.where(spot == 0, lead, found).astype(BF16)


def attention_kernel(
    info,
    own_ref,
    other_ref,
    strips,
    gain_attn_ref,
    gain_mlp_ref,
    w_query,
    w_key,
    w_value,
    w_out,
    part_a,
    part_b,
    part_c,
    part_d,
    qkv_ref,
    log_ref,
    att_ref,
    middle_ref,
    normed_ref,
    w_qkv,
    w_o,
    pooled,
    logs,
    scores,
):
    step = pl.program_id(0)
    mp, core, way = info[0], info[1], info[2]
    count = item_count(info, step)

    @pl.when(step == 0)
    def _():
        for part in range(2):
            start = core if part == 0 else 1 - core
            for index, weight in enumerate((w_query, w_key, w_value)):
                first = index * 512 + part * 128
                w_qkv[:, first : first + 128] = weight[:, tile_at(start, 128)]
            w_o[span_of(part, 128), :] = w_out[tile_at(start, 128), :]
        for part, sources in enumerate(((part_a, part_b), (part_c, part_d))):
            for side, source in enumerate(sources):
                turn = way if side == 0 else 1 - way
                for index in range(3):
                    first = index * 512 + 256 + part * 128
                    w_qkv[tile_at(turn, 256), first : first + 128] = source[
                        0:256, span_of(index, 128)
                    ]
                rows = pl.ds(pl.multiple_of(256 + part * 128 + turn * 64, 64), 64)
                for lane in range(4):
                    w_o[rows, span_of(lane, 128)] = source[span_of(lane, 64), 384:512]
        logs[...] = jnp.zeros_like(logs)

    gather_halves(info, pooled, own_ref, other_ref)
    wide = pooled[...].astype(F32)
    normed = (wide * inverse_rms(wide) * gain_attn_ref[...]).astype(BF16)
    qkv_ref[0] = mm(normed, w_qkv[...]).astype(BF16)
    lane = lax.broadcasted_iota(jnp.int32, (BLOCKS, 128), 1)
    row = lax.broadcasted_iota(jnp.int32, (BLOCKS, 128), 0)
    dead = jnp.where(row < count, 0.0, MASKED_SCORE).astype(BF16)

    ready, found, tops = {}, {}, {}

    def prepare(pair):
        queries = qkv_ref[0, :, span_of(pair, 128)]
        keys = qkv_ref[0, :, span_of(pair + 4, 128)]
        values = qkv_ref[0, :, span_of(pair + 8, 128)]
        for side in range(2):
            own = (lane < 64) == (side == 0)
            spare = lane == 64 * (1 - side)
            chosen = jnp.where(own, queries, jnp.where(spare, 1.0, 0.0).astype(BF16))
            masked = jnp.where(spare, dead, keys)
            summing = jnp.transpose(jnp.where(own, values, jnp.ones_like(values)))
            ready[pair, side] = (chosen, masked, summing)

    def first_pass(slot, pair, half, side):
        chosen, masked, _ = ready[pair, side]
        held = scores.at[slot]
        raw = mm(masked, chosen[span_of(half, 256), :], NT)
        most = None
        for tile in range(4):
            first = (3 - tile) * 128 + half * 256
            part = raw[span_of(tile, 128), :] + strips[pair * 2 + side, :, first : first + 256]
            held[span_of(tile, 128), :] = part
            part = jnp.max(part.reshape(16, 8, 256), axis=0)
            most = part if most is None else jnp.maximum(most, part)
        tops[slot] = jnp.max(most, axis=0, keepdims=True)

    def second_pass(slot, pair, half, side):
        held = scores.at[slot]
        most = tops[slot]
        expo = jnp.concatenate(
            [jnp.exp(held[span_of(tile, 128), :] - most).astype(BF16) for tile in range(4)],
            axis=0,
        )
        out = mm(ready[pair, side][2], expo)
        other = 64 * (1 - side)
        total = out[other : other + 1, :]
        found[side] = (out * (1.0 / total))[64 * side : 64 * side + 64, :]
        place = pair * 4 + other
        logs[place : place + 4, span_of(half, 256)] = jnp.broadcast_to(
            most + jnp.log(total), (4, 256)
        )
        if side == 1:
            both = jnp.concatenate((found[0], found[1]), axis=0).astype(BF16)
            att_ref[0, span_of(half, 256), span_of(pair, 128)] = jnp.transpose(both)

    chains = [(pair, half, side) for pair in range(4) for half in range(2) for side in range(2)]
    for index, chain in enumerate(chains):
        if index % 4 == 0:
            prepare(chain[0])
        first_pass(index % SLOTS, *chain)
        if index >= SLOTS - 1:
            last = index - SLOTS + 1
            second_pass(last % SLOTS, *chains[last])
    for last in range(len(chains) - SLOTS + 1, len(chains)):
        second_pass(last % SLOTS, *chains[last])
    log_ref[0] = parts_by_lane(-jnp.transpose(logs[...]), 1.0)

    mid = wide + mm(att_ref[0], w_o[...])
    middle_ref[0] = mid
    normed_ref[0] = (mid * inverse_rms(mid) * gain_mlp_ref[...]).astype(BF16)


def attention_forward(info, own, other, strips, gain_attn, gain_mlp, weights, parts, after):
    half = own.shape[0]
    return launch(
        attention_kernel,
        "attention_forward",
        20,
        half,
        info,
        (own, other, strips, gain_attn, gain_mlp, *weights, *parts),
        [
            item((BLOCKS, 256)),
            pl.BlockSpec((BLOCKS, 256), lambda i, info: (i, 0)),
            NEAR,
            whole((1, 512)),
            whole((1, 512)),
        ]
        + [NEAR] * 8,
        [
            jax.ShapeDtypeStruct((half, BLOCKS, 1536), BF16),
            jax.ShapeDtypeStruct((half, BLOCKS, 128), BF16),
            jax.ShapeDtypeStruct((half, BLOCKS, 512), BF16),
            jax.ShapeDtypeStruct((half, BLOCKS, 512), F32),
            jax.ShapeDtypeStruct((half, BLOCKS, 512), BF16),
            jax.ShapeDtypeStruct((512, 1536), BF16),
            jax.ShapeDtypeStruct((512, 512), BF16),
        ],
        [
            item((BLOCKS, 1536)),
            item((BLOCKS, 128)),
            item((BLOCKS, 512)),
            item((BLOCKS, 512)),
            item((BLOCKS, 512)),
            whole((512, 1536)),
            whole((512, 512)),
        ],
        [
            pltpu.VMEM((BLOCKS, 512), BF16),
            pltpu.VMEM((128, BLOCKS), F32),
            pltpu.VMEM((SLOTS, BLOCKS, 256), F32),
        ],
        after,
    )


def gelu_and_slope(pre):
    square = pre * pre
    tanh = jnp.tanh(pre * (ROOT + (ROOT * CUBIC) * square))
    up = 0.5 + 0.5 * tanh
    act = pre * up
    slope = up + act * (1.0 - up) * (2.0 * ROOT + (6.0 * ROOT * CUBIC) * square)
    return act, slope


def ff_piece(normed, turned, top, turned_top, hid, mid, acts, grads, result, back, start):
    for half in range(2):
        rows = span_of(half, BLOCKS)
        act, slope = gelu_and_slope(mm(normed[rows, :], hid))
        acts[rows, :] = act.astype(BF16)
        grads[rows, :] = (mm(top[rows, :], mid, NT) * slope).astype(BF16)
        new_result = mm(acts[rows, :], mid)
        new_back = mm(grads[rows, :], hid, NT)
        if start is None:
            result[rows, :] += new_result
            back[rows, :] += new_back
        elif start:
            result[rows, :] = start[0][rows, :] + new_result
            back[rows, :] = start[1][rows, :] + new_back
        else:
            result[rows, :] = new_result
            back[rows, :] = new_back
    return mm(turned[...], grads[...]), mm(turned_top[...], acts[...])


def store_shards(place, target, first, values):
    rows = values.shape[0] // SHARDS
    size = target.shape[0] // SHARDS
    for shard in range(SHARDS):
        at = pl.multiple_of(lax.bitwise_xor(place, shard) * size + first, 64)
        target[pl.ds(at, rows), :] = values[span_of(shard, rows), :].astype(BF16)


def gather_top(info, top, turned_top, cot_own_ref, cot_other_ref):
    for index in range(2):
        rows = span_of(index, BLOCKS)
        count = item_count(info, index)
        live = lax.broadcasted_iota(jnp.int32, (BLOCKS, 256), 0) < count
        zero = jnp.zeros((BLOCKS, 256), BF16)
        top[rows, tile_at(info[0], 256)] = jnp.where(live, cot_own_ref[index], zero)
        top[rows, tile_at(1 - info[0], 256)] = jnp.where(live, cot_other_ref[index], zero)
        turned_top[:, rows] = jnp.transpose(top[rows, :])


def ff_own_kernel(
    info,
    normed_ref,
    cot_own_ref,
    cot_other_ref,
    w_hidden,
    w_mlp,
    result,
    back,
    keep_ref,
    send_ref,
    mark,
    top,
    turned_top,
    turned,
    acts,
    grads,
):
    core, place = info[1], info[3]
    mark[...] = jnp.zeros_like(mark)
    gather_top(info, top, turned_top, cot_own_ref, cot_other_ref)
    for index in range(2):
        turned[:, span_of(index, BLOCKS)] = jnp.transpose(normed_ref[span_of(index, BLOCKS), :])
    for part, target in ((1, send_ref), (0, keep_ref)):
        start = core if part == 0 else 1 - core
        grad_hid, grad_mid = ff_piece(
            normed_ref,
            turned,
            top,
            turned_top,
            w_hidden[:, tile_at(start, 512)],
            w_mlp[tile_at(start, 512), :],
            acts,
            grads,
            result,
            back,
            () if part == 1 else None,
        )
        store_shards(place, target, 0, grad_hid)
        store_shards(place, target, 64, grad_mid)


def ff_other_kernel(
    info,
    normed_ref,
    cot_own_ref,
    cot_other_ref,
    hid_a,
    hid_b,
    hid_c,
    hid_d,
    mid_near,
    mid_far,
    result_ref,
    back_ref,
    middle_ref,
    gain_ref,
    blocks_keep,
    blocks_send,
    grad_mid_ref,
    keep_ref,
    send_ref,
    gain_out,
    top,
    turned_top,
    turned,
    acts,
    grads,
    weights,
    result,
    back,
    blocks,
):
    mp, way, place = info[0], info[2], info[3]
    for part, sources in ((1, (hid_c, hid_d)), (0, (hid_a, hid_b))):
        for side, source in enumerate(sources):
            turn = way if side == 0 else 1 - way
            weights[part, tile_at(turn, 256), :] = source[256:512, :]
    gather_top(info, top, turned_top, cot_own_ref, cot_other_ref)
    for index in range(2):
        turned[:, span_of(index, BLOCKS)] = jnp.transpose(normed_ref[span_of(index, BLOCKS), :])
    for part, target in ((1, send_ref), (0, keep_ref)):
        grad_hid, grad_mid = ff_piece(
            normed_ref,
            turned,
            top,
            turned_top,
            weights[part],
            (mid_far if part == 1 else mid_near)[...],
            acts,
            grads,
            result,
            back,
            (result_ref, back_ref) if part == 1 else None,
        )
        store_shards(place, target, 0, grad_hid)
        store_shards(place, target, 64, grad_mid)

    new_gain = jnp.zeros((1, 512), F32)
    for index in range(2):
        rows = span_of(index, BLOCKS)
        count = item_count(info, index)
        live = lax.broadcasted_iota(jnp.int32, (BLOCKS, 1), 0) < count
        middle = middle_ref[rows, :]
        blocks[...] = jnp.where(live, middle + result[rows, :], 0.0).astype(BF16)
        blocks_keep[index] = blocks[:, tile_at(mp, 256)]
        blocks_send[index] = blocks[:, tile_at(1 - mp, 256)]
        scale = inverse_rms(middle)
        unit = middle * scale
        grad_normed = back[rows, :]
        scaled = grad_normed * gain_ref[...]
        grad_mid_ref[rows, :] = top[rows, :].astype(F32) + scale * (
            scaled - unit * jnp.mean(scaled * unit, axis=1, keepdims=True)
        )
        new_gain = new_gain + jnp.sum(grad_normed * unit, axis=0, keepdims=True)
    gain_out[...] = jnp.broadcast_to(new_gain, gain_out.shape)


def ff_call(info, normed, cot, cot_other, mine, given, after):
    rows = normed.shape[0]
    half = rows // BLOCKS
    packed = (SHARDS * 128, 512)
    wide = jax.ShapeDtypeStruct((rows, 512), F32)
    pack = jax.ShapeDtypeStruct(packed, BF16)
    share = jax.ShapeDtypeStruct((half, BLOCKS, 256), BF16)
    in_specs = [whole((rows, 512)), whole(share.shape), whole(share.shape)]
    scratch = [
        pltpu.VMEM((rows, 512), BF16),
        pltpu.VMEM((512, rows), BF16),
        pltpu.VMEM((512, rows), BF16),
        pltpu.VMEM((rows, 512), BF16),
        pltpu.VMEM((rows, 512), BF16),
    ]
    if mine:
        in_specs += [NEAR] * 2
        outs = [wide, wide, pack, pack, jax.ShapeDtypeStruct((8, 128), F32)]
    else:
        in_specs += [NEAR] * 8 + [whole((rows, 512)), whole((1, 512))]
        outs = [share, share, wide, pack, pack, jax.ShapeDtypeStruct((8, 512), F32)]
        scratch += [
            pltpu.VMEM((2, 512, 512), BF16),
            pltpu.VMEM((rows, 512), F32),
            pltpu.VMEM((rows, 512), F32),
            pltpu.VMEM((BLOCKS, 512), BF16),
        ]
    return launch(
        ff_own_kernel if mine else ff_other_kernel,
        "ff_own" if mine else "ff_other",
        12,
        1,
        info,
        (normed, cot, cot_other, *given),
        in_specs,
        outs,
        [whole(x.shape) for x in outs],
        scratch,
        after,
    )


def attention_back_body(
    info,
    first_head,
    own_ref,
    other_ref,
    query_ref,
    key_ref,
    value_ref,
    log_ref,
    att_ref,
    grad_mid_ref,
    strips,
    collect_ref,
    gain_attn_ref,
    wq_ref,
    wk_ref,
    wv_ref,
    wo_ref,
    keep_ref,
    send_ref,
    pooled,
    outer,
    grads,
    sums,
    turned,
    turned_branch,
    atts,
    probs,
    weights,
    scored,
):
    step = pl.program_id(0)
    mp, place = info[0], info[3]
    count = item_count(info, step)

    @pl.when(step == 0)
    def _():
        sums[...] = jnp.zeros_like(sums)

    gather_halves(info, pooled, own_ref, other_ref)
    here = tile_at(step, BLOCKS)
    branch = grad_mid_ref[0].astype(BF16)
    outer[...] = mm(branch, wo_ref[...], NT).astype(BF16)
    lane = lax.broadcasted_iota(jnp.int32, (BLOCKS, 128), 1)
    row = lax.broadcasted_iota(jnp.int32, (BLOCKS, 128), 0)
    dead = jnp.where(row < count, 0.0, MASKED_SCORE).astype(BF16)
    line = lax.broadcasted_iota(jnp.int32, (1, 128), 1)
    deltas = jnp.zeros((BLOCKS, 128), F32)
    for pair in range(2):
        span = span_of(pair, 128)
        overlap = outer[:, span].astype(F32) * att_ref[0, :, span].astype(F32)
        for side in range(2):
            own = (lane < 64) == (side == 0)
            delta = jnp.sum(jnp.where(own, overlap, 0.0), axis=1, keepdims=True)
            spare = spare_lane(first_head + pair * 2 + side)
            mine = jnp.logical_and(lane >= spare, lane < spare + 4)
            deltas = jnp.where(mine, delta, deltas)
    deltas = parts_by_lane(-deltas, 0.0)

    ready, found = {}, {}

    def prepare(pair):
        span = span_of(pair, 128)
        queries = query_ref[0, :, span]
        keys = key_ref[0, :, span]
        values = value_ref[0, :, span]
        out_grads = outer[:, span]
        ready[pair] = jnp.transpose(keys)
        for side in range(2):
            own = (lane < 64) == (side == 0)
            spare = spare_lane(first_head + pair * 2 + side)
            added = jnp.logical_and(line > spare, line < spare + 4)
            ones = jnp.where(added, 1.0, 0.0).astype(BF16)
            chosen = jnp.where(own, queries, log_ref[0])
            masked = jnp.where(own, keys, jnp.where(lane == spare, dead, ones))
            drawn = jnp.where(own, out_grads, deltas)
            weighed = jnp.where(own, values, ones)
            ready[pair, side] = (chosen, masked, drawn, weighed)

    def first_pass(slot, pair, side, half):
        chosen, masked, _, _ = ready[pair, side]
        raw = mm(masked, chosen[span_of(half, 256), :], NT)
        for tile in range(4):
            first = (3 - tile) * 128 + half * 256
            rows = span_of(tile, 128)
            part = jnp.exp(
                raw[rows, :] + strips[first_head + pair * 2 + side, :, first : first + 256]
            )
            probs[slot, rows, :] = part
            weights[slot, rows, :] = part.astype(BF16)

    def second_pass(slot, pair, side, half):
        _, _, drawn, weighed = ready[pair, side]
        head = pair * 2 + side
        slope = mm(weighed, drawn[span_of(half, 256), :], NT)
        product = [probs[slot, span_of(tile, 128), :] * slope[span_of(tile, 128), :] for tile in range(4)]
        for tile in range(4):
            scored[slot, span_of(tile, 128), :] = product[tile].astype(BF16)
        for diagonal in range(5):
            first = (3 - diagonal + 1) * 128 + half * 256
            total = None
            for tile in range(4):
                column = tile - diagonal + 1
                if 0 <= column < 2:
                    block = product[tile][:, span_of(column, 128)]
                    total = block if total is None else total + block
            sums[head, :, first : first + 128] += total

    def third_pass(slot, pair, side, half):
        span = span_of(pair, 128)
        rows = span_of(half, 256)
        turned_query = mm(ready[pair], scored[slot])
        grad_key = mm(scored[slot], query_ref[0, rows, span])
        grad_value = mm(weights[slot], outer[rows, span])
        if half == 0:
            found[side] = ([turned_query], grad_key, grad_value)
        else:
            before = found[side]
            found[side] = (
                before[0] + [turned_query],
                before[1] + grad_key,
                before[2] + grad_value,
            )
        if side == 1 and half == 1:
            for index in range(2):
                both = jnp.concatenate(
                    (found[0][0][index][0:64, :], found[1][0][index][64:128, :]), axis=0
                ).astype(BF16)
                grads[
                    pl.ds(pl.multiple_of(step * BLOCKS + index * 256, 256), 256), span
                ] = jnp.transpose(both)
            for index in range(1, 3):
                first = index * 256 + pair * 128
                grads[here, first : first + 128] = jnp.where(
                    lane < 64, found[0][index], found[1][index]
                ).astype(BF16)

    units = [(pair, side, half) for pair in range(2) for side in range(2) for half in range(2)]
    for index in range(len(units) + 2):
        if index < len(units):
            if index % 4 == 0:
                prepare(units[index][0])
            first_pass(index % 4, *units[index])
        if 1 <= index <= len(units):
            second_pass((index - 1) % 4, *units[index - 1])
        if index >= 2:
            third_pass((index - 2) % 4, *units[index - 2])

    wide = pooled[...].astype(F32)
    scale = inverse_rms(wide)
    unit = wide * scale
    normed = (unit * gain_attn_ref[...]).astype(BF16)
    turned[:, here] = jnp.transpose(normed)
    turned_branch[:, here] = jnp.transpose(branch)
    atts[here, :] = att_ref[0]

    @pl.when(step == 1)
    def _():
        new = mm(turned[...], grads[...])
        new_out = mm(turned_branch[...], atts[...])
        for part, targets in ((1, send_ref), (0, keep_ref)):
            for shard in range(SHARDS):
                at = lax.bitwise_xor(place, shard)
                if isinstance(targets, tuple):
                    target, at = targets[shard % 2], lax.shift_right_logical(at, 1)
                else:
                    target = targets
                at = tile_at(at, 64)
                here_rows = span_of(shard, 64)
                for index in range(3):
                    first = index * 256 + part * 128
                    target[at, span_of(index, 128)] = new[here_rows, first : first + 128].astype(
                        BF16
                    )
                target[at, 384:512] = new_out[here_rows, span_of(part, 128)].astype(BF16)

    grad_normed = (
        mm(grads[here, 0:256], wq_ref[...], NT)
        + mm(grads[here, 256:512], wk_ref[...], NT)
        + mm(grads[here, 512:768], wv_ref[...], NT)
    )
    return unit, scale, grad_normed


def fold_bias(sums, collect_ref):
    rows = []
    for head in range(4):
        folded = jnp.concatenate((sums[head], jnp.zeros((128, 128), F32)), axis=1)
        size = 64
        while size >= 8:
            folded = folded[:size] + pltpu.roll(folded[size : 2 * size], WRAP - size, 1)
            size //= 2
        rows.append(folded)
    lines = jnp.concatenate(triple(jnp.concatenate(rows, axis=0)), axis=0)
    found = mm(lines, collect_ref[...])
    found = found[0:32] + found[32:64] + found[64:96]
    row = lax.broadcasted_iota(jnp.int32, found.shape, 0) & 7
    spot = lax.shift_right_logical(lax.broadcasted_iota(jnp.int32, found.shape, 1), 5)
    found = jnp.where(row == spot, found, 0.0)
    rows = []
    for head in range(4):
        total = jnp.sum(found[span_of(head, 8), :], axis=0, keepdims=True)
        total = total[:, 0:128] + total[:, 128:256]
        total = total + pltpu.roll(total, 64, 1)
        rows.append(total + pltpu.roll(total, 32, 1))
    return jnp.concatenate(rows + rows, axis=0)


def attention_back_first_kernel(info, *refs):
    heads, (grad_ref, keep_ref, send_ref, rel_ref), scratch = refs[:15], refs[15:19], refs[19:]
    _, _, grad_normed = attention_back_body(info, 4, *heads, keep_ref, send_ref, *scratch)
    grad_ref[0] = grad_normed

    @pl.when(pl.program_id(0) == 1)
    def _():
        rel_ref[...] = fold_bias(scratch[3], heads[9])


def attention_back_second_kernel(info, *refs):
    heads, (held_ref, rel_ref, gain_mid_ref), refs = refs[:15], refs[15:18], refs[18:]
    (keep_rows, send_rows, keep_ref, even_ref, odd_ref, tiny_ref), scratch = refs[:6], refs[6:]
    send_ref = (even_ref, odd_ref)
    scratch, acc_gain = scratch[:-1], scratch[-1]
    unit, scale, grad_normed = attention_back_body(info, 0, *heads, keep_ref, send_ref, *scratch)
    mp, core = info[0], info[1]
    step = pl.program_id(0)
    pooled = scratch[0]
    grad_normed = grad_normed + held_ref[0]
    scaled = grad_normed * heads[10][...]
    grad_pooled = heads[7][0] + scale * (
        scaled - unit * jnp.mean(scaled * unit, axis=1, keepdims=True)
    )
    pooled[...] = grad_pooled.astype(BF16)
    keep_rows[0] = pooled[:, tile_at(mp, 256)]
    send_rows[tile_at(step, BLOCKS), :] = pooled[:, tile_at(1 - mp, 256)]
    new_gain = jnp.sum(grad_normed * unit, axis=0, keepdims=True)

    @pl.when(step == 0)
    def _():
        acc_gain[...] = jnp.broadcast_to(new_gain, acc_gain.shape)

    @pl.when(step == 1)
    def _():
        found = fold_bias(scratch[3], heads[9])
        line = lax.broadcasted_iota(jnp.int32, (8, 128), 0)
        rows = jnp.zeros((8, 128), F32)
        for head in range(8):
            source = found if head < 4 else rel_ref[...]
            true_head = (
                lax.bitwise_xor(mp, head // 4) * 4
                + lax.bitwise_xor(core, (head // 2) % 2) * 2
                + head % 2
            )
            rows = jnp.where(line == true_head, source[head % 4 : head % 4 + 1, :], rows)
        tiny_ref[...] = jnp.zeros_like(tiny_ref)
        tiny_ref[0:1, :] = acc_gain[0:1, :] + new_gain
        tiny_ref[1:2, :] = gain_mid_ref[0:1, :]
        tiny_ref[8:16, 0:128] = rows


def attention_back(
    info, mine, rows_args, strips, collect, gain_attn, joined, w_o, given, after
):
    own, other, qkv, logs, att, grad_mid = rows_args
    half = own.shape[0]
    where = 0 if mine else 1

    def lanes(index):
        return pl.BlockSpec((1, BLOCKS, 256), lambda i, info: (i, 0, index))

    def columns(index):
        return pl.BlockSpec((512, 256), lambda i, info: (0, index))

    in_specs = [
        item((BLOCKS, 256)),
        pl.BlockSpec((BLOCKS, 256), lambda i, info: (i, 0)),
        lanes(where),
        lanes(2 + where),
        lanes(4 + where),
        item((BLOCKS, 128)),
        lanes(where),
        item((BLOCKS, 512)),
        NEAR,
        whole((WRAP, 256)),
        whole((1, 512)),
        columns(where),
        columns(2 + where),
        columns(4 + where),
        pl.BlockSpec((256, 512), lambda i, info: (where, 0)),
    ]
    args = [own, other, qkv, qkv, qkv, logs, att, grad_mid, strips, collect, gain_attn]
    args += [joined, joined, joined, w_o]
    packed = (SHARDS * 64, 512)
    pack = jax.ShapeDtypeStruct(packed, BF16)
    scratch = [
        pltpu.VMEM((BLOCKS, 512), BF16),
        pltpu.VMEM((BLOCKS, 256), BF16),
        pltpu.VMEM((half * BLOCKS, 768), BF16),
        pltpu.VMEM((4, 128, 896), F32),
        pltpu.VMEM((512, half * BLOCKS), BF16),
        pltpu.VMEM((512, half * BLOCKS), BF16),
        pltpu.VMEM((half * BLOCKS, 256), BF16),
        pltpu.VMEM((4, BLOCKS, 256), F32),
        pltpu.VMEM((4, BLOCKS, 256), BF16),
        pltpu.VMEM((4, BLOCKS, 256), BF16),
    ]
    if mine:
        share = jax.ShapeDtypeStruct((half, BLOCKS, 256), BF16)
        in_specs += [item((BLOCKS, 512)), whole((8, 128)), whole((8, 512))]
        sent = jax.ShapeDtypeStruct((half * BLOCKS, 256), BF16)
        few = (SHARDS * 32, 512)
        packs = [pack, jax.ShapeDtypeStruct(few, BF16), jax.ShapeDtypeStruct(few, BF16)]
        outs = [share, sent, *packs, jax.ShapeDtypeStruct((16, 512), F32)]
        out_specs = [item((BLOCKS, 256)), whole(sent.shape), whole(packed), whole(few), whole(few)]
        out_specs += [whole((16, 512))]
        scratch += [pltpu.VMEM((8, 512), F32)]
    else:
        outs = [
            jax.ShapeDtypeStruct((half, BLOCKS, 512), F32),
            pack,
            pack,
            jax.ShapeDtypeStruct((8, 128), F32),
        ]
        out_specs = [item((BLOCKS, 512)), whole(packed), whole(packed), whole((8, 128))]
    return launch(
        attention_back_second_kernel if mine else attention_back_first_kernel,
        "attention_back_own" if mine else "attention_back_other",
        17,
        half,
        info,
        (*args, *given),
        in_specs,
        outs,
        out_specs,
        scratch,
        after,
    )


def place_kernel(info, ff_near, ff_far, hid_ref, mid_ref, mark):
    mark[...] = jnp.zeros_like(mark)
    core, place = info[1], info[3]
    for source, side in ((ff_near, core), (ff_far, 1 - core)):
        turned = []
        for shard in range(SHARDS):
            at = lax.bitwise_xor(place, shard)
            at = at * 2
            hid_ref[span_of(shard, 64), tile_at(side, 512)] = source[tile_at(at, 64), :].astype(F32)
            turned.append(source[tile_at(at + 1, 64), :])
        mid_ref[tile_at(side, 512), :] = jnp.transpose(
            jnp.concatenate(turned, axis=0).astype(F32)
        )


def pack_kernel(wq, wk, wv, wo, wh, rel, out, sems):
    near = lax.axis_index("near")
    core, way = lax.rem(near, 2), lax.div(near, 2)
    rows = tile_at(way, 256)
    pairs = []
    for index, weight in enumerate((wq, wk, wv)):
        lanes = pl.ds(index * 128, 128)
        pairs.append((weight.at[rows, tile_at(core, 128)], out.at[pl.ds(0, 256), lanes]))
    few = pl.ds(pl.multiple_of(core * 128 + way * 64, 64), 64)
    for lane in range(4):
        pairs.append(
            (
                wo.at[few, pl.ds(lane * 128, 128)],
                out.at[pl.ds(lane * 64, 64), pl.ds(384, 128)],
            )
        )
    pairs.append((wh.at[rows, tile_at(core, 512)], out.at[pl.ds(256, 256), :]))
    copies = started(pairs, sems)
    for copy in copies:
        copy.start()
    out[512:528, :] = jnp.zeros((16, 512), BF16)
    for index, part in enumerate(triple(rel[...])):
        out[512:516, index * 128 : index * 128 + BUCKETS] = part
    for copy in copies:
        copy.wait()


def pack(weights, rel):
    return pl.pallas_call(
        pack_kernel,
        grid=(1,),
        in_specs=[HBM] * 5 + [pl.BlockSpec(rel.shape, lambda i: (0, 0))],
        out_specs=pl.BlockSpec((528, 512), lambda i: (0, 0)),
        out_shape=jax.ShapeDtypeStruct((528, 512), BF16),
        scratch_shapes=[pltpu.SemaphoreType.DMA((8,))],
        compiler_params=pltpu.CompilerParams(
            vmem_limit_bytes=VMEM_MOST, dimension_semantics=("arbitrary",)
        ),
        cost_estimate=cost(1),
        name="pack",
    )(*weights[:5], rel)


def pack_more_kernel(info, wm, cot, mid_out, cot_out, cot_own, sems):
    mine, theirs = share_out(info)
    pairs = [(wm.at[tile_at(info[1], 512), :], mid_out)]
    for index in range(2):
        pairs.append((cot.at[theirs[index]], cot_out.at[index, pl.ds(0, BLOCKS), :]))
        pairs.append((cot.at[mine[index]], cot_own.at[index]))
    copies = started(pairs, sems)
    for copy in copies:
        copy.start()
    cot_out[:, BLOCKS:, :] = jnp.zeros((2, 32, cot_out.shape[2]), BF16)
    for copy in copies:
        copy.wait()


def pack_more(info, w_mlp, cotangent, after):
    half, share = cotangent.shape[0] // 2, cotangent.shape[2]
    outs = [jax.ShapeDtypeStruct((512, 512), BF16)]
    outs += [jax.ShapeDtypeStruct((half, rows, share), BF16) for rows in (BLOCKS + 32, BLOCKS)]
    return launch(
        pack_more_kernel,
        "pack_more",
        1,
        1,
        info,
        (w_mlp, cotangent),
        [HBM] * 2,
        outs,
        [whole(x.shape) for x in outs],
        [pltpu.SemaphoreType.DMA((5,))],
        after,
        vmem=VMEM_MOST,
    )


def final_kernel(
    info,
    near,
    far,
    mine_ref,
    theirs_ref,
    pos_ref,
    frontier_ref,
    blocks_kept,
    blocks_got,
    query_ref,
    key_ref,
    value_ref,
    out_ref,
    front_ref,
    gain_attn_ref,
    gain_mlp_ref,
    rel_ref,
    blocks_ref,
    sems,
):
    mp, core, place = info[0], info[1], info[3]
    pairs = []
    mine, theirs = share_out(info)
    for index in range(2):
        pairs.append((blocks_kept.at[index], blocks_ref.at[mine[index]]))
        pairs.append((blocks_got.at[index], blocks_ref.at[theirs[index]]))
    copies = started(pairs, sems)
    for copy in copies:
        copy.start()
    for source, side in ((near, core), (far, 1 - core)):
        turned = []
        for shard in range(SHARDS):
            at = tile_at(lax.bitwise_xor(place, shard), 64)
            for index, target in enumerate((query_ref, key_ref, value_ref)):
                target[span_of(shard, 64), tile_at(side, 128)] = source[
                    at, span_of(index, 128)
                ].astype(F32)
            turned.append(source[at, 384:512])
        out_ref[tile_at(side, 128), :] = jnp.transpose(
            jnp.concatenate(turned, axis=0).astype(F32)
        )
    tiny = near[512:528, :].astype(F32) + far[512:528, :].astype(F32)
    gain_attn_ref[...] = tiny[0:1, :]
    gain_mlp_ref[...] = tiny[1:2, :]
    heads = jnp.where(mp == 0, tiny[8:12, 0:128], tiny[12:16, 0:128])
    rel_ref[...] = heads[:, 0:BUCKETS]
    frontier_kernel(info, mine_ref, theirs_ref, pos_ref, frontier_ref, front_ref)
    for copy in copies:
        copy.wait()


def finish(
    info, near, far, mine, theirs, positions, frontier, blocks_kept, blocks_got, after
):
    args = (near, far, mine, theirs, positions, frontier)
    square = jax.ShapeDtypeStruct((512, 256), F32)
    row = jax.ShapeDtypeStruct((1, 512), F32)
    outs = [square, square, square, jax.ShapeDtypeStruct((256, 512), F32)]
    outs += [jax.ShapeDtypeStruct(frontier.shape, F32), row, row]
    outs += [jax.ShapeDtypeStruct((4, BUCKETS), F32)]
    return launch(
        final_kernel,
        "finish",
        4,
        1,
        info,
        (*args, blocks_kept, blocks_got),
        [whole(x.shape) for x in args] + [ANY] * 2,
        outs + [jax.ShapeDtypeStruct((4,) + blocks_kept.shape[1:], BF16)],
        [whole(x.shape) for x in outs] + [HBM],
        [pltpu.SemaphoreType.DMA((4,))],
        after,
    )


def ff_place(info, near, far, shapes, after):
    return launch(
        place_kernel,
        "ff_place",
        4,
        1,
        info,
        (near, far),
        [whole(near.shape), whole(far.shape)],
        [jax.ShapeDtypeStruct(shape, F32) for shape in shapes],
        [whole(shape) for shape in shapes],
        (),
        after,
    )


def shards(
    devices,
    byte_states,
    frontier,
    lengths,
    gain_attn,
    w_query,
    w_key,
    w_value,
    w_attn_out,
    rel_bias,
    gain_mlp,
    w_hidden,
    w_mlp_out,
    cotangent,
):
    bits = devices.bit_length() - 1
    mp = lax.axis_index("mp").astype(jnp.int32)
    dp = lax.axis_index(("far", "near")).astype(jnp.int32)
    core = dp & 1
    way = (dp >> 1) & 1
    place = (((dp >> 1) & 1) << 2) | (((dp >> 2) & 1) << 1)
    info = jnp.concatenate((jnp.stack((mp, core, way, place)), lengths))

    def across(value):
        return lax.ppermute(value, "mp", [(0, 1), (1, 0)])

    def swap(value, bit):
        pairs = [(i, i ^ (1 << bit)) for i in range(devices)]
        return lax.ppermute(value, ("far", "near"), pairs)

    def swap_four(value, index):
        turn = ((index & 1) << 2) | ((index >> 1) << 1)
        return lax.ppermute(value, ("far", "near"), [(i, i ^ turn) for i in range(devices)])

    def rows(count):
        return ((count, 512), BF16)

    weights = (w_query, w_key, w_value, w_attn_out, w_hidden, w_mlp_out)
    rel_own = rel_bias.T
    first_sent = pack(weights, rel_own)
    first = across(first_sent)
    backward, collect = offset_tables()
    backward, collect = jnp.asarray(backward), jnp.asarray(collect, BF16)

    pooled_own, pooled_sent, positions, meta = pool_forward(
        info, frontier, byte_states, (first_sent,)
    )
    pooled_other = across(pooled_sent)
    (first,) = combine("meet", nothing, after=(pooled_sent,), through=(first,))
    second = swap(first, 1)
    mid_sent, cot_sent, cot_own = pack_more(info, w_mlp_out, cotangent, (pooled_sent,))

    strips = bias_strips(info, rel_own, first, backward, (cot_own,))
    second, mid_sent = combine(
        "meet", nothing, after=(pooled_other, strips), through=(second, mid_sent)
    )
    parts = (first, second, swap(first, 0), swap(second, 0))
    cot_other = across(cot_sent)
    mid_first = across(mid_sent)

    gain_attn_row = gain_attn.reshape(1, -1)
    gain_mlp_row = gain_mlp.reshape(1, -1)
    qkv, logs, att, middle, normed, joined, w_o = attention_forward(
        info,
        pooled_own,
        pooled_other,
        strips,
        gain_attn_row,
        gain_mlp_row,
        weights[:4],
        parts,
        (),
    )
    half = pooled_own.shape[0]
    normed = normed.reshape(half * BLOCKS, -1)
    middle = middle.reshape(half * BLOCKS, -1)

    result, back, near_keep, near_sent, mark = ff_call(
        info, normed, cot_own, cot_other, True, (w_hidden, w_mlp_out), ()
    )
    got_near = swap(near_sent, 0)
    (mid_first,) = combine("meet", nothing, after=(mark,), through=(mid_first,))
    blocks_kept, blocks_sent, grad_mid, far_keep, far_sent, gain_mid = ff_call(
        info,
        normed,
        cot_own,
        cot_other,
        False,
        (*parts, mid_first, swap(mid_first, 0), result, back, middle, gain_mlp_row),
        (),
    )
    near_low, near_high, far_sent = combine(
        "near_cores",
        sum_into,
        (near_keep, got_near),
        (rows(512), rows(528)),
        (gain_mid,),
        (far_sent,),
    )
    far_low, far_high, near_high = combine(
        "far_cores",
        sum_into,
        (far_keep, swap(far_sent, 0)),
        (rows(512), rows(512)),
        (),
        (near_high,),
    )
    got_far = swap(far_high, 1)
    blocks_other = across(blocks_sent)

    grad_mid = grad_mid.reshape(half, BLOCKS, -1)
    rows_args = (pooled_own, pooled_other, qkv, logs, att, grad_mid)
    grad_normed, far_keep, far_sent, far_rel = attention_back(
        info,
        False,
        rows_args,
        strips,
        collect,
        gain_attn_row,
        joined,
        w_o,
        (),
        (far_low,),
    )
    far_ff, far_sent, near_high = combine(
        "far_y", sum_into, (far_low, got_far), (rows(528),), (far_rel, blocks_other), (far_sent, near_high)
    )
    got_near = swap(near_high, 1)
    far_attn, far_ff = combine(
        "far_cores", sum_into, (far_keep, swap(far_sent, 0)), (rows(544),), (), (far_ff,)
    )
    got_attn = across(far_attn)
    got_far = across(far_ff)
    grad_keep, grad_sent, near_keep, near_even, near_odd, tiny = attention_back(
        info,
        True,
        rows_args,
        strips,
        collect,
        gain_attn_row,
        joined,
        w_o,
        (grad_normed, far_rel, gain_mid),
        (far_attn,),
    )
    grad_other = across(grad_sent)

    def step_zero(ins, outs):
        for index in range(4):
            for odd in range(2):
                at = span_of(index * 2 + odd, 64)
                total = ins[0][at, :].astype(F32) + ins[1 + odd][span_of(index, 64), :].astype(F32)
                outs[index][span_of(odd, 64), :] = (total + ins[3][at, :].astype(F32)).astype(BF16)
            outs[index][128:144, :] = ins[4][...].astype(BF16)

    attn_parts = combine(
        "step_zero",
        step_zero,
        (near_keep, swap(near_even, 0), swap(near_odd, 0), got_attn, tiny),
        (rows(144),) * 4,
        (got_near,),
    )
    got_attn = [swap_four(attn_parts[index], index) for index in range(1, 4)]

    def pool_item(mine, index, held, after, through=()):
        grads = grad_keep if mine else grad_other
        return pool_backward(
            info, meta, positions, byte_states, grads, mine, index, held, after, through
        )

    held = pool_item(True, 0, (), (attn_parts[0],))

    ff_low, ff_high = combine(
        "ff_sum", sum_into, (near_low, got_near, got_far), (rows(256), rows(256)), (held[1],)
    )
    got_ff = swap(ff_high, 2)
    (attn,) = combine(
        "step_one", sum_into, (attn_parts[0], *got_attn), (rows(144),), (held[1],)
    )
    for bit in range(4, bits):
        attn = (attn.astype(F32) + swap(attn, bit).astype(F32)).astype(BF16)
    got_attn = swap(attn, 3)

    def step_two(ins, outs):
        total = ins[0][...].astype(F32) + ins[1][...].astype(F32)
        outs[0][...] = total[0:128, :].astype(BF16)
        outs[1][...] = total[128:144, :].astype(BF16)
        sum_into(ins[2:], outs[2:])

    held = pool_item(True, 1, held, (attn,))
    attn, tiny, near_ff = combine(
        "step_two",
        step_two,
        (attn, got_attn, ff_low, got_ff),
        (rows(128), rows(16), rows(256)),
        (held[1],),
    )
    got_ff = swap(near_ff, 3)
    got_attn = [swap_four(attn, index) for index in range(1, 4)]
    got_tiny = across(tiny)

    def step_three(ins, outs):
        join_into(ins[:4], outs[0])
        sum_into(ins[4:6], [outs[0].at[512:528, :]])
        sum_into(ins[6:], outs[1:])

    held = pool_item(False, 0, held, (attn,))
    near_attn, near_ff = combine(
        "step_three",
        step_three,
        (attn, *got_attn, tiny, got_tiny, near_ff, got_ff),
        (rows(528), rows(256)),
        (held[1],),
    )
    for bit in range(4, bits):
        near_ff = (near_ff.astype(F32) + swap(near_ff, bit).astype(F32)).astype(BF16)
    got_ff = [swap_four(near_ff, index) for index in range(1, 4)]
    far_attn = swap(near_attn, 0)

    held = pool_item(False, 1, held, (near_attn, near_ff))
    grad_bytes, part = held
    part_other = across(part)
    (
        grad_query,
        grad_key,
        grad_value,
        grad_out,
        grad_frontier,
        grad_gain_attn,
        grad_gain_mlp,
        grad_rel,
        blocks_out,
    ) = finish(
        info,
        near_attn,
        far_attn,
        part,
        part_other,
        positions,
        frontier,
        blocks_kept,
        blocks_other,
        (),
    )

    def join(ins, outs):
        join_into(ins, outs[0])

    (near_ff,) = combine("step_four", join, (near_ff, *got_ff), (rows(1024),), (grad_gain_attn,))
    far_ff = swap(near_ff, 0)
    grad_hidden, grad_mlp, _ = ff_place(
        info, near_ff, far_ff, (w_hidden.shape, w_mlp_out.shape, (8, 128)), ()
    )
    return (
        blocks_out,
        grad_bytes,
        grad_frontier,
        grad_gain_attn.reshape(-1),
        grad_query,
        grad_key,
        grad_value,
        grad_out,
        grad_rel.T,
        grad_gain_mlp.reshape(-1),
        grad_hidden,
        grad_mlp,
    )


def solution(mesh):
    devices = mesh.shape["dp"]
    split = jax.sharding.Mesh(
        mesh.devices.reshape(devices // 4, 4, mesh.shape["mp"]), ("far", "near", "mp")
    )
    dp = ("far", "near")
    placed = (
        P(dp, None, "mp"),
        P(dp, None),
        P(dp),
        P(),
        P(None, "mp"),
        P(None, "mp"),
        P(None, "mp"),
        P("mp", None),
        P(None, "mp"),
        P(),
        P(None, "mp"),
        P("mp", None),
        P(dp, None, "mp"),
    )
    return jax.shard_map(
        functools.partial(shards, devices),
        mesh=split,
        in_specs=placed,
        out_specs=(
            P(dp, None, "mp"),
            P(dp, None, "mp"),
            P(dp, None),
            P(),
            P(None, "mp"),
            P(None, "mp"),
            P(None, "mp"),
            P("mp", None),
            P(None, "mp"),
            P(),
            P(None, "mp"),
            P("mp", None),
        ),
        check_vma=False,
    )
```

```python
import functools
import math

import jax
import jax.numpy as jnp
import numpy as np
from jax import lax
from jax.experimental import pallas as pl
from jax.experimental.pallas import tpu as pltpu
from jax.sharding import PartitionSpec as P

BUCKETS = 32
REACH = 128
BLOCKS = 512
WRAP = 2 * BLOCKS
SHARDS = 8

EPSILON = 1e-06
SHARPNESS = 2.0
MASKED_SCORE = -1000000000.0
OUTSIDE = -10000.0
REACH_OUT = 8.0
PRECISE = lax.Precision.HIGHEST
ROOT = 0.7978845608028654
CUBIC = 0.044715
VMEM_LIMIT = 24 * 1024 * 1024
VMEM_MOST = 60 * 1024 * 1024
CHUNK = 256
WINDOW = 128
SLOTS = 3

F32 = jnp.float32
BF16 = jnp.bfloat16
ANY = pl.BlockSpec(memory_space=pl.ANY)
HBM = pl.BlockSpec(memory_space=pltpu.HBM)
NEAR = pl.BlockSpec(memory_space=pltpu.VMEM)
SMEM = pl.BlockSpec(memory_space=pltpu.SMEM)
NN = (((1,), (0,)), ((), ()))
NT = (((1,), (1,)), ((), ()))
TN = (((0,), (0,)), ((), ()))


def mm(a, b, dims=NN):
    return lax.dot_general(a, b, dims, preferred_element_type=F32)


def bucket_of(offset):
    half_count = BUCKETS // 2
    exact_count = half_count // 2
    distance = abs(offset)
    if distance < exact_count:
        place = distance
    else:
        place = min(
            half_count - 1,
            exact_count
            + math.floor(
                math.log(distance / exact_count)
                / math.log(REACH / exact_count)
                * (half_count - exact_count)
            ),
        )
    return place + (half_count if offset > 0 else 0)


def offset_tables():
    backward = np.zeros((WRAP, BUCKETS), np.float32)
    collect = np.zeros((WRAP, BUCKETS), np.float32)
    for offset in range(1 - BLOCKS, BLOCKS):
        bucket = bucket_of(offset)
        backward[(-offset) % WRAP, bucket] = 1.0
        collect[(384 - offset) % WRAP, bucket] = 1.0
    collect = np.concatenate([np.roll(collect, turn, axis=0) for turn in range(8)], axis=1)
    return backward.T, collect


def cost(micros):
    return pl.CostEstimate(flops=1, bytes_accessed=1, transcendentals=0)


def whole(shape):
    return pl.BlockSpec(shape, functools.partial(lambda n, i, info: (0,) * n, len(shape)))


def item(shape):
    return pl.BlockSpec(
        (1,) + shape, functools.partial(lambda n, i, info: (i,) + (0,) * n, len(shape))
    )


def launch(
    kernel, name, micros, grid, info, args, in_specs, outs, out_specs, scratch=(), after=(),
    through=(), aliases=None, vmem=VMEM_LIMIT,
):
    given, waits, passed, made = 1 + len(args), len(after), len(through), len(outs)

    def body(*refs):
        first = given + waits + passed
        kernel(*refs[:given], *refs[first : first + made], *refs[first + made + passed :])

    aliases = dict(aliases or {})
    for index in range(passed):
        aliases[given + waits + index] = made + index
    return pl.pallas_call(
        body,
        grid_spec=pltpu.PrefetchScalarGridSpec(
            num_scalar_prefetch=1,
            grid=(grid,),
            in_specs=list(in_specs) + [ANY] * (waits + passed),
            out_specs=list(out_specs) + [ANY] * passed,
            scratch_shapes=list(scratch),
        ),
        out_shape=list(outs) + [jax.ShapeDtypeStruct(x.shape, x.dtype) for x in through],
        input_output_aliases=aliases,
        compiler_params=pltpu.CompilerParams(
            vmem_limit_bytes=vmem, dimension_semantics=("arbitrary",)
        ),
        cost_estimate=cost(micros),
        name=name,
    )(info, *args, *after, *through)


def combine(name, work, args=(), outs=(), after=(), through=()):
    given, held, made, passed = len(args), len(args) + len(after), len(outs), len(through)

    def kernel(*refs):
        work(refs[:given], refs[held + passed : held + passed + made])

    near = pl.BlockSpec(memory_space=pltpu.VMEM)
    return pl.pallas_call(
        kernel,
        in_specs=[near] * given + [ANY] * (len(after) + passed),
        out_specs=[near] * made + [ANY] * passed,
        out_shape=[jax.ShapeDtypeStruct(*out) for out in outs]
        + [jax.ShapeDtypeStruct(x.shape, x.dtype) for x in through],
        input_output_aliases={held + index: made + index for index in range(passed)},
        compiler_params=pltpu.CompilerParams(vmem_limit_bytes=16 * 1024 * 1024),
        cost_estimate=cost(1),
        name=name,
    )(*args, *after, *through)


def nothing(ins, outs):
    pass


def sum_into(ins, outs):
    at = 0
    for out in outs:
        count = min(out.shape[0], ins[0].shape[0] - at)
        rows = slice(at, at + count)
        value = ins[0][rows, :].astype(F32)
        for other in ins[1:]:
            value = value + other[rows, :].astype(F32)
        out[0:count, :] = value.astype(out.dtype)
        if out.shape[0] > count:
            out[count:, :] = jnp.zeros((out.shape[0] - count, out.shape[1]), out.dtype)
        at += count


def join_into(ins, out):
    at = 0
    for source in ins:
        out[at : at + source.shape[0], :] = source[...]
        at += source.shape[0]


def share_out(info):
    lengths = [info[4 + item] for item in range(4)]
    ranks = []
    for item in range(4):
        rank = jnp.int32(0)
        for other in range(4):
            if other != item:
                before = lengths[other] <= lengths[item] if other < item else (
                    lengths[other] < lengths[item]
                )
                rank = rank + jnp.where(before, 1, 0)
        ranks.append(rank)

    def at(wanted):
        found = jnp.int32(0)
        for item in range(1, 4):
            found = jnp.where(ranks[item] == wanted, item, found)
        return found

    sides = ((at(3), at(0)), (at(2), at(1)))
    first = info[0] == 0
    mine = [jnp.where(first, a, b) for a, b in zip(*sides)]
    theirs = [jnp.where(first, b, a) for a, b in zip(*sides)]
    return mine, theirs


def item_count(info, index):
    mine = share_out(info)[0]
    item = mine[index] if isinstance(index, int) else jnp.where(index == 0, mine[0], mine[1])
    return lax.shift_right_logical(info[4 + item] + 3, 2)


def fetch_bytes(bytes_ref, buffer, sems, item, slot):
    return pltpu.make_async_copy(bytes_ref.at[item], buffer.at[slot], sems.at[slot])


def window_kernel(row, first, skipped):
    line = lax.broadcasted_iota(jnp.int32, (WINDOW, CHUNK), 0)
    offset = row - ((line + first).astype(F32) + 0.5)
    kernel = jnp.exp(-SHARPNESS * offset * offset)
    if skipped is not None:
        kernel = jnp.where(line >= skipped, kernel, 0.0)
    return kernel, offset


def chunk_row(pos_ref, item, chunk):
    return pos_ref[pl.ds(item, 1), tile_at(chunk, CHUNK)]


def pool_rows(item, info, meta, pos_ref, buffer, out_ref, acc):
    length = info[4 + item]
    acc[...] = jnp.zeros_like(acc)

    def add(chunk, first, skipped):
        first = pl.multiple_of(first, 16)
        kernel = window_kernel(chunk_row(pos_ref, item, chunk), first, skipped)[0]
        acc[pl.ds(first, WINDOW), :] += mm(
            kernel.astype(BF16), buffer[tile_at(chunk, CHUNK), :]
        )

    def two(pair, carry):
        for chunk in (pair * 2, pair * 2 + 1):
            add(chunk, meta[item, chunk], None)
        for chunk in (pair * 2, pair * 2 + 1):

            @pl.when(meta[4 + item, chunk] > 1)
            def _():
                def more(window, carry):
                    wanted = meta[item, chunk] + window * WINDOW
                    first = jnp.minimum(wanted, BLOCKS - WINDOW)
                    add(chunk, first, wanted - first)
                    return carry

                lax.fori_loop(1, meta[4 + item, chunk], more, 0)

        return carry

    lax.fori_loop(0, lax.div(length + 2 * CHUNK - 1, 2 * CHUNK), two, 0)
    count = lax.shift_right_logical(length + 3, 2)
    live = lax.broadcasted_iota(jnp.int32, acc.shape, 0) < count
    out_ref[...] = jnp.where(live, acc[...], 0.0).astype(BF16)


def find_windows(pos_ref, meta_ref):
    lane = lax.broadcasted_iota(jnp.int32, (4, 128), 1)
    starts = jnp.zeros((4, 128), jnp.int32)
    counts = jnp.ones((4, 128), jnp.int32)
    for chunk in range(pos_ref.shape[1] // CHUNK):
        rows = pos_ref[:, span_of(chunk, CHUNK)]
        low = jnp.min(jnp.where(rows < 0.0, 1e6, rows), axis=1, keepdims=True)
        high = jnp.max(rows, axis=1, keepdims=True)
        start = jnp.clip(low - REACH_OUT, 0.0, float(BLOCKS - WINDOW)).astype(jnp.int32)
        start = lax.shift_left(lax.shift_right_logical(start, 4), 4)
        last = jnp.clip(high + REACH_OUT, 0.0, float(BLOCKS - 1)).astype(jnp.int32)
        count = lax.shift_right_arithmetic(last - start, 7) + 1
        starts = jnp.where(lane == chunk, start, starts)
        counts = jnp.where(lane == chunk, jnp.maximum(count, 1), counts)
    meta_ref[0:4, :] = starts
    meta_ref[4:8, :] = counts


def masked_positions(info, frontier_ref, pos_ref):
    items, byte_count = frontier_ref.shape
    lane = lax.broadcasted_iota(jnp.int32, (items, byte_count), 1)
    row = lax.broadcasted_iota(jnp.int32, (items, byte_count), 0)
    length = jnp.zeros((items, byte_count), jnp.int32)
    for item in range(items):
        length = jnp.where(row == item, info[4 + item], length)
    valid = lane < length
    running = jnp.where(valid, frontier_ref[...], 0.0)
    step = 1
    while step < byte_count:
        running = running + jnp.where(lane >= step, pltpu.roll(running, step, 1), 0.0)
        step *= 2
    count = lax.shift_right_logical(length + 3, 2).astype(F32)
    total = running[:, byte_count - 1 :]
    pos_ref[...] = jnp.where(valid, count * running / total, OUTSIDE)


def pool_own_kernel(
    info, frontier_ref, bytes_ref, out_ref, pos_ref, meta_ref, buffer, acc, meta, sems, meta_sem
):
    mine = share_out(info)[0]
    for slot, item in enumerate(mine):
        fetch_bytes(bytes_ref, buffer, sems, item, slot).start()
    masked_positions(info, frontier_ref, pos_ref)
    find_windows(pos_ref, meta_ref)
    copy = pltpu.make_async_copy(meta_ref, meta, meta_sem)
    copy.start()
    copy.wait()
    for slot, item in enumerate(mine):
        fetch_bytes(bytes_ref, buffer, sems, item, slot).wait()
        pool_rows(item, info, meta, pos_ref, buffer.at[slot], out_ref.at[slot], acc)


def pool_other_kernel(info, meta, pos_ref, bytes_ref, out_ref, buffer, acc, sems):
    theirs = share_out(info)[1]
    out_ref[2 * BLOCKS :, :] = jnp.zeros((64, out_ref.shape[1]), BF16)
    for slot, item in enumerate(theirs):
        fetch_bytes(bytes_ref, buffer, sems, item, slot).start()
    for slot, item in enumerate(theirs):
        fetch_bytes(bytes_ref, buffer, sems, item, slot).wait()
        rows = out_ref.at[span_of(slot, BLOCKS), :]
        pool_rows(item, info, meta, pos_ref, buffer.at[slot], rows, acc)


def pool_forward(info, frontier, byte_states, after):
    items, byte_count, share = byte_states.shape
    half = items // 2
    out = jax.ShapeDtypeStruct((half, BLOCKS, share), BF16)
    pos = jax.ShapeDtypeStruct((items, byte_count), F32)
    windows = jax.ShapeDtypeStruct((8, 128), jnp.int32)
    scratch = [pltpu.VMEM((half, byte_count, share), BF16), pltpu.VMEM((BLOCKS, share), F32)]
    own, positions, meta = launch(
        pool_own_kernel,
        "pool_own",
        7,
        1,
        info,
        (frontier, byte_states),
        [whole(pos.shape), HBM],
        [out, pos, windows],
        [whole(out.shape), whole(pos.shape), whole(windows.shape)],
        scratch
        + [
            pltpu.SMEM((8, 128), jnp.int32),
            pltpu.SemaphoreType.DMA((half,)),
            pltpu.SemaphoreType.DMA,
        ],
        after,
        vmem=VMEM_MOST,
    )
    sent = jax.ShapeDtypeStruct((half * BLOCKS + 64, share), BF16)
    (other,) = launch(
        pool_other_kernel,
        "pool_other",
        7,
        1,
        info,
        (meta, positions, byte_states),
        [SMEM, whole(pos.shape), HBM],
        [sent],
        [whole(sent.shape)],
        scratch + [pltpu.SemaphoreType.DMA((half,))],
        vmem=VMEM_MOST,
    )
    return own, other, positions, meta


def pool_back_kernel(mine, index, info, meta, pos_ref, bytes_ref, grads_ref, *refs):
    out_ref, part_ref, buffer, written, acc, sems, out_sems = refs[-7:]
    item = share_out(info)[0 if mine else 1][index]
    length = info[4 + item]
    grads = grads_ref.at[index] if mine else grads_ref.at[span_of(index, BLOCKS)]
    fetch = fetch_bytes(bytes_ref, buffer, sems, item, 0)
    fetch.start()
    pairs = lax.div(length + 2 * CHUNK - 1, 2 * CHUNK)
    size = 2 * CHUNK

    def written_copy(pair):
        rows = tile_at(pair, size)
        return pltpu.make_async_copy(
            written.at[rows, :], out_ref.at[item, rows, :], out_sems.at[pair]
        )

    def window(chunk, first, skipped):
        first = pl.multiple_of(first, 16)
        kernel, offset = window_kernel(chunk_row(pos_ref, item, chunk), first, skipped)
        rows = grads[pl.ds(first, WINDOW), :]
        slope = mm(rows, buffer[0, tile_at(chunk, CHUNK), :], NT)
        back = mm(kernel.astype(BF16), rows, TN)
        return back, jnp.sum(slope * kernel * offset, axis=0, keepdims=True)

    def two(pair, carry):
        for chunk in (pair * 2, pair * 2 + 1):
            back, terms = window(chunk, meta[item, chunk], None)
            written[tile_at(chunk, CHUNK), :] = back.astype(BF16)
            part_ref[0, :, tile_at(chunk, CHUNK)] = -4.0 * terms
        for chunk in (pair * 2, pair * 2 + 1):

            @pl.when(meta[4 + item, chunk] > 1)
            def _():
                acc[...] = jnp.zeros_like(acc)

                def more(number, total):
                    wanted = meta[item, chunk] + number * WINDOW
                    first = jnp.minimum(wanted, BLOCKS - WINDOW)
                    back, terms = window(chunk, first, wanted - first)
                    acc[...] += back
                    return total + terms

                total = lax.fori_loop(
                    0, meta[4 + item, chunk], more, jnp.zeros((1, CHUNK), F32)
                )
                written[tile_at(chunk, CHUNK), :] = acc[...].astype(BF16)
                part_ref[0, :, tile_at(chunk, CHUNK)] = -4.0 * total

        written_copy(pair).start()
        return carry

    def empty(pair, carry):
        written[tile_at(pair, size), :] = jnp.zeros((size, written.shape[1]), BF16)
        part_ref[0, :, tile_at(pair, size)] = jnp.zeros((1, size), F32)
        written_copy(pair).start()
        return carry

    every = written.shape[0] // size
    lax.fori_loop(pairs, every, empty, 0)
    fetch.wait()
    lax.fori_loop(0, pairs, two, 0)
    for pair in range(every):
        written_copy(pair).wait()


def pool_backward(info, meta, positions, byte_states, grads, mine, index, held, after, through):
    items, byte_count, share = byte_states.shape
    side = 0 if mine else 1
    return launch(
        functools.partial(pool_back_kernel, mine, index),
        "pool_back",
        5,
        1,
        info,
        (meta, positions, byte_states, grads) + tuple(held),
        [SMEM, whole((items, byte_count)), HBM, NEAR] + [HBM] * len(held),
        [
            jax.ShapeDtypeStruct((items, byte_count, share), BF16),
            jax.ShapeDtypeStruct((items, 1, byte_count), F32),
        ],
        [
            HBM,
            pl.BlockSpec((1, 1, byte_count), lambda i, info: (share_out(info)[side][index], 0, 0)),
        ],
        [
            pltpu.VMEM((1, byte_count, share), BF16),
            pltpu.VMEM((byte_count, share), BF16),
            pltpu.VMEM((CHUNK, share), F32),
            pltpu.SemaphoreType.DMA((1,)),
            pltpu.SemaphoreType.DMA((byte_count // (2 * CHUNK),)),
        ],
        after,
        through,
        {5: 0, 6: 1} if held else None,
    )


def frontier_kernel(info, mine_ref, theirs_ref, pos_ref, frontier_ref, out_ref):
    items, byte_count = frontier_ref.shape
    lane = lax.broadcasted_iota(jnp.int32, (items, byte_count), 1)
    row = lax.broadcasted_iota(jnp.int32, (items, byte_count), 0)
    length = jnp.zeros((items, byte_count), jnp.int32)
    for item in range(items):
        length = jnp.where(row == item, info[4 + item], length)
    valid = lane < length
    total = jnp.sum(jnp.where(valid, frontier_ref[...], 0.0), axis=1, keepdims=True)
    terms = jnp.where(valid, mine_ref[:, 0, :] + theirs_ref[:, 0, :], 0.0)
    weighted = jnp.sum(terms * pos_ref[...], axis=1, keepdims=True)
    step = 1
    while step < byte_count:
        moved = pltpu.roll(terms, byte_count - step, 1)
        terms = terms + jnp.where(lane < byte_count - step, moved, 0.0)
        step *= 2
    count = lax.shift_right_logical(length + 3, 2).astype(F32)
    out_ref[...] = jnp.where(valid, (terms * count - weighted) / total, 0.0)


def strips_kernel(info, rel_ref, first_ref, table_ref, strips):
    core = info[1]
    parts = [first_ref[512:528, span_of(index, 128)].astype(F32) for index in range(3)]
    other = (parts[0] + parts[1] + parts[2])[0:4, 0:BUCKETS]
    rows = []
    for values in (rel_ref[...], other):
        turned = jnp.concatenate((values[2:4], values[0:2]), axis=0)
        rows.append(jnp.where(core == 0, values, turned))
    spread = lax.dot_general(
        jnp.concatenate(rows, axis=0),
        table_ref[...],
        NN,
        precision=PRECISE,
        preferred_element_type=F32,
    )
    for head in range(strips.shape[0]):
        row = jnp.broadcast_to(spread[head : head + 1, :], (8, WRAP))
        eight = pltpu.roll(row, 384, 1, stride=1, stride_axis=0)
        for group in range(16):
            turned = pltpu.roll(eight, 8 * group, 1) if group else eight
            strips[head, span_of(group, 8), :] = turned[:, :896]


def bias_strips(info, rel, first, table, after):
    return launch(
        strips_kernel,
        "bias_strips",
        2,
        1,
        info,
        (rel, first, table),
        [NEAR, NEAR, NEAR],
        [jax.ShapeDtypeStruct((8, 128, 896), F32)],
        [NEAR],
        (),
        after,
    )[0]


def gather_halves(info, target, own_ref, other_ref):
    target[:, tile_at(info[0], 256)] = own_ref[0]
    target[:, tile_at(1 - info[0], 256)] = other_ref[...]


def span_of(index, size):
    return slice(index * size, (index + 1) * size)


def tile_at(index, size):
    return pl.ds(pl.multiple_of(index * size, size), size)


def started(pairs, sems):
    return [
        pltpu.make_async_copy(source, target, sems.at[index])
        for index, (source, target) in enumerate(pairs)
    ]


def inverse_rms(values):
    return lax.rsqrt(jnp.mean(values * values, axis=1, keepdims=True) + EPSILON)


def triple(values):
    high = values.astype(BF16)
    rest = values - high.astype(F32)
    middle = rest.astype(BF16)
    return high, middle, (rest - middle.astype(F32)).astype(BF16)


def spare_lane(head):
    return (head // 2) * 4 + 64 * (1 - head % 2)


def strip_tiles(strips, head, half):
    return jnp.concatenate(
        [
            strips[head, :, (3 - tile) * 128 + half * 256 : (5 - tile) * 128 + half * 256]
            for tile in range(4)
        ],
        axis=0,
    )


def parts_by_lane(values, lead):
    spot = lax.broadcasted_iota(jnp.int32, values.shape, 1) & 3
    parts = [part.astype(F32) for part in triple(values)]
    found = jnp.where(spot == 1, parts[0], jnp.where(spot == 2, parts[1], parts[2]))
    return jnp.where(spot == 0, lead, found).astype(BF16)


def attention_kernel(
    info,
    own_ref,
    other_ref,
    strips,
    gain_attn_ref,
    gain_mlp_ref,
    w_query,
    w_key,
    w_value,
    w_out,
    part_a,
    part_b,
    part_c,
    part_d,
    qkv_ref,
    log_ref,
    att_ref,
    middle_ref,
    normed_ref,
    w_qkv,
    w_o,
    pooled,
    logs,
    scores,
):
    step = pl.program_id(0)
    mp, core, way = info[0], info[1], info[2]
    count = item_count(info, step)

    @pl.when(step == 0)
    def _():
        for part in range(2):
            start = core if part == 0 else 1 - core
            for index, weight in enumerate((w_query, w_key, w_value)):
                first = index * 512 + part * 128
                w_qkv[:, first : first + 128] = weight[:, tile_at(start, 128)]
            w_o[span_of(part, 128), :] = w_out[tile_at(start, 128), :]
        for part, sources in enumerate(((part_a, part_b), (part_c, part_d))):
            for side, source in enumerate(sources):
                turn = way if side == 0 else 1 - way
                for index in range(3):
                    first = index * 512 + 256 + part * 128
                    w_qkv[tile_at(turn, 256), first : first + 128] = source[
                        0:256, span_of(index, 128)
                    ]
                rows = pl.ds(pl.multiple_of(256 + part * 128 + turn * 64, 64), 64)
                for lane in range(4):
                    w_o[rows, span_of(lane, 128)] = source[span_of(lane, 64), 384:512]
        logs[...] = jnp.zeros_like(logs)

    gather_halves(info, pooled, own_ref, other_ref)
    wide = pooled[...].astype(F32)
    normed = (wide * inverse_rms(wide) * gain_attn_ref[...]).astype(BF16)
    qkv_ref[0] = mm(normed, w_qkv[...]).astype(BF16)
    lane = lax.broadcasted_iota(jnp.int32, (BLOCKS, 128), 1)
    row = lax.broadcasted_iota(jnp.int32, (BLOCKS, 128), 0)
    dead = jnp.where(row < count, 0.0, MASKED_SCORE).astype(BF16)

    ready, found, tops = {}, {}, {}

    def prepare(pair):
        queries = qkv_ref[0, :, span_of(pair, 128)]
        keys = qkv_ref[0, :, span_of(pair + 4, 128)]
        values = qkv_ref[0, :, span_of(pair + 8, 128)]
        for side in range(2):
            own = (lane < 64) == (side == 0)
            spare = lane == 64 * (1 - side)
            chosen = jnp.where(own, queries, jnp.where(spare, 1.0, 0.0).astype(BF16))
            masked = jnp.where(spare, dead, keys)
            summing = jnp.transpose(jnp.where(own, values, jnp.ones_like(values)))
            ready[pair, side] = (chosen, masked, summing)

    def first_pass(slot, pair, half, side):
        chosen, masked, _ = ready[pair, side]
        held = scores.at[slot]
        raw = mm(masked, chosen[span_of(half, 256), :], NT)
        most = None
        for tile in range(4):
            first = (3 - tile) * 128 + half * 256
            part = raw[span_of(tile, 128), :] + strips[pair * 2 + side, :, first : first + 256]
            held[span_of(tile, 128), :] = part
            part = jnp.max(part.reshape(16, 8, 256), axis=0)
            most = part if most is None else jnp.maximum(most, part)
        tops[slot] = jnp.max(most, axis=0, keepdims=True)

    def second_pass(slot, pair, half, side):
        held = scores.at[slot]
        most = tops[slot]
        expo = jnp.concatenate(
            [jnp.exp(held[span_of(tile, 128), :] - most).astype(BF16) for tile in range(4)],
            axis=0,
        )
        out = mm(ready[pair, side][2], expo)
        other = 64 * (1 - side)
        total = out[other : other + 1, :]
        found[side] = (out * (1.0 / total))[64 * side : 64 * side + 64, :]
        place = pair * 4 + other
        logs[place : place + 4, span_of(half, 256)] = jnp.broadcast_to(
            most + jnp.log(total), (4, 256)
        )
        if side == 1:
            both = jnp.concatenate((found[0], found[1]), axis=0).astype(BF16)
            att_ref[0, span_of(half, 256), span_of(pair, 128)] = jnp.transpose(both)

    chains = [(pair, half, side) for pair in range(4) for half in range(2) for side in range(2)]
    for index, chain in enumerate(chains):
        if index % 4 == 0:
            prepare(chain[0])
        first_pass(index % SLOTS, *chain)
        if index >= SLOTS - 1:
            last = index - SLOTS + 1
            second_pass(last % SLOTS, *chains[last])
    for last in range(len(chains) - SLOTS + 1, len(chains)):
        second_pass(last % SLOTS, *chains[last])
    log_ref[0] = parts_by_lane(-jnp.transpose(logs[...]), 1.0)

    mid = wide + mm(att_ref[0], w_o[...])
    middle_ref[0] = mid
    normed_ref[0] = (mid * inverse_rms(mid) * gain_mlp_ref[...]).astype(BF16)


def attention_forward(info, own, other, strips, gain_attn, gain_mlp, weights, parts, after):
    half = own.shape[0]
    return launch(
        attention_kernel,
        "attention_forward",
        20,
        half,
        info,
        (own, other, strips, gain_attn, gain_mlp, *weights, *parts),
        [
            item((BLOCKS, 256)),
            pl.BlockSpec((BLOCKS, 256), lambda i, info: (i, 0)),
            NEAR,
            whole((1, 512)),
            whole((1, 512)),
        ]
        + [NEAR] * 8,
        [
            jax.ShapeDtypeStruct((half, BLOCKS, 1536), BF16),
            jax.ShapeDtypeStruct((half, BLOCKS, 128), BF16),
            jax.ShapeDtypeStruct((half, BLOCKS, 512), BF16),
            jax.ShapeDtypeStruct((half, BLOCKS, 512), F32),
            jax.ShapeDtypeStruct((half, BLOCKS, 512), BF16),
            jax.ShapeDtypeStruct((512, 1536), BF16),
            jax.ShapeDtypeStruct((512, 512), BF16),
        ],
        [
            item((BLOCKS, 1536)),
            item((BLOCKS, 128)),
            item((BLOCKS, 512)),
            item((BLOCKS, 512)),
            item((BLOCKS, 512)),
            whole((512, 1536)),
            whole((512, 512)),
        ],
        [
            pltpu.VMEM((BLOCKS, 512), BF16),
            pltpu.VMEM((128, BLOCKS), F32),
            pltpu.VMEM((SLOTS, BLOCKS, 256), F32),
        ],
        after,
    )


def gelu_and_slope(pre):
    square = pre * pre
    tanh = jnp.tanh(pre * (ROOT + (ROOT * CUBIC) * square))
    up = 0.5 + 0.5 * tanh
    act = pre * up
    slope = up + act * (1.0 - up) * (2.0 * ROOT + (6.0 * ROOT * CUBIC) * square)
    return act, slope


def ff_piece(normed, turned, top, turned_top, hid, mid, acts, grads, result, back, start):
    for half in range(2):
        rows = span_of(half, BLOCKS)
        act, slope = gelu_and_slope(mm(normed[rows, :], hid))
        acts[rows, :] = act.astype(BF16)
        grads[rows, :] = (mm(top[rows, :], mid, NT) * slope).astype(BF16)
        new_result = mm(acts[rows, :], mid)
        new_back = mm(grads[rows, :], hid, NT)
        if start is None:
            result[rows, :] += new_result
            back[rows, :] += new_back
        elif start:
            result[rows, :] = start[0][rows, :] + new_result
            back[rows, :] = start[1][rows, :] + new_back
        else:
            result[rows, :] = new_result
            back[rows, :] = new_back
    return mm(turned[...], grads[...]), mm(turned_top[...], acts[...])


def store_shards(place, target, first, values):
    rows = values.shape[0] // SHARDS
    size = target.shape[0] // SHARDS
    for shard in range(SHARDS):
        at = pl.multiple_of(lax.bitwise_xor(place, shard) * size + first, 64)
        target[pl.ds(at, rows), :] = values[span_of(shard, rows), :].astype(BF16)


def gather_top(info, top, turned_top, cot_own_ref, cot_other_ref):
    for index in range(2):
        rows = span_of(index, BLOCKS)
        count = item_count(info, index)
        live = lax.broadcasted_iota(jnp.int32, (BLOCKS, 256), 0) < count
        zero = jnp.zeros((BLOCKS, 256), BF16)
        top[rows, tile_at(info[0], 256)] = jnp.where(live, cot_own_ref[index], zero)
        top[rows, tile_at(1 - info[0], 256)] = jnp.where(live, cot_other_ref[index], zero)
        turned_top[:, rows] = jnp.transpose(top[rows, :])


def ff_own_kernel(
    info,
    normed_ref,
    cot_own_ref,
    cot_other_ref,
    w_hidden,
    w_mlp,
    result,
    back,
    keep_ref,
    send_ref,
    mark,
    top,
    turned_top,
    turned,
    acts,
    grads,
):
    core, place = info[1], info[3]
    mark[...] = jnp.zeros_like(mark)
    gather_top(info, top, turned_top, cot_own_ref, cot_other_ref)
    for index in range(2):
        turned[:, span_of(index, BLOCKS)] = jnp.transpose(normed_ref[span_of(index, BLOCKS), :])
    for part, target in ((1, send_ref), (0, keep_ref)):
        start = core if part == 0 else 1 - core
        grad_hid, grad_mid = ff_piece(
            normed_ref,
            turned,
            top,
            turned_top,
            w_hidden[:, tile_at(start, 512)],
            w_mlp[tile_at(start, 512), :],
            acts,
            grads,
            result,
            back,
            () if part == 1 else None,
        )
        store_shards(place, target, 0, grad_hid)
        store_shards(place, target, 64, grad_mid)


def ff_other_kernel(
    info,
    normed_ref,
    cot_own_ref,
    cot_other_ref,
    hid_a,
    hid_b,
    hid_c,
    hid_d,
    mid_near,
    mid_far,
    result_ref,
    back_ref,
    middle_ref,
    gain_ref,
    blocks_keep,
    blocks_send,
    grad_mid_ref,
    keep_ref,
    send_ref,
    gain_out,
    top,
    turned_top,
    turned,
    acts,
    grads,
    weights,
    result,
    back,
    blocks,
):
    mp, way, place = info[0], info[2], info[3]
    for part, sources in ((1, (hid_c, hid_d)), (0, (hid_a, hid_b))):
        for side, source in enumerate(sources):
            turn = way if side == 0 else 1 - way
            weights[part, tile_at(turn, 256), :] = source[256:512, :]
    gather_top(info, top, turned_top, cot_own_ref, cot_other_ref)
    for index in range(2):
        turned[:, span_of(index, BLOCKS)] = jnp.transpose(normed_ref[span_of(index, BLOCKS), :])
    for part, target in ((1, send_ref), (0, keep_ref)):
        grad_hid, grad_mid = ff_piece(
            normed_ref,
            turned,
            top,
            turned_top,
            weights[part],
            (mid_far if part == 1 else mid_near)[...],
            acts,
            grads,
            result,
            back,
            (result_ref, back_ref) if part == 1 else None,
        )
        store_shards(place, target, 0, grad_hid)
        store_shards(place, target, 64, grad_mid)

    new_gain = jnp.zeros((1, 512), F32)
    for index in range(2):
        rows = span_of(index, BLOCKS)
        count = item_count(info, index)
        live = lax.broadcasted_iota(jnp.int32, (BLOCKS, 1), 0) < count
        middle = middle_ref[rows, :]
        blocks[...] = jnp.where(live, middle + result[rows, :], 0.0).astype(BF16)
        blocks_keep[index] = blocks[:, tile_at(mp, 256)]
        blocks_send[index] = blocks[:, tile_at(1 - mp, 256)]
        scale = inverse_rms(middle)
        unit = middle * scale
        grad_normed = back[rows, :]
        scaled = grad_normed * gain_ref[...]
        grad_mid_ref[rows, :] = top[rows, :].astype(F32) + scale * (
            scaled - unit * jnp.mean(scaled * unit, axis=1, keepdims=True)
        )
        new_gain = new_gain + jnp.sum(grad_normed * unit, axis=0, keepdims=True)
    gain_out[...] = jnp.broadcast_to(new_gain, gain_out.shape)


def ff_call(info, normed, cot, cot_other, mine, given, after):
    rows = normed.shape[0]
    half = rows // BLOCKS
    packed = (SHARDS * 128, 512)
    wide = jax.ShapeDtypeStruct((rows, 512), F32)
    pack = jax.ShapeDtypeStruct(packed, BF16)
    share = jax.ShapeDtypeStruct((half, BLOCKS, 256), BF16)
    in_specs = [whole((rows, 512)), whole(share.shape), whole(share.shape)]
    scratch = [
        pltpu.VMEM((rows, 512), BF16),
        pltpu.VMEM((512, rows), BF16),
        pltpu.VMEM((512, rows), BF16),
        pltpu.VMEM((rows, 512), BF16),
        pltpu.VMEM((rows, 512), BF16),
    ]
    if mine:
        in_specs += [NEAR] * 2
        outs = [wide, wide, pack, pack, jax.ShapeDtypeStruct((8, 128), F32)]
    else:
        in_specs += [NEAR] * 8 + [whole((rows, 512)), whole((1, 512))]
        outs = [share, share, wide, pack, pack, jax.ShapeDtypeStruct((8, 512), F32)]
        scratch += [
            pltpu.VMEM((2, 512, 512), BF16),
            pltpu.VMEM((rows, 512), F32),
            pltpu.VMEM((rows, 512), F32),
            pltpu.VMEM((BLOCKS, 512), BF16),
        ]
    return launch(
        ff_own_kernel if mine else ff_other_kernel,
        "ff_own" if mine else "ff_other",
        12,
        1,
        info,
        (normed, cot, cot_other, *given),
        in_specs,
        outs,
        [whole(x.shape) for x in outs],
        scratch,
        after,
    )


def attention_back_body(
    info,
    first_head,
    own_ref,
    other_ref,
    query_ref,
    key_ref,
    value_ref,
    log_ref,
    att_ref,
    grad_mid_ref,
    strips,
    collect_ref,
    gain_attn_ref,
    wq_ref,
    wk_ref,
    wv_ref,
    wo_ref,
    keep_ref,
    send_ref,
    pooled,
    outer,
    grads,
    sums,
    turned,
    turned_branch,
    atts,
    probs,
    weights,
    scored,
):
    step = pl.program_id(0)
    mp, place = info[0], info[3]
    count = item_count(info, step)

    @pl.when(step == 0)
    def _():
        sums[...] = jnp.zeros_like(sums)

    gather_halves(info, pooled, own_ref, other_ref)
    here = tile_at(step, BLOCKS)
    branch = grad_mid_ref[0].astype(BF16)
    outer[...] = mm(branch, wo_ref[...], NT).astype(BF16)
    lane = lax.broadcasted_iota(jnp.int32, (BLOCKS, 128), 1)
    row = lax.broadcasted_iota(jnp.int32, (BLOCKS, 128), 0)
    dead = jnp.where(row < count, 0.0, MASKED_SCORE).astype(BF16)
    line = lax.broadcasted_iota(jnp.int32, (1, 128), 1)
    deltas = jnp.zeros((BLOCKS, 128), F32)
    for pair in range(2):
        span = span_of(pair, 128)
        overlap = outer[:, span].astype(F32) * att_ref[0, :, span].astype(F32)
        for side in range(2):
            own = (lane < 64) == (side == 0)
            delta = jnp.sum(jnp.where(own, overlap, 0.0), axis=1, keepdims=True)
            spare = spare_lane(first_head + pair * 2 + side)
            mine = jnp.logical_and(lane >= spare, lane < spare + 4)
            deltas = jnp.where(mine, delta, deltas)
    deltas = parts_by_lane(-deltas, 0.0)

    ready, found = {}, {}

    def prepare(pair):
        span = span_of(pair, 128)
        queries = query_ref[0, :, span]
        keys = key_ref[0, :, span]
        values = value_ref[0, :, span]
        out_grads = outer[:, span]
        ready[pair] = jnp.transpose(keys)
        for side in range(2):
            own = (lane < 64) == (side == 0)
            spare = spare_lane(first_head + pair * 2 + side)
            added = jnp.logical_and(line > spare, line < spare + 4)
            ones = jnp.where(added, 1.0, 0.0).astype(BF16)
            chosen = jnp.where(own, queries, log_ref[0])
            masked = jnp.where(own, keys, jnp.where(lane == spare, dead, ones))
            drawn = jnp.where(own, out_grads, deltas)
            weighed = jnp.where(own, values, ones)
            ready[pair, side] = (chosen, masked, drawn, weighed)

    def first_pass(slot, pair, side, half):
        chosen, masked, _, _ = ready[pair, side]
        raw = mm(masked, chosen[span_of(half, 256), :], NT)
        for tile in range(4):
            first = (3 - tile) * 128 + half * 256
            rows = span_of(tile, 128)
            part = jnp.exp(
                raw[rows, :] + strips[first_head + pair * 2 + side, :, first : first + 256]
            )
            probs[slot, rows, :] = part
            weights[slot, rows, :] = part.astype(BF16)

    def second_pass(slot, pair, side, half):
        _, _, drawn, weighed = ready[pair, side]
        head = pair * 2 + side
        slope = mm(weighed, drawn[span_of(half, 256), :], NT)
        product = [probs[slot, span_of(tile, 128), :] * slope[span_of(tile, 128), :] for tile in range(4)]
        for tile in range(4):
            scored[slot, span_of(tile, 128), :] = product[tile].astype(BF16)
        for diagonal in range(5):
            first = (3 - diagonal + 1) * 128 + half * 256
            total = None
            for tile in range(4):
                column = tile - diagonal + 1
                if 0 <= column < 2:
                    block = product[tile][:, span_of(column, 128)]
                    total = block if total is None else total + block
            sums[head, :, first : first + 128] += total

    def third_pass(slot, pair, side, half):
        span = span_of(pair, 128)
        rows = span_of(half, 256)
        turned_query = mm(ready[pair], scored[slot])
        grad_key = mm(scored[slot], query_ref[0, rows, span])
        grad_value = mm(weights[slot], outer[rows, span])
        if half == 0:
            found[side] = ([turned_query], grad_key, grad_value)
        else:
            before = found[side]
            found[side] = (
                before[0] + [turned_query],
                before[1] + grad_key,
                before[2] + grad_value,
            )
        if side == 1 and half == 1:
            for index in range(2):
                both = jnp.concatenate(
                    (found[0][0][index][0:64, :], found[1][0][index][64:128, :]), axis=0
                ).astype(BF16)
                grads[
                    pl.ds(pl.multiple_of(step * BLOCKS + index * 256, 256), 256), span
                ] = jnp.transpose(both)
            for index in range(1, 3):
                first = index * 256 + pair * 128
                grads[here, first : first + 128] = jnp.where(
                    lane < 64, found[0][index], found[1][index]
                ).astype(BF16)

    units = [(pair, side, half) for pair in range(2) for side in range(2) for half in range(2)]
    for index in range(len(units) + 2):
        if index < len(units):
            if index % 4 == 0:
                prepare(units[index][0])
            first_pass(index % 4, *units[index])
        if 1 <= index <= len(units):
            second_pass((index - 1) % 4, *units[index - 1])
        if index >= 2:
            third_pass((index - 2) % 4, *units[index - 2])

    wide = pooled[...].astype(F32)
    scale = inverse_rms(wide)
    unit = wide * scale
    normed = (unit * gain_attn_ref[...]).astype(BF16)
    turned[:, here] = jnp.transpose(normed)
    turned_branch[:, here] = jnp.transpose(branch)
    atts[here, :] = att_ref[0]

    @pl.when(step == 1)
    def _():
        new = mm(turned[...], grads[...])
        new_out = mm(turned_branch[...], atts[...])
        for part, targets in ((1, send_ref), (0, keep_ref)):
            for shard in range(SHARDS):
                at = lax.bitwise_xor(place, shard)
                if isinstance(targets, tuple):
                    target, at = targets[shard % 2], lax.shift_right_logical(at, 1)
                else:
                    target = targets
                at = tile_at(at, 64)
                here_rows = span_of(shard, 64)
                for index in range(3):
                    first = index * 256 + part * 128
                    target[at, span_of(index, 128)] = new[here_rows, first : first + 128].astype(
                        BF16
                    )
                target[at, 384:512] = new_out[here_rows, span_of(part, 128)].astype(BF16)

    grad_normed = (
        mm(grads[here, 0:256], wq_ref[...], NT)
        + mm(grads[here, 256:512], wk_ref[...], NT)
        + mm(grads[here, 512:768], wv_ref[...], NT)
    )
    return unit, scale, grad_normed


def fold_bias(sums, collect_ref):
    rows = []
    for head in range(4):
        folded = jnp.concatenate((sums[head], jnp.zeros((128, 128), F32)), axis=1)
        size = 64
        while size >= 8:
            folded = folded[:size] + pltpu.roll(folded[size : 2 * size], WRAP - size, 1)
            size //= 2
        rows.append(folded)
    lines = jnp.concatenate(triple(jnp.concatenate(rows, axis=0)), axis=0)
    found = mm(lines, collect_ref[...])
    found = found[0:32] + found[32:64] + found[64:96]
    row = lax.broadcasted_iota(jnp.int32, found.shape, 0) & 7
    spot = lax.shift_right_logical(lax.broadcasted_iota(jnp.int32, found.shape, 1), 5)
    found = jnp.where(row == spot, found, 0.0)
    rows = []
    for head in range(4):
        total = jnp.sum(found[span_of(head, 8), :], axis=0, keepdims=True)
        total = total[:, 0:128] + total[:, 128:256]
        total = total + pltpu.roll(total, 64, 1)
        rows.append(total + pltpu.roll(total, 32, 1))
    return jnp.concatenate(rows + rows, axis=0)


def attention_back_first_kernel(info, *refs):
    heads, (grad_ref, keep_ref, send_ref, rel_ref), scratch = refs[:15], refs[15:19], refs[19:]
    _, _, grad_normed = attention_back_body(info, 4, *heads, keep_ref, send_ref, *scratch)
    grad_ref[0] = grad_normed

    @pl.when(pl.program_id(0) == 1)
    def _():
        rel_ref[...] = fold_bias(scratch[3], heads[9])


def attention_back_second_kernel(info, *refs):
    heads, (held_ref, rel_ref, gain_mid_ref), refs = refs[:15], refs[15:18], refs[18:]
    (keep_rows, send_rows, keep_ref, even_ref, odd_ref, tiny_ref), scratch = refs[:6], refs[6:]
    send_ref = (even_ref, odd_ref)
    scratch, acc_gain = scratch[:-1], scratch[-1]
    unit, scale, grad_normed = attention_back_body(info, 0, *heads, keep_ref, send_ref, *scratch)
    mp, core = info[0], info[1]
    step = pl.program_id(0)
    pooled = scratch[0]
    grad_normed = grad_normed + held_ref[0]
    scaled = grad_normed * heads[10][...]
    grad_pooled = heads[7][0] + scale * (
        scaled - unit * jnp.mean(scaled * unit, axis=1, keepdims=True)
    )
    pooled[...] = grad_pooled.astype(BF16)
    keep_rows[0] = pooled[:, tile_at(mp, 256)]
    send_rows[tile_at(step, BLOCKS), :] = pooled[:, tile_at(1 - mp, 256)]
    new_gain = jnp.sum(grad_normed * unit, axis=0, keepdims=True)

    @pl.when(step == 0)
    def _():
        acc_gain[...] = jnp.broadcast_to(new_gain, acc_gain.shape)

    @pl.when(step == 1)
    def _():
        found = fold_bias(scratch[3], heads[9])
        line = lax.broadcasted_iota(jnp.int32, (8, 128), 0)
        rows = jnp.zeros((8, 128), F32)
        for head in range(8):
            source = found if head < 4 else rel_ref[...]
            true_head = (
                lax.bitwise_xor(mp, head // 4) * 4
                + lax.bitwise_xor(core, (head // 2) % 2) * 2
                + head % 2
            )
            rows = jnp.where(line == true_head, source[head % 4 : head % 4 + 1, :], rows)
        tiny_ref[...] = jnp.zeros_like(tiny_ref)
        tiny_ref[0:1, :] = acc_gain[0:1, :] + new_gain
        tiny_ref[1:2, :] = gain_mid_ref[0:1, :]
        tiny_ref[8:16, 0:128] = rows


def attention_back(
    info, mine, rows_args, strips, collect, gain_attn, joined, w_o, given, after
):
    own, other, qkv, logs, att, grad_mid = rows_args
    half = own.shape[0]
    where = 0 if mine else 1

    def lanes(index):
        return pl.BlockSpec((1, BLOCKS, 256), lambda i, info: (i, 0, index))

    def columns(index):
        return pl.BlockSpec((512, 256), lambda i, info: (0, index))

    in_specs = [
        item((BLOCKS, 256)),
        pl.BlockSpec((BLOCKS, 256), lambda i, info: (i, 0)),
        lanes(where),
        lanes(2 + where),
        lanes(4 + where),
        item((BLOCKS, 128)),
        lanes(where),
        item((BLOCKS, 512)),
        NEAR,
        whole((WRAP, 256)),
        whole((1, 512)),
        columns(where),
        columns(2 + where),
        columns(4 + where),
        pl.BlockSpec((256, 512), lambda i, info: (where, 0)),
    ]
    args = [own, other, qkv, qkv, qkv, logs, att, grad_mid, strips, collect, gain_attn]
    args += [joined, joined, joined, w_o]
    packed = (SHARDS * 64, 512)
    pack = jax.ShapeDtypeStruct(packed, BF16)
    scratch = [
        pltpu.VMEM((BLOCKS, 512), BF16),
        pltpu.VMEM((BLOCKS, 256), BF16),
        pltpu.VMEM((half * BLOCKS, 768), BF16),
        pltpu.VMEM((4, 128, 896), F32),
        pltpu.VMEM((512, half * BLOCKS), BF16),
        pltpu.VMEM((512, half * BLOCKS), BF16),
        pltpu.VMEM((half * BLOCKS, 256), BF16),
        pltpu.VMEM((4, BLOCKS, 256), F32),
        pltpu.VMEM((4, BLOCKS, 256), BF16),
        pltpu.VMEM((4, BLOCKS, 256), BF16),
    ]
    if mine:
        share = jax.ShapeDtypeStruct((half, BLOCKS, 256), BF16)
        in_specs += [item((BLOCKS, 512)), whole((8, 128)), whole((8, 512))]
        sent = jax.ShapeDtypeStruct((half * BLOCKS, 256), BF16)
        few = (SHARDS * 32, 512)
        packs = [pack, jax.ShapeDtypeStruct(few, BF16), jax.ShapeDtypeStruct(few, BF16)]
        outs = [share, sent, *packs, jax.ShapeDtypeStruct((16, 512), F32)]
        out_specs = [item((BLOCKS, 256)), whole(sent.shape), whole(packed), whole(few), whole(few)]
        out_specs += [whole((16, 512))]
        scratch += [pltpu.VMEM((8, 512), F32)]
    else:
        outs = [
            jax.ShapeDtypeStruct((half, BLOCKS, 512), F32),
            pack,
            pack,
            jax.ShapeDtypeStruct((8, 128), F32),
        ]
        out_specs = [item((BLOCKS, 512)), whole(packed), whole(packed), whole((8, 128))]
    return launch(
        attention_back_second_kernel if mine else attention_back_first_kernel,
        "attention_back_own" if mine else "attention_back_other",
        17,
        half,
        info,
        (*args, *given),
        in_specs,
        outs,
        out_specs,
        scratch,
        after,
    )


def place_kernel(info, ff_near, ff_far, hid_ref, mid_ref, mark):
    mark[...] = jnp.zeros_like(mark)
    core, place = info[1], info[3]
    for source, side in ((ff_near, core), (ff_far, 1 - core)):
        turned = []
        for shard in range(SHARDS):
            at = lax.bitwise_xor(place, shard)
            at = at * 2
            hid_ref[span_of(shard, 64), tile_at(side, 512)] = source[tile_at(at, 64), :].astype(F32)
            turned.append(source[tile_at(at + 1, 64), :])
        mid_ref[tile_at(side, 512), :] = jnp.transpose(
            jnp.concatenate(turned, axis=0).astype(F32)
        )


def pack_kernel(wq, wk, wv, wo, wh, rel, out, sems):
    near = lax.axis_index("near")
    core, way = lax.rem(near, 2), lax.div(near, 2)
    rows = tile_at(way, 256)
    pairs = []
    for index, weight in enumerate((wq, wk, wv)):
        lanes = pl.ds(index * 128, 128)
        pairs.append((weight.at[rows, tile_at(core, 128)], out.at[pl.ds(0, 256), lanes]))
    few = pl.ds(pl.multiple_of(core * 128 + way * 64, 64), 64)
    for lane in range(4):
        pairs.append(
            (
                wo.at[few, pl.ds(lane * 128, 128)],
                out.at[pl.ds(lane * 64, 64), pl.ds(384, 128)],
            )
        )
    pairs.append((wh.at[rows, tile_at(core, 512)], out.at[pl.ds(256, 256), :]))
    copies = started(pairs, sems)
    for copy in copies:
        copy.start()
    out[512:528, :] = jnp.zeros((16, 512), BF16)
    for index, part in enumerate(triple(rel[...])):
        out[512:516, index * 128 : index * 128 + BUCKETS] = part
    for copy in copies:
        copy.wait()


def pack(weights, rel):
    return pl.pallas_call(
        pack_kernel,
        grid=(1,),
        in_specs=[HBM] * 5 + [pl.BlockSpec(rel.shape, lambda i: (0, 0))],
        out_specs=pl.BlockSpec((528, 512), lambda i: (0, 0)),
        out_shape=jax.ShapeDtypeStruct((528, 512), BF16),
        scratch_shapes=[pltpu.SemaphoreType.DMA((8,))],
        compiler_params=pltpu.CompilerParams(
            vmem_limit_bytes=VMEM_MOST, dimension_semantics=("arbitrary",)
        ),
        cost_estimate=cost(1),
        name="pack",
    )(*weights[:5], rel)


def pack_more_kernel(info, wm, cot, mid_out, cot_out, cot_own, sems):
    mine, theirs = share_out(info)
    pairs = [(wm.at[tile_at(info[1], 512), :], mid_out)]
    for index in range(2):
        pairs.append((cot.at[theirs[index]], cot_out.at[index, pl.ds(0, BLOCKS), :]))
        pairs.append((cot.at[mine[index]], cot_own.at[index]))
    copies = started(pairs, sems)
    for copy in copies:
        copy.start()
    cot_out[:, BLOCKS:, :] = jnp.zeros((2, 32, cot_out.shape[2]), BF16)
    for copy in copies:
        copy.wait()


def pack_more(info, w_mlp, cotangent, after):
    half, share = cotangent.shape[0] // 2, cotangent.shape[2]
    outs = [jax.ShapeDtypeStruct((512, 512), BF16)]
    outs += [jax.ShapeDtypeStruct((half, rows, share), BF16) for rows in (BLOCKS + 32, BLOCKS)]
    return launch(
        pack_more_kernel,
        "pack_more",
        1,
        1,
        info,
        (w_mlp, cotangent),
        [HBM] * 2,
        outs,
        [whole(x.shape) for x in outs],
        [pltpu.SemaphoreType.DMA((5,))],
        after,
        vmem=VMEM_MOST,
    )


def final_kernel(
    info,
    near,
    far,
    mine_ref,
    theirs_ref,
    pos_ref,
    frontier_ref,
    blocks_kept,
    blocks_got,
    query_ref,
    key_ref,
    value_ref,
    out_ref,
    front_ref,
    gain_attn_ref,
    gain_mlp_ref,
    rel_ref,
    blocks_ref,
    sems,
):
    mp, core, place = info[0], info[1], info[3]
    pairs = []
    mine, theirs = share_out(info)
    for index in range(2):
        pairs.append((blocks_kept.at[index], blocks_ref.at[mine[index]]))
        pairs.append((blocks_got.at[index], blocks_ref.at[theirs[index]]))
    copies = started(pairs, sems)
    for copy in copies:
        copy.start()
    for source, side in ((near, core), (far, 1 - core)):
        turned = []
        for shard in range(SHARDS):
            at = tile_at(lax.bitwise_xor(place, shard), 64)
            for index, target in enumerate((query_ref, key_ref, value_ref)):
                target[span_of(shard, 64), tile_at(side, 128)] = source[
                    at, span_of(index, 128)
                ].astype(F32)
            turned.append(source[at, 384:512])
        out_ref[tile_at(side, 128), :] = jnp.transpose(
            jnp.concatenate(turned, axis=0).astype(F32)
        )
    tiny = near[512:528, :].astype(F32) + far[512:528, :].astype(F32)
    gain_attn_ref[...] = tiny[0:1, :]
    gain_mlp_ref[...] = tiny[1:2, :]
    heads = jnp.where(mp == 0, tiny[8:12, 0:128], tiny[12:16, 0:128])
    rel_ref[...] = heads[:, 0:BUCKETS]
    frontier_kernel(info, mine_ref, theirs_ref, pos_ref, frontier_ref, front_ref)
    for copy in copies:
        copy.wait()


def finish(
    info, near, far, mine, theirs, positions, frontier, blocks_kept, blocks_got, after
):
    args = (near, far, mine, theirs, positions, frontier)
    square = jax.ShapeDtypeStruct((512, 256), F32)
    row = jax.ShapeDtypeStruct((1, 512), F32)
    outs = [square, square, square, jax.ShapeDtypeStruct((256, 512), F32)]
    outs += [jax.ShapeDtypeStruct(frontier.shape, F32), row, row]
    outs += [jax.ShapeDtypeStruct((4, BUCKETS), F32)]
    return launch(
        final_kernel,
        "finish",
        4,
        1,
        info,
        (*args, blocks_kept, blocks_got),
        [whole(x.shape) for x in args] + [ANY] * 2,
        outs + [jax.ShapeDtypeStruct((4,) + blocks_kept.shape[1:], BF16)],
        [whole(x.shape) for x in outs] + [HBM],
        [pltpu.SemaphoreType.DMA((4,))],
        after,
    )


def ff_place(info, near, far, shapes, after):
    return launch(
        place_kernel,
        "ff_place",
        4,
        1,
        info,
        (near, far),
        [NEAR, NEAR],
        [jax.ShapeDtypeStruct(shape, F32) for shape in shapes],
        [whole(shape) for shape in shapes],
        (),
        after,
    )


def shards(
    devices,
    byte_states,
    frontier,
    lengths,
    gain_attn,
    w_query,
    w_key,
    w_value,
    w_attn_out,
    rel_bias,
    gain_mlp,
    w_hidden,
    w_mlp_out,
    cotangent,
):
    bits = devices.bit_length() - 1
    mp = lax.axis_index("mp").astype(jnp.int32)
    dp = lax.axis_index(("far", "near")).astype(jnp.int32)
    core = dp & 1
    way = (dp >> 1) & 1
    place = (((dp >> 1) & 1) << 2) | (((dp >> 2) & 1) << 1)
    info = jnp.concatenate((jnp.stack((mp, core, way, place)), lengths))

    def across(value):
        return lax.ppermute(value, "mp", [(0, 1), (1, 0)])

    def swap(value, bit):
        pairs = [(i, i ^ (1 << bit)) for i in range(devices)]
        return lax.ppermute(value, ("far", "near"), pairs)

    def swap_four(value, index):
        turn = ((index & 1) << 2) | ((index >> 1) << 1)
        return lax.ppermute(value, ("far", "near"), [(i, i ^ turn) for i in range(devices)])

    def rows(count):
        return ((count, 512), BF16)

    weights = (w_query, w_key, w_value, w_attn_out, w_hidden, w_mlp_out)
    rel_own = rel_bias.T
    first_sent = pack(weights, rel_own)
    first = across(first_sent)
    backward, collect = offset_tables()
    backward, collect = jnp.asarray(backward), jnp.asarray(collect, BF16)

    pooled_own, pooled_sent, positions, meta = pool_forward(
        info, frontier, byte_states, (first_sent,)
    )
    pooled_other = across(pooled_sent)
    (first,) = combine("meet", nothing, after=(pooled_sent,), through=(first,))
    second = swap(first, 1)
    mid_sent, cot_sent, cot_own = pack_more(info, w_mlp_out, cotangent, (pooled_sent,))

    strips = bias_strips(info, rel_own, first, backward, (cot_own,))
    second, mid_sent = combine(
        "meet", nothing, after=(pooled_other, strips), through=(second, mid_sent)
    )
    parts = (first, second, swap(first, 0), swap(second, 0))
    cot_other = across(cot_sent)
    mid_first = across(mid_sent)

    gain_attn_row = gain_attn.reshape(1, -1)
    gain_mlp_row = gain_mlp.reshape(1, -1)
    qkv, logs, att, middle, normed, joined, w_o = attention_forward(
        info,
        pooled_own,
        pooled_other,
        strips,
        gain_attn_row,
        gain_mlp_row,
        weights[:4],
        parts,
        (),
    )
    half = pooled_own.shape[0]
    normed = normed.reshape(half * BLOCKS, -1)
    middle = middle.reshape(half * BLOCKS, -1)

    result, back, near_keep, near_sent, mark = ff_call(
        info, normed, cot_own, cot_other, True, (w_hidden, w_mlp_out), ()
    )
    got_near = swap(near_sent, 0)
    (mid_first,) = combine("meet", nothing, after=(mark,), through=(mid_first,))
    blocks_kept, blocks_sent, grad_mid, far_keep, far_sent, gain_mid = ff_call(
        info,
        normed,
        cot_own,
        cot_other,
        False,
        (*parts, mid_first, swap(mid_first, 0), result, back, middle, gain_mlp_row),
        (),
    )
    near_low, near_high, far_sent = combine(
        "near_cores",
        sum_into,
        (near_keep, got_near),
        (rows(512), rows(528)),
        (gain_mid,),
        (far_sent,),
    )
    far_low, far_high, near_high = combine(
        "far_cores",
        sum_into,
        (far_keep, swap(far_sent, 0)),
        (rows(512), rows(512)),
        (),
        (near_high,),
    )
    got_far = swap(far_high, 1)
    blocks_other = across(blocks_sent)

    grad_mid = grad_mid.reshape(half, BLOCKS, -1)
    rows_args = (pooled_own, pooled_other, qkv, logs, att, grad_mid)
    grad_normed, far_keep, far_sent, far_rel = attention_back(
        info,
        False,
        rows_args,
        strips,
        collect,
        gain_attn_row,
        joined,
        w_o,
        (),
        (far_low,),
    )
    far_ff, far_sent, near_high = combine(
        "far_y", sum_into, (far_low, got_far), (rows(528),), (far_rel, blocks_other), (far_sent, near_high)
    )
    got_near = swap(near_high, 1)
    far_attn, far_ff = combine(
        "far_cores", sum_into, (far_keep, swap(far_sent, 0)), (rows(544),), (), (far_ff,)
    )
    got_attn = across(far_attn)
    got_far = across(far_ff)
    grad_keep, grad_sent, near_keep, near_even, near_odd, tiny = attention_back(
        info,
        True,
        rows_args,
        strips,
        collect,
        gain_attn_row,
        joined,
        w_o,
        (grad_normed, far_rel, gain_mid),
        (far_attn,),
    )
    grad_other = across(grad_sent)

    def step_zero(ins, outs):
        for index in range(4):
            for odd in range(2):
                at = span_of(index * 2 + odd, 64)
                total = ins[0][at, :].astype(F32) + ins[1 + odd][span_of(index, 64), :].astype(F32)
                outs[index][span_of(odd, 64), :] = (total + ins[3][at, :].astype(F32)).astype(BF16)
            outs[index][128:144, :] = ins[4][...].astype(BF16)

    attn_parts = combine(
        "step_zero",
        step_zero,
        (near_keep, swap(near_even, 0), swap(near_odd, 0), got_attn, tiny),
        (rows(144),) * 4,
        (got_near,),
    )
    got_attn = [swap_four(attn_parts[index], index) for index in range(1, 4)]

    def pool_item(mine, index, held, after, through=()):
        grads = grad_keep if mine else grad_other
        return pool_backward(
            info, meta, positions, byte_states, grads, mine, index, held, after, through
        )

    held = pool_item(True, 0, (), (attn_parts[0],))

    ff_low, ff_high = combine(
        "ff_sum", sum_into, (near_low, got_near, got_far), (rows(256), rows(256)), (held[1],)
    )
    got_ff = swap(ff_high, 2)
    (attn,) = combine(
        "step_one", sum_into, (attn_parts[0], *got_attn), (rows(144),), (held[1],)
    )
    for bit in range(4, bits):
        attn = (attn.astype(F32) + swap(attn, bit).astype(F32)).astype(BF16)
    got_attn = swap(attn, 3)

    def step_two(ins, outs):
        total = ins[0][...].astype(F32) + ins[1][...].astype(F32)
        outs[0][...] = total[0:128, :].astype(BF16)
        outs[1][...] = total[128:144, :].astype(BF16)
        sum_into(ins[2:], outs[2:])

    held = pool_item(True, 1, held, (attn,))
    attn, tiny, near_ff = combine(
        "step_two",
        step_two,
        (attn, got_attn, ff_low, got_ff),
        (rows(128), rows(16), rows(256)),
        (held[1],),
    )
    got_ff = swap(near_ff, 3)
    got_attn = [swap_four(attn, index) for index in range(1, 4)]
    got_tiny = across(tiny)

    def step_three(ins, outs):
        join_into(ins[:4], outs[0])
        sum_into(ins[4:6], [outs[0].at[512:528, :]])
        sum_into(ins[6:], outs[1:])

    held = pool_item(False, 0, held, (attn,))
    near_attn, near_ff = combine(
        "step_three",
        step_three,
        (attn, *got_attn, tiny, got_tiny, near_ff, got_ff),
        (rows(528), rows(256)),
        (held[1],),
    )
    for bit in range(4, bits):
        near_ff = (near_ff.astype(F32) + swap(near_ff, bit).astype(F32)).astype(BF16)
    got_ff = [swap_four(near_ff, index) for index in range(1, 4)]
    far_attn = swap(near_attn, 0)

    held = pool_item(False, 1, held, (near_attn, near_ff))
    grad_bytes, part = held
    part_other = across(part)
    (
        grad_query,
        grad_key,
        grad_value,
        grad_out,
        grad_frontier,
        grad_gain_attn,
        grad_gain_mlp,
        grad_rel,
        blocks_out,
    ) = finish(
        info,
        near_attn,
        far_attn,
        part,
        part_other,
        positions,
        frontier,
        blocks_kept,
        blocks_other,
        (),
    )

    def join(ins, outs):
        join_into(ins, outs[0])

    (near_ff,) = combine("step_four", join, (near_ff, *got_ff), (rows(1024),), (grad_gain_attn,))
    far_ff = swap(near_ff, 0)
    grad_hidden, grad_mlp, _ = ff_place(
        info, near_ff, far_ff, (w_hidden.shape, w_mlp_out.shape, (8, 128)), ()
    )
    return (
        blocks_out,
        grad_bytes,
        grad_frontier,
        grad_gain_attn.reshape(-1),
        grad_query,
        grad_key,
        grad_value,
        grad_out,
        grad_rel.T,
        grad_gain_mlp.reshape(-1),
        grad_hidden,
        grad_mlp,
    )


def solution(mesh):
    devices = mesh.shape["dp"]
    split = jax.sharding.Mesh(
        mesh.devices.reshape(devices // 4, 4, mesh.shape["mp"]), ("far", "near", "mp")
    )
    dp = ("far", "near")
    placed = (
        P(dp, None, "mp"),
        P(dp, None),
        P(dp),
        P(),
        P(None, "mp"),
        P(None, "mp"),
        P(None, "mp"),
        P("mp", None),
        P(None, "mp"),
        P(),
        P(None, "mp"),
        P("mp", None),
        P(dp, None, "mp"),
    )
    return jax.shard_map(
        functools.partial(shards, devices),
        mesh=split,
        in_specs=placed,
        out_specs=(
            P(dp, None, "mp"),
            P(dp, None, "mp"),
            P(dp, None),
            P(),
            P(None, "mp"),
            P(None, "mp"),
            P(None, "mp"),
            P("mp", None),
            P(None, "mp"),
            P(),
            P(None, "mp"),
            P("mp", None),
        ),
        check_vma=False,
    )
```
